32 devices in a mesh: dp: 4 (over x, core), pix: 8 (over z, y).
Axes of the slice: x: 2, y: 2, z: 4, core: 2. Of those that a mesh axis runs over, the one named last changes fastest.
Arguments:
- image_sides: int32 [4, 2, 8], P('dp'), may hold values from 32 to 64, as said below
- pixels: bfloat16 [4, 2, 32768, 261], P('dp', None, 'pix'), may hold values from -6 to 6
- latent_array: bfloat16 [512, 1024], P('pix'), may hold values from -6 to 6
- pixel_gain: bfloat16 [261], replicated, may hold values from 0.099609375 to 1.8984375
- latent_gain: bfloat16 [1024], P('pix'), may hold values from 0.099609375 to 1.8984375
- query_weight: bfloat16 [1024, 1024], P('pix'), may hold values from -0.1875 to 0.1875
- key_weight: bfloat16 [261, 1024], P(None, 'pix'), may hold values from -0.375 to 0.375
- value_weight: bfloat16 [261, 1024], P(None, 'pix'), may hold values from -0.375 to 0.375
- cross_out_weight: bfloat16 [1024, 1024], P('pix'), may hold values from -6 to 6
- cross_mlp_gain: bfloat16 [1024], P('pix'), may hold values from 0.099609375 to 1.8984375
- cross_mlp_in: bfloat16 [1024, 1024], P('pix'), may hold values from -0.1875 to 0.1875
- cross_mlp_out: bfloat16 [1024, 1024], P('pix'), may hold values from -0.1875 to 0.1875
- self_gain: bfloat16 [1024], P('pix'), may hold values from 0.099609375 to 1.8984375
- self_qkv_weight: bfloat16 [1024, 3072], P('pix'), may hold values from -0.1875 to 0.1875
- self_out_weight: bfloat16 [1024, 1024], P('pix'), may hold values from -3 to 3
- self_mlp_gain: bfloat16 [1024], P('pix'), may hold values from 0.099609375 to 1.8984375
- self_mlp_in: bfloat16 [1024, 1024], P('pix'), may hold values from -0.1875 to 0.1875
- self_mlp_out: bfloat16 [1024, 1024], P('pix'), may hold values from -0.1875 to 0.1875
- cotangent: bfloat16 [4, 2, 8, 512, 1024], P('dp', None, None, 'pix'), may hold values from -6 to 6
Outputs:
- latent_out: bfloat16 [4, 2, 8, 512, 1024], P('dp', None, None, 'pix')
- pixel_grad: float32 [4, 2, 32768, 261], P('dp', None, 'pix')
- latent_grad: float32 [512, 1024], P('pix')
- pixel_gain_grad: float32 [261], replicated
- latent_gain_grad: float32 [1024], P('pix')
- query_grad: float32 [1024, 1024], P('pix')
- key_grad: float32 [261, 1024], P(None, 'pix')
- value_grad: float32 [261, 1024], P(None, 'pix')
- cross_out_grad: float32 [1024, 1024], P('pix')
- cross_mlp_gain_grad: float32 [1024], P('pix')
- cross_mlp_in_grad: float32 [1024, 1024], P('pix')
- cross_mlp_out_grad: float32 [1024, 1024], P('pix')
- self_gain_grad: float32 [1024], P('pix')
- self_qkv_grad: float32 [1024, 3072], P('pix')
- self_out_grad: float32 [1024, 1024], P('pix')
- self_mlp_gain_grad: float32 [1024], P('pix')
- self_mlp_in_grad: float32 [1024, 1024], P('pix')
- self_mlp_out_grad: float32 [1024, 1024], P('pix')
The draws below stay inside these ranges and needn't reach their ends.
Inputs may be any that keep to these rules, and one draw needn't show every extreme that they name: `image_sides`: every side is 64 // 4 times 2, 3 or 4; each group (one index of dp, one micro-batch) holds at least one image of side 64 and one of side 64 // 2.
All inputs are finite; a program needn't handle non-finite values.
Results may differ from the reference program's by a relative error of at most 0.034.
Values may be sent and summed in bfloat16 or wider, within the bound.
A program may use at most 208 MiB of HBM per device.

```python
import jax
import jax.numpy as jnp
from jax import lax

D = 1024
NLAT = 512
FEAT = 261
HEADS = 8
SIDE = 64
IMB = 8
MICRO = 2
SLOTS = 32768
N_DP = 4


def draw_image_sides(key, part):
    key = jax.random.fold_in(key, 5)
    streams = jax.random.split(key, 3)
    quarter = jax.random.randint(streams[0], (N_DP, MICRO, IMB), 2, 5)
    largest = jax.random.randint(streams[1], (N_DP, MICRO, 1), 0, IMB)
    offset = jax.random.randint(streams[2], (N_DP, MICRO, 1), 1, IMB)
    smallest = (largest + offset) % IMB
    position = jnp.arange(IMB, dtype=jnp.int32)[None, None, :]
    quarter = jnp.where(position == largest, 4, jnp.where(position == smallest, 2, quarter))
    return (quarter * (SIDE // 4)).astype(jnp.int32)


def level_of(stream_key, extent, cuts, least, top_value):
    def one(dim, parts):
        steps = jax.random.uniform(jax.random.fold_in(jax.random.fold_in(stream_key, 6), dim), (parts,), jnp.float32, least / len(cuts), top_value / len(cuts))
        return jnp.repeat(jnp.exp(steps), extent[dim] // parts).reshape((-1,) + (1,) * (len(extent) - dim - 1))

    loudness = one(*cuts[0])
    for cut in cuts[1:]:
        loudness = loudness * one(*cut)
    return loudness


def noise(stream_key, dims, spread, most, cuts=(), held_as=jnp.bfloat16):
    level = level_of(stream_key, dims, cuts, -0.22, 0.18) if cuts else 1.0
    values = jax.random.normal(stream_key, dims, jnp.float32) * spread * level
    return jnp.minimum(jnp.maximum(values, -most), most).astype(held_as)


def setup_inputs(seed: int = 0) -> dict:
    splits = jax.random.split(jax.random.key(seed), 20)
    return {
        "image_sides": draw_image_sides(jax.random.fold_in(splits[19], 71), 0),
        "pixels": noise(splits[1], (N_DP, MICRO, SLOTS, FEAT), 1.0, 6.0, ((0, 4), (2, 8))),
        "latent_array": noise(splits[2], (NLAT, D), 1.0, 6.0, ((0, 8),)),
        "pixel_gain": jnp.clip(1.0 + 0.18 * jax.random.normal(splits[3], (FEAT,), jnp.float32), 0.099609375, 1.8984375).astype(jnp.bfloat16),
        "latent_gain": jnp.clip(1.0 + 0.18 * jax.random.normal(splits[4], (D,), jnp.float32), 0.099609375, 1.8984375).astype(jnp.bfloat16),
        "query_weight": noise(splits[5], (D, D), D ** -0.5, 0.1875, ((0, 8),)),
        "key_weight": noise(splits[6], (FEAT, D), FEAT ** -0.5, 0.375, ((1, 8),)),
        "value_weight": noise(splits[7], (FEAT, D), FEAT ** -0.5, 0.375, ((1, 8),)),
        "cross_out_weight": noise(splits[8], (D, D), (max(1, D // (SIDE * SIDE // 4))) ** -0.5, 6.0, ((0, 8),)),
        "cross_mlp_gain": jnp.clip(1.0 + 0.18 * jax.random.normal(splits[9], (D,), jnp.float32), 0.099609375, 1.8984375).astype(jnp.bfloat16),
        "cross_mlp_in": noise(splits[10], (D, D), D ** -0.5, 0.1875, ((0, 8),)),
        "cross_mlp_out": noise(splits[11], (D, D), D ** -0.5, 0.1875, ((0, 8),)),
        "self_gain": jnp.clip(1.0 + 0.18 * jax.random.normal(splits[12], (D,), jnp.float32), 0.099609375, 1.8984375).astype(jnp.bfloat16),
        "self_qkv_weight": noise(splits[13], (D, 3 * D), D ** -0.5, 0.1875, ((0, 8),)),
        "self_out_weight": noise(splits[14], (D, D), (max(1, D // (NLAT // 2))) ** -0.5, 3.0, ((0, 8),)),
        "self_mlp_gain": jnp.clip(1.0 + 0.18 * jax.random.normal(splits[15], (D,), jnp.float32), 0.099609375, 1.8984375).astype(jnp.bfloat16),
        "self_mlp_in": noise(splits[16], (D, D), D ** -0.5, 0.1875, ((0, 8),)),
        "self_mlp_out": noise(splits[17], (D, D), D ** -0.5, 0.1875, ((0, 8),)),
        "cotangent": noise(splits[18], (N_DP, MICRO, IMB, NLAT, D), 1.0, 6.0, ((0, 4), (3, 8))),
    }


highest = lax.Precision.HIGHEST

@jax.custom_vjp
def low(v):
    return lax.optimization_barrier(v.astype(jnp.bfloat16)).astype(jnp.float32)

@jax.custom_vjp
def low_back(v):
    return v

def low_keep(v):
    return (low(v), None)

def low_pass(kept, grad):
    return (grad,)

def back_keep(v):
    return (v, None)

def back_low(kept, grad):
    return (low(grad),)
low.defvjp(low_keep, low_pass)
low_back.defvjp(back_keep, back_low)

def product(left, right):
    return jnp.dot(left, right, precision=highest, preferred_element_type=jnp.float32)

def layer_norm(values, gain):
    average = lax.optimization_barrier(jnp.mean(values, -1, keepdims=True))
    centered = values - average
    return centered * lax.rsqrt(lax.optimization_barrier(jnp.mean(centered * centered, -1, keepdims=True)) + 1e-05) * gain

def feed_forward(inputs, gain, w_in, w_out):
    normed = low(layer_norm(inputs, gain))
    hidden = low_back(product(normed, w_in))
    active = low(jax.nn.gelu(hidden))
    return inputs + low_back(product(active, w_out))

def cross_block(queries, keys_img, values_img, valid, latents, w_out):
    scores = low_back(product(queries, keys_img.T) * D ** (-0.5))
    masked = jnp.where(valid[None, :], scores, -1e+30)
    top = lax.optimization_barrier(jnp.max(masked, -1, keepdims=True))
    weights = jnp.where(valid[None, :], jnp.exp(masked - top), 0.0)
    total = low_back(lax.optimization_barrier(jnp.sum(weights, -1, keepdims=True)))
    summed = product(low(weights), values_img)
    attended = summed / total
    return latents + low_back(product(low(attended), w_out))

def self_block(inputs, gain, w_packed, w_out):
    normed = low(layer_norm(inputs, gain))
    packed = low(low_back(product(normed, w_packed)))
    packed = packed.reshape(NLAT, HEADS, 3, D // HEADS).transpose(2, 1, 0, 3)
    scores = low_back(jnp.einsum('hqd,hkd->hqk', packed[0], packed[1], precision=highest) * (D // HEADS) ** (-0.5))
    top = lax.optimization_barrier(jnp.max(scores, -1, keepdims=True))
    weights = jnp.exp(scores - top)
    total = lax.optimization_barrier(jnp.sum(weights, -1, keepdims=True))
    summed = jnp.einsum('hqk,hkd->hqd', low(weights), packed[2], precision=highest)
    attended = (summed / total).transpose(1, 0, 2).reshape(NLAT, D)
    return inputs + low_back(product(low(attended), w_out))

def reference(image_sides, pixels, latent_array, pixel_gain, latent_gain, query_weight, key_weight, value_weight, cross_out_weight, cross_mlp_gain, cross_mlp_in, cross_mlp_out, self_gain, self_qkv_weight, self_out_weight, self_mlp_gain, self_mlp_in, self_mlp_out, cotangent):
    group_sides = image_sides.reshape(N_DP * MICRO, IMB).astype(jnp.int32)

    def forward(pixel_data, latents, gain_pix, gain_lat, w_query, w_key, w_value, w_cross, gain_cross, cross_in, cross_out, gain_self, w_packed, w_self, gain_mlp, mlp_in, mlp_out):
        normed_lat = low(layer_norm(latents, gain_lat))
        queries = low(low_back(product(normed_lat, w_query)))
        group_pixels = pixel_data.reshape(N_DP * MICRO, SLOTS, FEAT)

        def one_group(carry, items):
            side_list, group_data = items
            counts = (side_list * side_list).astype(jnp.int32)
            starts = (jnp.cumsum(counts) - counts).astype(jnp.int32)
            normed_pix = low(layer_norm(group_data, gain_pix))
            pad_rows = jnp.zeros((SIDE * SIDE, D), jnp.float32)
            keys_all = jnp.concatenate([low(low_back(product(normed_pix, w_key))), pad_rows], 0)
            values_all = jnp.concatenate([low(low_back(product(normed_pix, w_value))), pad_rows], 0)

            def one_image(index):
                start = starts[index].astype(jnp.int32)
                keys_img = lax.dynamic_slice_in_dim(keys_all, start, SIDE * SIDE, 0)
                values_img = lax.dynamic_slice_in_dim(values_all, start, SIDE * SIDE, 0)
                valid = jnp.arange(SIDE * SIDE, dtype=jnp.int32) < counts[index]
                after = cross_block(queries, keys_img, values_img, valid, latents, w_cross)
                after = feed_forward(after, gain_cross, cross_in, cross_out)
                after = self_block(after, gain_self, w_packed, w_self)
                return feed_forward(after, gain_mlp, mlp_in, mlp_out)
            return (carry, lax.map(jax.checkpoint(one_image), jnp.arange(IMB, dtype=jnp.int32)))
        unused, result = lax.scan(jax.checkpoint(one_group), jnp.zeros((), jnp.float32), (group_sides, group_pixels))
        return result.reshape(N_DP, MICRO, IMB, NLAT, D)
    floats = [item.astype(jnp.float32) for item in (pixels, latent_array, pixel_gain, latent_gain, query_weight, key_weight, value_weight, cross_out_weight, cross_mlp_gain, cross_mlp_in, cross_mlp_out, self_gain, self_qkv_weight, self_out_weight, self_mlp_gain, self_mlp_in, self_mlp_out)]
    result, pullback = jax.vjp(forward, *floats)
    grads = pullback(cotangent.astype(jnp.float32))
    return (result.astype(jnp.bfloat16), grads[0], grads[1], grads[2], grads[3], grads[4], grads[5], grads[6], grads[7], grads[8], grads[9], grads[10], grads[11], grads[12], grads[13], grads[14], grads[15], grads[16])
```

```python
import functools

import jax
import jax.numpy as jnp
from jax import lax
from jax.experimental import pallas as pl
from jax.experimental.pallas import tpu as pltpu
from jax.sharding import PartitionSpec as P

HEADS = 8
SIDE = 64


highest = lax.Precision.HIGHEST
big_value = 1e30


def layer_norm(values, gain):
    average = jnp.mean(values, -1, keepdims=True)
    centered = values - average
    return centered * lax.rsqrt(jnp.mean(centered * centered, -1, keepdims=True) + 1e-05) * gain


def matmul(left, right):
    return jnp.dot(left, right, preferred_element_type=jnp.float32)


def left_matmul(left, right):
    return lax.dot_general(
        left, right, (((0,), (0,)), ((), ())), preferred_element_type=jnp.float32
    )


def right_matmul(left, right):
    return lax.dot_general(
        left, right, (((1,), (1,)), ((), ())), preferred_element_type=jnp.float32
    )


def norm_back(values, gain, grad):
    unused, pullback = jax.vjp(layer_norm, values, gain)
    return pullback(grad)


def mlp_forward(inputs, gain, w_in, w_out):
    normed = layer_norm(inputs, gain).astype(jnp.bfloat16)
    hidden = matmul(normed, w_in)
    active = jax.nn.gelu(hidden).astype(jnp.bfloat16)
    return (inputs + matmul(active, w_out), (normed, hidden, active))


def mlp_backward(grad, inputs, gain, w_in, w_out, kept):
    normed, hidden, active = kept
    grad_low = grad.astype(jnp.bfloat16)
    grad_out = left_matmul(active, grad_low)
    grad_active = right_matmul(grad_low, w_out)
    unused, pullback = jax.vjp(jax.nn.gelu, hidden)
    grad_hidden = pullback(grad_active)[0].astype(jnp.bfloat16)
    grad_in = left_matmul(normed, grad_hidden)
    grad_normed = right_matmul(grad_hidden, w_in)
    grad_inputs, grad_gain = norm_back(inputs, gain, grad_normed)
    return (grad + grad_inputs, grad_gain, grad_in, grad_out)


def starting_body(
    image_sides,
    pixels,
    latent_array,
    pixel_gain,
    latent_gain,
    query_weight,
    key_weight,
    value_weight,
    cross_out_weight,
    cross_mlp_gain,
    cross_mlp_in,
    cross_mlp_out,
    self_gain,
    self_qkv_weight,
    self_out_weight,
    self_mlp_gain,
    self_mlp_in,
    self_mlp_out,
    cotangent,
):
    pieces = lax.axis_size("pix")
    position = lax.axis_index("pix")
    micros = image_sides.shape[1]
    images = image_sides.shape[2]
    capacity = pixels.shape[2]
    row_count = latent_array.shape[0]
    model_width = latent_array.shape[1]
    head_size = model_width // HEADS
    unit_count = images * HEADS // pieces
    window = min(images, (capacity - 2) // (SIDE * SIDE // 4) + 2)
    cross_scale = model_width ** (-0.5)
    self_scale = head_size ** (-0.5)
    shards = (
        latent_array,
        latent_gain,
        query_weight,
        key_weight,
        value_weight,
        cross_out_weight,
        cross_mlp_gain,
        cross_mlp_in,
        cross_mlp_out,
        self_gain,
        self_qkv_weight,
        self_out_weight,
        self_mlp_gain,
        self_mlp_in,
        self_mlp_out,
    )
    lat_rows = latent_array.astype(jnp.float32)
    gain_pix = pixel_gain.astype(jnp.float32)
    grad_rows = jnp.zeros((row_count, model_width), jnp.float32)
    grad_pix_gain = jnp.zeros(gain_pix.shape, jnp.float32)
    outputs = []
    pixel_grads = []
    totals = None
    for step_index in range(micros):
        gathered = (
            lax.all_gather(shards[0], "pix", axis=0, tiled=True),
            lax.all_gather(shards[1], "pix", axis=0, tiled=True),
            lax.all_gather(shards[2], "pix", axis=0, tiled=True),
            lax.all_gather(shards[3], "pix", axis=1, tiled=True),
            lax.all_gather(shards[4], "pix", axis=1, tiled=True),
            lax.all_gather(shards[5], "pix", axis=0, tiled=True),
            lax.all_gather(shards[6], "pix", axis=0, tiled=True),
            lax.all_gather(shards[7], "pix", axis=0, tiled=True),
            lax.all_gather(shards[8], "pix", axis=0, tiled=True),
            lax.all_gather(shards[9], "pix", axis=0, tiled=True),
            lax.all_gather(shards[10], "pix", axis=0, tiled=True),
            lax.all_gather(shards[11], "pix", axis=0, tiled=True),
            lax.all_gather(shards[12], "pix", axis=0, tiled=True),
            lax.all_gather(shards[13], "pix", axis=0, tiled=True),
            lax.all_gather(shards[14], "pix", axis=0, tiled=True),
        )
        lat_full, g_lat, wq, wk, wv, wo, g_cross, w1c, w2c, g_self, wqkv, wos, g_mlp, w1s, w2s = (
            gathered
        )
        g_lat_f = g_lat.astype(jnp.float32)
        gc_f = g_cross.astype(jnp.float32)
        gs_f = g_self.astype(jnp.float32)
        gm_f = g_mlp.astype(jnp.float32)
        if step_index == 0:
            normed_lat = layer_norm(lat_full.astype(jnp.float32), g_lat_f).astype(jnp.bfloat16)
            queries = matmul(normed_lat, wq).astype(jnp.bfloat16)
        side_list = image_sides[0, step_index]
        lengths = side_list * side_list
        ends = jnp.cumsum(lengths)
        slot_ids = position * capacity + jnp.arange(capacity, dtype=jnp.int32)
        segment = jnp.sum((slot_ids[:, None] >= ends[None, :]).astype(jnp.int32), 1)
        window_ids = segment[0] + jnp.arange(window, dtype=jnp.int32)
        select = (window_ids[:, None] == jnp.arange(images, dtype=jnp.int32)[None, :]).astype(
            jnp.float32
        )
        in_window = segment[None, :] == window_ids[:, None]
        raw_pixels = pixels[0, step_index].astype(jnp.float32)
        normed_pix = layer_norm(raw_pixels, gain_pix).astype(jnp.bfloat16)
        pixel_keys = matmul(normed_pix, wk).astype(jnp.bfloat16)
        pixel_values = matmul(normed_pix, wv).astype(jnp.bfloat16)
        scores = right_matmul(queries, pixel_keys) * cross_scale
        local_top = jnp.max(jnp.where(in_window[:, None, :], scores[None], -big_value), 2)
        image_top = jnp.max(jnp.where(select[:, :, None] > 0, local_top[:, None, :], -big_value), 0)
        image_top = lax.pmax(image_top, "pix")
        window_top = jnp.einsum("wb,br->wr", select, image_top, precision=highest)
        weights = jnp.where(
            in_window[:, None, :], jnp.exp(scores[None] - window_top[:, :, None]), 0.0
        )
        partial_den = jnp.sum(weights, 2)
        partial_num = jnp.einsum(
            "wrc,cd->wrd",
            weights.astype(jnp.bfloat16),
            pixel_values,
            preferred_element_type=jnp.float32,
        )
        full_num = jnp.einsum("wb,wrd->brd", select, partial_num, precision=highest)
        full_den = jnp.einsum("wb,wr->br", select, partial_den, precision=highest)
        num_rows, den_rows = (
            lax.psum_scatter(
                full_num.astype(jnp.bfloat16), "pix", scatter_dimension=1, tiled=True
            ).astype(jnp.float32),
            lax.psum_scatter(
                full_den.astype(jnp.bfloat16), "pix", scatter_dimension=1, tiled=True
            ).astype(jnp.float32),
        )
        attended = num_rows / den_rows[:, :, None]
        attended_low = attended.astype(jnp.bfloat16).reshape(images * row_count, model_width)
        start_rows = jnp.broadcast_to(lat_rows[None], (images, row_count, model_width)).reshape(
            images * row_count, model_width
        )
        after_cross = start_rows + matmul(attended_low, wo)
        after_mlp, cross_kept = mlp_forward(after_cross, gc_f, w1c, w2c)
        normed_self = layer_norm(after_mlp, gs_f).astype(jnp.bfloat16)
        packed = matmul(normed_self, wqkv).astype(jnp.bfloat16)
        packed = packed.reshape(images, row_count, HEADS, 3 * head_size).transpose(0, 2, 1, 3)
        packed = packed.reshape(pieces, unit_count, row_count, 3 * head_size)
        packed = lax.all_to_all(packed, "pix", split_axis=0, concat_axis=2, tiled=True)[0]
        head_query = packed[:, :, :head_size]
        head_key = packed[:, :, head_size : 2 * head_size]
        head_value = packed[:, :, 2 * head_size :]
        self_scores = (
            jnp.einsum("uqd,ukd->uqk", head_query, head_key, preferred_element_type=jnp.float32)
            * self_scale
        )
        self_top = jnp.max(self_scores, 2, keepdims=True)
        self_weights = jnp.exp(self_scores - self_top)
        self_den = jnp.sum(self_weights, 2, keepdims=True)
        self_num = jnp.einsum(
            "uqk,ukd->uqd",
            self_weights.astype(jnp.bfloat16),
            head_value,
            preferred_element_type=jnp.float32,
        )
        self_out = self_num / self_den
        returned = lax.all_to_all(
            self_out.astype(jnp.bfloat16), "pix", split_axis=1, concat_axis=0, tiled=True
        )
        returned = (
            returned.reshape(images, HEADS, row_count, head_size)
            .transpose(0, 2, 1, 3)
            .reshape(images * row_count, model_width)
        )
        after_self = after_mlp + matmul(returned, wos)
        final, final_kept = mlp_forward(after_self, gm_f, w1s, w2s)
        outputs.append(final.astype(jnp.bfloat16).reshape(images, row_count, model_width))
        grad = cotangent[0, step_index].astype(jnp.float32).reshape(images * row_count, model_width)
        grad, d_gm, d_w1s, d_w2s = mlp_backward(grad, after_self, gm_f, w1s, w2s, final_kept)
        grad_low = grad.astype(jnp.bfloat16)
        d_wos = left_matmul(returned, grad_low)
        grad_self = right_matmul(grad_low, wos)
        grad_self = grad_self.reshape(images, row_count, HEADS, head_size).transpose(0, 2, 1, 3)
        grad_self = grad_self.reshape(pieces, unit_count, row_count, head_size)
        grad_self = lax.all_to_all(
            grad_self.astype(jnp.bfloat16), "pix", split_axis=0, concat_axis=2, tiled=True
        ).astype(grad_self.dtype)[0]
        grad_num = (grad_self / self_den).astype(jnp.bfloat16)
        grad_den = -jnp.sum(grad_self * self_out, 2, keepdims=True) / self_den
        again_scores = (
            jnp.einsum("uqd,ukd->uqk", head_query, head_key, preferred_element_type=jnp.float32)
            * self_scale
        )
        again_weights = jnp.exp(again_scores - self_top)
        grad_weights = (
            jnp.einsum("uqd,ukd->uqk", grad_num, head_value, preferred_element_type=jnp.float32)
            + grad_den
        )
        grad_scores = (again_weights * grad_weights).astype(jnp.bfloat16)
        grad_query = (
            jnp.einsum("uqk,ukd->uqd", grad_scores, head_key, preferred_element_type=jnp.float32)
            * self_scale
        )
        grad_key = (
            jnp.einsum("uqk,uqd->ukd", grad_scores, head_query, preferred_element_type=jnp.float32)
            * self_scale
        )
        grad_value = jnp.einsum(
            "uqk,uqd->ukd",
            again_weights.astype(jnp.bfloat16),
            grad_num,
            preferred_element_type=jnp.float32,
        )
        grad_packed = jnp.concatenate([grad_query, grad_key, grad_value], 2).astype(jnp.bfloat16)
        grad_packed = lax.all_to_all(grad_packed, "pix", split_axis=1, concat_axis=0, tiled=True)
        grad_packed = (
            grad_packed.reshape(images, HEADS, row_count, 3 * head_size)
            .transpose(0, 2, 1, 3)
            .reshape(images * row_count, 3 * model_width)
        )
        d_wqkv = left_matmul(normed_self, grad_packed)
        grad_normed = right_matmul(grad_packed, wqkv)
        grad_inputs, d_gs = norm_back(after_mlp, gs_f, grad_normed)
        grad = grad + grad_inputs
        grad, d_gc, d_w1c, d_w2c = mlp_backward(grad, after_cross, gc_f, w1c, w2c, cross_kept)
        grad_rows = grad_rows + jnp.sum(grad.reshape(images, row_count, model_width), 0)
        grad_low = grad.astype(jnp.bfloat16)
        d_wo = left_matmul(attended_low, grad_low)
        grad_cross = right_matmul(grad_low, wo).reshape(images, row_count, model_width)
        cross_gnum = (grad_cross / den_rows[:, :, None]).astype(jnp.bfloat16)
        cross_gden = (-jnp.sum(grad_cross * attended, 2) / den_rows).astype(jnp.bfloat16)
        all_num, all_den = (
            lax.all_gather(cross_gnum, "pix", axis=1, tiled=True),
            lax.all_gather(cross_gden, "pix", axis=1, tiled=True),
        )
        select_low = select.astype(jnp.bfloat16)
        window_num = jnp.einsum(
            "wb,brd->wrd", select_low, all_num, preferred_element_type=jnp.float32
        ).astype(jnp.bfloat16)
        window_den = jnp.einsum(
            "wb,br->wr", select_low, all_den, preferred_element_type=jnp.float32
        )
        scores = right_matmul(queries, pixel_keys) * cross_scale
        weights = jnp.where(
            in_window[:, None, :], jnp.exp(scores[None] - window_top[:, :, None]), 0.0
        )
        cross_gweights = (
            jnp.einsum("wrd,cd->wrc", window_num, pixel_values, preferred_element_type=jnp.float32)
            + window_den[:, :, None]
        )
        cross_gscores = jnp.sum(weights * cross_gweights, 0).astype(jnp.bfloat16)
        query_terms = matmul(cross_gscores, pixel_keys) * cross_scale
        grad_keys = (left_matmul(cross_gscores, queries) * cross_scale).astype(jnp.bfloat16)
        grad_values = jnp.einsum(
            "wrc,wrd->cd",
            weights.astype(jnp.bfloat16),
            window_num,
            preferred_element_type=jnp.float32,
        ).astype(jnp.bfloat16)
        d_wk = left_matmul(normed_pix, grad_keys)
        d_wv = left_matmul(normed_pix, grad_values)
        grad_normed_pix = right_matmul(grad_keys, wk) + right_matmul(grad_values, wv)
        grad_pixels, d_gpix = norm_back(raw_pixels, gain_pix, grad_normed_pix)
        pixel_grads.append(grad_pixels)
        grad_pix_gain = grad_pix_gain + d_gpix
        terms = (
            d_wk,
            d_wv,
            d_wo,
            d_gc,
            d_w1c,
            d_w2c,
            d_gs,
            d_wqkv,
            d_wos,
            d_gm,
            d_w1s,
            d_w2s,
            query_terms,
        )
        reduced = (
            lax.psum_scatter(
                terms[0].astype(jnp.bfloat16), "pix", scatter_dimension=1, tiled=True
            ).astype(jnp.float32),
            lax.psum_scatter(
                terms[1].astype(jnp.bfloat16), "pix", scatter_dimension=1, tiled=True
            ).astype(jnp.float32),
            lax.psum_scatter(
                terms[2].astype(jnp.bfloat16), "pix", scatter_dimension=0, tiled=True
            ).astype(jnp.float32),
            lax.psum_scatter(
                terms[3].astype(jnp.bfloat16), "pix", scatter_dimension=0, tiled=True
            ).astype(jnp.float32),
            lax.psum_scatter(
                terms[4].astype(jnp.bfloat16), "pix", scatter_dimension=0, tiled=True
            ).astype(jnp.float32),
            lax.psum_scatter(
                terms[5].astype(jnp.bfloat16), "pix", scatter_dimension=0, tiled=True
            ).astype(jnp.float32),
            lax.psum_scatter(
                terms[6].astype(jnp.bfloat16), "pix", scatter_dimension=0, tiled=True
            ).astype(jnp.float32),
            lax.psum_scatter(
                terms[7].astype(jnp.bfloat16), "pix", scatter_dimension=0, tiled=True
            ).astype(jnp.float32),
            lax.psum_scatter(
                terms[8].astype(jnp.bfloat16), "pix", scatter_dimension=0, tiled=True
            ).astype(jnp.float32),
            lax.psum_scatter(
                terms[9].astype(jnp.bfloat16), "pix", scatter_dimension=0, tiled=True
            ).astype(jnp.float32),
            lax.psum_scatter(
                terms[10].astype(jnp.bfloat16), "pix", scatter_dimension=0, tiled=True
            ).astype(jnp.float32),
            lax.psum_scatter(
                terms[11].astype(jnp.bfloat16), "pix", scatter_dimension=0, tiled=True
            ).astype(jnp.float32),
            lax.psum_scatter(
                terms[12].astype(jnp.bfloat16), "pix", scatter_dimension=0, tiled=True
            ).astype(jnp.float32),
        )
        totals = reduced if totals is None else jax.tree.map(jnp.add, totals, reduced)
    s_wk, s_wv, s_wo, s_gc, s_w1c, s_w2c, s_gs, s_wqkv, s_wos, s_gm, s_w1s, s_w2s, s_query = totals
    summed = (
        lax.psum(s_wk.astype(jnp.bfloat16), "dp").astype(jnp.float32),
        lax.psum(s_wv.astype(jnp.bfloat16), "dp").astype(jnp.float32),
        lax.psum(s_wo.astype(jnp.bfloat16), "dp").astype(jnp.float32),
        lax.psum(s_gc.astype(jnp.bfloat16), "dp").astype(jnp.float32),
        lax.psum(s_w1c.astype(jnp.bfloat16), "dp").astype(jnp.float32),
        lax.psum(s_w2c.astype(jnp.bfloat16), "dp").astype(jnp.float32),
        lax.psum(s_gs.astype(jnp.bfloat16), "dp").astype(jnp.float32),
        lax.psum(s_wqkv.astype(jnp.bfloat16), "dp").astype(jnp.float32),
        lax.psum(s_wos.astype(jnp.bfloat16), "dp").astype(jnp.float32),
        lax.psum(s_gm.astype(jnp.bfloat16), "dp").astype(jnp.float32),
        lax.psum(s_w1s.astype(jnp.bfloat16), "dp").astype(jnp.float32),
        lax.psum(s_w2s.astype(jnp.bfloat16), "dp").astype(jnp.float32),
        lax.psum(s_query.astype(jnp.bfloat16), "dp").astype(jnp.float32),
        lax.psum(grad_rows.astype(jnp.bfloat16), "dp").astype(jnp.float32),
    )
    (
        f_wk,
        f_wv,
        f_wo,
        f_gc,
        f_w1c,
        f_w2c,
        f_gs,
        f_wqkv,
        f_wos,
        f_gm,
        f_w1s,
        f_w2s,
        query_rows,
        rows_total,
    ) = summed
    query_low = query_rows.astype(jnp.bfloat16)
    normed_rows = lax.dynamic_slice_in_dim(normed_lat, position * row_count, row_count, 0)
    d_wq_part = left_matmul(normed_rows, query_low)
    grad_normed_rows = right_matmul(query_low, wq)
    grad_lat_norm, d_glat_part = norm_back(lat_rows, g_lat_f, grad_normed_rows)
    d_wq, d_glat = (
        lax.psum_scatter(
            d_wq_part.astype(jnp.bfloat16), "pix", scatter_dimension=0, tiled=True
        ).astype(jnp.float32),
        lax.psum_scatter(
            d_glat_part.astype(jnp.bfloat16), "pix", scatter_dimension=0, tiled=True
        ).astype(jnp.float32),
    )
    d_gpix = lax.psum(grad_pix_gain, ("dp", "pix"))
    latent_out = jnp.stack(outputs)[None]
    pixel_out = jnp.stack(pixel_grads)[None]
    return (
        latent_out,
        pixel_out,
        rows_total + grad_lat_norm,
        d_gpix,
        d_glat,
        d_wq,
        f_wk,
        f_wv,
        f_wo,
        f_gc,
        f_w1c,
        f_w2c,
        f_gs,
        f_wqkv,
        f_wos,
        f_gm,
        f_w1s,
        f_w2s,
    )


MESH = pl.DeviceIdType.MESH
HBM = pl.BlockSpec(memory_space=pl.ANY)
VMEM = pl.BlockSpec(memory_space=pltpu.VMEM)
MIB = 1024 * 1024
PIECE = 256
BLOCK = 1024
FROWS = 272
DEN_ROW = 261
TOP_ROW = 263


def place():
    dp, pix = lax.axis_index("dp"), lax.axis_index("pix")
    return dp // 2, dp % 2, pix // 2, pix % 2


def device(x, c, z, y):
    return {"dp": x * 2 + c, "pix": z * 2 + y}


def greet(partners):
    barrier = pltpu.get_barrier_semaphore()
    for partner in partners:
        pl.semaphore_signal(barrier, inc=1, device_id=partner, device_id_type=MESH)
    pl.semaphore_wait(barrier, len(partners))


def remote(source, target, sems, index, partner):
    return pltpu.make_async_remote_copy(
        src_ref=source,
        dst_ref=target,
        send_sem=sems[0].at[index],
        recv_sem=sems[1].at[index],
        device_id=partner,
        device_id_type=MESH,
    )


def remote_params(collective_id, vmem=48 * MIB):
    return pltpu.CompilerParams(
        collective_id=collective_id, has_side_effects=True, vmem_limit_bytes=vmem
    )


def gather_kernel(splits, *refs):
    count = len(splits)
    shards, cot = refs[:count], refs[count]
    wholes, cot_rows = refs[count + 1 : 2 * count + 1], refs[2 * count + 1]
    send, recv, local, cot_send, cot_recv = refs[2 * count + 2 :]
    x, c, z, y = place()
    pix = lax.axis_index("pix")
    sems = (send, recv)
    others = [(pix + i) % 8 for i in range(1, 8)]
    core, across, beside = device(x, 1 - c, z, y), device(1 - x, c, z, y), device(x, c, z, 1 - y)
    greet([{"dp": x * 2 + c, "pix": other} for other in others] + [core, across])

    def part(ref, split):
        return ref.at[x, c] if split else ref.at[:, c]

    locals_ = []
    for k in range(count):
        copy = pltpu.make_async_copy(shards[k], wholes[k].at[z, y], local.at[k])
        copy.start()
        locals_.append(copy)
    copy = pltpu.make_async_copy(cot.at[:, pix], cot_rows.at[:, pix], local.at[count])
    copy.start()
    locals_.append(copy)
    along, side, over, between = {}, {}, {}, {}
    for k in range(count):
        mine, home = part(shards[k], splits[k]), part(wholes[k].at[z, y], splits[k])
        for i in (1, 2, 3):
            along[k, i] = remote(mine, home, sems, (k, i - 1), device(x, c, (z + i) % 4, y))
            along[k, i].start()
        side[k, 0] = remote(mine, home, sems, (k, 3), beside)
        side[k, 0].start()
    cots = []
    for i, other in enumerate(others):
        copy = remote(
            cot.at[:, other],
            cot_rows.at[:, pix],
            (cot_send, cot_recv),
            i,
            {"dp": x * 2 + c, "pix": other},
        )
        copy.start()
        cots.append(copy)

    def to_side(k):
        for i in (1, 2, 3):
            along[k, i].wait_recv()
            block = part(wholes[k].at[(z + 4 - i) % 4, y], splits[k])
            side[k, i] = remote(block, block, sems, (k, 3 + i), beside)
            side[k, i].start()

    def over_part(k, i):
        if i == 0:
            return wholes[k].at[z, 1 - y, x, c]
        return wholes[k].at[(z + 4 - i) % 4, :, x, c]

    def core_part(k, i):
        if i == 0:
            return wholes[k].at[z, 1 - y, :, c]
        return wholes[k].at[(z + 4 - i) % 4, :, :, c]

    def to_over(k):
        for i in range(4):
            side[k, i].wait_recv()
            if splits[k]:
                over[k, i] = remote(
                    over_part(k, i), over_part(k, i), sems, (k, 7 + i), across
                )
                over[k, i].start()

    def to_core(k):
        for i in range(4):
            if splits[k]:
                over[k, i].wait_recv()
            between[k, i] = remote(core_part(k, i), core_part(k, i), sems, (k, 11 + i), core)
            between[k, i].start()

    for step in range(count + 2):
        if step < count:
            to_side(step)
        if 1 <= step <= count:
            to_over(step - 1)
        if step >= 2:
            to_core(step - 2)
    for copy in locals_:
        copy.wait()
    for copy in cots:
        copy.wait()
    for copy in between.values():
        copy.wait()
    for group in (along, side, over):
        for copy in group.values():
            copy.wait_send()


def gather_weights(shards, splits, cot):
    count = len(shards)
    views = [
        shard.reshape(2, 2, shard.shape[0] // 4, shard.shape[1]) for shard in shards
    ]
    outs = [jax.ShapeDtypeStruct((4, 2, *view.shape), view.dtype) for view in views]
    results = pl.pallas_call(
        functools.partial(gather_kernel, splits),
        out_shape=[*outs, jax.ShapeDtypeStruct(cot.shape, cot.dtype)],
        in_specs=[HBM] * (count + 1),
        out_specs=[HBM] * (count + 1),
        scratch_shapes=[
            pltpu.SemaphoreType.DMA((count, 15)),
            pltpu.SemaphoreType.DMA((count, 15)),
            pltpu.SemaphoreType.DMA((count + 1,)),
            pltpu.SemaphoreType.DMA((7,)),
            pltpu.SemaphoreType.DMA((7,)),
        ],
        compiler_params=remote_params(0),
        name="gather_weights",
    )(*views, cot)
    wholes = [
        whole.reshape(8 * shard.shape[0], shard.shape[1])
        for whole, shard in zip(results[:-1], shards, strict=True)
    ]
    return wholes, results[-1]


def normed_block(raw, gain, wide_ref):
    features = raw.shape[1]
    values = raw.astype(jnp.float32)
    average = jnp.sum(values, 1, keepdims=True) * (1.0 / features)
    centered = values - average
    scale = lax.rsqrt(jnp.sum(centered * centered, 1, keepdims=True) * (1.0 / features) + 1e-05)
    unit = centered * scale
    lanes = lax.broadcasted_iota(jnp.int32, wide_ref.shape, 1)
    wide_ref[...] = jnp.where(lanes == DEN_ROW, 1.0, 0.0).astype(jnp.bfloat16)
    wide_ref[:, :features] = (unit * gain).astype(jnp.bfloat16)
    return unit, scale


def three_parts(row):
    first = row.astype(jnp.bfloat16).astype(jnp.float32)
    rest = row - first
    second = rest.astype(jnp.bfloat16).astype(jnp.float32)
    return first, second, rest - second


def with_rows(tail, den, top):
    rows = lax.broadcasted_iota(jnp.int32, tail.shape, 0) + (FROWS - 16)
    high = den.astype(jnp.bfloat16).astype(jnp.float32)
    first, second, third = three_parts(top)
    tail = jnp.where(rows == DEN_ROW, high, tail)
    tail = jnp.where(rows == DEN_ROW + 1, den - high, tail)
    tail = jnp.where(rows == TOP_ROW, first, tail)
    tail = jnp.where(rows == TOP_ROW + 1, second, tail)
    return jnp.where(rows == TOP_ROW + 2, third, tail)


def read_rows(tail):
    at = DEN_ROW - (FROWS - 16)
    den = tail[at : at + 1] + tail[at + 1 : at + 2]
    at = TOP_ROW - (FROWS - 16)
    top = tail[at : at + 1] + tail[at + 1 : at + 2] + tail[at + 2 : at + 3]
    return den, top


def pixel_forward_kernel(
    segs, pixels, gain, queries, weights, tops, sums, wide_ref, total, largest
):
    micro, block = pl.program_id(0), pl.program_id(1)
    pieces = BLOCK // PIECE
    per_micro = pieces * pl.num_programs(1)
    images = total.shape[0]

    @pl.when(block == 0)
    def _():
        total[...] = jnp.zeros_like(total)
        largest[...] = jnp.full(largest.shape, -big_value, jnp.float32)

    normed_block(pixels[0], gain[...], wide_ref)
    for k in range(pieces):
        rows = pl.ds(k * PIECE, PIECE)
        wide = wide_ref[rows, :]
        scores = jnp.dot(wide, queries[...], preferred_element_type=jnp.float32)
        top = jnp.max(scores, 0, keepdims=True)
        low = jnp.exp(scores - top).astype(jnp.bfloat16)
        weights[0, rows, :] = low
        tops[0, k] = top
        added = lax.dot_general(
            wide[:, :FROWS], low, (((0,), (0,)), ((), ())), preferred_element_type=jnp.float32
        )
        seg = segs[micro * per_micro + block * pieces + k]

        @pl.when(seg < images)
        def _():
            before = largest[seg, 0:1]
            now = jnp.maximum(before, top)
            total[seg] = total[seg] * jnp.exp(before - now) + added * jnp.exp(top - now)
            largest[seg, 0:1] = now

    @pl.when(block == pl.num_programs(1) - 1)
    def _():
        def finish(image, carry):
            sums[0, image, : FROWS - 16] = total[image, : FROWS - 16].astype(jnp.bfloat16)
            tail = total[image, FROWS - 16 :]
            den = total[image, DEN_ROW : DEN_ROW + 1]
            sums[0, image, FROWS - 16 :] = with_rows(tail, den, largest[image, 0:1]).astype(
                jnp.bfloat16
            )
            return carry

        lax.fori_loop(0, images, finish, 0)


def pixel_forward(segs, pixels, gain, queries, images):
    micros, slots, features = pixels.shape
    latents = queries.shape[1]
    blocks = slots // BLOCK
    return pl.pallas_call(
        pixel_forward_kernel,
        grid_spec=pltpu.PrefetchScalarGridSpec(
            num_scalar_prefetch=1,
            grid=(micros, blocks),
            in_specs=[
                pl.BlockSpec((1, BLOCK, features), lambda m, b, s: (m, b, 0)),
                pl.BlockSpec((1, features), lambda m, b, s: (0, 0)),
                pl.BlockSpec(queries.shape, lambda m, b, s: (0, 0)),
            ],
            out_specs=[
                pl.BlockSpec((1, BLOCK, latents), lambda m, b, s: (m, b, 0)),
                pl.BlockSpec((1, BLOCK // PIECE, 1, latents), lambda m, b, s: (m, b, 0, 0)),
                pl.BlockSpec((1, images, FROWS, latents), lambda m, b, s: (m, 0, 0, 0)),
            ],
            scratch_shapes=[
                pltpu.VMEM((BLOCK, queries.shape[0]), jnp.bfloat16),
                pltpu.VMEM((images, FROWS, latents), jnp.float32),
                pltpu.VMEM((images, 8, latents), jnp.float32),
            ],
        ),
        out_shape=[
            jax.ShapeDtypeStruct((micros, slots, latents), jnp.bfloat16),
            jax.ShapeDtypeStruct((micros, slots // PIECE, 1, latents), jnp.float32),
            jax.ShapeDtypeStruct((micros, images, FROWS, latents), jnp.bfloat16),
        ],
        compiler_params=pltpu.CompilerParams(vmem_limit_bytes=48 * MIB),
        name="pixel_forward",
    )(segs, pixels, gain, queries)


def pixel_backward_kernel(
    segs,
    pixels,
    gain,
    queries,
    weights,
    tops,
    grads,
    out,
    query_sums,
    gain_sums,
    wide_ref,
    scores_ref,
    back_ref,
):
    micro, block = pl.program_id(0), pl.program_id(1)
    pieces = BLOCK // PIECE
    per_micro = pieces * pl.num_programs(1)
    images = grads.shape[1]
    features = pixels.shape[2]

    @pl.when((block == 0) & (micro == 0))
    def _():
        query_sums[...] = jnp.zeros_like(query_sums)
        gain_sums[...] = jnp.zeros_like(gain_sums)

    unit, scale = normed_block(pixels[0], gain[...], wide_ref)
    for k in range(pieces):
        rows = pl.ds(k * PIECE, PIECE)
        seg = segs[micro * per_micro + block * pieces + k]
        image = jnp.minimum(seg, images - 1)
        grad = grads[0, image]
        unused, top = read_rows(grads[0, image, FROWS - 16 :].astype(jnp.float32))
        factor = jnp.where(seg < images, jnp.exp(tops[0, k] - top), 0.0)
        full = weights[0, rows, :].astype(jnp.float32) * factor
        slopes = jnp.dot(
            wide_ref[rows, :FROWS], grad, preferred_element_type=jnp.float32
        )
        scores_ref[rows, :] = (full * slopes).astype(jnp.bfloat16)
        back_ref[rows, :] = lax.dot_general(
            full.astype(jnp.bfloat16),
            grad,
            (((1,), (1,)), ((), ())),
            preferred_element_type=jnp.float32,
        )
    scores = scores_ref[...]
    query_sums[...] += lax.dot_general(
        wide_ref[:, :FROWS], scores, (((0,), (0,)), ((), ())), preferred_element_type=jnp.float32
    )
    back = back_ref[...] + lax.dot_general(
        scores, queries[:FROWS], (((1,), (1,)), ((), ())), preferred_element_type=jnp.float32
    )
    back = back[:, :features]
    gain_sums[...] += jnp.sum(back * unit, 0, keepdims=True)
    back = back * gain[...]
    mean = jnp.sum(back, 1, keepdims=True) * (1.0 / features)
    slope = jnp.sum(back * unit, 1, keepdims=True) * (1.0 / features)
    out[0] = (back - mean - unit * slope) * scale


def pixel_backward(segs, pixels, gain, queries, weights, tops, grads):
    micros, slots, features = pixels.shape
    latents = queries.shape[1]
    blocks = slots // BLOCK
    images = grads.shape[1]
    return pl.pallas_call(
        pixel_backward_kernel,
        grid_spec=pltpu.PrefetchScalarGridSpec(
            num_scalar_prefetch=1,
            grid=(micros, blocks),
            in_specs=[
                pl.BlockSpec((1, BLOCK, features), lambda m, b, s: (m, b, 0)),
                pl.BlockSpec((1, features), lambda m, b, s: (0, 0)),
                pl.BlockSpec(queries.shape, lambda m, b, s: (0, 0)),
                pl.BlockSpec((1, BLOCK, latents), lambda m, b, s: (m, b, 0)),
                pl.BlockSpec((1, BLOCK // PIECE, 1, latents), lambda m, b, s: (m, b, 0, 0)),
                pl.BlockSpec((1, images, FROWS, latents), lambda m, b, s: (m, 0, 0, 0)),
            ],
            out_specs=[
                pl.BlockSpec((1, BLOCK, features), lambda m, b, s: (m, b, 0)),
                pl.BlockSpec((FROWS, latents), lambda m, b, s: (0, 0)),
                pl.BlockSpec((1, features), lambda m, b, s: (0, 0)),
            ],
            scratch_shapes=[
                pltpu.VMEM((BLOCK, queries.shape[0]), jnp.bfloat16),
                pltpu.VMEM((BLOCK, latents), jnp.bfloat16),
                pltpu.VMEM((BLOCK, FROWS), jnp.float32),
            ],
        ),
        out_shape=[
            jax.ShapeDtypeStruct((micros, slots, features), jnp.float32),
            jax.ShapeDtypeStruct((FROWS, latents), jnp.float32),
            jax.ShapeDtypeStruct((1, features), jnp.float32),
        ],
        compiler_params=pltpu.CompilerParams(vmem_limit_bytes=48 * MIB),
        name="pixel_backward",
    )(segs, pixels, gain, queries, weights, tops, grads)


def merge(pieces):
    bodies = [piece[: FROWS - 16].astype(jnp.float32) for piece in pieces]
    tails = [piece[FROWS - 16 :].astype(jnp.float32) for piece in pieces]
    read = [read_rows(tail) for tail in tails]
    top = functools.reduce(jnp.maximum, [row for unused, row in read])
    factors = [jnp.exp(row - top) for unused, row in read]
    body = sum(values * factor for values, factor in zip(bodies, factors, strict=True))
    tail = sum(values * factor for values, factor in zip(tails, factors, strict=True))
    den = sum(row * factor for (row, unused), factor in zip(read, factors, strict=True))
    return body, tail, den, top


def owner_kernel(sums, out, rows_out, own, side_in, along_in, send, recv, local):
    x, c, z, y = place()
    sems = (send, recv)
    micros = out.shape[0]
    beside = device(x, c, z, 1 - y)
    greet([device(x, c, (z + i) % 4, y) for i in (1, 2, 3)] + [beside])
    sides, loads = {}, {}
    for i in (1, 2, 3, 0):
        sides[i] = remote(sums.at[:, (z + i) % 4, 1 - y], side_in.at[i], sems, i, beside)
        sides[i].start()
        loads[i] = pltpu.make_async_copy(sums.at[:, (z + i) % 4, y], own.at[i], local.at[i])
        loads[i].start()
    alongs = []
    for i in (1, 2, 3, 0):
        loads[i].wait()
        sides[i].wait_recv()
        for m in range(micros):
            body, tail, den, top = merge([own[i, m], side_in[i, m]])
            own[i, m, : FROWS - 16] = body.astype(jnp.bfloat16)
            own[i, m, FROWS - 16 :] = with_rows(tail, den, top).astype(jnp.bfloat16)
        if i:
            copy = remote(own.at[i], along_in.at[i - 1], sems, 3 + i, device(x, c, (z + i) % 4, y))
            copy.start()
            alongs.append(copy)
    for copy in alongs:
        copy.wait_recv()
    for m in range(micros):
        body, tail, den, top = merge([own[0, m]] + [along_in[i, m] for i in range(3)])
        rows = lax.broadcasted_iota(jnp.int32, tail.shape, 0) + (FROWS - 16)
        out[m, : FROWS - 16] = (body / den).astype(jnp.bfloat16)
        out[m, FROWS - 16 :] = jnp.where(rows < DEN_ROW, tail / den, 0.0).astype(jnp.bfloat16)
        rows_out[m, 0:1] = den
        rows_out[m, 1:2] = top
    for copy in alongs:
        copy.wait_send()
    for copy in sides.values():
        copy.wait_send()


def to_owners(sums):
    micros, images, rows, latents = sums.shape
    views = sums.reshape(micros, 4, 2, rows, latents)
    return pl.pallas_call(
        owner_kernel,
        out_shape=[
            jax.ShapeDtypeStruct((micros, rows, latents), jnp.bfloat16),
            jax.ShapeDtypeStruct((micros, 2, latents), jnp.float32),
        ],
        in_specs=[HBM],
        out_specs=[VMEM, VMEM],
        scratch_shapes=[
            pltpu.VMEM((4, micros, rows, latents), jnp.bfloat16),
            pltpu.VMEM((4, micros, rows, latents), jnp.bfloat16),
            pltpu.VMEM((3, micros, rows, latents), jnp.bfloat16),
            pltpu.SemaphoreType.DMA((7,)),
            pltpu.SemaphoreType.DMA((7,)),
            pltpu.SemaphoreType.DMA((4,)),
        ],
        compiler_params=remote_params(1),
        name="to_owners",
    )(views)


def holder_kernel(grads, rows_in, out, packed, send, recv, local):
    x, c, z, y = place()
    sems = (send, recv)
    micros = grads.shape[0]
    beside = device(x, c, z, 1 - y)
    greet([device(x, c, (z + i) % 4, y) for i in (1, 2, 3)] + [beside])
    for m in range(micros):
        packed[m, : FROWS - 16] = grads[m, : FROWS - 16].astype(jnp.bfloat16)
        tail = grads[m, FROWS - 16 :]
        rows = lax.broadcasted_iota(jnp.int32, tail.shape, 0) + (FROWS - 16)
        tail = with_rows(tail, rows_in[m, 0:1], rows_in[m, 1:2])
        tail = jnp.where(rows == DEN_ROW + 1, 0.0, tail)
        packed[m, FROWS - 16 :] = tail.astype(jnp.bfloat16)
    home = out.at[:, z, y]
    alongs, sides = {}, {}
    for i in (1, 2, 3):
        alongs[i] = remote(packed, home, sems, i, device(x, c, (z + i) % 4, y))
        alongs[i].start()
    sides[0] = remote(packed, home, sems, 0, beside)
    sides[0].start()
    keep = pltpu.make_async_copy(packed, home, local)
    keep.start()
    for i in (1, 2, 3):
        alongs[i].wait_recv()
        block = out.at[:, (z + 4 - i) % 4, y]
        sides[i] = remote(block, block, sems, 3 + i, beside)
        sides[i].start()
    for copy in sides.values():
        copy.wait()
    for copy in alongs.values():
        copy.wait_send()
    keep.wait()


def to_holders(grads, rows):
    micros, frows, latents = grads.shape
    out = pl.pallas_call(
        holder_kernel,
        out_shape=jax.ShapeDtypeStruct((micros, 4, 2, frows, latents), jnp.bfloat16),
        in_specs=[VMEM, VMEM],
        out_specs=HBM,
        scratch_shapes=[
            pltpu.VMEM((micros, frows, latents), jnp.bfloat16),
            pltpu.SemaphoreType.DMA((7,)),
            pltpu.SemaphoreType.DMA((7,)),
            pltpu.SemaphoreType.DMA,
        ],
        compiler_params=remote_params(2),
        name="to_holders",
    )(grads, rows)
    return out.reshape(micros, 8, frows, latents)


def softmax_parts(packed, scale):
    width = packed.shape[1] // 3
    query, key, value = packed[:, :width], packed[:, width : 2 * width], packed[:, 2 * width :]
    scores = right_matmul(query, key) * scale
    weights = jnp.exp(scores - jnp.max(scores, 1, keepdims=True))
    return query, key, value, weights, jnp.sum(weights, 1, keepdims=True)


def attention_kernel(scale, packed, out):
    query, key, value, weights, den = softmax_parts(packed[0], scale)
    out[0] = (matmul(weights.astype(jnp.bfloat16), value) / den).astype(jnp.bfloat16)


def attention_back_kernel(scale, packed, grad, out):
    width = grad.shape[2]
    query, key, value, weights, den = softmax_parts(packed[0], scale)
    grad_num = (grad[0] / den).astype(jnp.bfloat16)
    slopes = right_matmul(grad_num, value)
    grad_den = -jnp.sum(weights * slopes, 1, keepdims=True) / den
    scores = (weights * (slopes + grad_den)).astype(jnp.bfloat16)
    out[0, :, :width] = (matmul(scores, key) * scale).astype(jnp.bfloat16)
    out[0, :, width : 2 * width] = (left_matmul(scores, query) * scale).astype(jnp.bfloat16)
    out[0, :, 2 * width :] = left_matmul(weights.astype(jnp.bfloat16), grad_num).astype(
        jnp.bfloat16
    )


def head_spec(rows, width):
    return pl.BlockSpec((1, rows, width), lambda m, h: (m, 0, h))


def attention(packed, scale):
    micros, rows, columns = packed.shape
    width = columns // HEADS
    return pl.pallas_call(
        functools.partial(attention_kernel, scale),
        grid=(micros, HEADS),
        in_specs=[head_spec(rows, width)],
        out_specs=head_spec(rows, width // 3),
        out_shape=jax.ShapeDtypeStruct((micros, rows, columns // 3), jnp.bfloat16),
        compiler_params=pltpu.CompilerParams(vmem_limit_bytes=48 * MIB),
        name="attention",
    )(packed)


def attention_back(packed, grad, scale):
    micros, rows, columns = packed.shape
    width = columns // HEADS
    return pl.pallas_call(
        functools.partial(attention_back_kernel, scale),
        grid=(micros, HEADS),
        in_specs=[head_spec(rows, width), head_spec(rows, width // 3)],
        out_specs=head_spec(rows, width),
        out_shape=jax.ShapeDtypeStruct(packed.shape, jnp.bfloat16),
        compiler_params=pltpu.CompilerParams(vmem_limit_bytes=48 * MIB),
        name="attention_back",
    )(packed, grad)


def reduce_kernel(splits, *refs):
    count = len(splits)
    grads, rows_in = refs[:count], refs[count]
    finals, rows_out = refs[count + 1 : 2 * count + 1], refs[2 * count + 1]
    rest = refs[2 * count + 2 :]
    own, core_in, over_in, side_in, along_in = (
        rest[i * count : (i + 1) * count] for i in range(5)
    )
    send, recv, local, row_send, row_recv = rest[5 * count :]
    x, c, z, y = place()
    pix = lax.axis_index("pix")
    sems = (send, recv)
    others = [(pix + i) % 8 for i in range(1, 8)]
    core, across, beside = device(x, 1 - c, z, y), device(1 - x, c, z, y), device(x, c, z, 1 - y)
    greet([{"dp": x * 2 + c, "pix": other} for other in others] + [core, across])
    loads, between, over, side, along, back, last = [], [], {}, {}, {}, {}, {}
    for k in range(count):
        between.append(remote(grads[k].at[:, :, :, 1 - c], core_in[k], sems, (k, 0), core))
        between[k].start()
        loads.append(pltpu.make_async_copy(grads[k].at[:, :, :, c], own[k], local.at[k]))
        loads[k].start()
    keep = pltpu.make_async_copy(rows_in.at[:, pix], rows_out.at[:, pix], local.at[count])
    keep.start()
    rows = []
    for i, other in enumerate(others):
        copy = remote(
            rows_in.at[:, other],
            rows_out.at[:, pix],
            (row_send, row_recv),
            i,
            {"dp": x * 2 + c, "pix": other},
        )
        copy.start()
        rows.append(copy)

    def after_core(k):
        loads[k].wait()
        between[k].wait()

        def add(i, carry):
            own[k][i // 2, i % 2] = own[k][i // 2, i % 2] + core_in[k][i // 2, i % 2]
            return carry

        lax.fori_loop(0, 8, add, 0)
        if splits[k]:
            over[k] = remote(own[k].at[:, :, 1 - x], over_in[k], sems, (k, 1), across)
            over[k].start()

    def after_over(k):
        if splits[k]:
            over[k].wait()

            def add(i, carry):
                own[k][i // 2, i % 2, x] = own[k][i // 2, i % 2, x] + over_in[k][i // 2, i % 2]
                return carry

            lax.fori_loop(0, 8, add, 0)
            source = own[k].at[:, 1 - y, x]
        else:
            source = own[k].at[:, 1 - y]
        side[k] = remote(source, side_in[k], sems, (k, 2), beside)
        side[k].start()

    def after_side(k):
        side[k].wait()

        def add(i, carry):
            if splits[k]:
                own[k][i, y, x] = own[k][i, y, x] + side_in[k][i]
            else:
                own[k][i, y] = own[k][i, y] + side_in[k][i]
            return carry

        lax.fori_loop(0, 4, add, 0)
        for i in (1, 2, 3):
            block = own[k].at[(z + i) % 4, y]
            along[k, i] = remote(
                block.at[x] if splits[k] else block,
                along_in[k].at[i - 1],
                sems,
                (k, 2 + i),
                device(x, c, (z + i) % 4, y),
            )
            along[k, i].start()

    def after_along(k):
        for i in (1, 2, 3):
            along[k, i].wait()
        block = own[k][z, y, x] if splits[k] else own[k][z, y]
        total = block.astype(jnp.float32)
        for i in range(3):
            total = total + along_in[k][i].astype(jnp.float32)
        total = total.astype(jnp.bfloat16)
        if splits[k]:
            finals[k][x, c] = total
            back[k] = remote(finals[k].at[x, c], finals[k].at[x, c], sems, (k, 6), across)
        else:
            own[k][z, y] = total
            back[k] = remote(own[k].at[z, y], over_in[k], sems, (k, 6), across)
        back[k].start()

    def after_back(k):
        back[k].wait()
        if not splits[k]:
            finals[k][:, c] = own[k][z, y] + over_in[k][...]
        last[k] = remote(finals[k].at[:, c], finals[k].at[:, c], sems, (k, 7), core)
        last[k].start()

    stages = (after_core, after_over, after_side, after_along, after_back)
    for step in range(count + len(stages) - 1):
        for number, stage in enumerate(stages):
            if 0 <= step - number < count:
                stage(step - number)
    for k in range(count):
        last[k].wait()
    for copy in rows:
        copy.wait()
    keep.wait()


def reduce_grads(grads, splits, rows):
    count = len(grads)
    views = [
        grad.reshape(4, 2, 2, 2, grad.shape[0] // 32, grad.shape[1]).astype(jnp.bfloat16)
        for grad in grads
    ]
    buffers = ([], [], [], [], [])
    for view, split in zip(views, splits, strict=True):
        block = view.shape[4:]
        lead = () if split else (2,)
        for group, shape in zip(
            buffers,
            (
                (4, 2, 2, *block),
                (4, 2, 2, *block),
                (4, 2, *block) if split else (2, *block),
                (4, *lead, *block),
                (3, *lead, *block),
            ),
            strict=True,
        ):
            group.append(pltpu.VMEM(shape, jnp.bfloat16))
    results = pl.pallas_call(
        functools.partial(reduce_kernel, splits),
        out_shape=[jax.ShapeDtypeStruct((2, 2, *view.shape[4:]), jnp.bfloat16) for view in views]
        + [jax.ShapeDtypeStruct(rows.shape, rows.dtype)],
        in_specs=[HBM] * (count + 1),
        out_specs=[VMEM] * count + [HBM],
        scratch_shapes=[
            *(shape for group in buffers for shape in group),
            pltpu.SemaphoreType.DMA((count, 8)),
            pltpu.SemaphoreType.DMA((count, 8)),
            pltpu.SemaphoreType.DMA((count + 1,)),
            pltpu.SemaphoreType.DMA((7,)),
            pltpu.SemaphoreType.DMA((7,)),
        ],
        compiler_params=remote_params(3, 56 * MIB),
        name="reduce_grads",
    )(*views, rows)
    shards = [
        result.reshape(grad.shape[0] // 8, grad.shape[1])
        for result, grad in zip(results[:-1], grads, strict=True)
    ]
    return shards, results[-1]


def spread_kernel(block, out, send, recv):
    pix, dp = lax.axis_index("pix"), lax.axis_index("dp")
    others = [(pix + i) % 8 for i in range(1, 8)]
    greet([{"dp": dp, "pix": other} for other in others])
    copies = []
    for i, other in enumerate(others):
        copy = remote(block, out.at[pix], (send, recv), i, {"dp": dp, "pix": other})
        copy.start()
        copies.append(copy)
    out[pix] = block[...]
    for copy in copies:
        copy.wait()


def spread(block):
    return pl.pallas_call(
        spread_kernel,
        out_shape=jax.ShapeDtypeStruct((8, *block.shape), block.dtype),
        in_specs=[VMEM],
        out_specs=VMEM,
        scratch_shapes=[pltpu.SemaphoreType.DMA((7,)), pltpu.SemaphoreType.DMA((7,))],
        compiler_params=remote_params(4),
        name="spread",
    )(block)


def image_body(
    image_sides,
    pixels,
    latent_array,
    pixel_gain,
    latent_gain,
    query_weight,
    key_weight,
    value_weight,
    cross_out_weight,
    cross_mlp_gain,
    cross_mlp_in,
    cross_mlp_out,
    self_gain,
    self_qkv_weight,
    self_out_weight,
    self_mlp_gain,
    self_mlp_in,
    self_mlp_out,
    cotangent,
):
    position = lax.axis_index("pix")
    micros, images = image_sides.shape[1:]
    capacity, features = pixels.shape[2:]
    row_count, width = latent_array.shape
    latents = row_count * 8
    head_size = width // HEADS
    cross_scale = width ** (-0.5)
    self_scale = head_size ** (-0.5)
    f32, bf16 = jnp.float32, jnp.bfloat16

    def widen(values, columns):
        return jnp.pad(values, ((0, 0), (0, columns - values.shape[1])))

    gains = jnp.stack([latent_gain, cross_mlp_gain, self_gain, self_mlp_gain], 1)
    misc = jnp.concatenate(
        [widen(key_weight.T, 384), widen(value_weight.T, 384), widen(gains, 256)], 1
    )
    shards = (
        latent_array,
        query_weight,
        misc,
        cross_out_weight,
        cross_mlp_in,
        cross_mlp_out,
        self_qkv_weight,
        self_out_weight,
        self_mlp_in,
        self_mlp_out,
    )
    splits = (True, True, True, True, True, True, True, True, True, True)
    wholes, cot_rows = gather_weights(shards, splits, cotangent[0])
    lat_full, wq, misc, wo, w1c, w2c, wqkv, wos, w1s, w2s = wholes
    key_t, value_t = misc[:, :384], misc[:, 384 : 384 + FROWS]
    g_lat, g_cross, g_self, g_mlp = (misc[:, 768 + i].astype(f32) for i in range(4))
    lat_f = lat_full.astype(f32)
    normed_lat = layer_norm(lat_f, g_lat).astype(bf16)
    queries = matmul(normed_lat, wq).astype(bf16)
    query_t = (
        lax.dot_general(key_t, queries, (((0,), (1,)), ((), ())), preferred_element_type=f32)
        * cross_scale
    ).astype(bf16)

    lengths = image_sides[0] * image_sides[0]
    ends = jnp.cumsum(lengths, 1)
    firsts = position * capacity + PIECE * jnp.arange(capacity // PIECE, dtype=jnp.int32)
    segs = jnp.sum((firsts[None, :, None] >= ends[:, None, :]).astype(jnp.int32), 2).reshape(-1)
    gain_pix = pixel_gain.astype(f32)[None]
    pix_weights, pix_tops, sums = pixel_forward(segs, pixels[0], gain_pix, query_t, images)
    means, rows = to_owners(sums)
    den, top = rows[:, 0], rows[:, 1]

    att = jnp.einsum("mfr,df->mrd", means, value_t, preferred_element_type=f32)
    att_low = att.astype(bf16).reshape(micros * latents, width)
    start_rows = jnp.broadcast_to(lat_f[None], (micros, latents, width)).reshape(-1, width)
    after_cross = start_rows + matmul(att_low, wo)
    after_mlp, cross_kept = mlp_forward(after_cross, g_cross, w1c, w2c)
    normed_self = layer_norm(after_mlp, g_self).astype(bf16)
    packed = matmul(normed_self, wqkv).astype(bf16).reshape(micros, latents, 3 * width)
    self_att = attention(packed, self_scale).reshape(-1, width)
    after_self = after_mlp + matmul(self_att, wos)
    final, final_kept = mlp_forward(after_self, g_mlp, w1s, w2s)
    final = final.astype(bf16).reshape(micros, 8, row_count, width)

    grad = cot_rows.astype(f32).reshape(-1, width)
    grad, d_gm, d_w1s, d_w2s = mlp_backward(grad, after_self, g_mlp, w1s, w2s, final_kept)
    grad_low = grad.astype(bf16)
    d_wos = left_matmul(self_att, grad_low)
    grad_att = right_matmul(grad_low, wos).reshape(micros, latents, width)
    grad_packed = attention_back(packed, grad_att, self_scale).reshape(-1, 3 * width)
    d_wqkv = left_matmul(normed_self, grad_packed)
    grad_inputs, d_gs = norm_back(after_mlp, g_self, right_matmul(grad_packed, wqkv))
    grad = grad + grad_inputs
    grad, d_gc, d_w1c, d_w2c = mlp_backward(grad, after_cross, g_cross, w1c, w2c, cross_kept)
    grad_lat = jnp.sum(grad.reshape(micros, latents, width), 0)
    grad_low = grad.astype(bf16)
    d_wo = left_matmul(att_low, grad_low)
    grad_att = right_matmul(grad_low, wo).reshape(micros, latents, width)
    grad_num = (grad_att / den[:, :, None]).astype(bf16)
    grad_den = -jnp.sum(grad_att * att, 2) / den
    grad_sums = jnp.einsum("mrd,df->mfr", grad_num, value_t, preferred_element_type=f32)
    d_wv = jnp.einsum("mrd,mfr->df", grad_att.astype(bf16), means, preferred_element_type=f32)
    all_grads = to_holders(grad_sums, jnp.stack([grad_den, top], 1))
    pixel_grad, query_sums, pix_gain_sums = pixel_backward(
        segs, pixels[0], gain_pix, query_t, pix_weights, pix_tops, all_grads
    )

    gain_grads = jnp.stack([d_gc, d_gs, d_gm], 1)
    small = jnp.concatenate([widen(d_wv, 384), widen(gain_grads, 128)], 1)
    halves = grad_lat.reshape(8, row_count, 2, width // 2).transpose(0, 2, 1, 3)
    small = jnp.concatenate([small, halves.reshape(8 * 2 * row_count, width // 2)], 1)
    query_rows = widen(query_sums.T, 384).reshape(8, row_count, 384)
    pix_gain_rows = jnp.pad(
        widen(pix_gain_sums, 384)[None], ((0, 7), (0, row_count - 1), (0, 0))
    )
    query_rows = jnp.concatenate([query_rows, pix_gain_rows], 1).reshape(-1, 384)
    parts = (
        d_w2s,
        d_w1s,
        d_wos,
        d_wqkv,
        d_w2c,
        d_w1c,
        d_wo,
        small,
        query_rows,
    )
    splits = (True, False, True, True, False, True, False, True, True)
    reduced, latent_out = reduce_grads(parts, splits, final)
    f_w2s, f_w1s, f_wos, f_wqkv, f_w2c, f_w1c, f_wo, small, query_rows = reduced
    query_all = spread(query_rows)
    d_gpix = query_all[0, row_count, :features].astype(f32)
    query_all = query_all[:, :row_count].reshape(latents, 384)

    grad_queries = (right_matmul(query_all, key_t) * cross_scale).astype(bf16)
    columns = lax.dynamic_slice_in_dim(normed_lat, position * (width // 8), width // 8, 1)
    d_wq = left_matmul(columns, grad_queries)
    query_columns = lax.dynamic_slice_in_dim(queries, position * (width // 8), width // 8, 1)
    d_wk = (left_matmul(query_all, query_columns) * cross_scale)[:features]
    grad_norm_lat, d_glat = norm_back(lat_f, g_lat, right_matmul(grad_queries, wq))
    d_glat = lax.dynamic_slice_in_dim(d_glat, position * (width // 8), width // 8, 0)
    grad_norm_rows = lax.dynamic_slice_in_dim(grad_norm_lat, position * row_count, row_count, 0)
    grad_lat = small[:, width // 2 :].astype(f32).reshape(2, row_count, width // 2)
    grad_lat = grad_lat.transpose(1, 0, 2).reshape(row_count, width)
    return (
        latent_out[None],
        pixel_grad[None],
        grad_lat + grad_norm_rows,
        d_gpix,
        d_glat,
        d_wq,
        d_wk,
        small[:, :features].astype(f32).T,
        f_wo.astype(f32),
        small[:, 384].astype(f32),
        f_w1c.astype(f32),
        f_w2c.astype(f32),
        small[:, 385].astype(f32),
        f_wqkv.astype(f32),
        f_wos.astype(f32),
        small[:, 386].astype(f32),
        f_w1s.astype(f32),
        f_w2s.astype(f32),
    )


def solution(mesh):
    fits = dict(mesh.shape) == {"dp": 4, "pix": 8}
    return jax.shard_map(
        image_body if fits else starting_body,
        mesh=mesh,
        in_specs=(
            P("dp", None, None),
            P("dp", None, "pix", None),
            P("pix", None),
            P(),
            P("pix"),
            P("pix", None),
            P(None, "pix"),
            P(None, "pix"),
            P("pix", None),
            P("pix"),
            P("pix", None),
            P("pix", None),
            P("pix"),
            P("pix", None),
            P("pix", None),
            P("pix"),
            P("pix", None),
            P("pix", None),
            P("dp", None, None, "pix", None),
        ),
        out_specs=(
            P("dp", None, None, "pix", None),
            P("dp", None, "pix", None),
            P("pix", None),
            P(),
            P("pix"),
            P("pix", None),
            P(None, "pix"),
            P(None, "pix"),
            P("pix", None),
            P("pix"),
            P("pix", None),
            P("pix", None),
            P("pix"),
            P("pix", None),
            P("pix", None),
            P("pix"),
            P("pix", None),
            P("pix", None),
        ),
        check_vma=False,
    )
```

```python
import functools

import jax
import jax.numpy as jnp
from jax import lax
from jax.experimental import pallas as pl
from jax.experimental.pallas import tpu as pltpu
from jax.sharding import PartitionSpec as P

HEADS = 8
SIDE = 64


highest = lax.Precision.HIGHEST
big_value = 1e30


def layer_norm(values, gain):
    average = jnp.mean(values, -1, keepdims=True)
    centered = values - average
    return centered * lax.rsqrt(jnp.mean(centered * centered, -1, keepdims=True) + 1e-05) * gain


def matmul(left, right):
    return jnp.dot(left, right, preferred_element_type=jnp.float32)


def left_matmul(left, right):
    return lax.dot_general(
        left, right, (((0,), (0,)), ((), ())), preferred_element_type=jnp.float32
    )


def right_matmul(left, right):
    return lax.dot_general(
        left, right, (((1,), (1,)), ((), ())), preferred_element_type=jnp.float32
    )


def norm_back(values, gain, grad):
    unused, pullback = jax.vjp(layer_norm, values, gain)
    return pullback(grad)


def mlp_forward(inputs, gain, w_in, w_out):
    normed = layer_norm(inputs, gain).astype(jnp.bfloat16)
    hidden = matmul(normed, w_in)
    active = jax.nn.gelu(hidden).astype(jnp.bfloat16)
    return (inputs + matmul(active, w_out), (normed, hidden, active))


def mlp_backward(grad, inputs, gain, w_in, w_out, kept):
    normed, hidden, active = kept
    grad_low = grad.astype(jnp.bfloat16)
    grad_out = left_matmul(active, grad_low)
    grad_active = right_matmul(grad_low, w_out)
    unused, pullback = jax.vjp(jax.nn.gelu, hidden)
    grad_hidden = pullback(grad_active)[0].astype(jnp.bfloat16)
    grad_in = left_matmul(normed, grad_hidden)
    grad_normed = right_matmul(grad_hidden, w_in)
    grad_inputs, grad_gain = norm_back(inputs, gain, grad_normed)
    return (grad + grad_inputs, grad_gain, grad_in, grad_out)


def starting_body(
    image_sides,
    pixels,
    latent_array,
    pixel_gain,
    latent_gain,
    query_weight,
    key_weight,
    value_weight,
    cross_out_weight,
    cross_mlp_gain,
    cross_mlp_in,
    cross_mlp_out,
    self_gain,
    self_qkv_weight,
    self_out_weight,
    self_mlp_gain,
    self_mlp_in,
    self_mlp_out,
    cotangent,
):
    pieces = lax.axis_size("pix")
    position = lax.axis_index("pix")
    micros = image_sides.shape[1]
    images = image_sides.shape[2]
    capacity = pixels.shape[2]
    row_count = latent_array.shape[0]
    model_width = latent_array.shape[1]
    head_size = model_width // HEADS
    unit_count = images * HEADS // pieces
    window = min(images, (capacity - 2) // (SIDE * SIDE // 4) + 2)
    cross_scale = model_width ** (-0.5)
    self_scale = head_size ** (-0.5)
    shards = (
        latent_array,
        latent_gain,
        query_weight,
        key_weight,
        value_weight,
        cross_out_weight,
        cross_mlp_gain,
        cross_mlp_in,
        cross_mlp_out,
        self_gain,
        self_qkv_weight,
        self_out_weight,
        self_mlp_gain,
        self_mlp_in,
        self_mlp_out,
    )
    lat_rows = latent_array.astype(jnp.float32)
    gain_pix = pixel_gain.astype(jnp.float32)
    grad_rows = jnp.zeros((row_count, model_width), jnp.float32)
    grad_pix_gain = jnp.zeros(gain_pix.shape, jnp.float32)
    outputs = []
    pixel_grads = []
    totals = None
    for step_index in range(micros):
        gathered = (
            lax.all_gather(shards[0], "pix", axis=0, tiled=True),
            lax.all_gather(shards[1], "pix", axis=0, tiled=True),
            lax.all_gather(shards[2], "pix", axis=0, tiled=True),
            lax.all_gather(shards[3], "pix", axis=1, tiled=True),
            lax.all_gather(shards[4], "pix", axis=1, tiled=True),
            lax.all_gather(shards[5], "pix", axis=0, tiled=True),
            lax.all_gather(shards[6], "pix", axis=0, tiled=True),
            lax.all_gather(shards[7], "pix", axis=0, tiled=True),
            lax.all_gather(shards[8], "pix", axis=0, tiled=True),
            lax.all_gather(shards[9], "pix", axis=0, tiled=True),
            lax.all_gather(shards[10], "pix", axis=0, tiled=True),
            lax.all_gather(shards[11], "pix", axis=0, tiled=True),
            lax.all_gather(shards[12], "pix", axis=0, tiled=True),
            lax.all_gather(shards[13], "pix", axis=0, tiled=True),
            lax.all_gather(shards[14], "pix", axis=0, tiled=True),
        )
        lat_full, g_lat, wq, wk, wv, wo, g_cross, w1c, w2c, g_self, wqkv, wos, g_mlp, w1s, w2s = (
            gathered
        )
        g_lat_f = g_lat.astype(jnp.float32)
        gc_f = g_cross.astype(jnp.float32)
        gs_f = g_self.astype(jnp.float32)
        gm_f = g_mlp.astype(jnp.float32)
        if step_index == 0:
            normed_lat = layer_norm(lat_full.astype(jnp.float32), g_lat_f).astype(jnp.bfloat16)
            queries = matmul(normed_lat, wq).astype(jnp.bfloat16)
        side_list = image_sides[0, step_index]
        lengths = side_list * side_list
        ends = jnp.cumsum(lengths)
        slot_ids = position * capacity + jnp.arange(capacity, dtype=jnp.int32)
        segment = jnp.sum((slot_ids[:, None] >= ends[None, :]).astype(jnp.int32), 1)
        window_ids = segment[0] + jnp.arange(window, dtype=jnp.int32)
        select = (window_ids[:, None] == jnp.arange(images, dtype=jnp.int32)[None, :]).astype(
            jnp.float32
        )
        in_window = segment[None, :] == window_ids[:, None]
        raw_pixels = pixels[0, step_index].astype(jnp.float32)
        normed_pix = layer_norm(raw_pixels, gain_pix).astype(jnp.bfloat16)
        pixel_keys = matmul(normed_pix, wk).astype(jnp.bfloat16)
        pixel_values = matmul(normed_pix, wv).astype(jnp.bfloat16)
        scores = right_matmul(queries, pixel_keys) * cross_scale
        local_top = jnp.max(jnp.where(in_window[:, None, :], scores[None], -big_value), 2)
        image_top = jnp.max(jnp.where(select[:, :, None] > 0, local_top[:, None, :], -big_value), 0)
        image_top = lax.pmax(image_top, "pix")
        window_top = jnp.einsum("wb,br->wr", select, image_top, precision=highest)
        weights = jnp.where(
            in_window[:, None, :], jnp.exp(scores[None] - window_top[:, :, None]), 0.0
        )
        partial_den = jnp.sum(weights, 2)
        partial_num = jnp.einsum(
            "wrc,cd->wrd",
            weights.astype(jnp.bfloat16),
            pixel_values,
            preferred_element_type=jnp.float32,
        )
        full_num = jnp.einsum("wb,wrd->brd", select, partial_num, precision=highest)
        full_den = jnp.einsum("wb,wr->br", select, partial_den, precision=highest)
        num_rows, den_rows = (
            lax.psum_scatter(
                full_num.astype(jnp.bfloat16), "pix", scatter_dimension=1, tiled=True
            ).astype(jnp.float32),
            lax.psum_scatter(
                full_den.astype(jnp.bfloat16), "pix", scatter_dimension=1, tiled=True
            ).astype(jnp.float32),
        )
        attended = num_rows / den_rows[:, :, None]
        attended_low = attended.astype(jnp.bfloat16).reshape(images * row_count, model_width)
        start_rows = jnp.broadcast_to(lat_rows[None], (images, row_count, model_width)).reshape(
            images * row_count, model_width
        )
        after_cross = start_rows + matmul(attended_low, wo)
        after_mlp, cross_kept = mlp_forward(after_cross, gc_f, w1c, w2c)
        normed_self = layer_norm(after_mlp, gs_f).astype(jnp.bfloat16)
        packed = matmul(normed_self, wqkv).astype(jnp.bfloat16)
        packed = packed.reshape(images, row_count, HEADS, 3 * head_size).transpose(0, 2, 1, 3)
        packed = packed.reshape(pieces, unit_count, row_count, 3 * head_size)
        packed = lax.all_to_all(packed, "pix", split_axis=0, concat_axis=2, tiled=True)[0]
        head_query = packed[:, :, :head_size]
        head_key = packed[:, :, head_size : 2 * head_size]
        head_value = packed[:, :, 2 * head_size :]
        self_scores = (
            jnp.einsum("uqd,ukd->uqk", head_query, head_key, preferred_element_type=jnp.float32)
            * self_scale
        )
        self_top = jnp.max(self_scores, 2, keepdims=True)
        self_weights = jnp.exp(self_scores - self_top)
        self_den = jnp.sum(self_weights, 2, keepdims=True)
        self_num = jnp.einsum(
            "uqk,ukd->uqd",
            self_weights.astype(jnp.bfloat16),
            head_value,
            preferred_element_type=jnp.float32,
        )
        self_out = self_num / self_den
        returned = lax.all_to_all(
            self_out.astype(jnp.bfloat16), "pix", split_axis=1, concat_axis=0, tiled=True
        )
        returned = (
            returned.reshape(images, HEADS, row_count, head_size)
            .transpose(0, 2, 1, 3)
            .reshape(images * row_count, model_width)
        )
        after_self = after_mlp + matmul(returned, wos)
        final, final_kept = mlp_forward(after_self, gm_f, w1s, w2s)
        outputs.append(final.astype(jnp.bfloat16).reshape(images, row_count, model_width))
        grad = cotangent[0, step_index].astype(jnp.float32).reshape(images * row_count, model_width)
        grad, d_gm, d_w1s, d_w2s = mlp_backward(grad, after_self, gm_f, w1s, w2s, final_kept)
        grad_low = grad.astype(jnp.bfloat16)
        d_wos = left_matmul(returned, grad_low)
        grad_self = right_matmul(grad_low, wos)
        grad_self = grad_self.reshape(images, row_count, HEADS, head_size).transpose(0, 2, 1, 3)
        grad_self = grad_self.reshape(pieces, unit_count, row_count, head_size)
        grad_self = lax.all_to_all(
            grad_self.astype(jnp.bfloat16), "pix", split_axis=0, concat_axis=2, tiled=True
        ).astype(grad_self.dtype)[0]
        grad_num = (grad_self / self_den).astype(jnp.bfloat16)
        grad_den = -jnp.sum(grad_self * self_out, 2, keepdims=True) / self_den
        again_scores = (
            jnp.einsum("uqd,ukd->uqk", head_query, head_key, preferred_element_type=jnp.float32)
            * self_scale
        )
        again_weights = jnp.exp(again_scores - self_top)
        grad_weights = (
            jnp.einsum("uqd,ukd->uqk", grad_num, head_value, preferred_element_type=jnp.float32)
            + grad_den
        )
        grad_scores = (again_weights * grad_weights).astype(jnp.bfloat16)
        grad_query = (
            jnp.einsum("uqk,ukd->uqd", grad_scores, head_key, preferred_element_type=jnp.float32)
            * self_scale
        )
        grad_key = (
            jnp.einsum("uqk,uqd->ukd", grad_scores, head_query, preferred_element_type=jnp.float32)
            * self_scale
        )
        grad_value = jnp.einsum(
            "uqk,uqd->ukd",
            again_weights.astype(jnp.bfloat16),
            grad_num,
            preferred_element_type=jnp.float32,
        )
        grad_packed = jnp.concatenate([grad_query, grad_key, grad_value], 2).astype(jnp.bfloat16)
        grad_packed = lax.all_to_all(grad_packed, "pix", split_axis=1, concat_axis=0, tiled=True)
        grad_packed = (
            grad_packed.reshape(images, HEADS, row_count, 3 * head_size)
            .transpose(0, 2, 1, 3)
            .reshape(images * row_count, 3 * model_width)
        )
        d_wqkv = left_matmul(normed_self, grad_packed)
        grad_normed = right_matmul(grad_packed, wqkv)
        grad_inputs, d_gs = norm_back(after_mlp, gs_f, grad_normed)
        grad = grad + grad_inputs
        grad, d_gc, d_w1c, d_w2c = mlp_backward(grad, after_cross, gc_f, w1c, w2c, cross_kept)
        grad_rows = grad_rows + jnp.sum(grad.reshape(images, row_count, model_width), 0)
        grad_low = grad.astype(jnp.bfloat16)
        d_wo = left_matmul(attended_low, grad_low)
        grad_cross = right_matmul(grad_low, wo).reshape(images, row_count, model_width)
        cross_gnum = (grad_cross / den_rows[:, :, None]).astype(jnp.bfloat16)
        cross_gden = (-jnp.sum(grad_cross * attended, 2) / den_rows).astype(jnp.bfloat16)
        all_num, all_den = (
            lax.all_gather(cross_gnum, "pix", axis=1, tiled=True),
            lax.all_gather(cross_gden, "pix", axis=1, tiled=True),
        )
        select_low = select.astype(jnp.bfloat16)
        window_num = jnp.einsum(
            "wb,brd->wrd", select_low, all_num, preferred_element_type=jnp.float32
        ).astype(jnp.bfloat16)
        window_den = jnp.einsum(
            "wb,br->wr", select_low, all_den, preferred_element_type=jnp.float32
        )
        scores = right_matmul(queries, pixel_keys) * cross_scale
        weights = jnp.where(
            in_window[:, None, :], jnp.exp(scores[None] - window_top[:, :, None]), 0.0
        )
        cross_gweights = (
            jnp.einsum("wrd,cd->wrc", window_num, pixel_values, preferred_element_type=jnp.float32)
            + window_den[:, :, None]
        )
        cross_gscores = jnp.sum(weights * cross_gweights, 0).astype(jnp.bfloat16)
        query_terms = matmul(cross_gscores, pixel_keys) * cross_scale
        grad_keys = (left_matmul(cross_gscores, queries) * cross_scale).astype(jnp.bfloat16)
        grad_values = jnp.einsum(
            "wrc,wrd->cd",
            weights.astype(jnp.bfloat16),
            window_num,
            preferred_element_type=jnp.float32,
        ).astype(jnp.bfloat16)
        d_wk = left_matmul(normed_pix, grad_keys)
        d_wv = left_matmul(normed_pix, grad_values)
        grad_normed_pix = right_matmul(grad_keys, wk) + right_matmul(grad_values, wv)
        grad_pixels, d_gpix = norm_back(raw_pixels, gain_pix, grad_normed_pix)
        pixel_grads.append(grad_pixels)
        grad_pix_gain = grad_pix_gain + d_gpix
        terms = (
            d_wk,
            d_wv,
            d_wo,
            d_gc,
            d_w1c,
            d_w2c,
            d_gs,
            d_wqkv,
            d_wos,
            d_gm,
            d_w1s,
            d_w2s,
            query_terms,
        )
        reduced = (
            lax.psum_scatter(
                terms[0].astype(jnp.bfloat16), "pix", scatter_dimension=1, tiled=True
            ).astype(jnp.float32),
            lax.psum_scatter(
                terms[1].astype(jnp.bfloat16), "pix", scatter_dimension=1, tiled=True
            ).astype(jnp.float32),
            lax.psum_scatter(
                terms[2].astype(jnp.bfloat16), "pix", scatter_dimension=0, tiled=True
            ).astype(jnp.float32),
            lax.psum_scatter(
                terms[3].astype(jnp.bfloat16), "pix", scatter_dimension=0, tiled=True
            ).astype(jnp.float32),
            lax.psum_scatter(
                terms[4].astype(jnp.bfloat16), "pix", scatter_dimension=0, tiled=True
            ).astype(jnp.float32),
            lax.psum_scatter(
                terms[5].astype(jnp.bfloat16), "pix", scatter_dimension=0, tiled=True
            ).astype(jnp.float32),
            lax.psum_scatter(
                terms[6].astype(jnp.bfloat16), "pix", scatter_dimension=0, tiled=True
            ).astype(jnp.float32),
            lax.psum_scatter(
                terms[7].astype(jnp.bfloat16), "pix", scatter_dimension=0, tiled=True
            ).astype(jnp.float32),
            lax.psum_scatter(
                terms[8].astype(jnp.bfloat16), "pix", scatter_dimension=0, tiled=True
            ).astype(jnp.float32),
            lax.psum_scatter(
                terms[9].astype(jnp.bfloat16), "pix", scatter_dimension=0, tiled=True
            ).astype(jnp.float32),
            lax.psum_scatter(
                terms[10].astype(jnp.bfloat16), "pix", scatter_dimension=0, tiled=True
            ).astype(jnp.float32),
            lax.psum_scatter(
                terms[11].astype(jnp.bfloat16), "pix", scatter_dimension=0, tiled=True
            ).astype(jnp.float32),
            lax.psum_scatter(
                terms[12].astype(jnp.bfloat16), "pix", scatter_dimension=0, tiled=True
            ).astype(jnp.float32),
        )
        totals = reduced if totals is None else jax.tree.map(jnp.add, totals, reduced)
    s_wk, s_wv, s_wo, s_gc, s_w1c, s_w2c, s_gs, s_wqkv, s_wos, s_gm, s_w1s, s_w2s, s_query = totals
    summed = (
        lax.psum(s_wk.astype(jnp.bfloat16), "dp").astype(jnp.float32),
        lax.psum(s_wv.astype(jnp.bfloat16), "dp").astype(jnp.float32),
        lax.psum(s_wo.astype(jnp.bfloat16), "dp").astype(jnp.float32),
        lax.psum(s_gc.astype(jnp.bfloat16), "dp").astype(jnp.float32),
        lax.psum(s_w1c.astype(jnp.bfloat16), "dp").astype(jnp.float32),
        lax.psum(s_w2c.astype(jnp.bfloat16), "dp").astype(jnp.float32),
        lax.psum(s_gs.astype(jnp.bfloat16), "dp").astype(jnp.float32),
        lax.psum(s_wqkv.astype(jnp.bfloat16), "dp").astype(jnp.float32),
        lax.psum(s_wos.astype(jnp.bfloat16), "dp").astype(jnp.float32),
        lax.psum(s_gm.astype(jnp.bfloat16), "dp").astype(jnp.float32),
        lax.psum(s_w1s.astype(jnp.bfloat16), "dp").astype(jnp.float32),
        lax.psum(s_w2s.astype(jnp.bfloat16), "dp").astype(jnp.float32),
        lax.psum(s_query.astype(jnp.bfloat16), "dp").astype(jnp.float32),
        lax.psum(grad_rows.astype(jnp.bfloat16), "dp").astype(jnp.float32),
    )
    (
        f_wk,
        f_wv,
        f_wo,
        f_gc,
        f_w1c,
        f_w2c,
        f_gs,
        f_wqkv,
        f_wos,
        f_gm,
        f_w1s,
        f_w2s,
        query_rows,
        rows_total,
    ) = summed
    query_low = query_rows.astype(jnp.bfloat16)
    normed_rows = lax.dynamic_slice_in_dim(normed_lat, position * row_count, row_count, 0)
    d_wq_part = left_matmul(normed_rows, query_low)
    grad_normed_rows = right_matmul(query_low, wq)
    grad_lat_norm, d_glat_part = norm_back(lat_rows, g_lat_f, grad_normed_rows)
    d_wq, d_glat = (
        lax.psum_scatter(
            d_wq_part.astype(jnp.bfloat16), "pix", scatter_dimension=0, tiled=True
        ).astype(jnp.float32),
        lax.psum_scatter(
            d_glat_part.astype(jnp.bfloat16), "pix", scatter_dimension=0, tiled=True
        ).astype(jnp.float32),
    )
    d_gpix = lax.psum(grad_pix_gain, ("dp", "pix"))
    latent_out = jnp.stack(outputs)[None]
    pixel_out = jnp.stack(pixel_grads)[None]
    return (
        latent_out,
        pixel_out,
        rows_total + grad_lat_norm,
        d_gpix,
        d_glat,
        d_wq,
        f_wk,
        f_wv,
        f_wo,
        f_gc,
        f_w1c,
        f_w2c,
        f_gs,
        f_wqkv,
        f_wos,
        f_gm,
        f_w1s,
        f_w2s,
    )


MESH = pl.DeviceIdType.MESH
HBM = pl.BlockSpec(memory_space=pl.ANY)
VMEM = pl.BlockSpec(memory_space=pltpu.VMEM)
MIB = 1024 * 1024
PIECE = 256
BLOCK = 1024
FROWS = 272
DEN_ROW = 261
TOP_ROW = 263
GAIN_LANE = 264


def place():
    dp, pix = lax.axis_index("dp"), lax.axis_index("pix")
    return dp // 2, dp % 2, pix // 2, pix % 2


def device(x, c, z, y):
    return {"dp": x * 2 + c, "pix": z * 2 + y}


def greet(partners):
    barrier = pltpu.get_barrier_semaphore()
    for partner in partners:
        pl.semaphore_signal(barrier, inc=1, device_id=partner, device_id_type=MESH)
    pl.semaphore_wait(barrier, len(partners))


def remote(source, target, sems, index, partner):
    return pltpu.make_async_remote_copy(
        src_ref=source,
        dst_ref=target,
        send_sem=sems[0].at[index],
        recv_sem=sems[1].at[index],
        device_id=partner,
        device_id_type=MESH,
    )


def remote_params(collective_id, vmem=48 * MIB):
    return pltpu.CompilerParams(
        collective_id=collective_id, has_side_effects=True, vmem_limit_bytes=vmem
    )


def normed_block(raw, gain, wide_ref):
    features = raw.shape[1]
    values = raw.astype(jnp.float32)
    average = jnp.sum(values, 1, keepdims=True) * (1.0 / features)
    centered = values - average
    scale = lax.rsqrt(jnp.sum(centered * centered, 1, keepdims=True) * (1.0 / features) + 1e-05)
    unit = centered * scale
    lanes = lax.broadcasted_iota(jnp.int32, wide_ref.shape, 1)
    wide_ref[...] = jnp.where(lanes == DEN_ROW, 1.0, 0.0).astype(jnp.bfloat16)
    wide_ref[:, :features] = (unit * gain).astype(jnp.bfloat16)
    return unit, scale


def three_parts(row):
    first = row.astype(jnp.bfloat16).astype(jnp.float32)
    rest = row - first
    second = rest.astype(jnp.bfloat16).astype(jnp.float32)
    return first, second, rest - second


def with_rows(tail, den, top):
    rows = lax.broadcasted_iota(jnp.int32, tail.shape, 0) + (FROWS - 16)
    high = den.astype(jnp.bfloat16).astype(jnp.float32)
    first, second, third = three_parts(top)
    tail = jnp.where(rows == DEN_ROW, high, tail)
    tail = jnp.where(rows == DEN_ROW + 1, den - high, tail)
    tail = jnp.where(rows == TOP_ROW, first, tail)
    tail = jnp.where(rows == TOP_ROW + 1, second, tail)
    return jnp.where(rows == TOP_ROW + 2, third, tail)


def read_rows(tail):
    at = DEN_ROW - (FROWS - 16)
    den = tail[at : at + 1] + tail[at + 1 : at + 2]
    at = TOP_ROW - (FROWS - 16)
    top = tail[at : at + 1] + tail[at + 1 : at + 2] + tail[at + 2 : at + 3]
    return den, top


def merge(pieces):
    bodies = [piece[: FROWS - 16].astype(jnp.float32) for piece in pieces]
    tails = [piece[FROWS - 16 :].astype(jnp.float32) for piece in pieces]
    read = [read_rows(tail) for tail in tails]
    top = functools.reduce(jnp.maximum, [row for unused, row in read])
    factors = [jnp.exp(row - top) for unused, row in read]
    body = sum(values * factor for values, factor in zip(bodies, factors, strict=True))
    tail = sum(values * factor for values, factor in zip(tails, factors, strict=True))
    den = sum(row * factor for (row, unused), factor in zip(read, factors, strict=True))
    return body, tail, den, top


class Gather:
    def __init__(self, shards, wholes, splits, send, recv, local):
        self.shards, self.wholes, self.splits = shards, wholes, splits
        self.sems, self.local = (send, recv), local
        self.place = place()
        x, c, z, y = self.place
        self.core, self.across = device(x, 1 - c, z, y), device(1 - x, c, z, y)
        self.beside = device(x, c, z, 1 - y)
        self.along, self.side, self.over, self.between, self.keep = {}, {}, {}, {}, {}

    def part(self, k, ref):
        x, c, z, y = self.place
        return ref.at[x, c] if self.splits[k] else ref.at[:, c]

    def start(self, k):
        x, c, z, y = self.place
        mine, home = self.part(k, self.shards[k]), self.part(k, self.wholes[k].at[z, y])
        for i in (1, 2, 3):
            target = device(x, c, (z + i) % 4, y)
            self.along[k, i] = remote(mine, home, self.sems, (k, i - 1), target)
            self.along[k, i].start()
        self.side[k, 0] = remote(mine, home, self.sems, (k, 3), self.beside)
        self.side[k, 0].start()
        self.keep[k] = pltpu.make_async_copy(
            self.shards[k], self.wholes[k].at[z, y], self.local.at[k]
        )
        self.keep[k].start()

    def to_side(self, k):
        x, c, z, y = self.place
        for i in (1, 2, 3):
            self.along[k, i].wait_recv()
            block = self.part(k, self.wholes[k].at[(z + 4 - i) % 4, y])
            self.side[k, i] = remote(block, block, self.sems, (k, 3 + i), self.beside)
            self.side[k, i].start()

    def to_over(self, k):
        x, c, z, y = self.place
        for i in range(4):
            self.side[k, i].wait_recv()
            if self.splits[k]:
                if i == 0:
                    block = self.wholes[k].at[z, 1 - y, x, c]
                else:
                    block = self.wholes[k].at[(z + 4 - i) % 4, :, x, c]
                self.over[k, i] = remote(block, block, self.sems, (k, 7 + i), self.across)
                self.over[k, i].start()

    def to_core(self, k):
        x, c, z, y = self.place
        for i in range(4):
            if self.splits[k]:
                self.over[k, i].wait_recv()
            if i == 0:
                block = self.wholes[k].at[z, 1 - y, :, c]
            else:
                block = self.wholes[k].at[(z + 4 - i) % 4, :, :, c]
            self.between[k, i] = remote(block, block, self.sems, (k, 11 + i), self.core)
            self.between[k, i].start()

    def arrive(self, k):
        self.keep[k].wait()
        for i in range(4):
            self.between[k, i].wait_recv()

    def finish(self):
        for group in (self.along, self.side, self.over, self.between):
            for copy in group.values():
                copy.wait_send()


def opening_kernel(splits, scale, *refs):
    count = len(splits)
    same, last = refs[:2]
    shards, cot, pixels, pix_gain = refs[2 : count + 2], *refs[count + 2 : count + 5]
    refs = refs[count + 5 :]
    wholes, cot_rows, weights_out = refs[:count], refs[count], refs[count + 1]
    normed_out, queries_out, query_out, tops, means, rows_out = refs[count + 2 : count + 8]
    refs = refs[count + 8 :]
    raw, wide, weights, scores_ref, lat, wq, key, total, largest, pieces, sums = refs[:11]
    side_in, own, along_in = refs[11:14]
    send, recv, local, cot_send, cot_recv, own_send, own_recv, load = refs[14:]
    x, c, z, y = place()
    dp, pix = lax.axis_index("dp"), lax.axis_index("pix")
    micros, slots, features = pixels.shape
    blocks = slots // BLOCK
    per_block = BLOCK // PIECE
    images = sums.shape[1]
    others = [{"dp": dp, "pix": (pix + i) % 8} for i in range(1, 8)]
    gather = Gather(shards, wholes, splits, send, recv, local)
    greet([*others, gather.core, gather.across])

    fetch = pltpu.make_async_copy(pixels, raw, load.at[0])
    fetch.start()
    for k in range(count):
        gather.start(k)
    gain = pix_gain[...]

    def norm(start, stop):
        def one(i, carry):
            rows = pl.ds(pl.multiple_of((i % blocks) * BLOCK, BLOCK), BLOCK)
            normed_block(raw[i // blocks, rows, :], gain, wide.at[i // blocks, rows])
            return carry

        lax.fori_loop(start, stop, one, 0)

    fetch.wait()
    norm(0, 2)
    for k in range(3):
        gather.to_side(k)
    norm(2, 4)
    for k in range(3):
        gather.to_over(k)
    norm(4, 6)
    for k in range(3):
        gather.to_core(k)
    gather.to_side(3)
    gather.to_side(4)
    norm(6, 2 * blocks)
    gather.to_over(3)
    fetches = []
    for k, target in enumerate((lat, wq, key)):
        gather.arrive(k)
        fetches.append(pltpu.make_async_copy(wholes[k], target, load.at[1 + k]))
        fetches[k].start()
    gather.to_side(5)
    gather.to_over(4)
    for copy in fetches:
        copy.wait()

    lat_values = lat[...].reshape(sums.shape[3], -1).astype(jnp.float32)
    key_values = key[...].reshape(lat_values.shape[1], -1)
    columns = key_values[:, 256:384].astype(jnp.float32).T
    normed = layer_norm(lat_values, columns[GAIN_LANE - 256 : GAIN_LANE - 255])
    normed_out[...] = normed.astype(jnp.bfloat16)
    wq_values = wq[...].reshape(lat_values.shape[1], -1)
    queries_out[...] = matmul(normed_out[...], wq_values).astype(jnp.bfloat16)
    query_t = (
        lax.dot_general(
            key_values, queries_out[...], (((0,), (1,)), ((), ())),
            preferred_element_type=jnp.float32,
        )
        * scale
    )
    rows = lax.broadcasted_iota(jnp.int32, query_t.shape, 0)
    query_out[...] = jnp.where(rows < features, query_t, 0.0).astype(jnp.bfloat16)

    gather.to_side(6)
    gather.to_over(5)
    gather.to_core(3)
    gather.to_core(4)

    def forward(m):
        total[...] = jnp.zeros_like(total)
        largest[...] = jnp.full(largest.shape, -big_value, jnp.float32)

        def one(b, carry):
            rows = pl.ds(pl.multiple_of(b * BLOCK, BLOCK), BLOCK)
            scores_ref[...] = matmul(wide[m, rows, :], query_out[...])
            for k in range(per_block):
                rows = pl.ds(pl.multiple_of(b * BLOCK + k * PIECE, PIECE), PIECE)
                scores = scores_ref[k * PIECE : (k + 1) * PIECE]
                top = jnp.max(scores, 0, keepdims=True)
                low = jnp.exp(scores - top).astype(jnp.bfloat16)
                weights[m, rows, :] = low
                piece = b * per_block + k
                tops[m, piece] = top
                added = left_matmul(wide[m, rows, :FROWS], low)
                before = jnp.where(
                    same[m * blocks * per_block + piece] > 0, largest[...], -big_value
                )
                now = jnp.maximum(before, top)
                largest[...] = now
                older, newer = jnp.exp(before - now), jnp.exp(top - now)
                summed = total[...] * older + added * newer
                total[...] = summed
                pieces[piece, : FROWS - 16] = summed[: FROWS - 16].astype(jnp.bfloat16)
                at = DEN_ROW - (FROWS - 16)
                tail = summed[FROWS - 16 :]
                pieces[piece, FROWS - 16 :] = with_rows(tail, tail[at : at + 1], now).astype(
                    jnp.bfloat16
                )
            return carry

        lax.fori_loop(0, blocks, one, 0)
        for image in range(images):
            index = last[m * images + image]
            present = index >= 0
            piece = pieces[jnp.maximum(index, 0)].astype(jnp.float32)
            sums[m, image, : FROWS - 16] = jnp.where(present, piece[: FROWS - 16], 0.0).astype(
                jnp.bfloat16
            )
            nothing = jnp.zeros((1, piece.shape[1]), jnp.float32)
            absent = with_rows(
                jnp.zeros((16, piece.shape[1]), jnp.float32), nothing, nothing - big_value
            )
            sums[m, image, FROWS - 16 :] = jnp.where(
                present, piece[FROWS - 16 :], absent
            ).astype(jnp.bfloat16)

    own_sems = (own_send, own_recv)
    sides, alongs, keeps = {}, {}, []

    def send_sums(m):
        for i in (1, 2, 3, 0):
            source = sums.at[m, ((z + i) % 4) * 2 + 1 - y]
            sides[m, i] = remote(source, side_in.at[m, i], own_sems, (m, i), gather.beside)
            sides[m, i].start()
        keeps.append(pltpu.make_async_copy(weights.at[m], weights_out.at[m], load.at[4 + m]))
        keeps[-1].start()

    def pass_sums(m):
        for i in (1, 2, 3, 0):
            sides[m, i].wait_recv()
            body, tail, den, top = merge([sums[m, ((z + i) % 4) * 2 + y], side_in[m, i]])
            own[m, i, : FROWS - 16] = body.astype(jnp.bfloat16)
            own[m, i, FROWS - 16 :] = with_rows(tail, den, top).astype(jnp.bfloat16)
            if i:
                target = device(x, c, (z + i) % 4, y)
                alongs[m, i] = remote(
                    own.at[m, i], along_in.at[m, i - 1], own_sems, (m, 3 + i), target
                )
                alongs[m, i].start()

    def finish_sums(m):
        for i in (1, 2, 3):
            alongs[m, i].wait_recv()
        body, tail, den, top = merge([own[m, 0]] + [along_in[m, i] for i in range(3)])
        rows = lax.broadcasted_iota(jnp.int32, tail.shape, 0) + (FROWS - 16)
        means[m, : FROWS - 16] = (body / den).astype(jnp.bfloat16)
        means[m, FROWS - 16 :] = jnp.where(rows < DEN_ROW, tail / den, 0.0).astype(jnp.bfloat16)
        rows_out[m, 0:1] = den
        rows_out[m, 1:2] = top

    forward(0)
    send_sums(0)
    gather.to_side(7)
    gather.to_over(6)
    gather.to_core(5)
    forward(1)
    send_sums(1)
    pass_sums(0)
    gather.to_side(8)
    gather.to_over(7)
    gather.to_core(6)
    pass_sums(1)
    cots = [pltpu.make_async_copy(cot.at[:, pix], cot_rows.at[:, pix], local.at[count])]
    for i, other in enumerate(others):
        cots.append(
            remote(
                cot.at[:, (pix + i + 1) % 8],
                cot_rows.at[:, pix],
                (cot_send, cot_recv),
                i,
                other,
            )
        )
    for copy in cots:
        copy.start()
    gather.to_side(9)
    gather.to_side(10)
    gather.to_over(8)
    gather.to_core(7)
    gather.to_over(9)
    finish_sums(0)
    gather.to_over(10)
    gather.to_core(8)
    finish_sums(1)
    gather.to_core(9)
    gather.to_core(10)
    for k in range(3, count):
        gather.arrive(k)
    for copy in (*cots, *keeps):
        copy.wait()
    gather.finish()
    for copy in (*sides.values(), *alongs.values()):
        copy.wait_send()


def opening(same, last, shards, splits, cot, pixels, gain, scale):
    count = len(shards)
    bf16, f32 = jnp.bfloat16, jnp.float32
    micros, slots, features = pixels.shape
    latents, width = 8 * shards[0].shape[0], shards[0].shape[1]
    images = cot.shape[1]
    views = [shard.reshape(2, 2, shard.shape[0] // 4, shard.shape[1]) for shard in shards]
    outs = [jax.ShapeDtypeStruct((4, 2, *view.shape), view.dtype) for view in views]
    piece = (FROWS, latents)
    smem = pl.BlockSpec(memory_space=pltpu.SMEM)
    results = pl.pallas_call(
        functools.partial(opening_kernel, splits, scale),
        out_shape=[
            *outs,
            jax.ShapeDtypeStruct(cot.shape, cot.dtype),
            jax.ShapeDtypeStruct((micros, slots, latents), bf16),
            jax.ShapeDtypeStruct((latents, width), bf16),
            jax.ShapeDtypeStruct((latents, width), bf16),
            jax.ShapeDtypeStruct((384, latents), bf16),
            jax.ShapeDtypeStruct((micros, slots // PIECE, 1, latents), f32),
            jax.ShapeDtypeStruct((micros, *piece), bf16),
            jax.ShapeDtypeStruct((micros, 2, latents), f32),
        ],
        in_specs=[smem, smem] + [HBM] * (count + 2) + [VMEM],
        out_specs=[HBM] * (count + 2) + [VMEM] * 6,
        scratch_shapes=[
            pltpu.VMEM(pixels.shape, bf16),
            pltpu.VMEM((micros, slots, 384), bf16),
            pltpu.VMEM((micros, slots, latents), bf16),
            pltpu.VMEM((BLOCK, latents), f32),
            pltpu.VMEM(outs[0].shape, bf16),
            pltpu.VMEM(outs[1].shape, bf16),
            pltpu.VMEM(outs[2].shape, bf16),
            pltpu.VMEM(piece, f32),
            pltpu.VMEM((1, latents), f32),
            pltpu.VMEM((slots // PIECE, *piece), bf16),
            pltpu.VMEM((micros, images, *piece), bf16),
            pltpu.VMEM((micros, 4, *piece), bf16),
            pltpu.VMEM((micros, 4, *piece), bf16),
            pltpu.VMEM((micros, 3, *piece), bf16),
            pltpu.SemaphoreType.DMA((count, 15)),
            pltpu.SemaphoreType.DMA((count, 15)),
            pltpu.SemaphoreType.DMA((count + 1,)),
            pltpu.SemaphoreType.DMA((7,)),
            pltpu.SemaphoreType.DMA((7,)),
            pltpu.SemaphoreType.DMA((micros, 7)),
            pltpu.SemaphoreType.DMA((micros, 7)),
            pltpu.SemaphoreType.DMA((4 + micros,)),
        ],
        compiler_params=remote_params(0, 60 * MIB),
        name="opening",
    )(same, last, *views, cot, pixels, gain)
    wholes = [
        whole.reshape(8 * shard.shape[0], shard.shape[1])
        for whole, shard in zip(results[:count], shards, strict=True)
    ]
    return wholes, results[count:]


def pixel_backward_kernel(
    segs,
    pixels,
    gain,
    queries,
    weights,
    tops,
    grads,
    out,
    query_sums,
    gain_sums,
    wide_ref,
    scores_ref,
    back_ref,
):
    micro, block = pl.program_id(0), pl.program_id(1)
    pieces = BLOCK // PIECE
    per_micro = pieces * pl.num_programs(1)
    images = grads.shape[1]
    features = pixels.shape[2]

    @pl.when((block == 0) & (micro == 0))
    def _():
        query_sums[...] = jnp.zeros_like(query_sums)
        gain_sums[...] = jnp.zeros_like(gain_sums)

    unit, scale = normed_block(pixels[0], gain[...], wide_ref)
    for k in range(pieces):
        rows = pl.ds(k * PIECE, PIECE)
        seg = segs[micro * per_micro + block * pieces + k]
        image = jnp.minimum(seg, images - 1)
        grad = grads[0, image]
        unused, top = read_rows(grads[0, image, FROWS - 16 :].astype(jnp.float32))
        factor = jnp.where(seg < images, jnp.exp(tops[0, k] - top), 0.0)
        full = weights[0, rows, :].astype(jnp.float32) * factor
        slopes = jnp.dot(
            wide_ref[rows, :FROWS], grad, preferred_element_type=jnp.float32
        )
        scores_ref[rows, :] = (full * slopes).astype(jnp.bfloat16)
        back_ref[rows, :] = lax.dot_general(
            full.astype(jnp.bfloat16),
            grad,
            (((1,), (1,)), ((), ())),
            preferred_element_type=jnp.float32,
        )
    scores = scores_ref[...]
    query_sums[...] += lax.dot_general(
        wide_ref[:, :FROWS], scores, (((0,), (0,)), ((), ())), preferred_element_type=jnp.float32
    )
    back = back_ref[...] + lax.dot_general(
        scores, queries[:FROWS], (((1,), (1,)), ((), ())), preferred_element_type=jnp.float32
    )
    back = back[:, :features]
    gain_sums[...] += jnp.sum(back * unit, 0, keepdims=True)
    back = back * gain[...]
    mean = jnp.sum(back, 1, keepdims=True) * (1.0 / features)
    slope = jnp.sum(back * unit, 1, keepdims=True) * (1.0 / features)
    out[0] = (back - mean - unit * slope) * scale


def pixel_backward(segs, pixels, gain, queries, weights, tops, grads):
    micros, slots, features = pixels.shape
    latents = queries.shape[1]
    blocks = slots // BLOCK
    images = grads.shape[1]
    return pl.pallas_call(
        pixel_backward_kernel,
        grid_spec=pltpu.PrefetchScalarGridSpec(
            num_scalar_prefetch=1,
            grid=(micros, blocks),
            in_specs=[
                pl.BlockSpec((1, BLOCK, features), lambda m, b, s: (m, b, 0)),
                pl.BlockSpec((1, features), lambda m, b, s: (0, 0)),
                pl.BlockSpec(queries.shape, lambda m, b, s: (0, 0)),
                pl.BlockSpec((1, BLOCK, latents), lambda m, b, s: (m, b, 0)),
                pl.BlockSpec((1, BLOCK // PIECE, 1, latents), lambda m, b, s: (m, b, 0, 0)),
                pl.BlockSpec((1, images, FROWS, latents), lambda m, b, s: (m, 0, 0, 0)),
            ],
            out_specs=[
                pl.BlockSpec((1, BLOCK, features), lambda m, b, s: (m, b, 0)),
                pl.BlockSpec((FROWS, latents), lambda m, b, s: (0, 0)),
                pl.BlockSpec((1, features), lambda m, b, s: (0, 0)),
            ],
            scratch_shapes=[
                pltpu.VMEM((BLOCK, queries.shape[0]), jnp.bfloat16),
                pltpu.VMEM((BLOCK, latents), jnp.bfloat16),
                pltpu.VMEM((BLOCK, FROWS), jnp.float32),
            ],
        ),
        out_shape=[
            jax.ShapeDtypeStruct((micros, slots, features), jnp.float32),
            jax.ShapeDtypeStruct((FROWS, latents), jnp.float32),
            jax.ShapeDtypeStruct((1, features), jnp.float32),
        ],
        compiler_params=pltpu.CompilerParams(vmem_limit_bytes=48 * MIB),
        name="pixel_backward",
    )(segs, pixels, gain, queries, weights, tops, grads)


def holder_kernel(grads, rows_in, out, packed, send, recv, local):
    x, c, z, y = place()
    sems = (send, recv)
    micros = grads.shape[0]
    beside = device(x, c, z, 1 - y)
    greet([device(x, c, (z + i) % 4, y) for i in (1, 2, 3)] + [beside])
    for m in range(micros):
        packed[m, : FROWS - 16] = grads[m, : FROWS - 16].astype(jnp.bfloat16)
        tail = grads[m, FROWS - 16 :]
        rows = lax.broadcasted_iota(jnp.int32, tail.shape, 0) + (FROWS - 16)
        tail = with_rows(tail, rows_in[m, 0:1], rows_in[m, 1:2])
        tail = jnp.where(rows == DEN_ROW + 1, 0.0, tail)
        packed[m, FROWS - 16 :] = tail.astype(jnp.bfloat16)
    home = out.at[:, z, y]
    alongs, sides = {}, {}
    for i in (1, 2, 3):
        alongs[i] = remote(packed, home, sems, i, device(x, c, (z + i) % 4, y))
        alongs[i].start()
    sides[0] = remote(packed, home, sems, 0, beside)
    sides[0].start()
    keep = pltpu.make_async_copy(packed, home, local)
    keep.start()
    for i in (1, 2, 3):
        alongs[i].wait_recv()
        block = out.at[:, (z + 4 - i) % 4, y]
        sides[i] = remote(block, block, sems, 3 + i, beside)
        sides[i].start()
    for copy in sides.values():
        copy.wait()
    for copy in alongs.values():
        copy.wait_send()
    keep.wait()


def to_holders(grads, rows):
    micros, frows, latents = grads.shape
    out = pl.pallas_call(
        holder_kernel,
        out_shape=jax.ShapeDtypeStruct((micros, 4, 2, frows, latents), jnp.bfloat16),
        in_specs=[VMEM, VMEM],
        out_specs=HBM,
        scratch_shapes=[
            pltpu.VMEM((micros, frows, latents), jnp.bfloat16),
            pltpu.SemaphoreType.DMA((7,)),
            pltpu.SemaphoreType.DMA((7,)),
            pltpu.SemaphoreType.DMA,
        ],
        compiler_params=remote_params(2),
        name="to_holders",
    )(grads, rows)
    return out.reshape(micros, 8, frows, latents)


def softmax_parts(packed, scale):
    width = packed.shape[1] // 3
    query, key, value = packed[:, :width], packed[:, width : 2 * width], packed[:, 2 * width :]
    scores = right_matmul(query, key) * scale
    weights = jnp.exp(scores - jnp.max(scores, 1, keepdims=True))
    return query, key, value, weights, jnp.sum(weights, 1, keepdims=True)


def attention_kernel(scale, packed, out):
    query, key, value, weights, den = softmax_parts(packed[0], scale)
    out[0] = (matmul(weights.astype(jnp.bfloat16), value) / den).astype(jnp.bfloat16)


def attention_back_kernel(scale, packed, grad, out):
    width = grad.shape[2]
    query, key, value, weights, den = softmax_parts(packed[0], scale)
    grad_num = (grad[0] / den).astype(jnp.bfloat16)
    slopes = right_matmul(grad_num, value)
    grad_den = -jnp.sum(weights * slopes, 1, keepdims=True) / den
    scores = (weights * (slopes + grad_den)).astype(jnp.bfloat16)
    out[0, :, :width] = (matmul(scores, key) * scale).astype(jnp.bfloat16)
    out[0, :, width : 2 * width] = (left_matmul(scores, query) * scale).astype(jnp.bfloat16)
    out[0, :, 2 * width :] = left_matmul(weights.astype(jnp.bfloat16), grad_num).astype(
        jnp.bfloat16
    )


def head_spec(rows, width):
    return pl.BlockSpec((1, rows, width), lambda m, h: (m, 0, h))


def attention(packed, scale):
    micros, rows, columns = packed.shape
    width = columns // HEADS
    return pl.pallas_call(
        functools.partial(attention_kernel, scale),
        grid=(micros, HEADS),
        in_specs=[head_spec(rows, width)],
        out_specs=head_spec(rows, width // 3),
        out_shape=jax.ShapeDtypeStruct((micros, rows, columns // 3), jnp.bfloat16),
        compiler_params=pltpu.CompilerParams(vmem_limit_bytes=48 * MIB),
        name="attention",
    )(packed)


def attention_back(packed, grad, scale):
    micros, rows, columns = packed.shape
    width = columns // HEADS
    return pl.pallas_call(
        functools.partial(attention_back_kernel, scale),
        grid=(micros, HEADS),
        in_specs=[head_spec(rows, width), head_spec(rows, width // 3)],
        out_specs=head_spec(rows, width),
        out_shape=jax.ShapeDtypeStruct(packed.shape, jnp.bfloat16),
        compiler_params=pltpu.CompilerParams(vmem_limit_bytes=48 * MIB),
        name="attention_back",
    )(packed, grad)


def reduce_kernel(splits, *refs):
    count = len(splits)
    grads, rows_in = refs[:count], refs[count]
    finals, rows_out = refs[count + 1 : 2 * count + 1], refs[2 * count + 1]
    rest = refs[2 * count + 2 :]
    own, core_in, over_in, side_in, along_in = (
        rest[i * count : (i + 1) * count] for i in range(5)
    )
    send, recv, local, row_send, row_recv = rest[5 * count :]
    x, c, z, y = place()
    pix = lax.axis_index("pix")
    sems = (send, recv)
    others = [(pix + i) % 8 for i in range(1, 8)]
    core, across, beside = device(x, 1 - c, z, y), device(1 - x, c, z, y), device(x, c, z, 1 - y)
    greet([{"dp": x * 2 + c, "pix": other} for other in others] + [core, across])
    loads, between, over, side, along, back, last = [], [], {}, {}, {}, {}, {}
    for k in range(count):
        between.append(remote(grads[k].at[:, :, :, 1 - c], core_in[k], sems, (k, 0), core))
        between[k].start()
        loads.append(pltpu.make_async_copy(grads[k].at[:, :, :, c], own[k], local.at[k]))
        loads[k].start()
    keep = pltpu.make_async_copy(rows_in.at[:, pix], rows_out.at[:, pix], local.at[count])
    keep.start()
    rows = []
    for i, other in enumerate(others):
        copy = remote(
            rows_in.at[:, other],
            rows_out.at[:, pix],
            (row_send, row_recv),
            i,
            {"dp": x * 2 + c, "pix": other},
        )
        copy.start()
        rows.append(copy)

    def after_core(k):
        loads[k].wait()
        between[k].wait()

        def add(i, carry):
            own[k][i // 2, i % 2] = own[k][i // 2, i % 2] + core_in[k][i // 2, i % 2]
            return carry

        lax.fori_loop(0, 8, add, 0)
        if splits[k]:
            over[k] = remote(own[k].at[:, :, 1 - x], over_in[k], sems, (k, 1), across)
            over[k].start()

    def after_over(k):
        if splits[k]:
            over[k].wait()

            def add(i, carry):
                own[k][i // 2, i % 2, x] = own[k][i // 2, i % 2, x] + over_in[k][i // 2, i % 2]
                return carry

            lax.fori_loop(0, 8, add, 0)
            source = own[k].at[:, 1 - y, x]
        else:
            source = own[k].at[:, 1 - y]
        side[k] = remote(source, side_in[k], sems, (k, 2), beside)
        side[k].start()

    def after_side(k):
        side[k].wait()

        def add(i, carry):
            if splits[k]:
                own[k][i, y, x] = own[k][i, y, x] + side_in[k][i]
            else:
                own[k][i, y] = own[k][i, y] + side_in[k][i]
            return carry

        lax.fori_loop(0, 4, add, 0)
        for i in (1, 2, 3):
            block = own[k].at[(z + i) % 4, y]
            along[k, i] = remote(
                block.at[x] if splits[k] else block,
                along_in[k].at[i - 1],
                sems,
                (k, 2 + i),
                device(x, c, (z + i) % 4, y),
            )
            along[k, i].start()

    def after_along(k):
        for i in (1, 2, 3):
            along[k, i].wait()
        block = own[k][z, y, x] if splits[k] else own[k][z, y]
        total = block.astype(jnp.float32)
        for i in range(3):
            total = total + along_in[k][i].astype(jnp.float32)
        total = total.astype(jnp.bfloat16)
        if splits[k]:
            finals[k][x, c] = total
            back[k] = remote(finals[k].at[x, c], finals[k].at[x, c], sems, (k, 6), across)
        else:
            own[k][z, y] = total
            back[k] = remote(own[k].at[z, y], over_in[k], sems, (k, 6), across)
        back[k].start()

    def after_back(k):
        back[k].wait()
        if not splits[k]:
            finals[k][:, c] = own[k][z, y] + over_in[k][...]
        last[k] = remote(finals[k].at[:, c], finals[k].at[:, c], sems, (k, 7), core)
        last[k].start()

    stages = (after_core, after_over, after_side, after_along, after_back)
    for step in range(count + len(stages) - 1):
        for number, stage in enumerate(stages):
            if 0 <= step - number < count:
                stage(step - number)
    for k in range(count):
        last[k].wait()
    for copy in rows:
        copy.wait()
    keep.wait()


def reduce_grads(grads, splits, rows):
    count = len(grads)
    views = [
        grad.reshape(4, 2, 2, 2, grad.shape[0] // 32, grad.shape[1]).astype(jnp.bfloat16)
        for grad in grads
    ]
    buffers = ([], [], [], [], [])
    for view, split in zip(views, splits, strict=True):
        block = view.shape[4:]
        lead = () if split else (2,)
        for group, shape in zip(
            buffers,
            (
                (4, 2, 2, *block),
                (4, 2, 2, *block),
                (4, 2, *block) if split else (2, *block),
                (4, *lead, *block),
                (3, *lead, *block),
            ),
            strict=True,
        ):
            group.append(pltpu.VMEM(shape, jnp.bfloat16))
    results = pl.pallas_call(
        functools.partial(reduce_kernel, splits),
        out_shape=[jax.ShapeDtypeStruct((2, 2, *view.shape[4:]), jnp.bfloat16) for view in views]
        + [jax.ShapeDtypeStruct(rows.shape, rows.dtype)],
        in_specs=[HBM] * (count + 1),
        out_specs=[VMEM] * count + [HBM],
        scratch_shapes=[
            *(shape for group in buffers for shape in group),
            pltpu.SemaphoreType.DMA((count, 8)),
            pltpu.SemaphoreType.DMA((count, 8)),
            pltpu.SemaphoreType.DMA((count + 1,)),
            pltpu.SemaphoreType.DMA((7,)),
            pltpu.SemaphoreType.DMA((7,)),
        ],
        compiler_params=remote_params(3, 56 * MIB),
        name="reduce_grads",
    )(*views, rows)
    shards = [
        result.reshape(grad.shape[0] // 8, grad.shape[1])
        for result, grad in zip(results[:-1], grads, strict=True)
    ]
    return shards, results[-1]


def spread_kernel(block, out, send, recv):
    pix, dp = lax.axis_index("pix"), lax.axis_index("dp")
    others = [(pix + i) % 8 for i in range(1, 8)]
    greet([{"dp": dp, "pix": other} for other in others])
    copies = []
    for i, other in enumerate(others):
        copy = remote(block, out.at[pix], (send, recv), i, {"dp": dp, "pix": other})
        copy.start()
        copies.append(copy)
    out[pix] = block[...]
    for copy in copies:
        copy.wait()


def spread(block):
    return pl.pallas_call(
        spread_kernel,
        out_shape=jax.ShapeDtypeStruct((8, *block.shape), block.dtype),
        in_specs=[VMEM],
        out_specs=VMEM,
        scratch_shapes=[pltpu.SemaphoreType.DMA((7,)), pltpu.SemaphoreType.DMA((7,))],
        compiler_params=remote_params(4),
        name="spread",
    )(block)


def image_body(
    image_sides,
    pixels,
    latent_array,
    pixel_gain,
    latent_gain,
    query_weight,
    key_weight,
    value_weight,
    cross_out_weight,
    cross_mlp_gain,
    cross_mlp_in,
    cross_mlp_out,
    self_gain,
    self_qkv_weight,
    self_out_weight,
    self_mlp_gain,
    self_mlp_in,
    self_mlp_out,
    cotangent,
):
    position = lax.axis_index("pix")
    micros, images = image_sides.shape[1:]
    capacity, features = pixels.shape[2:]
    row_count, width = latent_array.shape
    latents = row_count * 8
    head_size = width // HEADS
    cross_scale = width ** (-0.5)
    self_scale = head_size ** (-0.5)
    f32, bf16 = jnp.float32, jnp.bfloat16

    def widen(values, columns):
        return jnp.pad(values, ((0, 0), (0, columns - values.shape[1])))

    gains = jnp.stack([latent_gain, cross_mlp_gain, self_gain, self_mlp_gain], 1)
    gains = jnp.pad(gains, ((0, 0), (GAIN_LANE, 384 - GAIN_LANE - 4)))
    shards = (
        latent_array,
        query_weight,
        widen(key_weight.T, 384) + gains,
        widen(value_weight.T, 384),
        cross_out_weight,
        cross_mlp_in,
        cross_mlp_out,
        self_qkv_weight,
        self_out_weight,
        self_mlp_in,
        self_mlp_out,
    )
    splits = (True,) * len(shards)
    lengths = image_sides[0] * image_sides[0]
    ends = jnp.cumsum(lengths, 1)
    firsts = position * capacity + PIECE * jnp.arange(capacity // PIECE, dtype=jnp.int32)
    segs = jnp.sum((firsts[None, :, None] >= ends[:, None, :]).astype(jnp.int32), 2)
    same = jnp.pad((segs[:, 1:] == segs[:, :-1]).astype(jnp.int32), ((0, 0), (1, 0))).reshape(-1)
    here = segs[:, :, None] == jnp.arange(images, dtype=jnp.int32)[None, None, :]
    order = jnp.arange(capacity // PIECE, dtype=jnp.int32)[None, :, None]
    last = jnp.max(jnp.where(here, order, -1), 1).reshape(-1)
    segs = segs.reshape(-1)
    gain_pix = pixel_gain.astype(f32)[None]
    wholes, results = opening(
        same, last, shards, splits, cotangent[0], pixels[0], gain_pix, cross_scale
    )
    lat_full, wq, key_t, value_t, wo, w1c, w2c, wqkv, wos, w1s, w2s = wholes
    cot_rows, pix_weights, normed_lat, queries, query_t, pix_tops, means, rows = results
    g_lat, g_cross, g_self, g_mlp = (key_t[:, GAIN_LANE + i].astype(f32) for i in range(4))
    value_t = value_t[:, :FROWS]
    lat_f = lat_full.astype(f32)
    den, top = rows[:, 0], rows[:, 1]

    att = jnp.einsum("mfr,df->mrd", means, value_t, preferred_element_type=f32)
    att_low = att.astype(bf16).reshape(micros * latents, width)
    start_rows = jnp.broadcast_to(lat_f[None], (micros, latents, width)).reshape(-1, width)
    after_cross = start_rows + matmul(att_low, wo)
    after_mlp, cross_kept = mlp_forward(after_cross, g_cross, w1c, w2c)
    normed_self = layer_norm(after_mlp, g_self).astype(bf16)
    packed = matmul(normed_self, wqkv).astype(bf16).reshape(micros, latents, 3 * width)
    self_att = attention(packed, self_scale).reshape(-1, width)
    after_self = after_mlp + matmul(self_att, wos)
    final, final_kept = mlp_forward(after_self, g_mlp, w1s, w2s)
    final = final.astype(bf16).reshape(micros, 8, row_count, width)

    grad = cot_rows.astype(f32).reshape(-1, width)
    grad, d_gm, d_w1s, d_w2s = mlp_backward(grad, after_self, g_mlp, w1s, w2s, final_kept)
    grad_low = grad.astype(bf16)
    d_wos = left_matmul(self_att, grad_low)
    grad_att = right_matmul(grad_low, wos).reshape(micros, latents, width)
    grad_packed = attention_back(packed, grad_att, self_scale).reshape(-1, 3 * width)
    d_wqkv = left_matmul(normed_self, grad_packed)
    grad_inputs, d_gs = norm_back(after_mlp, g_self, right_matmul(grad_packed, wqkv))
    grad = grad + grad_inputs
    grad, d_gc, d_w1c, d_w2c = mlp_backward(grad, after_cross, g_cross, w1c, w2c, cross_kept)
    grad_lat = jnp.sum(grad.reshape(micros, latents, width), 0)
    grad_low = grad.astype(bf16)
    d_wo = left_matmul(att_low, grad_low)
    grad_att = right_matmul(grad_low, wo).reshape(micros, latents, width)
    grad_num = (grad_att / den[:, :, None]).astype(bf16)
    grad_den = -jnp.sum(grad_att * att, 2) / den
    grad_sums = jnp.einsum("mrd,df->mfr", grad_num, value_t, preferred_element_type=f32)
    d_wv = jnp.einsum("mrd,mfr->df", grad_att.astype(bf16), means, preferred_element_type=f32)
    all_grads = to_holders(grad_sums, jnp.stack([grad_den, top], 1))
    pixel_grad, query_sums, pix_gain_sums = pixel_backward(
        segs, pixels[0], gain_pix, query_t, pix_weights, pix_tops, all_grads
    )

    gain_grads = jnp.stack([d_gc, d_gs, d_gm], 1)
    small = jnp.concatenate([widen(d_wv, 384), widen(gain_grads, 128)], 1)
    halves = grad_lat.reshape(8, row_count, 2, width // 2).transpose(0, 2, 1, 3)
    small = jnp.concatenate([small, halves.reshape(8 * 2 * row_count, width // 2)], 1)
    query_rows = widen(query_sums.T, 384).reshape(8, row_count, 384)
    pix_gain_rows = jnp.pad(
        widen(pix_gain_sums, 384)[None], ((0, 7), (0, row_count - 1), (0, 0))
    )
    query_rows = jnp.concatenate([query_rows, pix_gain_rows], 1).reshape(-1, 384)
    parts = (
        d_w2s,
        d_w1s,
        d_wos,
        d_wqkv,
        d_w2c,
        d_w1c,
        d_wo,
        small,
        query_rows,
    )
    splits = (True, False, True, True, False, True, False, True, True)
    reduced, latent_out = reduce_grads(parts, splits, final)
    f_w2s, f_w1s, f_wos, f_wqkv, f_w2c, f_w1c, f_wo, small, query_rows = reduced
    query_all = spread(query_rows)
    d_gpix = query_all[0, row_count, :features].astype(f32)
    query_all = query_all[:, :row_count].reshape(latents, 384)

    grad_queries = (right_matmul(query_all, key_t) * cross_scale).astype(bf16)
    columns = lax.dynamic_slice_in_dim(normed_lat, position * (width // 8), width // 8, 1)
    d_wq = left_matmul(columns, grad_queries)
    query_columns = lax.dynamic_slice_in_dim(queries, position * (width // 8), width // 8, 1)
    d_wk = (left_matmul(query_all, query_columns) * cross_scale)[:features]
    grad_norm_lat, d_glat = norm_back(lat_f, g_lat, right_matmul(grad_queries, wq))
    d_glat = lax.dynamic_slice_in_dim(d_glat, position * (width // 8), width // 8, 0)
    grad_norm_rows = lax.dynamic_slice_in_dim(grad_norm_lat, position * row_count, row_count, 0)
    grad_lat = small[:, width // 2 :].astype(f32).reshape(2, row_count, width // 2)
    grad_lat = grad_lat.transpose(1, 0, 2).reshape(row_count, width)
    return (
        latent_out[None],
        pixel_grad[None],
        grad_lat + grad_norm_rows,
        d_gpix,
        d_glat,
        d_wq,
        d_wk,
        small[:, :features].astype(f32).T,
        f_wo.astype(f32),
        small[:, 384].astype(f32),
        f_w1c.astype(f32),
        f_w2c.astype(f32),
        small[:, 385].astype(f32),
        f_wqkv.astype(f32),
        f_wos.astype(f32),
        small[:, 386].astype(f32),
        f_w1s.astype(f32),
        f_w2s.astype(f32),
    )


def solution(mesh):
    fits = dict(mesh.shape) == {"dp": 4, "pix": 8}
    return jax.shard_map(
        image_body if fits else starting_body,
        mesh=mesh,
        in_specs=(
            P("dp", None, None),
            P("dp", None, "pix", None),
            P("pix", None),
            P(),
            P("pix"),
            P("pix", None),
            P(None, "pix"),
            P(None, "pix"),
            P("pix", None),
            P("pix"),
            P("pix", None),
            P("pix", None),
            P("pix"),
            P("pix", None),
            P("pix", None),
            P("pix"),
            P("pix", None),
            P("pix", None),
            P("dp", None, None, "pix", None),
        ),
        out_specs=(
            P("dp", None, None, "pix", None),
            P("dp", None, "pix", None),
            P("pix", None),
            P(),
            P("pix"),
            P("pix", None),
            P(None, "pix"),
            P(None, "pix"),
            P("pix", None),
            P("pix"),
            P("pix", None),
            P("pix", None),
            P("pix"),
            P("pix", None),
            P("pix", None),
            P("pix"),
            P("pix", None),
            P("pix", None),
        ),
        check_vma=False,
    )
```

```python
import functools

import jax
import jax.numpy as jnp
from jax import lax
from jax.experimental import pallas as pl
from jax.experimental.pallas import tpu as pltpu
from jax.sharding import PartitionSpec as P

HEADS = 8
SIDE = 64


highest = lax.Precision.HIGHEST
big_value = 1e30


def layer_norm(values, gain):
    average = jnp.mean(values, -1, keepdims=True)
    centered = values - average
    return centered * lax.rsqrt(jnp.mean(centered * centered, -1, keepdims=True) + 1e-05) * gain


def matmul(left, right):
    return jnp.dot(left, right, preferred_element_type=jnp.float32)


def left_matmul(left, right):
    return lax.dot_general(
        left, right, (((0,), (0,)), ((), ())), preferred_element_type=jnp.float32
    )


def right_matmul(left, right):
    return lax.dot_general(
        left, right, (((1,), (1,)), ((), ())), preferred_element_type=jnp.float32
    )


def norm_back(values, gain, grad):
    unused, pullback = jax.vjp(layer_norm, values, gain)
    return pullback(grad)


def mlp_forward(inputs, gain, w_in, w_out):
    normed = layer_norm(inputs, gain).astype(jnp.bfloat16)
    hidden = matmul(normed, w_in)
    active = jax.nn.gelu(hidden).astype(jnp.bfloat16)
    return (inputs + matmul(active, w_out), (normed, hidden, active))


def mlp_backward(grad, inputs, gain, w_in, w_out, kept):
    normed, hidden, active = kept
    grad_low = grad.astype(jnp.bfloat16)
    grad_out = left_matmul(active, grad_low)
    grad_active = right_matmul(grad_low, w_out)
    unused, pullback = jax.vjp(jax.nn.gelu, hidden)
    grad_hidden = pullback(grad_active)[0].astype(jnp.bfloat16)
    grad_in = left_matmul(normed, grad_hidden)
    grad_normed = right_matmul(grad_hidden, w_in)
    grad_inputs, grad_gain = norm_back(inputs, gain, grad_normed)
    return (grad + grad_inputs, grad_gain, grad_in, grad_out)


def starting_body(
    image_sides,
    pixels,
    latent_array,
    pixel_gain,
    latent_gain,
    query_weight,
    key_weight,
    value_weight,
    cross_out_weight,
    cross_mlp_gain,
    cross_mlp_in,
    cross_mlp_out,
    self_gain,
    self_qkv_weight,
    self_out_weight,
    self_mlp_gain,
    self_mlp_in,
    self_mlp_out,
    cotangent,
):
    pieces = lax.axis_size("pix")
    position = lax.axis_index("pix")
    micros = image_sides.shape[1]
    images = image_sides.shape[2]
    capacity = pixels.shape[2]
    row_count = latent_array.shape[0]
    model_width = latent_array.shape[1]
    head_size = model_width // HEADS
    unit_count = images * HEADS // pieces
    window = min(images, (capacity - 2) // (SIDE * SIDE // 4) + 2)
    cross_scale = model_width ** (-0.5)
    self_scale = head_size ** (-0.5)
    shards = (
        latent_array,
        latent_gain,
        query_weight,
        key_weight,
        value_weight,
        cross_out_weight,
        cross_mlp_gain,
        cross_mlp_in,
        cross_mlp_out,
        self_gain,
        self_qkv_weight,
        self_out_weight,
        self_mlp_gain,
        self_mlp_in,
        self_mlp_out,
    )
    lat_rows = latent_array.astype(jnp.float32)
    gain_pix = pixel_gain.astype(jnp.float32)
    grad_rows = jnp.zeros((row_count, model_width), jnp.float32)
    grad_pix_gain = jnp.zeros(gain_pix.shape, jnp.float32)
    outputs = []
    pixel_grads = []
    totals = None
    for step_index in range(micros):
        gathered = (
            lax.all_gather(shards[0], "pix", axis=0, tiled=True),
            lax.all_gather(shards[1], "pix", axis=0, tiled=True),
            lax.all_gather(shards[2], "pix", axis=0, tiled=True),
            lax.all_gather(shards[3], "pix", axis=1, tiled=True),
            lax.all_gather(shards[4], "pix", axis=1, tiled=True),
            lax.all_gather(shards[5], "pix", axis=0, tiled=True),
            lax.all_gather(shards[6], "pix", axis=0, tiled=True),
            lax.all_gather(shards[7], "pix", axis=0, tiled=True),
            lax.all_gather(shards[8], "pix", axis=0, tiled=True),
            lax.all_gather(shards[9], "pix", axis=0, tiled=True),
            lax.all_gather(shards[10], "pix", axis=0, tiled=True),
            lax.all_gather(shards[11], "pix", axis=0, tiled=True),
            lax.all_gather(shards[12], "pix", axis=0, tiled=True),
            lax.all_gather(shards[13], "pix", axis=0, tiled=True),
            lax.all_gather(shards[14], "pix", axis=0, tiled=True),
        )
        lat_full, g_lat, wq, wk, wv, wo, g_cross, w1c, w2c, g_self, wqkv, wos, g_mlp, w1s, w2s = (
            gathered
        )
        g_lat_f = g_lat.astype(jnp.float32)
        gc_f = g_cross.astype(jnp.float32)
        gs_f = g_self.astype(jnp.float32)
        gm_f = g_mlp.astype(jnp.float32)
        if step_index == 0:
            normed_lat = layer_norm(lat_full.astype(jnp.float32), g_lat_f).astype(jnp.bfloat16)
            queries = matmul(normed_lat, wq).astype(jnp.bfloat16)
        side_list = image_sides[0, step_index]
        lengths = side_list * side_list
        ends = jnp.cumsum(lengths)
        slot_ids = position * capacity + jnp.arange(capacity, dtype=jnp.int32)
        segment = jnp.sum((slot_ids[:, None] >= ends[None, :]).astype(jnp.int32), 1)
        window_ids = segment[0] + jnp.arange(window, dtype=jnp.int32)
        select = (window_ids[:, None] == jnp.arange(images, dtype=jnp.int32)[None, :]).astype(
            jnp.float32
        )
        in_window = segment[None, :] == window_ids[:, None]
        raw_pixels = pixels[0, step_index].astype(jnp.float32)
        normed_pix = layer_norm(raw_pixels, gain_pix).astype(jnp.bfloat16)
        pixel_keys = matmul(normed_pix, wk).astype(jnp.bfloat16)
        pixel_values = matmul(normed_pix, wv).astype(jnp.bfloat16)
        scores = right_matmul(queries, pixel_keys) * cross_scale
        local_top = jnp.max(jnp.where(in_window[:, None, :], scores[None], -big_value), 2)
        image_top = jnp.max(jnp.where(select[:, :, None] > 0, local_top[:, None, :], -big_value), 0)
        image_top = lax.pmax(image_top, "pix")
        window_top = jnp.einsum("wb,br->wr", select, image_top, precision=highest)
        weights = jnp.where(
            in_window[:, None, :], jnp.exp(scores[None] - window_top[:, :, None]), 0.0
        )
        partial_den = jnp.sum(weights, 2)
        partial_num = jnp.einsum(
            "wrc,cd->wrd",
            weights.astype(jnp.bfloat16),
            pixel_values,
            preferred_element_type=jnp.float32,
        )
        full_num = jnp.einsum("wb,wrd->brd", select, partial_num, precision=highest)
        full_den = jnp.einsum("wb,wr->br", select, partial_den, precision=highest)
        num_rows, den_rows = (
            lax.psum_scatter(
                full_num.astype(jnp.bfloat16), "pix", scatter_dimension=1, tiled=True
            ).astype(jnp.float32),
            lax.psum_scatter(
                full_den.astype(jnp.bfloat16), "pix", scatter_dimension=1, tiled=True
            ).astype(jnp.float32),
        )
        attended = num_rows / den_rows[:, :, None]
        attended_low = attended.astype(jnp.bfloat16).reshape(images * row_count, model_width)
        start_rows = jnp.broadcast_to(lat_rows[None], (images, row_count, model_width)).reshape(
            images * row_count, model_width
        )
        after_cross = start_rows + matmul(attended_low, wo)
        after_mlp, cross_kept = mlp_forward(after_cross, gc_f, w1c, w2c)
        normed_self = layer_norm(after_mlp, gs_f).astype(jnp.bfloat16)
        packed = matmul(normed_self, wqkv).astype(jnp.bfloat16)
        packed = packed.reshape(images, row_count, HEADS, 3 * head_size).transpose(0, 2, 1, 3)
        packed = packed.reshape(pieces, unit_count, row_count, 3 * head_size)
        packed = lax.all_to_all(packed, "pix", split_axis=0, concat_axis=2, tiled=True)[0]
        head_query = packed[:, :, :head_size]
        head_key = packed[:, :, head_size : 2 * head_size]
        head_value = packed[:, :, 2 * head_size :]
        self_scores = (
            jnp.einsum("uqd,ukd->uqk", head_query, head_key, preferred_element_type=jnp.float32)
            * self_scale
        )
        self_top = jnp.max(self_scores, 2, keepdims=True)
        self_weights = jnp.exp(self_scores - self_top)
        self_den = jnp.sum(self_weights, 2, keepdims=True)
        self_num = jnp.einsum(
            "uqk,ukd->uqd",
            self_weights.astype(jnp.bfloat16),
            head_value,
            preferred_element_type=jnp.float32,
        )
        self_out = self_num / self_den
        returned = lax.all_to_all(
            self_out.astype(jnp.bfloat16), "pix", split_axis=1, concat_axis=0, tiled=True
        )
        returned = (
            returned.reshape(images, HEADS, row_count, head_size)
            .transpose(0, 2, 1, 3)
            .reshape(images * row_count, model_width)
        )
        after_self = after_mlp + matmul(returned, wos)
        final, final_kept = mlp_forward(after_self, gm_f, w1s, w2s)
        outputs.append(final.astype(jnp.bfloat16).reshape(images, row_count, model_width))
        grad = cotangent[0, step_index].astype(jnp.float32).reshape(images * row_count, model_width)
        grad, d_gm, d_w1s, d_w2s = mlp_backward(grad, after_self, gm_f, w1s, w2s, final_kept)
        grad_low = grad.astype(jnp.bfloat16)
        d_wos = left_matmul(returned, grad_low)
        grad_self = right_matmul(grad_low, wos)
        grad_self = grad_self.reshape(images, row_count, HEADS, head_size).transpose(0, 2, 1, 3)
        grad_self = grad_self.reshape(pieces, unit_count, row_count, head_size)
        grad_self = lax.all_to_all(
            grad_self.astype(jnp.bfloat16), "pix", split_axis=0, concat_axis=2, tiled=True
        ).astype(grad_self.dtype)[0]
        grad_num = (grad_self / self_den).astype(jnp.bfloat16)
        grad_den = -jnp.sum(grad_self * self_out, 2, keepdims=True) / self_den
        again_scores = (
            jnp.einsum("uqd,ukd->uqk", head_query, head_key, preferred_element_type=jnp.float32)
            * self_scale
        )
        again_weights = jnp.exp(again_scores - self_top)
        grad_weights = (
            jnp.einsum("uqd,ukd->uqk", grad_num, head_value, preferred_element_type=jnp.float32)
            + grad_den
        )
        grad_scores = (again_weights * grad_weights).astype(jnp.bfloat16)
        grad_query = (
            jnp.einsum("uqk,ukd->uqd", grad_scores, head_key, preferred_element_type=jnp.float32)
            * self_scale
        )
        grad_key = (
            jnp.einsum("uqk,uqd->ukd", grad_scores, head_query, preferred_element_type=jnp.float32)
            * self_scale
        )
        grad_value = jnp.einsum(
            "uqk,uqd->ukd",
            again_weights.astype(jnp.bfloat16),
            grad_num,
            preferred_element_type=jnp.float32,
        )
        grad_packed = jnp.concatenate([grad_query, grad_key, grad_value], 2).astype(jnp.bfloat16)
        grad_packed = lax.all_to_all(grad_packed, "pix", split_axis=1, concat_axis=0, tiled=True)
        grad_packed = (
            grad_packed.reshape(images, HEADS, row_count, 3 * head_size)
            .transpose(0, 2, 1, 3)
            .reshape(images * row_count, 3 * model_width)
        )
        d_wqkv = left_matmul(normed_self, grad_packed)
        grad_normed = right_matmul(grad_packed, wqkv)
        grad_inputs, d_gs = norm_back(after_mlp, gs_f, grad_normed)
        grad = grad + grad_inputs
        grad, d_gc, d_w1c, d_w2c = mlp_backward(grad, after_cross, gc_f, w1c, w2c, cross_kept)
        grad_rows = grad_rows + jnp.sum(grad.reshape(images, row_count, model_width), 0)
        grad_low = grad.astype(jnp.bfloat16)
        d_wo = left_matmul(attended_low, grad_low)
        grad_cross = right_matmul(grad_low, wo).reshape(images, row_count, model_width)
        cross_gnum = (grad_cross / den_rows[:, :, None]).astype(jnp.bfloat16)
        cross_gden = (-jnp.sum(grad_cross * attended, 2) / den_rows).astype(jnp.bfloat16)
        all_num, all_den = (
            lax.all_gather(cross_gnum, "pix", axis=1, tiled=True),
            lax.all_gather(cross_gden, "pix", axis=1, tiled=True),
        )
        select_low = select.astype(jnp.bfloat16)
        window_num = jnp.einsum(
            "wb,brd->wrd", select_low, all_num, preferred_element_type=jnp.float32
        ).astype(jnp.bfloat16)
        window_den = jnp.einsum(
            "wb,br->wr", select_low, all_den, preferred_element_type=jnp.float32
        )
        scores = right_matmul(queries, pixel_keys) * cross_scale
        weights = jnp.where(
            in_window[:, None, :], jnp.exp(scores[None] - window_top[:, :, None]), 0.0
        )
        cross_gweights = (
            jnp.einsum("wrd,cd->wrc", window_num, pixel_values, preferred_element_type=jnp.float32)
            + window_den[:, :, None]
        )
        cross_gscores = jnp.sum(weights * cross_gweights, 0).astype(jnp.bfloat16)
        query_terms = matmul(cross_gscores, pixel_keys) * cross_scale
        grad_keys = (left_matmul(cross_gscores, queries) * cross_scale).astype(jnp.bfloat16)
        grad_values = jnp.einsum(
            "wrc,wrd->cd",
            weights.astype(jnp.bfloat16),
            window_num,
            preferred_element_type=jnp.float32,
        ).astype(jnp.bfloat16)
        d_wk = left_matmul(normed_pix, grad_keys)
        d_wv = left_matmul(normed_pix, grad_values)
        grad_normed_pix = right_matmul(grad_keys, wk) + right_matmul(grad_values, wv)
        grad_pixels, d_gpix = norm_back(raw_pixels, gain_pix, grad_normed_pix)
        pixel_grads.append(grad_pixels)
        grad_pix_gain = grad_pix_gain + d_gpix
        terms = (
            d_wk,
            d_wv,
            d_wo,
            d_gc,
            d_w1c,
            d_w2c,
            d_gs,
            d_wqkv,
            d_wos,
            d_gm,
            d_w1s,
            d_w2s,
            query_terms,
        )
        reduced = (
            lax.psum_scatter(
                terms[0].astype(jnp.bfloat16), "pix", scatter_dimension=1, tiled=True
            ).astype(jnp.float32),
            lax.psum_scatter(
                terms[1].astype(jnp.bfloat16), "pix", scatter_dimension=1, tiled=True
            ).astype(jnp.float32),
            lax.psum_scatter(
                terms[2].astype(jnp.bfloat16), "pix", scatter_dimension=0, tiled=True
            ).astype(jnp.float32),
            lax.psum_scatter(
                terms[3].astype(jnp.bfloat16), "pix", scatter_dimension=0, tiled=True
            ).astype(jnp.float32),
            lax.psum_scatter(
                terms[4].astype(jnp.bfloat16), "pix", scatter_dimension=0, tiled=True
            ).astype(jnp.float32),
            lax.psum_scatter(
                terms[5].astype(jnp.bfloat16), "pix", scatter_dimension=0, tiled=True
            ).astype(jnp.float32),
            lax.psum_scatter(
                terms[6].astype(jnp.bfloat16), "pix", scatter_dimension=0, tiled=True
            ).astype(jnp.float32),
            lax.psum_scatter(
                terms[7].astype(jnp.bfloat16), "pix", scatter_dimension=0, tiled=True
            ).astype(jnp.float32),
            lax.psum_scatter(
                terms[8].astype(jnp.bfloat16), "pix", scatter_dimension=0, tiled=True
            ).astype(jnp.float32),
            lax.psum_scatter(
                terms[9].astype(jnp.bfloat16), "pix", scatter_dimension=0, tiled=True
            ).astype(jnp.float32),
            lax.psum_scatter(
                terms[10].astype(jnp.bfloat16), "pix", scatter_dimension=0, tiled=True
            ).astype(jnp.float32),
            lax.psum_scatter(
                terms[11].astype(jnp.bfloat16), "pix", scatter_dimension=0, tiled=True
            ).astype(jnp.float32),
            lax.psum_scatter(
                terms[12].astype(jnp.bfloat16), "pix", scatter_dimension=0, tiled=True
            ).astype(jnp.float32),
        )
        totals = reduced if totals is None else jax.tree.map(jnp.add, totals, reduced)
    s_wk, s_wv, s_wo, s_gc, s_w1c, s_w2c, s_gs, s_wqkv, s_wos, s_gm, s_w1s, s_w2s, s_query = totals
    summed = (
        lax.psum(s_wk.astype(jnp.bfloat16), "dp").astype(jnp.float32),
        lax.psum(s_wv.astype(jnp.bfloat16), "dp").astype(jnp.float32),
        lax.psum(s_wo.astype(jnp.bfloat16), "dp").astype(jnp.float32),
        lax.psum(s_gc.astype(jnp.bfloat16), "dp").astype(jnp.float32),
        lax.psum(s_w1c.astype(jnp.bfloat16), "dp").astype(jnp.float32),
        lax.psum(s_w2c.astype(jnp.bfloat16), "dp").astype(jnp.float32),
        lax.psum(s_gs.astype(jnp.bfloat16), "dp").astype(jnp.float32),
        lax.psum(s_wqkv.astype(jnp.bfloat16), "dp").astype(jnp.float32),
        lax.psum(s_wos.astype(jnp.bfloat16), "dp").astype(jnp.float32),
        lax.psum(s_gm.astype(jnp.bfloat16), "dp").astype(jnp.float32),
        lax.psum(s_w1s.astype(jnp.bfloat16), "dp").astype(jnp.float32),
        lax.psum(s_w2s.astype(jnp.bfloat16), "dp").astype(jnp.float32),
        lax.psum(s_query.astype(jnp.bfloat16), "dp").astype(jnp.float32),
        lax.psum(grad_rows.astype(jnp.bfloat16), "dp").astype(jnp.float32),
    )
    (
        f_wk,
        f_wv,
        f_wo,
        f_gc,
        f_w1c,
        f_w2c,
        f_gs,
        f_wqkv,
        f_wos,
        f_gm,
        f_w1s,
        f_w2s,
        query_rows,
        rows_total,
    ) = summed
    query_low = query_rows.astype(jnp.bfloat16)
    normed_rows = lax.dynamic_slice_in_dim(normed_lat, position * row_count, row_count, 0)
    d_wq_part = left_matmul(normed_rows, query_low)
    grad_normed_rows = right_matmul(query_low, wq)
    grad_lat_norm, d_glat_part = norm_back(lat_rows, g_lat_f, grad_normed_rows)
    d_wq, d_glat = (
        lax.psum_scatter(
            d_wq_part.astype(jnp.bfloat16), "pix", scatter_dimension=0, tiled=True
        ).astype(jnp.float32),
        lax.psum_scatter(
            d_glat_part.astype(jnp.bfloat16), "pix", scatter_dimension=0, tiled=True
        ).astype(jnp.float32),
    )
    d_gpix = lax.psum(grad_pix_gain, ("dp", "pix"))
    latent_out = jnp.stack(outputs)[None]
    pixel_out = jnp.stack(pixel_grads)[None]
    return (
        latent_out,
        pixel_out,
        rows_total + grad_lat_norm,
        d_gpix,
        d_glat,
        d_wq,
        f_wk,
        f_wv,
        f_wo,
        f_gc,
        f_w1c,
        f_w2c,
        f_gs,
        f_wqkv,
        f_wos,
        f_gm,
        f_w1s,
        f_w2s,
    )


MESH = pl.DeviceIdType.MESH
HBM = pl.BlockSpec(memory_space=pl.ANY)
VMEM = pl.BlockSpec(memory_space=pltpu.VMEM)
MIB = 1024 * 1024
PIECE = 256
BLOCK = 1024
FROWS = 272
DEN_ROW = 261
TOP_ROW = 263
GAIN_LANE = 264
GAIN_ROW = 262


def place():
    dp, pix = lax.axis_index("dp"), lax.axis_index("pix")
    return dp // 2, dp % 2, pix // 2, pix % 2


def device(x, c, z, y):
    return {"dp": x * 2 + c, "pix": z * 2 + y}


def greet(partners):
    barrier = pltpu.get_barrier_semaphore()
    for partner in partners:
        pl.semaphore_signal(barrier, inc=1, device_id=partner, device_id_type=MESH)
    pl.semaphore_wait(barrier, len(partners))


def remote(source, target, sems, index, partner):
    return pltpu.make_async_remote_copy(
        src_ref=source,
        dst_ref=target,
        send_sem=sems[0].at[index],
        recv_sem=sems[1].at[index],
        device_id=partner,
        device_id_type=MESH,
    )


def remote_params(collective_id, vmem=48 * MIB):
    return pltpu.CompilerParams(
        collective_id=collective_id, has_side_effects=True, vmem_limit_bytes=vmem
    )


def normed_block(raw, gain, features):
    values = raw.astype(jnp.float32)
    rows = lax.broadcasted_iota(jnp.int32, values.shape, 0)
    average = jnp.sum(values, 0, keepdims=True) * (1.0 / features)
    centered = jnp.where(rows < features, values - average, 0.0)
    scale = lax.rsqrt(jnp.sum(centered * centered, 0, keepdims=True) * (1.0 / features) + 1e-05)
    unit = centered * scale
    wide = jnp.where(rows == DEN_ROW, 1.0, unit * gain)
    return wide.astype(jnp.bfloat16), unit, scale


def three_parts(row):
    first = row.astype(jnp.bfloat16).astype(jnp.float32)
    rest = row - first
    second = rest.astype(jnp.bfloat16).astype(jnp.float32)
    return first, second, rest - second


def with_rows(tail, den, top):
    rows = lax.broadcasted_iota(jnp.int32, tail.shape, 0) + (FROWS - 16)
    high = den.astype(jnp.bfloat16).astype(jnp.float32)
    first, second, third = three_parts(top)
    tail = jnp.where(rows == DEN_ROW, high, tail)
    tail = jnp.where(rows == DEN_ROW + 1, den - high, tail)
    tail = jnp.where(rows == TOP_ROW, first, tail)
    tail = jnp.where(rows == TOP_ROW + 1, second, tail)
    return jnp.where(rows == TOP_ROW + 2, third, tail)


def read_rows(tail):
    at = DEN_ROW - (FROWS - 16)
    den = tail[at : at + 1] + tail[at + 1 : at + 2]
    at = TOP_ROW - (FROWS - 16)
    top = tail[at : at + 1] + tail[at + 1 : at + 2] + tail[at + 2 : at + 3]
    return den, top


def merge(pieces):
    bodies = [piece[: FROWS - 16].astype(jnp.float32) for piece in pieces]
    tails = [piece[FROWS - 16 :].astype(jnp.float32) for piece in pieces]
    read = [read_rows(tail) for tail in tails]
    top = functools.reduce(jnp.maximum, [row for unused, row in read])
    factors = [jnp.exp(row - top) for unused, row in read]
    body = sum(values * factor for values, factor in zip(bodies, factors, strict=True))
    tail = sum(values * factor for values, factor in zip(tails, factors, strict=True))
    den = sum(row * factor for (row, unused), factor in zip(read, factors, strict=True))
    return body, tail, den, top


class Gather:
    def __init__(self, shards, wholes, splits, send, recv, local):
        self.shards, self.wholes, self.splits = shards, wholes, splits
        self.sems, self.local = (send, recv), local
        self.place = place()
        x, c, z, y = self.place
        self.core, self.across = device(x, 1 - c, z, y), device(1 - x, c, z, y)
        self.beside = device(x, c, z, 1 - y)
        self.along, self.side, self.over, self.between, self.keep = {}, {}, {}, {}, {}

    def part(self, k, ref):
        x, c, z, y = self.place
        return ref.at[x, c] if self.splits[k] else ref.at[:, c]

    def start(self, k):
        x, c, z, y = self.place
        mine, home = self.part(k, self.shards[k]), self.part(k, self.wholes[k].at[z, y])
        for i in (1, 2, 3):
            target = device(x, c, (z + i) % 4, y)
            self.along[k, i] = remote(mine, home, self.sems, (k, i - 1), target)
            self.along[k, i].start()
        self.side[k, 0] = remote(mine, home, self.sems, (k, 3), self.beside)
        self.side[k, 0].start()
        self.keep[k] = pltpu.make_async_copy(
            self.shards[k], self.wholes[k].at[z, y], self.local.at[k]
        )
        self.keep[k].start()

    def to_side(self, k):
        x, c, z, y = self.place
        for i in (1, 2, 3):
            self.along[k, i].wait_recv()
            block = self.part(k, self.wholes[k].at[(z + 4 - i) % 4, y])
            self.side[k, i] = remote(block, block, self.sems, (k, 3 + i), self.beside)
            self.side[k, i].start()

    def to_over(self, k):
        x, c, z, y = self.place
        for i in range(4):
            self.side[k, i].wait_recv()
            if self.splits[k]:
                if i == 0:
                    block = self.wholes[k].at[z, 1 - y, x, c]
                else:
                    block = self.wholes[k].at[(z + 4 - i) % 4, :, x, c]
                self.over[k, i] = remote(block, block, self.sems, (k, 7 + i), self.across)
                self.over[k, i].start()

    def to_core(self, k):
        x, c, z, y = self.place
        for i in range(4):
            if self.splits[k]:
                self.over[k, i].wait_recv()
            if i == 0:
                block = self.wholes[k].at[z, 1 - y, :, c]
            else:
                block = self.wholes[k].at[(z + 4 - i) % 4, :, :, c]
            self.between[k, i] = remote(block, block, self.sems, (k, 11 + i), self.core)
            self.between[k, i].start()

    def arrive(self, k):
        self.keep[k].wait()
        for i in range(4):
            self.between[k, i].wait_recv()

    def finish(self):
        for group in (self.along, self.side, self.over, self.between):
            for copy in group.values():
                copy.wait_send()


def opening_kernel(splits, scale, features, *refs):
    count = len(splits)
    same, last = refs[:2]
    shards, pixels, pix_gain = refs[2 : count + 2], *refs[count + 2 : count + 4]
    refs = refs[count + 4 :]
    wholes, weights_out = refs[:count], refs[count]
    normed_out, queries_out, query_out, tops, means, rows_out = refs[count + 1 : count + 7]
    refs = refs[count + 7 :]
    wide, weights, scores_ref, lat, wq, key, total, largest, pieces, sums = refs[:10]
    side_in, own, along_in = refs[10:13]
    send, recv, local, own_send, own_recv, load = refs[13:]
    x, c, z, y = place()
    micros, unused, slots = pixels.shape
    blocks = slots // BLOCK
    per_block = BLOCK // PIECE
    images = sums.shape[1]
    gather = Gather(shards, wholes, splits, send, recv, local)
    along = [device(x, c, (z + i) % 4, y) for i in (1, 2, 3)]
    greet([*along, gather.beside, gather.across, gather.core])

    fetch = pltpu.make_async_copy(pixels, wide, load.at[0])
    fetch.start()
    for k in range(count):
        gather.start(k)
    gain = pix_gain[...]

    def norm(start, stop):
        def one(i, carry):
            half = BLOCK // 2
            columns = pl.ds(pl.multiple_of((i % (2 * blocks)) * half, half), half)
            micro = i // (2 * blocks)
            wide[micro, :, columns] = normed_block(wide[micro, :, columns], gain, features)[0]
            return carry

        lax.fori_loop(2 * start, 2 * stop, one, 0)

    fetch.wait()
    norm(0, 2)
    for k in range(3):
        gather.to_side(k)
    norm(2, 4)
    for k in range(3):
        gather.to_over(k)
    norm(4, 6)
    for k in range(3):
        gather.to_core(k)
    gather.to_side(3)
    gather.to_side(4)
    norm(6, 2 * blocks)
    gather.to_over(3)
    fetches = []
    for k, target in enumerate((lat, wq, key)):
        gather.arrive(k)
        fetches.append(pltpu.make_async_copy(wholes[k], target, load.at[1 + k]))
        fetches[k].start()
    gather.to_side(5)
    gather.to_over(4)
    for copy in fetches:
        copy.wait()

    lat_values = lat[...].reshape(sums.shape[3], -1).astype(jnp.float32)
    key_values = key[...].reshape(lat_values.shape[1], -1)
    columns = key_values[:, 256:384].astype(jnp.float32).T
    normed = layer_norm(lat_values, columns[GAIN_LANE - 256 : GAIN_LANE - 255])
    normed_out[...] = normed.astype(jnp.bfloat16)
    wq_values = wq[...].reshape(lat_values.shape[1], -1)
    queries_out[...] = matmul(normed_out[...], wq_values).astype(jnp.bfloat16)
    query_t = (
        lax.dot_general(
            key_values, queries_out[...], (((0,), (1,)), ((), ())),
            preferred_element_type=jnp.float32,
        )
        * scale
    )
    query_t = query_t[:FROWS]
    rows = lax.broadcasted_iota(jnp.int32, query_t.shape, 0)
    query_out[...] = jnp.where(rows < features, query_t, 0.0).astype(jnp.bfloat16)

    gather.to_side(6)
    gather.to_over(5)
    gather.to_core(3)
    gather.to_core(4)

    def forward(m):
        total[...] = jnp.zeros_like(total)
        largest[...] = jnp.full(largest.shape, -big_value, jnp.float32)

        def one(b, carry):
            rows = pl.ds(pl.multiple_of(b * BLOCK, BLOCK), BLOCK)
            scores_ref[...] = left_matmul(wide[m, :, rows], query_out[...])
            for k in range(per_block):
                rows = pl.ds(pl.multiple_of(b * BLOCK + k * PIECE, PIECE), PIECE)
                scores = scores_ref[k * PIECE : (k + 1) * PIECE]
                top = jnp.max(scores, 0, keepdims=True)
                low = jnp.exp(scores - top).astype(jnp.bfloat16)
                weights[m, rows, :] = low
                piece = b * per_block + k
                tops[m, piece] = top
                added = matmul(wide[m, :, rows], low)
                before = jnp.where(
                    same[m * blocks * per_block + piece] > 0, largest[...], -big_value
                )
                now = jnp.maximum(before, top)
                largest[...] = now
                older, newer = jnp.exp(before - now), jnp.exp(top - now)
                summed = total[...] * older + added * newer
                total[...] = summed
                pieces[piece, : FROWS - 16] = summed[: FROWS - 16].astype(jnp.bfloat16)
                at = DEN_ROW - (FROWS - 16)
                tail = summed[FROWS - 16 :]
                pieces[piece, FROWS - 16 :] = with_rows(tail, tail[at : at + 1], now).astype(
                    jnp.bfloat16
                )
            return carry

        lax.fori_loop(0, blocks, one, 0)
        for image in range(images):
            index = last[m * images + image]
            present = index >= 0
            piece = pieces[jnp.maximum(index, 0)].astype(jnp.float32)
            sums[m, image, : FROWS - 16] = jnp.where(present, piece[: FROWS - 16], 0.0).astype(
                jnp.bfloat16
            )
            nothing = jnp.zeros((1, piece.shape[1]), jnp.float32)
            absent = with_rows(
                jnp.zeros((16, piece.shape[1]), jnp.float32), nothing, nothing - big_value
            )
            sums[m, image, FROWS - 16 :] = jnp.where(
                present, piece[FROWS - 16 :], absent
            ).astype(jnp.bfloat16)

    own_sems = (own_send, own_recv)
    sides, alongs, keeps = {}, {}, []

    def send_sums(m):
        for i in (1, 2, 3, 0):
            source = sums.at[m, ((z + i) % 4) * 2 + 1 - y]
            sides[m, i] = remote(source, side_in.at[m, i], own_sems, (m, i), gather.beside)
            sides[m, i].start()
        keeps.append(pltpu.make_async_copy(weights.at[m], weights_out.at[m], load.at[4 + m]))
        keeps[-1].start()

    def pass_sums(m):
        for i in (1, 2, 3, 0):
            sides[m, i].wait_recv()
            body, tail, den, top = merge([sums[m, ((z + i) % 4) * 2 + y], side_in[m, i]])
            own[m, i, : FROWS - 16] = body.astype(jnp.bfloat16)
            own[m, i, FROWS - 16 :] = with_rows(tail, den, top).astype(jnp.bfloat16)
            if i:
                target = device(x, c, (z + i) % 4, y)
                alongs[m, i] = remote(
                    own.at[m, i], along_in.at[m, i - 1], own_sems, (m, 3 + i), target
                )
                alongs[m, i].start()

    def finish_sums(m):
        for i in (1, 2, 3):
            alongs[m, i].wait_recv()
        body, tail, den, top = merge([own[m, 0]] + [along_in[m, i] for i in range(3)])
        rows = lax.broadcasted_iota(jnp.int32, tail.shape, 0) + (FROWS - 16)
        means[m, : FROWS - 16] = (body / den).astype(jnp.bfloat16)
        means[m, FROWS - 16 :] = jnp.where(rows < DEN_ROW, tail / den, 0.0).astype(jnp.bfloat16)
        rows_out[m, 0:1] = den
        rows_out[m, 1:2] = top

    forward(0)
    send_sums(0)
    gather.to_side(7)
    gather.to_over(6)
    gather.to_core(5)
    forward(1)
    send_sums(1)
    pass_sums(0)
    gather.to_side(8)
    gather.to_over(7)
    gather.to_core(6)
    pass_sums(1)
    gather.to_side(9)
    gather.to_side(10)
    gather.to_over(8)
    gather.to_core(7)
    gather.to_over(9)
    finish_sums(0)
    gather.to_over(10)
    gather.to_core(8)
    finish_sums(1)
    gather.to_core(9)
    gather.to_core(10)
    for k in range(3, count):
        gather.arrive(k)
    for copy in keeps:
        copy.wait()
    gather.finish()
    for copy in (*sides.values(), *alongs.values()):
        copy.wait_send()


def opening(same, last, shards, splits, pixels, gain, features, images, scale):
    count = len(shards)
    bf16, f32 = jnp.bfloat16, jnp.float32
    micros, unused, slots = pixels.shape
    latents, width = 8 * shards[0].shape[0], shards[0].shape[1]
    views = [shard.reshape(2, 2, shard.shape[0] // 4, shard.shape[1]) for shard in shards]
    outs = [jax.ShapeDtypeStruct((4, 2, *view.shape), view.dtype) for view in views]
    piece = (FROWS, latents)
    smem = pl.BlockSpec(memory_space=pltpu.SMEM)
    results = pl.pallas_call(
        functools.partial(opening_kernel, splits, scale, features),
        out_shape=[
            *outs,
            jax.ShapeDtypeStruct((micros, slots, latents), bf16),
            jax.ShapeDtypeStruct((latents, width), bf16),
            jax.ShapeDtypeStruct((latents, width), bf16),
            jax.ShapeDtypeStruct(piece, bf16),
            jax.ShapeDtypeStruct((micros, slots // PIECE, 1, latents), f32),
            jax.ShapeDtypeStruct((micros, *piece), bf16),
            jax.ShapeDtypeStruct((micros, 2, latents), f32),
        ],
        in_specs=[smem, smem] + [HBM] * (count + 1) + [VMEM],
        out_specs=[HBM] * (count + 1) + [VMEM] * 6,
        scratch_shapes=[
            pltpu.VMEM(pixels.shape, bf16),
            pltpu.VMEM((micros, slots, latents), bf16),
            pltpu.VMEM((BLOCK, latents), f32),
            pltpu.VMEM(outs[0].shape, bf16),
            pltpu.VMEM(outs[1].shape, bf16),
            pltpu.VMEM(outs[2].shape, bf16),
            pltpu.VMEM(piece, f32),
            pltpu.VMEM((1, latents), f32),
            pltpu.VMEM((slots // PIECE, *piece), bf16),
            pltpu.VMEM((micros, images, *piece), bf16),
            pltpu.VMEM((micros, 4, *piece), bf16),
            pltpu.VMEM((micros, 4, *piece), bf16),
            pltpu.VMEM((micros, 3, *piece), bf16),
            pltpu.SemaphoreType.DMA((count, 15)),
            pltpu.SemaphoreType.DMA((count, 15)),
            pltpu.SemaphoreType.DMA((count,)),
            pltpu.SemaphoreType.DMA((micros, 7)),
            pltpu.SemaphoreType.DMA((micros, 7)),
            pltpu.SemaphoreType.DMA((4 + micros,)),
        ],
        compiler_params=remote_params(0, 60 * MIB),
        name="opening",
    )(same, last, *views, pixels, gain)
    wholes = [
        whole.reshape(8 * shard.shape[0], shard.shape[1])
        for whole, shard in zip(results[:count], shards, strict=True)
    ]
    return wholes, results[count:]


def softmax_parts(packed, scale):
    width = packed.shape[1] // 3
    query, key, value = packed[:, :width], packed[:, width : 2 * width], packed[:, 2 * width :]
    scores = right_matmul(query, key) * scale
    weights = jnp.exp(scores - jnp.max(scores, 1, keepdims=True))
    return query, key, value, weights, jnp.sum(weights, 1, keepdims=True)


def attention_kernel(scale, packed, out):
    query, key, value, weights, den = softmax_parts(packed[0], scale)
    out[0] = (matmul(weights.astype(jnp.bfloat16), value) / den).astype(jnp.bfloat16)


def head_spec(rows, width):
    return pl.BlockSpec((1, rows, width), lambda m, h: (m, 0, h))


def attention(packed, scale):
    micros, rows, columns = packed.shape
    width = columns // HEADS
    return pl.pallas_call(
        functools.partial(attention_kernel, scale),
        grid=(micros, HEADS),
        in_specs=[head_spec(rows, width)],
        out_specs=head_spec(rows, width // 3),
        out_shape=jax.ShapeDtypeStruct((micros, rows, columns // 3), jnp.bfloat16),
        compiler_params=pltpu.CompilerParams(vmem_limit_bytes=48 * MIB),
        name="attention",
    )(packed)


def normed_rows(values, gain):
    average = jnp.mean(values, -1, keepdims=True)
    centered = values - average
    scale = lax.rsqrt(jnp.mean(centered * centered, -1, keepdims=True) + 1e-05)
    return (centered * scale * gain).astype(jnp.bfloat16), scale


def feed(inputs, gain, w_in, w_out):
    normed, scale = normed_rows(inputs, gain)
    hidden = matmul(normed, w_in)
    square = hidden * hidden
    const = (2 / jnp.pi) ** 0.5
    bent = jnp.tanh(const * hidden * (1 + 0.044715 * square))
    half = 0.5 * (1 + bent)
    active = (hidden * half).astype(jnp.bfloat16)
    slope = half + 0.5 * hidden * (1 - bent * bent) * const * (1 + 3 * 0.044715 * square)
    return inputs + matmul(active, w_out), (scale, normed, active, slope.astype(jnp.bfloat16))


STRIP = 256
CHUNK = 64


class Reduce:
    def __init__(self, staging, own, core_in, over_in, side_in, along_in, finals, temps, sems, local):
        self.staging, self.own = staging, own
        self.core_in, self.over_in, self.side_in = core_in, over_in, side_in
        self.along_in, self.finals, self.temps = along_in, finals, temps
        self.sems, self.local = sems, local
        self.place = place()
        x, c, z, y = self.place
        self.core, self.across = device(x, 1 - c, z, y), device(1 - x, c, z, y)
        self.beside = device(x, c, z, 1 - y)
        self.copies, self.loads, self.keeps, self.slots = {}, {}, {}, {}

    def send(self, k, number, source, target, partner):
        self.copies[k, number] = remote(source, target, self.sems, (k, number), partner)
        self.copies[k, number].start()

    def release(self, slot):
        for k, used in self.slots.items():
            if used == slot:
                self.copies[k, 0].wait_send()
                self.keeps[k].wait()
        self.slots = {k: used for k, used in self.slots.items() if used != slot}

    def push(self, k, slot):
        x, c, z, y = self.place
        staged = self.staging[slot]
        rows, columns = self.own[k].shape[-2:]
        away = staged.at[:, :, :, 1 - c, :rows, :columns]
        self.send(k, 0, away, self.core_in[k], self.core)
        self.keeps[k] = pltpu.make_async_copy(
            staged.at[:, :, :, c, :rows, :columns], self.own[k], self.local.at[k, 0]
        )
        self.keeps[k].start()
        self.slots[k] = slot

    def c1(self, k):
        self.copies[k, 0].wait_recv()
        rows, columns = self.own[k].shape[-2:]
        temp = self.temps[k][0].at[:, :, :, :rows, :columns]
        self.loads[k] = pltpu.make_async_copy(self.core_in[k], temp, self.local.at[k, 1])
        self.loads[k].start()

    def add(self, count, one):
        def step(i, carry):
            one(i)
            return carry

        lax.fori_loop(0, count, step, 0)

    def c2(self, k):
        x, c, z, y = self.place
        own, temp = self.own[k], self.temps[k][0]
        rows, columns = own.shape[-2:]
        if k in self.slots:
            self.keeps[k].wait()
            self.copies[k, 0].wait_send()
            del self.slots[k]
        self.loads[k].wait()

        def one(i):
            own[i // 2, i % 2] = own[i // 2, i % 2] + temp[i // 2, i % 2, :, :rows, :columns]

        self.add(8, one)
        self.send(k, 1, own.at[:, :, 1 - x], self.over_in[k], self.across)

    def x1(self, k):
        self.copies[k, 1].wait_recv()
        rows, columns = self.own[k].shape[-2:]
        temp = self.temps[k][1].at[:, :, :rows, :columns]
        self.loads[k] = pltpu.make_async_copy(self.over_in[k], temp, self.local.at[k, 2])
        self.loads[k].start()

    def x2(self, k):
        x, c, z, y = self.place
        own, temp = self.own[k], self.temps[k][1]
        rows, columns = own.shape[-2:]
        self.loads[k].wait()

        def one(i):
            own[i // 2, i % 2, x] = own[i // 2, i % 2, x] + temp[i // 2, i % 2, :rows, :columns]

        self.add(8, one)
        self.send(k, 2, own.at[:, 1 - y, x], self.side_in[k], self.beside)

    def y(self, k):
        x, c, z, y = self.place
        own, side_in = self.own[k], self.side_in[k]
        self.copies[k, 2].wait_recv()

        def one(i):
            own[i, y, x] = own[i, y, x] + side_in[i]

        self.add(4, one)
        for i in (1, 2, 3):
            target = device(x, c, (z + i) % 4, y)
            self.send(
                k, 2 + i, own.at[(z + i) % 4, y, x], self.along_in[k].at[i - 1], target
            )

    def z(self, k):
        x, c, z, y = self.place
        for i in (1, 2, 3):
            self.copies[k, 2 + i].wait_recv()
        total = self.own[k][z, y, x].astype(jnp.float32)
        for i in range(3):
            total = total + self.along_in[k][i].astype(jnp.float32)
        final = self.finals[k]
        final[x, c] = total.astype(jnp.bfloat16)
        self.send(k, 6, final.at[x, c], final.at[x, c], self.across)

    def b(self, k):
        x, c, z, y = self.place
        final = self.finals[k]
        self.copies[k, 6].wait_recv()
        self.send(k, 7, final.at[:, c], final.at[:, c], self.core)

    def run(self, *stages):
        for name, number in stages:
            getattr(self, name)(number)

    def finish(self):
        for (k, number), copy in self.copies.items():
            if number == 7:
                copy.wait_recv()
            if number or k in self.slots:
                copy.wait_send()
        for k in self.slots:
            self.keeps[k].wait()


def closing_kernel(scale, images, features, *refs):
    segs, pixels, pix_weights, cot, final = refs[:5]
    normed_m, active_s, slope_s, self_att, packed, normed_self, normed_c, active_c, slope_c = refs[5:14]
    att_low, w2s, w1s, wos, wqkv, w2c, w1c, wo = refs[14:22]
    row_scales, gains, means, rows_in, value_n, queries, tops, pix_gain = refs[22:30]
    refs = refs[30:]
    count = 12
    finals, core_in, over_in = refs[:count], refs[count : 2 * count], refs[2 * count : 3 * count]
    out_rows, pixel_out, query_out = refs[3 * count : 3 * count + 3]
    refs = refs[3 * count + 3 :]
    own, side_in, along_in = refs[:count], refs[count : 2 * count], refs[2 * count : 3 * count]
    refs = refs[3 * count :]
    staging, temps = refs[:3], refs[3:7]
    grad, acc, low, back_low, first, second, third, fourth, slope, head_grad = refs[7:17]
    gain_grads, packed_grads = refs[17], refs[18]
    all_grads = refs[19:21]
    raw, out_tile, query_sums, gain_sums = refs[21:25]
    sum_parts, sum_core, sum_over, sum_side, sum_along = refs[25:30]
    send, recv, local, load, row_send, row_recv, grad_send, grad_recv = refs[30:38]
    block_load, block_out, sum_send, sum_recv = refs[38:]
    tile = acc

    x, c, z, y = place()
    pix, dp = lax.axis_index("pix"), lax.axis_index("dp")
    others = [{"dp": dp, "pix": (pix + i) % 8} for i in range(1, 8)]
    temp_of = [temps[0:2]] * 10 + [temps[2:4], temps[0:2]]
    reduce = Reduce(
        staging, own, core_in, over_in, side_in, along_in, finals, temp_of, (send, recv), local
    )
    greet([*others, reduce.core, reduce.across])

    loads = {}

    def fetch(number, source, target):
        loads[number] = pltpu.make_async_copy(source, target, load.at[number])
        loads[number].start()

    def ready(*numbers):
        for number in numbers:
            loads.pop(number).wait()

    fetch(0, cot, low)
    fetch(1, active_s, first)
    fetch(2, w2s, third)
    fetch(3, slope_s, slope)
    fetch(4, normed_m, second)
    fetch(5, w1s, fourth)
    homes = [pltpu.make_async_copy(final.at[:, pix], out_rows.at[:, pix], load.at[31])]
    for i, other in enumerate(others):
        source, target = final.at[:, (pix + i + 1) % 8], out_rows.at[:, pix]
        homes.append(remote(source, target, (row_send, row_recv), i, other))
    for copy in homes:
        copy.start()
    gain_grads[...] = jnp.zeros_like(gain_grads)

    def strips(one):
        def step(i, carry):
            one(i, pl.ds(pl.multiple_of(i * STRIP, STRIP), STRIP))
            return carry

        lax.fori_loop(0, grad.shape[0] // STRIP, step, 0)

    def chunks(one):
        def step(j, carry):
            one(pl.ds(pl.multiple_of(j * CHUNK, CHUNK), CHUNK))
            return carry

        lax.fori_loop(0, STRIP // CHUNK, step, 0)

    def weight_grad(k, slot, left, right, columns):
        reduce.release(slot)
        staged = staging[slot]

        def one(i, strip):
            product = left_matmul(left[:, strip], right[:, :columns])
            staged[i, :, :, :, :, :columns] = (
                product.reshape(2, 2, 2, STRIP // 8, columns).astype(jnp.bfloat16)
            )

        strips(one)
        reduce.push(k, slot)

    def through_slope(weight):
        def one(i, strip):
            tile[:STRIP] = right_matmul(low[strip, :], weight[...])

            def chunk(part):
                at = pl.ds(pl.multiple_of(i * STRIP, STRIP) + part.start, CHUNK)
                back_low[at, :] = (tile[part, :] * slope[at, :].astype(jnp.float32)).astype(
                    jnp.bfloat16
                )

            chunks(chunk)

        strips(one)

    def through_norm(number, normed, product, fresh=False):
        gain = gains[number : number + 1]
        inverse = 1.0 / gain
        width = gain.shape[1]

        def one(i, strip):
            source = tile
            if product is None:
                source = acc
            else:
                tile[:STRIP] = product(strip)

            def chunk(part):
                at = pl.ds(pl.multiple_of(i * STRIP, STRIP) + part.start, CHUNK)
                upper = source[at if product is None else part, :]
                unit = normed[at, :].astype(jnp.float32) * inverse
                gain_grads[number : number + 1] += jnp.sum(upper * unit, 0, keepdims=True)
                upper = upper * gain
                mean = jnp.sum(upper, 1, keepdims=True) * (1.0 / width)
                tilt = jnp.sum(upper * unit, 1, keepdims=True) * (1.0 / width)
                before = low[at, :].astype(jnp.float32) if fresh else grad[at, :]
                row_scale = row_scales[at, number : number + 1]
                after = before + (upper - mean - unit * tilt) * row_scale
                grad[at, :] = after
                low[at, :] = after.astype(jnp.bfloat16)

            chunks(chunk)

        strips(one)

    ready(0, 1)
    weight_grad(0, 0, first, low, 1024)
    fetch(6, self_att, first)
    ready(2, 3)
    through_slope(third)
    fetch(7, wos, third)
    fetch(8, slope_c, slope)
    reduce.run(("c1", 0))
    ready(4)
    weight_grad(1, 1, second, back_low, 1024)
    reduce.run(("c2", 0), ("c1", 1))
    ready(5)
    through_norm(0, second, lambda strip: right_matmul(back_low[strip, :], fourth[...]), True)
    fetch(9, normed_self, second)
    half = head_grad.shape[1]
    fetch(10, wqkv.at[:, :half], fourth.at[:, :half])
    fetch(11, packed.at[:, :half], back_low.at[:, :half])
    reduce.run(("c2", 1))

    ready(6)
    weight_grad(2, 0, first, low, 1024)
    fetch(12, packed.at[:, half : 2 * half], first.at[:, :half])
    reduce.run(("c1", 2))
    ready(7, 9)
    acc[...] = jnp.zeros_like(acc)
    rows_of_image = means.shape[2]
    width = half // 6
    for pair in range(4):
        ready(11 + pair)
        block = (back_low, first)[pair % 2]

        def unit(i, carry, pair=pair, block=block):
            image, head = i // 2, i % 2
            rows = pl.ds(pl.multiple_of(image * rows_of_image, rows_of_image), rows_of_image)

            def columns(part):
                start = pl.multiple_of(head * (3 * width) + part * width, width)
                return pl.ds(start, width)

            query, key, value = (block[rows, columns(part)] for part in range(3))
            out_rows_ = pl.ds(pl.multiple_of((pair * 2 + head) * width, width), width)
            upper = right_matmul(low[rows, :], third[out_rows_, :])
            scores = right_matmul(query, key) * scale
            weights = jnp.exp(scores - jnp.max(scores, 1, keepdims=True))
            den = jnp.sum(weights, 1, keepdims=True)
            grad_num = (upper / den).astype(jnp.bfloat16)
            slopes = right_matmul(grad_num, value)
            grad_den = -jnp.sum(weights * slopes, 1, keepdims=True) / den
            grad_scores = (weights * (slopes + grad_den)).astype(jnp.bfloat16)
            head_grad[rows, columns(0)] = (matmul(grad_scores, key) * scale).astype(jnp.bfloat16)
            head_grad[rows, columns(1)] = (left_matmul(grad_scores, query) * scale).astype(
                jnp.bfloat16
            )
            head_grad[rows, columns(2)] = left_matmul(
                weights.astype(jnp.bfloat16), grad_num
            ).astype(jnp.bfloat16)
            return carry

        lax.fori_loop(0, 4, unit, 0)
        if pair < 2:
            start = (pair + 2) * half
            fetch(13 + pair, packed.at[:, start : start + half], block.at[:, :half])
        reduce.run(
            *((("c2", 2), ("x1", 0)), (("c2", 3), ("y", 0), ("x1", 1)), (("c2", 4), ("z", 0), ("y", 1), ("x1", 2)), (("c2", 5), ("b", 0), ("z", 1), ("y", 2), ("x1", 3)))[pair]
        )
        weight_grad(3 + pair, (pair + 1) % 2, second, head_grad, half)
        ready(10 if pair == 0 else 15 + pair)

        def spread(i, strip):
            acc[strip, :] += right_matmul(head_grad[strip, :], fourth[:, :half])

        strips(spread)
        if pair < 3:
            start = (pair + 1) * half
            fetch(16 + pair, wqkv.at[:, start : start + half], fourth.at[:, :half])
        reduce.run(
            *((("c1", 3), ("x2", 0)), (("c1", 4), ("x2", 1)), (("c1", 5), ("x2", 2)), (("c1", 6), ("x2", 3)))[pair]
        )
    fetch(20, active_c, first)
    fetch(21, w2c, third)
    fetch(22, w1c, fourth)
    through_norm(1, second, None)
    fetch(23, normed_c, second)
    reduce.run(("c2", 6), ("y", 3), ("b", 1), ("z", 2), ("x1", 4))

    ready(20)
    weight_grad(7, 1, first, low, 1024)
    fetch(24, att_low, first)
    reduce.run(("x2", 4))
    ready(21, 8)
    through_slope(third)
    fetch(25, wo, third)
    reduce.run(("c1", 7), ("y", 4), ("z", 3), ("b", 2), ("x1", 5))
    ready(23)
    weight_grad(8, 0, second, back_low, 1024)
    reduce.run(("c2", 7), ("x2", 5), ("c1", 8))
    ready(22)
    through_norm(2, second, lambda strip: right_matmul(back_low[strip, :], fourth[...]))
    reduce.run(("c2", 8), ("y", 5), ("z", 4), ("b", 3), ("x1", 6))

    ready(25)

    def upper_rows(i, strip):
        back_low[strip, :] = right_matmul(low[strip, :], third[...]).astype(jnp.bfloat16)

    strips(upper_rows)
    micros = means.shape[0]
    grad_sems = (grad_send, grad_recv)
    along = {}
    for m in range(micros):
        rows = pl.ds(m * rows_of_image, rows_of_image)
        sums = right_matmul(value_n[...], back_low[rows, :]) / rows_in[m, 0:1]
        grad_den = -jnp.sum(sums * means[m].astype(jnp.float32), 0, keepdims=True)
        packed_grads[m, : FROWS - 16] = sums[: FROWS - 16].astype(jnp.bfloat16)
        at = lax.broadcasted_iota(jnp.int32, (16, sums.shape[1]), 0) + (FROWS - 16)
        tail = with_rows(sums[FROWS - 16 :], grad_den, rows_in[m, 1:2])
        packed_grads[m, FROWS - 16 :] = jnp.where(at == DEN_ROW + 1, 0.0, tail).astype(
            jnp.bfloat16
        )
        mine, home = packed_grads.at[m], all_grads[m].at[z, y]
        for i in (1, 2, 3):
            along[m, i] = remote(
                mine, home, grad_sems, (m, i - 1), device(x, c, (z + i) % 4, y)
            )
            along[m, i].start()
        along[m, 4] = remote(mine, home, grad_sems, (m, 3), reduce.beside)
        along[m, 4].start()
        fetch(26 + m, mine, home)

    def pass_grads(m):
        for i in (1, 2, 3):
            along[m, i].wait_recv()
            block = all_grads[m].at[(z + 4 - i) % 4, y]
            along[m, 4 + i] = remote(block, block, grad_sems, (m, 3 + i), reduce.beside)
            along[m, 4 + i].start()

    def grads_ready(m):
        ready(26 + m)
        for i in range(4, 8):
            along[m, i].wait_recv()

    ready(24)
    weight_grad(9, 1, first, low, 1024)
    reduce.run(("x2", 6), ("c1", 9))
    value_grad = sum(
        matmul(means[m], back_low[m * rows_of_image : (m + 1) * rows_of_image, :])
        for m in range(micros)
    )
    staged = staging[2]
    shards = [
        jnp.concatenate(
            [
                value_grad[:, s * 128 : (s + 1) * 128],
                gain_grads[:, s * 128 : (s + 1) * 128],
                jnp.zeros((320 - FROWS - 8, 128), jnp.float32),
            ],
            0,
        )
        for s in range(8)
    ]
    for s in range(8):
        staged[s // 2, s % 2] = shards[s].reshape(2, 2, 80, 128).astype(jnp.bfloat16)
    reduce.push(10, 2)
    reduce.release(0)
    staged = staging[0]
    for s in range(8):
        at = s * 64
        both = grad[at : at + 64, :] + grad[at + rows_of_image : at + rows_of_image + 64, :]
        staged[s // 2, s % 2, :, :, :16] = both.reshape(2, 2, 16, both.shape[1]).astype(
            jnp.bfloat16
        )
    reduce.push(11, 0)
    reduce.run(("c2", 9), ("c1", 10), ("y", 6), ("c2", 10), ("c1", 11), ("z", 5), ("c2", 11), ("b", 4))

    slots = pixels.shape[2]
    blocks = slots // BLOCK
    pieces = BLOCK // PIECE
    halves = BLOCK // out_tile.shape[2]
    query_sums[...] = jnp.zeros_like(query_sums)
    gain_sums[...] = jnp.zeros_like(gain_sums)
    scores_ref, back_ref, wide = low, acc, slope
    weight_slots = (first, second)

    def block_loads(m, b):
        rows = pl.ds(b * BLOCK, BLOCK)
        slot = b % 2
        return (
            pltpu.make_async_copy(pixels.at[m, :, rows], raw.at[slot], block_load.at[0, slot]),
            pltpu.make_async_copy(
                pix_weights.at[m, rows],
                weight_slots[slot].at[:, :rows_of_image],
                block_load.at[1, slot],
            ),
        )

    def block_store(m, b, part):
        rows = pl.ds(b * BLOCK + part * (BLOCK // halves), BLOCK // halves)
        return pltpu.make_async_copy(
            out_tile.at[part], pixel_out.at[m, :, rows], block_out.at[part]
        )

    def pixels_back(m, after):
        for copy in block_loads(m, 0):
            copy.start()
        for b in range(blocks):
            if b + 1 < blocks:
                for copy in block_loads(m, b + 1):
                    copy.start()
            for copy in block_loads(m, b):
                copy.wait()
            normed, unit_, row_scale = normed_block(raw[b % 2], pix_gain[...], features)
            wide[:FROWS, :] = normed
            weights = weight_slots[b % 2]

            def piece(k, carry, b=b, weights=weights):
                rows = pl.ds(pl.multiple_of(k * PIECE, PIECE), PIECE)
                number = b * pieces + k
                seg = segs[m * blocks * pieces + number]
                image = jnp.minimum(seg, images - 1)
                upper = all_grads[m][image // 2, image % 2]
                unused, top = read_rows(upper[FROWS - 16 :].astype(jnp.float32))
                factor = jnp.where(seg < images, jnp.exp(tops[m, number] - top), 0.0)
                full = weights[rows, :rows_of_image].astype(jnp.float32) * factor
                slopes = left_matmul(wide[:FROWS, rows], upper)
                scores_ref[rows, :rows_of_image] = (full * slopes).astype(jnp.bfloat16)
                back_ref[:FROWS, rows] = right_matmul(upper, full.astype(jnp.bfloat16))
                return carry

            lax.fori_loop(0, pieces, piece, 0)
            scores = scores_ref[:, :rows_of_image]
            query_sums[...] += matmul(wide[:FROWS, :], scores)
            back = back_ref[:FROWS, :] + right_matmul(queries[...], scores)
            at = lax.broadcasted_iota(jnp.int32, back.shape, 0)
            back = jnp.where(at < features, back, 0.0)
            product = back * unit_
            gain_sums[:FROWS] += sum(
                product[:, j * 128 : (j + 1) * 128] for j in range(BLOCK // 128)
            )
            back = back * pix_gain[...]
            mean = jnp.sum(back, 0, keepdims=True) * (1.0 / features)
            tilt = jnp.sum(back * unit_, 0, keepdims=True) * (1.0 / features)
            result = (back - mean - unit_ * tilt) * row_scale
            size = BLOCK // halves
            for part in range(halves):
                if m or b:
                    block_store(m, b, part).wait()
                out_tile[part] = result[:, part * size : (part + 1) * size]
                block_store(m, b, part).start()
            reduce.run(*after[b])

    pass_grads(0)
    reduce.run(("x1", 7), ("x2", 7))
    pass_grads(1)
    reduce.run(("y", 7), ("z", 6), ("b", 5))
    grads_ready(0)
    pixels_back(0, ((), (("x1", 8), ("x2", 8)), (("z", 7), ("b", 6)), (("y", 8),)))
    grads_ready(1)
    pixels_back(1, ((("x1", 9), ("x2", 9)), (("z", 8), ("b", 7)), (("x1", 10), ("x2", 10), ("x1", 11), ("x2", 11)), (("y", 9),)))
    for part in range(halves):
        block_store(0, 0, part).wait()

    sums = query_sums[...]
    at = lax.broadcasted_iota(jnp.int32, sums.shape, 0)
    gain_row = jnp.sum(gain_sums[...].T, 0, keepdims=True)
    gain_row = jnp.concatenate([gain_row, jnp.zeros((1, 128), jnp.float32)], 1)
    sums = jnp.where(at == GAIN_ROW, gain_row, sums)
    for j in range(4):
        sum_parts[j // 2, j % 2] = sums[:, j * 128 : (j + 1) * 128].astype(jnp.bfloat16)
    sum_sems = (sum_send, sum_recv)
    copies = [remote(sum_parts.at[1 - c], sum_core, sum_sems, 0, reduce.core)]
    copies[0].start()
    reduce.run(("y", 10), ("y", 11), ("z", 9), ("b", 8))
    copies[0].wait_recv()
    sum_parts[c] = sum_parts[c] + sum_core[...]
    copies.append(remote(sum_parts.at[c, 1 - x], sum_over, sum_sems, 1, reduce.across))
    copies[1].start()
    reduce.run(("z", 10), ("z", 11))
    copies[1].wait_recv()
    sum_parts[c, x] = sum_parts[c, x] + sum_over[...]
    copies.append(remote(sum_parts.at[c, x], sum_side, sum_sems, 2, reduce.beside))
    copies[2].start()
    reduce.run(("b", 9))
    copies[2].wait_recv()
    sum_along[z] = sum_parts[c, x] + sum_side[...]
    for i in (1, 2, 3):
        target = device(x, c, (z + i) % 4, y)
        copies.append(remote(sum_along.at[z], sum_along.at[z], sum_sems, 2 + i, target))
        copies[2 + i].start()
    reduce.run(("b", 10), ("b", 11))
    for i in (1, 2, 3):
        copies[2 + i].wait_recv()
    total = sum(sum_along[i].astype(jnp.float32) for i in range(4))
    query_out[c, x] = total.astype(jnp.bfloat16)
    copies.append(remote(query_out.at[c, x], query_out.at[c, x], sum_sems, 6, reduce.across))
    copies[6].start()
    copies[6].wait_recv()
    copies.append(remote(query_out.at[c], query_out.at[c], sum_sems, 7, reduce.core))
    copies[7].start()
    copies[7].wait_recv()
    for copy in copies:
        copy.wait_send()
    for copy in along.values():
        copy.wait_send()
    for copy in homes:
        copy.wait()
    reduce.finish()


def closing(
    segs,
    pixels,
    pix_weights,
    cot,
    final,
    final_kept,
    self_att,
    packed,
    normed_self,
    cross_kept,
    att_low,
    weights,
    row_scales,
    gains,
    means,
    rows,
    value_n,
    queries,
    tops,
    pix_gain,
    features,
    images,
    scale,
):
    bf16, f32 = jnp.bfloat16, jnp.float32
    total_rows, width = cot.shape
    micros, unused, slots = pixels.shape
    latents = means.shape[2]
    half = 3 * width // 4
    full, part = (STRIP // 8, width), (STRIP // 8, half)
    shapes = [full] * 3 + [part] * 4 + [full] * 3 + [(80, 128), (16, width)]
    count = len(shapes)

    def grid(*lead):
        return [(*lead, *shape) for shape in shapes]

    def scratch(shape, dtype=bf16):
        return pltpu.VMEM(shape, dtype)

    def arrays(list_):
        return [jax.ShapeDtypeStruct(shape, bf16) for shape in list_]

    square = (total_rows, width)
    quarter = (FROWS, 128)
    smem = pl.BlockSpec(memory_space=pltpu.SMEM)
    results = pl.pallas_call(
        functools.partial(closing_kernel, scale, images, features),
        out_shape=[
            *arrays(grid(2, 2)),
            *arrays(grid(4, 2, 2)),
            *arrays(grid(4, 2)),
            jax.ShapeDtypeStruct(final.shape, bf16),
            jax.ShapeDtypeStruct(pixels.shape, f32),
            jax.ShapeDtypeStruct((2, 2, *quarter), bf16),
        ],
        in_specs=[smem] + [HBM] * 21 + [VMEM] * 8,
        out_specs=[VMEM] * count + [HBM] * (2 * count + 2) + [VMEM],
        scratch_shapes=[
            *map(scratch, grid(4, 2, 2)),
            *map(scratch, grid(4)),
            *map(scratch, grid(3)),
            *[scratch((4, 2, 2, 2, *shape)) for shape in (full, full, shapes[10])],
            *[
                scratch((4, 2, *lead, *shape))
                for shape in (full, shapes[10])
                for lead in ((2,), ())
            ],
            scratch(square, f32),
            scratch(square, f32),
            *[scratch(square) for _ in range(7)],
            scratch((total_rows, half)),
            scratch((8, width), f32),
            scratch((micros, FROWS, latents)),
            *[scratch((4, 2, FROWS, latents)) for _ in range(micros)],
            scratch((2, FROWS, BLOCK)),
            scratch((2, FROWS, BLOCK // 2), f32),
            scratch((FROWS, latents), f32),
            scratch((384, 128), f32),
            scratch((2, 2, *quarter)),
            scratch((2, *quarter)),
            scratch(quarter),
            scratch(quarter),
            scratch((4, *quarter)),
            pltpu.SemaphoreType.DMA((count, 8)),
            pltpu.SemaphoreType.DMA((count, 8)),
            pltpu.SemaphoreType.DMA((count, 3)),
            pltpu.SemaphoreType.DMA((32,)),
            pltpu.SemaphoreType.DMA((7,)),
            pltpu.SemaphoreType.DMA((7,)),
            pltpu.SemaphoreType.DMA((micros, 7)),
            pltpu.SemaphoreType.DMA((micros, 7)),
            pltpu.SemaphoreType.DMA((2, 2)),
            pltpu.SemaphoreType.DMA((2,)),
            pltpu.SemaphoreType.DMA((8,)),
            pltpu.SemaphoreType.DMA((8,)),
        ],
        compiler_params=remote_params(1, 64 * MIB - 1024),
        name="closing",
    )(
        segs,
        pixels,
        pix_weights,
        cot,
        final,
        *final_kept,
        self_att,
        packed,
        normed_self,
        *cross_kept,
        att_low,
        *weights,
        row_scales,
        gains,
        means,
        rows,
        value_n,
        queries,
        tops,
        pix_gain,
    )
    shards = [
        result.reshape(4 * shape[0], shape[1])
        for result, shape in zip(results[:count], shapes, strict=True)
    ]
    query_sums = results[-1].reshape(4, *quarter).transpose(1, 0, 2).reshape(FROWS, latents)
    return shards, results[-3], results[-2], query_sums


def image_body(
    image_sides,
    pixels,
    latent_array,
    pixel_gain,
    latent_gain,
    query_weight,
    key_weight,
    value_weight,
    cross_out_weight,
    cross_mlp_gain,
    cross_mlp_in,
    cross_mlp_out,
    self_gain,
    self_qkv_weight,
    self_out_weight,
    self_mlp_gain,
    self_mlp_in,
    self_mlp_out,
    cotangent,
):
    position = lax.axis_index("pix")
    micros, images = image_sides.shape[1:]
    capacity, features = pixels.shape[2:]
    row_count, width = latent_array.shape
    latents = row_count * 8
    head_size = width // HEADS
    cross_scale = width ** (-0.5)
    self_scale = head_size ** (-0.5)
    f32, bf16 = jnp.float32, jnp.bfloat16

    def widen(values, columns):
        return jnp.pad(values, ((0, 0), (0, columns - values.shape[1])))

    gains = jnp.stack([latent_gain, cross_mlp_gain, self_gain, self_mlp_gain], 1)
    gains = jnp.pad(gains, ((0, 0), (GAIN_LANE, 384 - GAIN_LANE - 4)))
    shards = (
        latent_array,
        query_weight,
        widen(key_weight.T, 384) + gains,
        widen(value_weight.T, 384),
        cross_out_weight,
        cross_mlp_in,
        cross_mlp_out,
        self_qkv_weight,
        self_out_weight,
        self_mlp_in,
        self_mlp_out,
    )
    splits = (True,) * len(shards)
    lengths = image_sides[0] * image_sides[0]
    ends = jnp.cumsum(lengths, 1)
    firsts = position * capacity + PIECE * jnp.arange(capacity // PIECE, dtype=jnp.int32)
    segs = jnp.sum((firsts[None, :, None] >= ends[:, None, :]).astype(jnp.int32), 2)
    same = jnp.pad((segs[:, 1:] == segs[:, :-1]).astype(jnp.int32), ((0, 0), (1, 0))).reshape(-1)
    here = segs[:, :, None] == jnp.arange(images, dtype=jnp.int32)[None, None, :]
    order = jnp.arange(capacity // PIECE, dtype=jnp.int32)[None, :, None]
    last = jnp.max(jnp.where(here, order, -1), 1).reshape(-1)
    segs = segs.reshape(-1)
    gain_pix = jnp.pad(pixel_gain.astype(f32), (0, FROWS - features))[:, None]
    pixel_rows = jnp.pad(
        pixels[0].transpose(0, 2, 1), ((0, 0), (0, FROWS - features), (0, 0))
    )
    wholes, results = opening(
        same, last, shards, splits, pixel_rows, gain_pix, features, images, cross_scale
    )
    lat_full, wq, key_t, value_t, wo, w1c, w2c, wqkv, wos, w1s, w2s = wholes
    pix_weights, normed_lat, queries, query_t, pix_tops, means, rows = results
    cot_slots, means = lax.optimization_barrier((cotangent[0], means))
    cot_rows = lax.all_to_all(cot_slots, "pix", split_axis=1, concat_axis=1, tiled=True)
    g_lat, g_cross, g_self, g_mlp = (key_t[:, GAIN_LANE + i].astype(f32) for i in range(4))
    value_t = value_t[:, :FROWS]
    lat_f = lat_full.astype(f32)
    den, top = rows[:, 0], rows[:, 1]

    att_low = jnp.einsum("mfr,df->mrd", means, value_t, preferred_element_type=f32)
    att_low = att_low.astype(bf16).reshape(micros * latents, width)
    start_rows = jnp.broadcast_to(lat_f[None], (micros, latents, width)).reshape(-1, width)
    after_cross = start_rows + matmul(att_low, wo)
    after_mlp, cross_kept = feed(after_cross, g_cross, w1c, w2c)
    normed_self, self_scale_rows = normed_rows(after_mlp, g_self)
    packed = matmul(normed_self, wqkv).astype(bf16)
    self_att = attention(packed.reshape(micros, latents, 3 * width), head_size ** (-0.5))
    self_att = self_att.reshape(-1, width)
    after_self = after_mlp + matmul(self_att, wos)
    final, final_kept = feed(after_self, g_mlp, w1s, w2s)
    final = final.astype(bf16).reshape(micros, 8, row_count, width)
    row_scales = jnp.concatenate([final_kept[0], self_scale_rows, cross_kept[0]], 1)
    row_scales = jnp.pad(row_scales, ((0, 0), (0, 125)))

    shards, latent_out, pixel_grad, query_sums = closing(
        segs,
        pixel_rows,
        pix_weights,
        cot_rows.reshape(-1, width),
        final,
        final_kept[1:],
        self_att,
        packed,
        normed_self,
        cross_kept[1:],
        att_low,
        (w2s, w1s, wos, wqkv, w2c, w1c, wo),
        row_scales,
        jnp.stack([g_mlp, g_self, g_cross]),
        means,
        rows,
        value_t.T,
        query_t,
        pix_tops,
        gain_pix,
        features,
        images,
        head_size ** (-0.5),
    )
    f_w2s, f_w1s, f_wos, *f_qkv, f_w2c, f_w1c, f_wo, f_vec, f_lat = shards
    d_gpix = query_sums[GAIN_ROW, :features].astype(f32)

    grad_queries = lax.dot_general(
        query_sums, key_t[:, :FROWS], (((0,), (1,)), ((), ())), preferred_element_type=f32
    )
    grad_queries = (grad_queries * cross_scale).astype(bf16)
    columns = lax.dynamic_slice_in_dim(normed_lat, position * (width // 8), width // 8, 1)
    d_wq = left_matmul(columns, grad_queries)
    query_columns = lax.dynamic_slice_in_dim(queries, position * (width // 8), width // 8, 1)
    d_wk = matmul(query_sums[:features], query_columns) * cross_scale
    grad_norm_lat, d_glat = norm_back(lat_f, g_lat, right_matmul(grad_queries, wq))
    d_glat = lax.dynamic_slice_in_dim(d_glat, position * (width // 8), width // 8, 0)
    grad_norm_rows = lax.dynamic_slice_in_dim(grad_norm_lat, position * row_count, row_count, 0)
    return (
        latent_out[None],
        pixel_grad[:, :features].transpose(0, 2, 1)[None],
        f_lat.astype(f32) + grad_norm_rows,
        d_gpix,
        d_glat,
        d_wq,
        d_wk,
        f_vec[:features].astype(f32),
        f_wo.astype(f32),
        f_vec[FROWS + 2].astype(f32),
        f_w1c.astype(f32),
        f_w2c.astype(f32),
        f_vec[FROWS + 1].astype(f32),
        jnp.concatenate(f_qkv, 1).astype(f32),
        f_wos.astype(f32),
        f_vec[FROWS].astype(f32),
        f_w1s.astype(f32),
        f_w2s.astype(f32),
    )


def solution(mesh):
    fits = dict(mesh.shape) == {"dp": 4, "pix": 8}
    return jax.shard_map(
        image_body if fits else starting_body,
        mesh=mesh,
        in_specs=(
            P("dp", None, None),
            P("dp", None, "pix", None),
            P("pix", None),
            P(),
            P("pix"),
            P("pix", None),
            P(None, "pix"),
            P(None, "pix"),
            P("pix", None),
            P("pix"),
            P("pix", None),
            P("pix", None),
            P("pix"),
            P("pix", None),
            P("pix", None),
            P("pix"),
            P("pix", None),
            P("pix", None),
            P("dp", None, None, "pix", None),
        ),
        out_specs=(
            P("dp", None, None, "pix", None),
            P("dp", None, "pix", None),
            P("pix", None),
            P(),
            P("pix"),
            P("pix", None),
            P(None, "pix"),
            P(None, "pix"),
            P("pix", None),
            P("pix"),
            P("pix", None),
            P("pix", None),
            P("pix"),
            P("pix", None),
            P("pix", None),
            P("pix"),
            P("pix", None),
            P("pix", None),
        ),
        check_vma=False,
    )
```

```python
import functools

import jax
import jax.numpy as jnp
from jax import lax
from jax.experimental import pallas as pl
from jax.experimental.pallas import tpu as pltpu
from jax.sharding import PartitionSpec as P

HEADS = 8
SIDE = 64


highest = lax.Precision.HIGHEST
big_value = 1e30


def layer_norm(values, gain):
    average = jnp.mean(values, -1, keepdims=True)
    centered = values - average
    return centered * lax.rsqrt(jnp.mean(centered * centered, -1, keepdims=True) + 1e-05) * gain


def matmul(left, right):
    return jnp.dot(left, right, preferred_element_type=jnp.float32)


def left_matmul(left, right):
    return lax.dot_general(
        left, right, (((0,), (0,)), ((), ())), preferred_element_type=jnp.float32
    )


def right_matmul(left, right):
    return lax.dot_general(
        left, right, (((1,), (1,)), ((), ())), preferred_element_type=jnp.float32
    )


def norm_back(values, gain, grad):
    unused, pullback = jax.vjp(layer_norm, values, gain)
    return pullback(grad)


def mlp_forward(inputs, gain, w_in, w_out):
    normed = layer_norm(inputs, gain).astype(jnp.bfloat16)
    hidden = matmul(normed, w_in)
    active = jax.nn.gelu(hidden).astype(jnp.bfloat16)
    return (inputs + matmul(active, w_out), (normed, hidden, active))


def mlp_backward(grad, inputs, gain, w_in, w_out, kept):
    normed, hidden, active = kept
    grad_low = grad.astype(jnp.bfloat16)
    grad_out = left_matmul(active, grad_low)
    grad_active = right_matmul(grad_low, w_out)
    unused, pullback = jax.vjp(jax.nn.gelu, hidden)
    grad_hidden = pullback(grad_active)[0].astype(jnp.bfloat16)
    grad_in = left_matmul(normed, grad_hidden)
    grad_normed = right_matmul(grad_hidden, w_in)
    grad_inputs, grad_gain = norm_back(inputs, gain, grad_normed)
    return (grad + grad_inputs, grad_gain, grad_in, grad_out)


def starting_body(
    image_sides,
    pixels,
    latent_array,
    pixel_gain,
    latent_gain,
    query_weight,
    key_weight,
    value_weight,
    cross_out_weight,
    cross_mlp_gain,
    cross_mlp_in,
    cross_mlp_out,
    self_gain,
    self_qkv_weight,
    self_out_weight,
    self_mlp_gain,
    self_mlp_in,
    self_mlp_out,
    cotangent,
):
    pieces = lax.axis_size("pix")
    position = lax.axis_index("pix")
    micros = image_sides.shape[1]
    images = image_sides.shape[2]
    capacity = pixels.shape[2]
    row_count = latent_array.shape[0]
    model_width = latent_array.shape[1]
    head_size = model_width // HEADS
    unit_count = images * HEADS // pieces
    window = min(images, (capacity - 2) // (SIDE * SIDE // 4) + 2)
    cross_scale = model_width ** (-0.5)
    self_scale = head_size ** (-0.5)
    shards = (
        latent_array,
        latent_gain,
        query_weight,
        key_weight,
        value_weight,
        cross_out_weight,
        cross_mlp_gain,
        cross_mlp_in,
        cross_mlp_out,
        self_gain,
        self_qkv_weight,
        self_out_weight,
        self_mlp_gain,
        self_mlp_in,
        self_mlp_out,
    )
    lat_rows = latent_array.astype(jnp.float32)
    gain_pix = pixel_gain.astype(jnp.float32)
    grad_rows = jnp.zeros((row_count, model_width), jnp.float32)
    grad_pix_gain = jnp.zeros(gain_pix.shape, jnp.float32)
    outputs = []
    pixel_grads = []
    totals = None
    for step_index in range(micros):
        gathered = (
            lax.all_gather(shards[0], "pix", axis=0, tiled=True),
            lax.all_gather(shards[1], "pix", axis=0, tiled=True),
            lax.all_gather(shards[2], "pix", axis=0, tiled=True),
            lax.all_gather(shards[3], "pix", axis=1, tiled=True),
            lax.all_gather(shards[4], "pix", axis=1, tiled=True),
            lax.all_gather(shards[5], "pix", axis=0, tiled=True),
            lax.all_gather(shards[6], "pix", axis=0, tiled=True),
            lax.all_gather(shards[7], "pix", axis=0, tiled=True),
            lax.all_gather(shards[8], "pix", axis=0, tiled=True),
            lax.all_gather(shards[9], "pix", axis=0, tiled=True),
            lax.all_gather(shards[10], "pix", axis=0, tiled=True),
            lax.all_gather(shards[11], "pix", axis=0, tiled=True),
            lax.all_gather(shards[12], "pix", axis=0, tiled=True),
            lax.all_gather(shards[13], "pix", axis=0, tiled=True),
            lax.all_gather(shards[14], "pix", axis=0, tiled=True),
        )
        lat_full, g_lat, wq, wk, wv, wo, g_cross, w1c, w2c, g_self, wqkv, wos, g_mlp, w1s, w2s = (
            gathered
        )
        g_lat_f = g_lat.astype(jnp.float32)
        gc_f = g_cross.astype(jnp.float32)
        gs_f = g_self.astype(jnp.float32)
        gm_f = g_mlp.astype(jnp.float32)
        if step_index == 0:
            normed_lat = layer_norm(lat_full.astype(jnp.float32), g_lat_f).astype(jnp.bfloat16)
            queries = matmul(normed_lat, wq).astype(jnp.bfloat16)
        side_list = image_sides[0, step_index]
        lengths = side_list * side_list
        ends = jnp.cumsum(lengths)
        slot_ids = position * capacity + jnp.arange(capacity, dtype=jnp.int32)
        segment = jnp.sum((slot_ids[:, None] >= ends[None, :]).astype(jnp.int32), 1)
        window_ids = segment[0] + jnp.arange(window, dtype=jnp.int32)
        select = (window_ids[:, None] == jnp.arange(images, dtype=jnp.int32)[None, :]).astype(
            jnp.float32
        )
        in_window = segment[None, :] == window_ids[:, None]
        raw_pixels = pixels[0, step_index].astype(jnp.float32)
        normed_pix = layer_norm(raw_pixels, gain_pix).astype(jnp.bfloat16)
        pixel_keys = matmul(normed_pix, wk).astype(jnp.bfloat16)
        pixel_values = matmul(normed_pix, wv).astype(jnp.bfloat16)
        scores = right_matmul(queries, pixel_keys) * cross_scale
        local_top = jnp.max(jnp.where(in_window[:, None, :], scores[None], -big_value), 2)
        image_top = jnp.max(jnp.where(select[:, :, None] > 0, local_top[:, None, :], -big_value), 0)
        image_top = lax.pmax(image_top, "pix")
        window_top = jnp.einsum("wb,br->wr", select, image_top, precision=highest)
        weights = jnp.where(
            in_window[:, None, :], jnp.exp(scores[None] - window_top[:, :, None]), 0.0
        )
        partial_den = jnp.sum(weights, 2)
        partial_num = jnp.einsum(
            "wrc,cd->wrd",
            weights.astype(jnp.bfloat16),
            pixel_values,
            preferred_element_type=jnp.float32,
        )
        full_num = jnp.einsum("wb,wrd->brd", select, partial_num, precision=highest)
        full_den = jnp.einsum("wb,wr->br", select, partial_den, precision=highest)
        num_rows, den_rows = (
            lax.psum_scatter(
                full_num.astype(jnp.bfloat16), "pix", scatter_dimension=1, tiled=True
            ).astype(jnp.float32),
            lax.psum_scatter(
                full_den.astype(jnp.bfloat16), "pix", scatter_dimension=1, tiled=True
            ).astype(jnp.float32),
        )
        attended = num_rows / den_rows[:, :, None]
        attended_low = attended.astype(jnp.bfloat16).reshape(images * row_count, model_width)
        start_rows = jnp.broadcast_to(lat_rows[None], (images, row_count, model_width)).reshape(
            images * row_count, model_width
        )
        after_cross = start_rows + matmul(attended_low, wo)
        after_mlp, cross_kept = mlp_forward(after_cross, gc_f, w1c, w2c)
        normed_self = layer_norm(after_mlp, gs_f).astype(jnp.bfloat16)
        packed = matmul(normed_self, wqkv).astype(jnp.bfloat16)
        packed = packed.reshape(images, row_count, HEADS, 3 * head_size).transpose(0, 2, 1, 3)
        packed = packed.reshape(pieces, unit_count, row_count, 3 * head_size)
        packed = lax.all_to_all(packed, "pix", split_axis=0, concat_axis=2, tiled=True)[0]
        head_query = packed[:, :, :head_size]
        head_key = packed[:, :, head_size : 2 * head_size]
        head_value = packed[:, :, 2 * head_size :]
        self_scores = (
            jnp.einsum("uqd,ukd->uqk", head_query, head_key, preferred_element_type=jnp.float32)
            * self_scale
        )
        self_top = jnp.max(self_scores, 2, keepdims=True)
        self_weights = jnp.exp(self_scores - self_top)
        self_den = jnp.sum(self_weights, 2, keepdims=True)
        self_num = jnp.einsum(
            "uqk,ukd->uqd",
            self_weights.astype(jnp.bfloat16),
            head_value,
            preferred_element_type=jnp.float32,
        )
        self_out = self_num / self_den
        returned = lax.all_to_all(
            self_out.astype(jnp.bfloat16), "pix", split_axis=1, concat_axis=0, tiled=True
        )
        returned = (
            returned.reshape(images, HEADS, row_count, head_size)
            .transpose(0, 2, 1, 3)
            .reshape(images * row_count, model_width)
        )
        after_self = after_mlp + matmul(returned, wos)
        final, final_kept = mlp_forward(after_self, gm_f, w1s, w2s)
        outputs.append(final.astype(jnp.bfloat16).reshape(images, row_count, model_width))
        grad = cotangent[0, step_index].astype(jnp.float32).reshape(images * row_count, model_width)
        grad, d_gm, d_w1s, d_w2s = mlp_backward(grad, after_self, gm_f, w1s, w2s, final_kept)
        grad_low = grad.astype(jnp.bfloat16)
        d_wos = left_matmul(returned, grad_low)
        grad_self = right_matmul(grad_low, wos)
        grad_self = grad_self.reshape(images, row_count, HEADS, head_size).transpose(0, 2, 1, 3)
        grad_self = grad_self.reshape(pieces, unit_count, row_count, head_size)
        grad_self = lax.all_to_all(
            grad_self.astype(jnp.bfloat16), "pix", split_axis=0, concat_axis=2, tiled=True
        ).astype(grad_self.dtype)[0]
        grad_num = (grad_self / self_den).astype(jnp.bfloat16)
        grad_den = -jnp.sum(grad_self * self_out, 2, keepdims=True) / self_den
        again_scores = (
            jnp.einsum("uqd,ukd->uqk", head_query, head_key, preferred_element_type=jnp.float32)
            * self_scale
        )
        again_weights = jnp.exp(again_scores - self_top)
        grad_weights = (
            jnp.einsum("uqd,ukd->uqk", grad_num, head_value, preferred_element_type=jnp.float32)
            + grad_den
        )
        grad_scores = (again_weights * grad_weights).astype(jnp.bfloat16)
        grad_query = (
            jnp.einsum("uqk,ukd->uqd", grad_scores, head_key, preferred_element_type=jnp.float32)
            * self_scale
        )
        grad_key = (
            jnp.einsum("uqk,uqd->ukd", grad_scores, head_query, preferred_element_type=jnp.float32)
            * self_scale
        )
        grad_value = jnp.einsum(
            "uqk,uqd->ukd",
            again_weights.astype(jnp.bfloat16),
            grad_num,
            preferred_element_type=jnp.float32,
        )
        grad_packed = jnp.concatenate([grad_query, grad_key, grad_value], 2).astype(jnp.bfloat16)
        grad_packed = lax.all_to_all(grad_packed, "pix", split_axis=1, concat_axis=0, tiled=True)
        grad_packed = (
            grad_packed.reshape(images, HEADS, row_count, 3 * head_size)
            .transpose(0, 2, 1, 3)
            .reshape(images * row_count, 3 * model_width)
        )
        d_wqkv = left_matmul(normed_self, grad_packed)
        grad_normed = right_matmul(grad_packed, wqkv)
        grad_inputs, d_gs = norm_back(after_mlp, gs_f, grad_normed)
        grad = grad + grad_inputs
        grad, d_gc, d_w1c, d_w2c = mlp_backward(grad, after_cross, gc_f, w1c, w2c, cross_kept)
        grad_rows = grad_rows + jnp.sum(grad.reshape(images, row_count, model_width), 0)
        grad_low = grad.astype(jnp.bfloat16)
        d_wo = left_matmul(attended_low, grad_low)
        grad_cross = right_matmul(grad_low, wo).reshape(images, row_count, model_width)
        cross_gnum = (grad_cross / den_rows[:, :, None]).astype(jnp.bfloat16)
        cross_gden = (-jnp.sum(grad_cross * attended, 2) / den_rows).astype(jnp.bfloat16)
        all_num, all_den = (
            lax.all_gather(cross_gnum, "pix", axis=1, tiled=True),
            lax.all_gather(cross_gden, "pix", axis=1, tiled=True),
        )
        select_low = select.astype(jnp.bfloat16)
        window_num = jnp.einsum(
            "wb,brd->wrd", select_low, all_num, preferred_element_type=jnp.float32
        ).astype(jnp.bfloat16)
        window_den = jnp.einsum(
            "wb,br->wr", select_low, all_den, preferred_element_type=jnp.float32
        )
        scores = right_matmul(queries, pixel_keys) * cross_scale
        weights = jnp.where(
            in_window[:, None, :], jnp.exp(scores[None] - window_top[:, :, None]), 0.0
        )
        cross_gweights = (
            jnp.einsum("wrd,cd->wrc", window_num, pixel_values, preferred_element_type=jnp.float32)
            + window_den[:, :, None]
        )
        cross_gscores = jnp.sum(weights * cross_gweights, 0).astype(jnp.bfloat16)
        query_terms = matmul(cross_gscores, pixel_keys) * cross_scale
        grad_keys = (left_matmul(cross_gscores, queries) * cross_scale).astype(jnp.bfloat16)
        grad_values = jnp.einsum(
            "wrc,wrd->cd",
            weights.astype(jnp.bfloat16),
            window_num,
            preferred_element_type=jnp.float32,
        ).astype(jnp.bfloat16)
        d_wk = left_matmul(normed_pix, grad_keys)
        d_wv = left_matmul(normed_pix, grad_values)
        grad_normed_pix = right_matmul(grad_keys, wk) + right_matmul(grad_values, wv)
        grad_pixels, d_gpix = norm_back(raw_pixels, gain_pix, grad_normed_pix)
        pixel_grads.append(grad_pixels)
        grad_pix_gain = grad_pix_gain + d_gpix
        terms = (
            d_wk,
            d_wv,
            d_wo,
            d_gc,
            d_w1c,
            d_w2c,
            d_gs,
            d_wqkv,
            d_wos,
            d_gm,
            d_w1s,
            d_w2s,
            query_terms,
        )
        reduced = (
            lax.psum_scatter(
                terms[0].astype(jnp.bfloat16), "pix", scatter_dimension=1, tiled=True
            ).astype(jnp.float32),
            lax.psum_scatter(
                terms[1].astype(jnp.bfloat16), "pix", scatter_dimension=1, tiled=True
            ).astype(jnp.float32),
            lax.psum_scatter(
                terms[2].astype(jnp.bfloat16), "pix", scatter_dimension=0, tiled=True
            ).astype(jnp.float32),
            lax.psum_scatter(
                terms[3].astype(jnp.bfloat16), "pix", scatter_dimension=0, tiled=True
            ).astype(jnp.float32),
            lax.psum_scatter(
                terms[4].astype(jnp.bfloat16), "pix", scatter_dimension=0, tiled=True
            ).astype(jnp.float32),
            lax.psum_scatter(
                terms[5].astype(jnp.bfloat16), "pix", scatter_dimension=0, tiled=True
            ).astype(jnp.float32),
            lax.psum_scatter(
                terms[6].astype(jnp.bfloat16), "pix", scatter_dimension=0, tiled=True
            ).astype(jnp.float32),
            lax.psum_scatter(
                terms[7].astype(jnp.bfloat16), "pix", scatter_dimension=0, tiled=True
            ).astype(jnp.float32),
            lax.psum_scatter(
                terms[8].astype(jnp.bfloat16), "pix", scatter_dimension=0, tiled=True
            ).astype(jnp.float32),
            lax.psum_scatter(
                terms[9].astype(jnp.bfloat16), "pix", scatter_dimension=0, tiled=True
            ).astype(jnp.float32),
            lax.psum_scatter(
                terms[10].astype(jnp.bfloat16), "pix", scatter_dimension=0, tiled=True
            ).astype(jnp.float32),
            lax.psum_scatter(
                terms[11].astype(jnp.bfloat16), "pix", scatter_dimension=0, tiled=True
            ).astype(jnp.float32),
            lax.psum_scatter(
                terms[12].astype(jnp.bfloat16), "pix", scatter_dimension=0, tiled=True
            ).astype(jnp.float32),
        )
        totals = reduced if totals is None else jax.tree.map(jnp.add, totals, reduced)
    s_wk, s_wv, s_wo, s_gc, s_w1c, s_w2c, s_gs, s_wqkv, s_wos, s_gm, s_w1s, s_w2s, s_query = totals
    summed = (
        lax.psum(s_wk.astype(jnp.bfloat16), "dp").astype(jnp.float32),
        lax.psum(s_wv.astype(jnp.bfloat16), "dp").astype(jnp.float32),
        lax.psum(s_wo.astype(jnp.bfloat16), "dp").astype(jnp.float32),
        lax.psum(s_gc.astype(jnp.bfloat16), "dp").astype(jnp.float32),
        lax.psum(s_w1c.astype(jnp.bfloat16), "dp").astype(jnp.float32),
        lax.psum(s_w2c.astype(jnp.bfloat16), "dp").astype(jnp.float32),
        lax.psum(s_gs.astype(jnp.bfloat16), "dp").astype(jnp.float32),
        lax.psum(s_wqkv.astype(jnp.bfloat16), "dp").astype(jnp.float32),
        lax.psum(s_wos.astype(jnp.bfloat16), "dp").astype(jnp.float32),
        lax.psum(s_gm.astype(jnp.bfloat16), "dp").astype(jnp.float32),
        lax.psum(s_w1s.astype(jnp.bfloat16), "dp").astype(jnp.float32),
        lax.psum(s_w2s.astype(jnp.bfloat16), "dp").astype(jnp.float32),
        lax.psum(s_query.astype(jnp.bfloat16), "dp").astype(jnp.float32),
        lax.psum(grad_rows.astype(jnp.bfloat16), "dp").astype(jnp.float32),
    )
    (
        f_wk,
        f_wv,
        f_wo,
        f_gc,
        f_w1c,
        f_w2c,
        f_gs,
        f_wqkv,
        f_wos,
        f_gm,
        f_w1s,
        f_w2s,
        query_rows,
        rows_total,
    ) = summed
    query_low = query_rows.astype(jnp.bfloat16)
    normed_rows = lax.dynamic_slice_in_dim(normed_lat, position * row_count, row_count, 0)
    d_wq_part = left_matmul(normed_rows, query_low)
    grad_normed_rows = right_matmul(query_low, wq)
    grad_lat_norm, d_glat_part = norm_back(lat_rows, g_lat_f, grad_normed_rows)
    d_wq, d_glat = (
        lax.psum_scatter(
            d_wq_part.astype(jnp.bfloat16), "pix", scatter_dimension=0, tiled=True
        ).astype(jnp.float32),
        lax.psum_scatter(
            d_glat_part.astype(jnp.bfloat16), "pix", scatter_dimension=0, tiled=True
        ).astype(jnp.float32),
    )
    d_gpix = lax.psum(grad_pix_gain, ("dp", "pix"))
    latent_out = jnp.stack(outputs)[None]
    pixel_out = jnp.stack(pixel_grads)[None]
    return (
        latent_out,
        pixel_out,
        rows_total + grad_lat_norm,
        d_gpix,
        d_glat,
        d_wq,
        f_wk,
        f_wv,
        f_wo,
        f_gc,
        f_w1c,
        f_w2c,
        f_gs,
        f_wqkv,
        f_wos,
        f_gm,
        f_w1s,
        f_w2s,
    )


MESH = pl.DeviceIdType.MESH
HBM = pl.BlockSpec(memory_space=pl.ANY)
VMEM = pl.BlockSpec(memory_space=pltpu.VMEM)
MIB = 1024 * 1024
PIECE = 256
BLOCK = 1024
STRIP = 256
CHUNK = 64
FROWS = 272
DEN_ROW = 261
TOP_ROW = 263
GAIN_LANE = 264
GAIN_ROW = 262


def place():
    dp, pix = lax.axis_index("dp"), lax.axis_index("pix")
    return dp // 2, dp % 2, pix // 2, pix % 2


def device(x, c, z, y):
    return {"dp": x * 2 + c, "pix": z * 2 + y}


def greet(partners):
    barrier = pltpu.get_barrier_semaphore()
    for partner in partners:
        pl.semaphore_signal(barrier, inc=1, device_id=partner, device_id_type=MESH)
    pl.semaphore_wait(barrier, len(partners))


def remote(source, target, sems, index, partner):
    return pltpu.make_async_remote_copy(
        src_ref=source,
        dst_ref=target,
        send_sem=sems[0].at[index],
        recv_sem=sems[1].at[index],
        device_id=partner,
        device_id_type=MESH,
    )


def remote_params(collective_id, vmem=48 * MIB):
    return pltpu.CompilerParams(
        collective_id=collective_id, has_side_effects=True, vmem_limit_bytes=vmem
    )


def normed_block(raw, gain, features):
    values = raw.astype(jnp.float32)
    rows = lax.broadcasted_iota(jnp.int32, values.shape, 0)
    average = jnp.sum(values, 0, keepdims=True) * (1.0 / features)
    centered = jnp.where(rows < features, values - average, 0.0)
    scale = lax.rsqrt(jnp.sum(centered * centered, 0, keepdims=True) * (1.0 / features) + 1e-05)
    unit = centered * scale
    wide = jnp.where(rows == DEN_ROW, 1.0, unit * gain)
    return wide.astype(jnp.bfloat16), unit, scale


def three_parts(row):
    first = row.astype(jnp.bfloat16).astype(jnp.float32)
    rest = row - first
    second = rest.astype(jnp.bfloat16).astype(jnp.float32)
    return first, second, rest - second


def with_rows(tail, den, top):
    rows = lax.broadcasted_iota(jnp.int32, tail.shape, 0) + (FROWS - 16)
    high = den.astype(jnp.bfloat16).astype(jnp.float32)
    first, second, third = three_parts(top)
    tail = jnp.where(rows == DEN_ROW, high, tail)
    tail = jnp.where(rows == DEN_ROW + 1, den - high, tail)
    tail = jnp.where(rows == TOP_ROW, first, tail)
    tail = jnp.where(rows == TOP_ROW + 1, second, tail)
    return jnp.where(rows == TOP_ROW + 2, third, tail)


def read_rows(tail):
    at = DEN_ROW - (FROWS - 16)
    den = tail[at : at + 1] + tail[at + 1 : at + 2]
    at = TOP_ROW - (FROWS - 16)
    top = tail[at : at + 1] + tail[at + 1 : at + 2] + tail[at + 2 : at + 3]
    return den, top


def merge(pieces):
    bodies = [piece[: FROWS - 16].astype(jnp.float32) for piece in pieces]
    tails = [piece[FROWS - 16 :].astype(jnp.float32) for piece in pieces]
    read = [read_rows(tail) for tail in tails]
    top = functools.reduce(jnp.maximum, [row for unused, row in read])
    factors = [jnp.exp(row - top) for unused, row in read]
    body = sum(values * factor for values, factor in zip(bodies, factors, strict=True))
    tail = sum(values * factor for values, factor in zip(tails, factors, strict=True))
    den = sum(row * factor for (row, unused), factor in zip(read, factors, strict=True))
    return body, tail, den, top


def gelu_and_slope(hidden):
    const = (2 / jnp.pi) ** 0.5
    square = hidden * hidden
    bent = jnp.tanh(const * hidden * (1 + 0.044715 * square))
    half = 0.5 * (1 + bent)
    slope = half + 0.5 * hidden * (1 - bent * bent) * const * (1 + 3 * 0.044715 * square)
    return hidden * half, slope


class Gather:
    def __init__(self, shards, wholes, splits, send, recv, local):
        self.shards, self.wholes, self.splits = shards, wholes, splits
        self.sems, self.local = (send, recv), local
        self.place = place()
        x, c, z, y = self.place
        self.core, self.across = device(x, 1 - c, z, y), device(1 - x, c, z, y)
        self.beside = device(x, c, z, 1 - y)
        self.along, self.side, self.over, self.between, self.keep = {}, {}, {}, {}, {}

    def part(self, k, ref):
        x, c, z, y = self.place
        return ref.at[x, c] if self.splits[k] else ref.at[:, c]

    def start(self, k):
        x, c, z, y = self.place
        mine, home = self.part(k, self.shards[k]), self.part(k, self.wholes[k].at[z, y])
        for i in (1, 2, 3):
            target = device(x, c, (z + i) % 4, y)
            self.along[k, i] = remote(mine, home, self.sems, (k, i - 1), target)
            self.along[k, i].start()
        self.side[k, 0] = remote(mine, home, self.sems, (k, 3), self.beside)
        self.side[k, 0].start()
        self.keep[k] = pltpu.make_async_copy(
            self.shards[k], self.wholes[k].at[z, y], self.local.at[k]
        )
        self.keep[k].start()

    def to_side(self, k):
        x, c, z, y = self.place
        for i in (1, 2, 3):
            self.along[k, i].wait_recv()
            block = self.part(k, self.wholes[k].at[(z + 4 - i) % 4, y])
            self.side[k, i] = remote(block, block, self.sems, (k, 3 + i), self.beside)
            self.side[k, i].start()

    def to_over(self, k):
        x, c, z, y = self.place
        for i in range(4):
            self.side[k, i].wait_recv()
            if self.splits[k]:
                if i == 0:
                    block = self.wholes[k].at[z, 1 - y, x, c]
                else:
                    block = self.wholes[k].at[(z + 4 - i) % 4, :, x, c]
                self.over[k, i] = remote(block, block, self.sems, (k, 7 + i), self.across)
                self.over[k, i].start()

    def to_core(self, k):
        x, c, z, y = self.place
        for i in range(4):
            if self.splits[k]:
                self.over[k, i].wait_recv()
            if i == 0:
                block = self.wholes[k].at[z, 1 - y, :, c]
            else:
                block = self.wholes[k].at[(z + 4 - i) % 4, :, :, c]
            self.between[k, i] = remote(block, block, self.sems, (k, 11 + i), self.core)
            self.between[k, i].start()

    def arrive(self, k):
        self.keep[k].wait()
        for i in range(4):
            self.between[k, i].wait_recv()

    def finish(self):
        for group in (self.along, self.side, self.over, self.between):
            for copy in group.values():
                copy.wait_send()


def opening_kernel(splits, scale, features, *refs):
    count = len(splits)
    same, last = refs[:2]
    shards, pixels, cot, pix_gain = refs[2 : count + 2], *refs[count + 2 : count + 5]
    refs = refs[count + 5 :]
    wholes, weights_out, cot_rows = refs[:count], refs[count], refs[count + 1]
    normed_c, active_c, slope_c, normed_s, packed, self_att = refs[count + 2 : count + 8]
    normed_m, active_s, slope_s, att_low, final = refs[count + 8 : count + 13]
    refs = refs[count + 13 :]
    normed_out, queries_out, query_out, tops, means, rows_out, row_scales, gains = refs[:8]
    refs = refs[8:]
    wide, weights, scores_ref, lat, wq, key, total, largest, pieces, sums = refs[:10]
    side_in, own, along_in = refs[10:13]
    value, stream, tile, first, second, third, fourth, left_w, right_w, heads = refs[13:23]
    send, recv, local, own_send, own_recv, load, cot_send, cot_recv, fetch_sem, store_sem = refs[23:]
    x, c, z, y = place()
    micros, unused, slots = pixels.shape
    blocks = slots // BLOCK
    per_block = BLOCK // PIECE
    images = sums.shape[1]
    gather = Gather(shards, wholes, splits, send, recv, local)
    pix, dp = lax.axis_index("pix"), lax.axis_index("dp")
    others = [{"dp": dp, "pix": (pix + i) % 8} for i in range(1, 8)]
    greet([*others, gather.across, gather.core])

    fetch = pltpu.make_async_copy(pixels, wide, load.at[0])
    fetch.start()
    for k in range(3):
        gather.start(k)
    gain = pix_gain[...]

    def norm(start, stop):
        def one(i, carry):
            half = BLOCK // 2
            columns = pl.ds(pl.multiple_of((i % (2 * blocks)) * half, half), half)
            micro = i // (2 * blocks)
            wide[micro, :, columns] = normed_block(wide[micro, :, columns], gain, features)[0]
            return carry

        lax.fori_loop(2 * start, 2 * stop, one, 0)

    fetch.wait()
    norm(0, 2)
    for k in range(3):
        gather.to_side(k)
    for k in range(3, 6):
        gather.start(k)
    norm(2, 4)
    for k in range(3):
        gather.to_over(k)
    for k in range(6, count):
        gather.start(k)
    norm(4, 6)
    for k in range(3):
        gather.to_core(k)
    gather.to_side(3)
    gather.to_side(4)
    norm(6, 2 * blocks)
    gather.to_over(3)
    fetches = []
    for k, target in enumerate((lat, wq, key)):
        gather.arrive(k)
        fetches.append(pltpu.make_async_copy(wholes[k], target, load.at[1 + k]))
        fetches[k].start()
    gather.to_side(5)
    gather.to_over(4)
    for copy in fetches:
        copy.wait()

    lat_values = lat[...].reshape(sums.shape[3], -1).astype(jnp.float32)
    key_values = key[...].reshape(lat_values.shape[1], -1)
    columns = key_values[:, 256:384].astype(jnp.float32).T
    gains[...] = columns[GAIN_LANE - 256 : GAIN_LANE - 248]
    normed = layer_norm(lat_values, gains[0:1])
    normed_out[...] = normed.astype(jnp.bfloat16)
    wq_values = wq[...].reshape(lat_values.shape[1], -1)
    queries_out[...] = matmul(normed_out[...], wq_values).astype(jnp.bfloat16)
    query_t = (
        lax.dot_general(
            key_values, queries_out[...], (((0,), (1,)), ((), ())),
            preferred_element_type=jnp.float32,
        )
        * scale
    )
    query_t = query_t[:FROWS]
    rows = lax.broadcasted_iota(jnp.int32, query_t.shape, 0)
    query_out[...] = jnp.where(rows < features, query_t, 0.0).astype(jnp.bfloat16)

    gather.to_side(6)
    gather.to_over(5)
    gather.to_core(3)
    gather.to_core(4)

    def forward(m):
        total[...] = jnp.zeros_like(total)
        largest[...] = jnp.full(largest.shape, -big_value, jnp.float32)

        def one(b, carry):
            rows = pl.ds(pl.multiple_of(b * BLOCK, BLOCK), BLOCK)
            scores_ref[...] = left_matmul(wide[m, :, rows], query_out[...])
            for k in range(per_block):
                rows = pl.ds(pl.multiple_of(b * BLOCK + k * PIECE, PIECE), PIECE)
                scores = scores_ref[k * PIECE : (k + 1) * PIECE]
                top = jnp.max(scores, 0, keepdims=True)
                low = jnp.exp(scores - top).astype(jnp.bfloat16)
                weights[m, rows, :] = low
                piece = b * per_block + k
                tops[m, piece] = top
                added = matmul(wide[m, :, rows], low)
                before = jnp.where(
                    same[m * blocks * per_block + piece] > 0, largest[...], -big_value
                )
                now = jnp.maximum(before, top)
                largest[...] = now
                older, newer = jnp.exp(before - now), jnp.exp(top - now)
                summed = total[...] * older + added * newer
                total[...] = summed
                pieces[piece, : FROWS - 16] = summed[: FROWS - 16].astype(jnp.bfloat16)
                at = DEN_ROW - (FROWS - 16)
                tail = summed[FROWS - 16 :]
                pieces[piece, FROWS - 16 :] = with_rows(tail, tail[at : at + 1], now).astype(
                    jnp.bfloat16
                )
            return carry

        lax.fori_loop(0, blocks, one, 0)
        for image in range(images):
            index = last[m * images + image]
            present = index >= 0
            piece = pieces[jnp.maximum(index, 0)].astype(jnp.float32)
            sums[m, image, : FROWS - 16] = jnp.where(present, piece[: FROWS - 16], 0.0).astype(
                jnp.bfloat16
            )
            nothing = jnp.zeros((1, piece.shape[1]), jnp.float32)
            absent = with_rows(
                jnp.zeros((16, piece.shape[1]), jnp.float32), nothing, nothing - big_value
            )
            sums[m, image, FROWS - 16 :] = jnp.where(
                present, piece[FROWS - 16 :], absent
            ).astype(jnp.bfloat16)

    own_sems = (own_send, own_recv)
    sides, alongs, keeps = {}, {}, []

    def send_sums(m):
        for i in (1, 2, 3, 0):
            source = sums.at[m, ((z + i) % 4) * 2 + 1 - y]
            sides[m, i] = remote(source, side_in.at[m, i], own_sems, (m, i), gather.beside)
            sides[m, i].start()
        keeps.append(pltpu.make_async_copy(weights.at[m], weights_out.at[m], load.at[4 + m]))
        keeps[-1].start()

    def pass_sums(m):
        for i in (1, 2, 3, 0):
            sides[m, i].wait_recv()
            body, tail, den, top = merge([sums[m, ((z + i) % 4) * 2 + y], side_in[m, i]])
            own[m, i, : FROWS - 16] = body.astype(jnp.bfloat16)
            own[m, i, FROWS - 16 :] = with_rows(tail, den, top).astype(jnp.bfloat16)
            if i:
                target = device(x, c, (z + i) % 4, y)
                alongs[m, i] = remote(
                    own.at[m, i], along_in.at[m, i - 1], own_sems, (m, 3 + i), target
                )
                alongs[m, i].start()

    def finish_sums(m):
        for i in (1, 2, 3):
            alongs[m, i].wait_recv()
        body, tail, den, top = merge([own[m, 0]] + [along_in[m, i] for i in range(3)])
        rows = lax.broadcasted_iota(jnp.int32, tail.shape, 0) + (FROWS - 16)
        means[m, : FROWS - 16] = (body / den).astype(jnp.bfloat16)
        means[m, FROWS - 16 :] = jnp.where(rows < DEN_ROW, tail / den, 0.0).astype(jnp.bfloat16)
        rows_out[m, 0:1] = den
        rows_out[m, 1:2] = top

    forward(0)
    send_sums(0)
    gather.to_side(7)
    gather.to_over(6)
    gather.to_core(5)
    forward(1)
    send_sums(1)
    pass_sums(0)
    gather.to_side(8)
    gather.to_over(7)
    gather.to_core(6)
    pass_sums(1)
    gather.to_side(9)
    gather.to_over(8)
    gather.to_side(10)
    gather.to_core(7)

    loads, stores = {}, {}

    def fetch(number, source, target):
        loads[number] = pltpu.make_async_copy(source, target, fetch_sem.at[number])
        loads[number].start()

    def store(number, source, target):
        stores[number] = pltpu.make_async_copy(source, target, store_sem.at[number])
        stores[number].start()

    def stored(*numbers):
        for number in numbers:
            stores.pop(number).wait()

    def ready(*numbers):
        for number in numbers:
            loads.pop(number).wait()

    gather.arrive(3)
    fetch(0, wholes[3], value)
    gather.arrive(4)
    fetch(1, wholes[4], left_w)
    gather.arrive(5)
    fetch(2, wholes[5], right_w)
    finish_sums(0)
    gather.to_over(9)
    finish_sums(1)
    cots = [pltpu.make_async_copy(cot.at[:, pix], cot_rows.at[:, pix], local.at[count])]
    for i, other in enumerate(others):
        source, target = cot.at[:, (pix + i + 1) % 8], cot_rows.at[:, pix]
        cots.append(remote(source, target, (cot_send, cot_recv), i, other))
    for copy in cots:
        copy.start()

    latents, model = lat_values.shape
    strip_count = stream.shape[0] // STRIP

    def strips(one):
        def step(i, carry):
            one(i, pl.ds(pl.multiple_of(i * STRIP, STRIP), STRIP))
            return carry

        lax.fori_loop(0, strip_count, step, 0)

    def chunks(one):
        def step(j, carry):
            one(pl.ds(pl.multiple_of(j * CHUNK, CHUNK), CHUNK))
            return carry

        lax.fori_loop(0, STRIP // CHUNK, step, 0)

    def square(ref):
        return ref[...].reshape(model, model)

    def add_and_norm(left, weight, number, target, base=None, last_out=None):
        def one(i, strip):
            if base is None:
                stream[strip, :] += matmul(left[strip, :], square(weight))
            else:
                stream[strip, :] = base(i) + matmul(left[strip, :], square(weight))

            def chunk(part):
                at = pl.ds(pl.multiple_of(i * STRIP, STRIP) + part.start, CHUNK)
                values = stream[at, :]
                centered = values - jnp.mean(values, 1, keepdims=True)
                row_scale = lax.rsqrt(jnp.mean(centered * centered, 1, keepdims=True) + 1e-05)
                row_scales[at, 3 - number : 4 - number] = row_scale
                target[at, :] = (centered * row_scale * gains[number : number + 1]).astype(
                    jnp.bfloat16
                )

            chunks(chunk)

        strips(one)

    def through_gelu(left, weight, active, slope):
        def one(i, strip):
            tile[...] = matmul(left[strip, :], square(weight))

            def chunk(part):
                at = pl.ds(pl.multiple_of(i * STRIP, STRIP) + part.start, CHUNK)
                acted, sloped = gelu_and_slope(tile[part, :])
                active[at, :] = acted.astype(jnp.bfloat16)
                slope[at, :] = sloped.astype(jnp.bfloat16)

            chunks(chunk)

        strips(one)

    ready(0)
    for m in range(micros):
        first[m * latents : (m + 1) * latents, :] = lax.dot_general(
            means[m],
            value[...].reshape(model, -1)[:, :FROWS],
            (((0,), (1,)), ((), ())),
            preferred_element_type=jnp.float32,
        ).astype(jnp.bfloat16)
    store(0, first, att_low)
    gather.to_over(10)
    gather.to_core(8)
    ready(1)

    def lat_strip(i):
        return lat[pl.ds((i % 2) * 2, 2)].reshape(STRIP, model).astype(jnp.float32)

    add_and_norm(first, left_w, 1, second, lat_strip)
    store(1, second, normed_c)
    gather.arrive(6)
    fetch(3, wholes[6], left_w)
    ready(2)
    through_gelu(second, right_w, third, fourth)
    store(2, third, active_c)
    store(3, fourth, slope_c)
    gather.to_core(9)
    gather.arrive(7)
    half = heads.shape[2]
    fetch(4, wholes[7].at[:, :, :, :, :, :half], right_w.at[:, :, :, :, :, :half])
    ready(3)
    stored(0)
    add_and_norm(third, left_w, 2, first)
    store(4, first, normed_s)
    fetch(5, wholes[7].at[:, :, :, :, :, half : 2 * half], left_w.at[:, :, :, :, :, :half])
    gather.to_core(10)
    stored(1)
    width = half // 6
    for pair in range(4):
        block = heads.at[pair % 2]
        weight = (right_w, left_w)[pair % 2]
        ready(4 + pair)
        if pair >= 2:
            stored(3 + pair)

        def project(i, strip, block=block, weight=weight):
            product = matmul(first[strip, :], weight[:, :, :, :, :, :half].reshape(model, half))
            block[strip, :] = product.astype(jnp.bfloat16)

        strips(project)
        store(5 + pair, block, packed.at[:, pair * half : (pair + 1) * half])
        if pair < 2:
            columns = pl.ds((pair + 2) * half, half)
            fetch(
                6 + pair,
                wholes[7].at[:, :, :, :, :, columns],
                weight.at[:, :, :, :, :, :half],
            )

        def unit(i, carry, pair=pair, block=block):
            image, head = i // 2, i % 2
            rows = pl.ds(pl.multiple_of(image * latents, latents), latents)

            def columns(part):
                start = pl.multiple_of(head * (3 * width) + part * width, width)
                return pl.ds(start, width)

            query, key_, value_ = (block[rows, columns(part)] for part in range(3))
            scores = right_matmul(query, key_) * width ** (-0.5)
            exps = jnp.exp(scores - jnp.max(scores, 1, keepdims=True))
            den = jnp.sum(exps, 1, keepdims=True)
            out = pl.ds(pl.multiple_of((pair * 2 + head) * width, width), width)
            second[rows, out] = (matmul(exps.astype(jnp.bfloat16), value_) / den).astype(
                jnp.bfloat16
            )
            return carry

        lax.fori_loop(0, 4, unit, 0)
    store(9, second, self_att)
    gather.arrive(8)
    fetch(8, wholes[8], right_w)
    gather.arrive(9)
    fetch(9, wholes[9], left_w)
    ready(8)
    stored(2)
    add_and_norm(second, right_w, 3, third)
    store(10, third, normed_m)
    gather.arrive(10)
    fetch(10, wholes[10], right_w)
    ready(9)
    stored(3, 4)
    through_gelu(third, left_w, fourth, first)
    store(11, fourth, active_s)
    store(12, first, slope_s)
    ready(10)
    stored(9)

    def finish_rows(i, strip):
        second[strip, :] = (
            stream[strip, :] + matmul(fourth[strip, :], square(right_w))
        ).astype(jnp.bfloat16)

    strips(finish_rows)
    store(13, second, final)
    stored(*list(stores))
    for copy in (*keeps, *cots):
        copy.wait()
    gather.finish()
    for copy in (*sides.values(), *alongs.values()):
        copy.wait_send()


def opening(same, last, shards, splits, pixels, cot, gain, features, scale):
    count = len(shards)
    bf16, f32 = jnp.bfloat16, jnp.float32
    micros, unused, slots = pixels.shape
    latents, width = 8 * shards[0].shape[0], shards[0].shape[1]
    views = [shard.reshape(2, 2, shard.shape[0] // 4, shard.shape[1]) for shard in shards]
    outs = [jax.ShapeDtypeStruct((4, 2, *view.shape), view.dtype) for view in views]
    images = cot.shape[1]
    piece = (FROWS, latents)
    total_rows = micros * latents
    square, wide = (total_rows, width), (total_rows, 3 * width)
    kept = [jax.ShapeDtypeStruct(wide if i == 4 else square, bf16) for i in range(11)]
    smem = pl.BlockSpec(memory_space=pltpu.SMEM)
    results = pl.pallas_call(
        functools.partial(opening_kernel, splits, scale, features),
        out_shape=[
            *outs,
            jax.ShapeDtypeStruct((micros, slots, latents), bf16),
            jax.ShapeDtypeStruct(cot.shape, bf16),
            *kept,
            jax.ShapeDtypeStruct((latents, width), bf16),
            jax.ShapeDtypeStruct((latents, width), bf16),
            jax.ShapeDtypeStruct(piece, bf16),
            jax.ShapeDtypeStruct((micros, slots // PIECE, 1, latents), f32),
            jax.ShapeDtypeStruct((micros, *piece), bf16),
            jax.ShapeDtypeStruct((micros, 2, latents), f32),
            jax.ShapeDtypeStruct((total_rows, 128), f32),
            jax.ShapeDtypeStruct((8, width), f32),
        ],
        in_specs=[smem, smem] + [HBM] * (count + 2) + [VMEM],
        out_specs=[HBM] * (count + 13) + [VMEM] * 8,
        scratch_shapes=[
            pltpu.VMEM(pixels.shape, bf16),
            pltpu.VMEM((micros, slots, latents), bf16),
            pltpu.VMEM((BLOCK, latents), f32),
            pltpu.VMEM(outs[0].shape, bf16),
            pltpu.VMEM(outs[1].shape, bf16),
            pltpu.VMEM(outs[2].shape, bf16),
            pltpu.VMEM(piece, f32),
            pltpu.VMEM((1, latents), f32),
            pltpu.VMEM((slots // PIECE, *piece), bf16),
            pltpu.VMEM((micros, images, *piece), bf16),
            pltpu.VMEM((micros, 4, *piece), bf16),
            pltpu.VMEM((micros, 4, *piece), bf16),
            pltpu.VMEM((micros, 3, *piece), bf16),
            pltpu.VMEM(outs[3].shape, bf16),
            pltpu.VMEM(square, f32),
            pltpu.VMEM((STRIP, width), f32),
            *[pltpu.VMEM(square, bf16) for _ in range(4)],
            *[pltpu.VMEM(outs[4].shape, bf16) for _ in range(2)],
            pltpu.VMEM((2, total_rows, 3 * width // 4), bf16),
            pltpu.SemaphoreType.DMA((count, 15)),
            pltpu.SemaphoreType.DMA((count, 15)),
            pltpu.SemaphoreType.DMA((count + 1,)),
            pltpu.SemaphoreType.DMA((micros, 7)),
            pltpu.SemaphoreType.DMA((micros, 7)),
            pltpu.SemaphoreType.DMA((4 + micros,)),
            pltpu.SemaphoreType.DMA((7,)),
            pltpu.SemaphoreType.DMA((7,)),
            pltpu.SemaphoreType.DMA((11,)),
            pltpu.SemaphoreType.DMA((14,)),
        ],
        compiler_params=remote_params(0, 64 * MIB - 1024),
        name="opening",
    )(same, last, *views, pixels, cot, gain)
    wholes = [
        whole.reshape(8 * shard.shape[0], shard.shape[1])
        for whole, shard in zip(results[:count], shards, strict=True)
    ]
    return wholes, results[count:]


class Reduce:
    def __init__(self, staging, own, core_in, over_in, side_in, along_in, finals, temps, sems, local):
        self.staging, self.own = staging, own
        self.core_in, self.over_in, self.side_in = core_in, over_in, side_in
        self.along_in, self.finals, self.temps = along_in, finals, temps
        self.sems, self.local = sems, local
        self.place = place()
        x, c, z, y = self.place
        self.core, self.across = device(x, 1 - c, z, y), device(1 - x, c, z, y)
        self.beside = device(x, c, z, 1 - y)
        self.copies, self.loads, self.keeps, self.slots = {}, {}, {}, {}

    def send(self, k, number, source, target, partner):
        self.copies[k, number] = remote(source, target, self.sems, (k, number), partner)
        self.copies[k, number].start()

    def release(self, slot):
        for k, used in self.slots.items():
            if used == slot:
                self.copies[k, 0].wait_send()
                self.keeps[k].wait()
        self.slots = {k: used for k, used in self.slots.items() if used != slot}

    def push(self, k, slot):
        x, c, z, y = self.place
        staged = self.staging[slot]
        rows, columns = self.own[k].shape[-2:]
        away = staged.at[:, :, :, 1 - c, :rows, :columns]
        self.send(k, 0, away, self.core_in[k], self.core)
        self.keeps[k] = pltpu.make_async_copy(
            staged.at[:, :, :, c, :rows, :columns], self.own[k], self.local.at[k, 0]
        )
        self.keeps[k].start()
        self.slots[k] = slot

    def c1(self, k):
        self.copies[k, 0].wait_recv()
        rows, columns = self.own[k].shape[-2:]
        temp = self.temps[k][0].at[:, :, :, :rows, :columns]
        self.loads[k] = pltpu.make_async_copy(self.core_in[k], temp, self.local.at[k, 1])
        self.loads[k].start()

    def add(self, count, one):
        def step(i, carry):
            one(i)
            return carry

        lax.fori_loop(0, count, step, 0)

    def c2(self, k):
        x, c, z, y = self.place
        own, temp = self.own[k], self.temps[k][0]
        rows, columns = own.shape[-2:]
        if k in self.slots:
            self.keeps[k].wait()
            self.copies[k, 0].wait_send()
            del self.slots[k]
        self.loads[k].wait()

        def one(i):
            own[i // 2, i % 2] = own[i // 2, i % 2] + temp[i // 2, i % 2, :, :rows, :columns]

        self.add(8, one)
        self.send(k, 1, own.at[:, :, 1 - x], self.over_in[k], self.across)

    def x1(self, k):
        self.copies[k, 1].wait_recv()
        rows, columns = self.own[k].shape[-2:]
        temp = self.temps[k][1].at[:, :, :rows, :columns]
        self.loads[k] = pltpu.make_async_copy(self.over_in[k], temp, self.local.at[k, 2])
        self.loads[k].start()

    def x2(self, k):
        x, c, z, y = self.place
        own, temp = self.own[k], self.temps[k][1]
        rows, columns = own.shape[-2:]
        self.loads[k].wait()

        def one(i):
            own[i // 2, i % 2, x] = own[i // 2, i % 2, x] + temp[i // 2, i % 2, :rows, :columns]

        self.add(8, one)
        self.send(k, 2, own.at[:, 1 - y, x], self.side_in[k], self.beside)

    def y(self, k):
        x, c, z, y = self.place
        own, side_in = self.own[k], self.side_in[k]
        self.copies[k, 2].wait_recv()

        def one(i):
            own[i, y, x] = own[i, y, x] + side_in[i]

        self.add(4, one)
        for i in (1, 2, 3):
            target = device(x, c, (z + i) % 4, y)
            self.send(
                k, 2 + i, own.at[(z + i) % 4, y, x], self.along_in[k].at[i - 1], target
            )

    def z(self, k):
        x, c, z, y = self.place
        for i in (1, 2, 3):
            self.copies[k, 2 + i].wait_recv()
        total = self.own[k][z, y, x].astype(jnp.float32)
        for i in range(3):
            total = total + self.along_in[k][i].astype(jnp.float32)
        final = self.finals[k]
        final[x, c] = total.astype(jnp.bfloat16)
        self.send(k, 6, final.at[x, c], final.at[x, c], self.across)

    def b(self, k):
        x, c, z, y = self.place
        final = self.finals[k]
        self.copies[k, 6].wait_recv()
        self.send(k, 7, final.at[:, c], final.at[:, c], self.core)

    def run(self, *stages):
        for name, number in stages:
            getattr(self, name)(number)

    def finish(self):
        for (k, number), copy in self.copies.items():
            if number == 7:
                copy.wait_recv()
            if number or k in self.slots:
                copy.wait_send()
        for k in self.slots:
            self.keeps[k].wait()


def closing_kernel(scale, images, features, *refs):
    segs, pixels, pix_weights, cot, final = refs[:5]
    normed_m, active_s, slope_s, self_att, packed, normed_self, normed_c, active_c, slope_c = refs[5:14]
    att_low, w2s, w1s, wos, wqkv, w2c, w1c, wo = refs[14:22]
    row_scales, gains, means, rows_in, value_n, queries, tops, pix_gain = refs[22:30]
    refs = refs[30:]
    count = 12
    finals, core_in, over_in = refs[:count], refs[count : 2 * count], refs[2 * count : 3 * count]
    out_rows, pixel_out, query_out = refs[3 * count : 3 * count + 3]
    refs = refs[3 * count + 3 :]
    own, side_in, along_in = refs[:count], refs[count : 2 * count], refs[2 * count : 3 * count]
    refs = refs[3 * count :]
    staging, temps = refs[:3], refs[3:7]
    grad, acc, low, back_low, first, second, third, fourth, slope, head_grad = refs[7:17]
    gain_grads, packed_grads = refs[17], refs[18]
    all_grads = refs[19:21]
    raw, out_tile, query_sums, gain_sums = refs[21:25]
    sum_parts, sum_core, sum_over, sum_side, sum_along = refs[25:30]
    send, recv, local, load, row_send, row_recv, grad_send, grad_recv = refs[30:38]
    block_load, block_out, sum_send, sum_recv = refs[38:]
    tile = acc

    x, c, z, y = place()
    pix, dp = lax.axis_index("pix"), lax.axis_index("dp")
    others = [{"dp": dp, "pix": (pix + i) % 8} for i in range(1, 8)]
    temp_of = [temps[0:2]] * 10 + [temps[2:4], temps[0:2]]
    reduce = Reduce(
        staging, own, core_in, over_in, side_in, along_in, finals, temp_of, (send, recv), local
    )
    greet([*others, reduce.core, reduce.across])

    loads = {}

    def fetch(number, source, target):
        loads[number] = pltpu.make_async_copy(source, target, load.at[number])
        loads[number].start()

    def ready(*numbers):
        for number in numbers:
            loads.pop(number).wait()

    fetch(0, cot, low)
    fetch(1, active_s, first)
    fetch(2, w2s, third)
    fetch(3, slope_s, slope)
    fetch(4, normed_m, second)
    fetch(5, w1s, fourth)
    homes = [pltpu.make_async_copy(final.at[:, pix], out_rows.at[:, pix], load.at[31])]
    for i, other in enumerate(others):
        source, target = final.at[:, (pix + i + 1) % 8], out_rows.at[:, pix]
        homes.append(remote(source, target, (row_send, row_recv), i, other))
    for copy in homes:
        copy.start()
    gain_grads[...] = jnp.zeros_like(gain_grads)

    def strips(one):
        def step(i, carry):
            one(i, pl.ds(pl.multiple_of(i * STRIP, STRIP), STRIP))
            return carry

        lax.fori_loop(0, grad.shape[0] // STRIP, step, 0)

    def chunks(one):
        def step(j, carry):
            one(pl.ds(pl.multiple_of(j * CHUNK, CHUNK), CHUNK))
            return carry

        lax.fori_loop(0, STRIP // CHUNK, step, 0)

    def weight_grad(k, slot, left, right, columns):
        reduce.release(slot)
        staged = staging[slot]

        def one(i, strip):
            product = left_matmul(left[:, strip], right[:, :columns])
            staged[i, :, :, :, :, :columns] = (
                product.reshape(2, 2, 2, STRIP // 8, columns).astype(jnp.bfloat16)
            )

        strips(one)
        reduce.push(k, slot)

    def through_slope(weight):
        def one(i, strip):
            tile[:STRIP] = right_matmul(low[strip, :], weight[...])

            def chunk(part):
                at = pl.ds(pl.multiple_of(i * STRIP, STRIP) + part.start, CHUNK)
                back_low[at, :] = (tile[part, :] * slope[at, :].astype(jnp.float32)).astype(
                    jnp.bfloat16
                )

            chunks(chunk)

        strips(one)

    def through_norm(number, normed, product, fresh=False):
        gain = gains[3 - number : 4 - number]
        inverse = 1.0 / gain
        width = gain.shape[1]

        def one(i, strip):
            source = tile
            if product is None:
                source = acc
            else:
                tile[:STRIP] = product(strip)

            def chunk(part):
                at = pl.ds(pl.multiple_of(i * STRIP, STRIP) + part.start, CHUNK)
                upper = source[at if product is None else part, :]
                unit = normed[at, :].astype(jnp.float32) * inverse
                gain_grads[number : number + 1] += jnp.sum(upper * unit, 0, keepdims=True)
                upper = upper * gain
                mean = jnp.sum(upper, 1, keepdims=True) * (1.0 / width)
                tilt = jnp.sum(upper * unit, 1, keepdims=True) * (1.0 / width)
                before = low[at, :].astype(jnp.float32) if fresh else grad[at, :]
                row_scale = row_scales[at, number : number + 1]
                after = before + (upper - mean - unit * tilt) * row_scale
                grad[at, :] = after
                low[at, :] = after.astype(jnp.bfloat16)

            chunks(chunk)

        strips(one)

    ready(0, 1)
    weight_grad(0, 0, first, low, 1024)
    fetch(6, self_att, first)
    ready(2, 3)
    through_slope(third)
    fetch(7, wos, third)
    fetch(8, slope_c, slope)
    reduce.run(("c1", 0))
    ready(4)
    weight_grad(1, 1, second, back_low, 1024)
    reduce.run(("c2", 0), ("c1", 1))
    ready(5)
    through_norm(0, second, lambda strip: right_matmul(back_low[strip, :], fourth[...]), True)
    fetch(9, normed_self, second)
    half = head_grad.shape[1]
    fetch(10, wqkv.at[:, :half], fourth.at[:, :half])
    fetch(11, packed.at[:, :half], back_low.at[:, :half])
    reduce.run(("c2", 1))

    ready(6)
    weight_grad(2, 0, first, low, 1024)
    fetch(12, packed.at[:, half : 2 * half], first.at[:, :half])
    reduce.run(("c1", 2))
    ready(7, 9)
    acc[...] = jnp.zeros_like(acc)
    rows_of_image = means.shape[2]
    width = half // 6
    for pair in range(4):
        ready(11 + pair)
        block = (back_low, first)[pair % 2]

        def unit(i, carry, pair=pair, block=block):
            image, head = i // 2, i % 2
            rows = pl.ds(pl.multiple_of(image * rows_of_image, rows_of_image), rows_of_image)

            def columns(part):
                start = pl.multiple_of(head * (3 * width) + part * width, width)
                return pl.ds(start, width)

            query, key, value = (block[rows, columns(part)] for part in range(3))
            out_rows_ = pl.ds(pl.multiple_of((pair * 2 + head) * width, width), width)
            upper = right_matmul(low[rows, :], third[out_rows_, :])
            scores = right_matmul(query, key) * scale
            weights = jnp.exp(scores - jnp.max(scores, 1, keepdims=True))
            den = jnp.sum(weights, 1, keepdims=True)
            grad_num = (upper / den).astype(jnp.bfloat16)
            slopes = right_matmul(grad_num, value)
            grad_den = -jnp.sum(weights * slopes, 1, keepdims=True) / den
            grad_scores = (weights * (slopes + grad_den)).astype(jnp.bfloat16)
            head_grad[rows, columns(0)] = (matmul(grad_scores, key) * scale).astype(jnp.bfloat16)
            head_grad[rows, columns(1)] = (left_matmul(grad_scores, query) * scale).astype(
                jnp.bfloat16
            )
            head_grad[rows, columns(2)] = left_matmul(
                weights.astype(jnp.bfloat16), grad_num
            ).astype(jnp.bfloat16)
            return carry

        lax.fori_loop(0, 4, unit, 0)
        if pair < 2:
            start = (pair + 2) * half
            fetch(13 + pair, packed.at[:, start : start + half], block.at[:, :half])
        reduce.run(
            *((("c2", 2), ("x1", 0)), (("c2", 3), ("y", 0), ("x1", 1)), (("c2", 4), ("z", 0), ("y", 1), ("x1", 2)), (("c2", 5), ("b", 0), ("z", 1), ("y", 2), ("x1", 3)))[pair]
        )
        weight_grad(3 + pair, (pair + 1) % 2, second, head_grad, half)
        ready(10 if pair == 0 else 15 + pair)

        def spread(i, strip):
            acc[strip, :] += right_matmul(head_grad[strip, :], fourth[:, :half])

        strips(spread)
        if pair < 3:
            start = (pair + 1) * half
            fetch(16 + pair, wqkv.at[:, start : start + half], fourth.at[:, :half])
        reduce.run(
            *((("c1", 3), ("x2", 0)), (("c1", 4), ("x2", 1)), (("c1", 5), ("x2", 2)), (("c1", 6), ("x2", 3)))[pair]
        )
    fetch(20, active_c, first)
    fetch(21, w2c, third)
    fetch(22, w1c, fourth)
    through_norm(1, second, None)
    fetch(23, normed_c, second)
    reduce.run(("c2", 6), ("y", 3), ("b", 1), ("z", 2), ("x1", 4))

    ready(20)
    weight_grad(7, 1, first, low, 1024)
    fetch(24, att_low, first)
    reduce.run(("x2", 4))
    ready(21, 8)
    through_slope(third)
    fetch(25, wo, third)
    reduce.run(("c1", 7), ("y", 4), ("z", 3), ("b", 2), ("x1", 5))
    ready(23)
    weight_grad(8, 0, second, back_low, 1024)
    reduce.run(("c2", 7), ("x2", 5), ("c1", 8))
    ready(22)
    through_norm(2, second, lambda strip: right_matmul(back_low[strip, :], fourth[...]))
    reduce.run(("c2", 8), ("y", 5), ("z", 4), ("b", 3), ("x1", 6))

    ready(25)

    def upper_rows(i, strip):
        back_low[strip, :] = right_matmul(low[strip, :], third[...]).astype(jnp.bfloat16)

    strips(upper_rows)
    micros = means.shape[0]
    grad_sems = (grad_send, grad_recv)
    along = {}
    for m in range(micros):
        rows = pl.ds(m * rows_of_image, rows_of_image)
        sums = right_matmul(value_n[...], back_low[rows, :]) / rows_in[m, 0:1]
        grad_den = -jnp.sum(sums * means[m].astype(jnp.float32), 0, keepdims=True)
        packed_grads[m, : FROWS - 16] = sums[: FROWS - 16].astype(jnp.bfloat16)
        at = lax.broadcasted_iota(jnp.int32, (16, sums.shape[1]), 0) + (FROWS - 16)
        tail = with_rows(sums[FROWS - 16 :], grad_den, rows_in[m, 1:2])
        packed_grads[m, FROWS - 16 :] = jnp.where(at == DEN_ROW + 1, 0.0, tail).astype(
            jnp.bfloat16
        )
        mine, home = packed_grads.at[m], all_grads[m].at[z, y]
        for i in (1, 2, 3):
            along[m, i] = remote(
                mine, home, grad_sems, (m, i - 1), device(x, c, (z + i) % 4, y)
            )
            along[m, i].start()
        along[m, 4] = remote(mine, home, grad_sems, (m, 3), reduce.beside)
        along[m, 4].start()
        fetch(26 + m, mine, home)

    def pass_grads(m):
        for i in (1, 2, 3):
            along[m, i].wait_recv()
            block = all_grads[m].at[(z + 4 - i) % 4, y]
            along[m, 4 + i] = remote(block, block, grad_sems, (m, 3 + i), reduce.beside)
            along[m, 4 + i].start()

    def grads_ready(m):
        ready(26 + m)
        for i in range(4, 8):
            along[m, i].wait_recv()

    ready(24)
    weight_grad(9, 1, first, low, 1024)
    reduce.run(("x2", 6), ("c1", 9))
    value_grad = sum(
        matmul(means[m], back_low[m * rows_of_image : (m + 1) * rows_of_image, :])
        for m in range(micros)
    )
    staged = staging[2]
    shards = [
        jnp.concatenate(
            [
                value_grad[:, s * 128 : (s + 1) * 128],
                gain_grads[:, s * 128 : (s + 1) * 128],
                jnp.zeros((320 - FROWS - 8, 128), jnp.float32),
            ],
            0,
        )
        for s in range(8)
    ]
    for s in range(8):
        staged[s // 2, s % 2] = shards[s].reshape(2, 2, 80, 128).astype(jnp.bfloat16)
    reduce.push(10, 2)
    reduce.release(0)
    staged = staging[0]
    for s in range(8):
        at = s * 64
        both = grad[at : at + 64, :] + grad[at + rows_of_image : at + rows_of_image + 64, :]
        staged[s // 2, s % 2, :, :, :16] = both.reshape(2, 2, 16, both.shape[1]).astype(
            jnp.bfloat16
        )
    reduce.push(11, 0)
    reduce.run(("c2", 9), ("c1", 10), ("y", 6), ("c2", 10), ("c1", 11), ("z", 5), ("c2", 11), ("b", 4))

    slots = pixels.shape[2]
    blocks = slots // BLOCK
    pieces = BLOCK // PIECE
    halves = BLOCK // out_tile.shape[2]
    query_sums[...] = jnp.zeros_like(query_sums)
    gain_sums[...] = jnp.zeros_like(gain_sums)
    scores_ref, back_ref, wide = low, acc, slope
    weight_slots = (first, second)

    def block_loads(m, b):
        rows = pl.ds(b * BLOCK, BLOCK)
        slot = b % 2
        return (
            pltpu.make_async_copy(pixels.at[m, :, rows], raw.at[slot], block_load.at[0, slot]),
            pltpu.make_async_copy(
                pix_weights.at[m, rows],
                weight_slots[slot].at[:, :rows_of_image],
                block_load.at[1, slot],
            ),
        )

    def block_store(m, b, part):
        rows = pl.ds(b * BLOCK + part * (BLOCK // halves), BLOCK // halves)
        return pltpu.make_async_copy(
            out_tile.at[part], pixel_out.at[m, :, rows], block_out.at[part]
        )

    def pixels_back(m, after):
        for copy in block_loads(m, 0):
            copy.start()
        for b in range(blocks):
            if b + 1 < blocks:
                for copy in block_loads(m, b + 1):
                    copy.start()
            for copy in block_loads(m, b):
                copy.wait()
            normed, unit_, row_scale = normed_block(raw[b % 2], pix_gain[...], features)
            wide[:FROWS, :] = normed
            weights = weight_slots[b % 2]

            def piece(k, carry, b=b, weights=weights):
                rows = pl.ds(pl.multiple_of(k * PIECE, PIECE), PIECE)
                number = b * pieces + k
                seg = segs[m * blocks * pieces + number]
                image = jnp.minimum(seg, images - 1)
                upper = all_grads[m][image // 2, image % 2]
                unused, top = read_rows(upper[FROWS - 16 :].astype(jnp.float32))
                factor = jnp.where(seg < images, jnp.exp(tops[m, number] - top), 0.0)
                full = weights[rows, :rows_of_image].astype(jnp.float32) * factor
                slopes = left_matmul(wide[:FROWS, rows], upper)
                scores_ref[rows, :rows_of_image] = (full * slopes).astype(jnp.bfloat16)
                back_ref[:FROWS, rows] = right_matmul(upper, full.astype(jnp.bfloat16))
                return carry

            lax.fori_loop(0, pieces, piece, 0)
            scores = scores_ref[:, :rows_of_image]
            query_sums[...] += matmul(wide[:FROWS, :], scores)
            back = back_ref[:FROWS, :] + right_matmul(queries[...], scores)
            at = lax.broadcasted_iota(jnp.int32, back.shape, 0)
            back = jnp.where(at < features, back, 0.0)
            product = back * unit_
            gain_sums[:FROWS] += sum(
                product[:, j * 128 : (j + 1) * 128] for j in range(BLOCK // 128)
            )
            back = back * pix_gain[...]
            mean = jnp.sum(back, 0, keepdims=True) * (1.0 / features)
            tilt = jnp.sum(back * unit_, 0, keepdims=True) * (1.0 / features)
            result = (back - mean - unit_ * tilt) * row_scale
            size = BLOCK // halves
            for part in range(halves):
                if m or b:
                    block_store(m, b, part).wait()
                out_tile[part] = result[:, part * size : (part + 1) * size]
                block_store(m, b, part).start()
            reduce.run(*after[b])

    pass_grads(0)
    reduce.run(("x1", 7), ("x2", 7))
    pass_grads(1)
    reduce.run(("y", 7), ("z", 6), ("b", 5))
    grads_ready(0)
    pixels_back(0, ((), (("x1", 8), ("x2", 8)), (("z", 7), ("b", 6)), (("y", 8),)))
    grads_ready(1)
    pixels_back(1, ((("x1", 9), ("x2", 9)), (("z", 8), ("b", 7)), (("x1", 10), ("x2", 10), ("x1", 11), ("x2", 11)), (("y", 9),)))
    for part in range(halves):
        block_store(0, 0, part).wait()

    sums = query_sums[...]
    at = lax.broadcasted_iota(jnp.int32, sums.shape, 0)
    gain_row = jnp.sum(gain_sums[...].T, 0, keepdims=True)
    gain_row = jnp.concatenate([gain_row, jnp.zeros((1, 128), jnp.float32)], 1)
    sums = jnp.where(at == GAIN_ROW, gain_row, sums)
    for j in range(4):
        sum_parts[j // 2, j % 2] = sums[:, j * 128 : (j + 1) * 128].astype(jnp.bfloat16)
    sum_sems = (sum_send, sum_recv)
    copies = [remote(sum_parts.at[1 - c], sum_core, sum_sems, 0, reduce.core)]
    copies[0].start()
    reduce.run(("y", 10), ("y", 11), ("z", 9), ("b", 8))
    copies[0].wait_recv()
    sum_parts[c] = sum_parts[c] + sum_core[...]
    copies.append(remote(sum_parts.at[c, 1 - x], sum_over, sum_sems, 1, reduce.across))
    copies[1].start()
    reduce.run(("z", 10), ("z", 11))
    copies[1].wait_recv()
    sum_parts[c, x] = sum_parts[c, x] + sum_over[...]
    copies.append(remote(sum_parts.at[c, x], sum_side, sum_sems, 2, reduce.beside))
    copies[2].start()
    reduce.run(("b", 9))
    copies[2].wait_recv()
    sum_along[z] = sum_parts[c, x] + sum_side[...]
    for i in (1, 2, 3):
        target = device(x, c, (z + i) % 4, y)
        copies.append(remote(sum_along.at[z], sum_along.at[z], sum_sems, 2 + i, target))
        copies[2 + i].start()
    reduce.run(("b", 10), ("b", 11))
    for i in (1, 2, 3):
        copies[2 + i].wait_recv()
    total = sum(sum_along[i].astype(jnp.float32) for i in range(4))
    query_out[c, x] = total.astype(jnp.bfloat16)
    copies.append(remote(query_out.at[c, x], query_out.at[c, x], sum_sems, 6, reduce.across))
    copies[6].start()
    copies[6].wait_recv()
    copies.append(remote(query_out.at[c], query_out.at[c], sum_sems, 7, reduce.core))
    copies[7].start()
    copies[7].wait_recv()
    for copy in copies:
        copy.wait_send()
    for copy in along.values():
        copy.wait_send()
    for copy in homes:
        copy.wait()
    reduce.finish()


def closing(
    segs,
    pixels,
    pix_weights,
    cot,
    final,
    final_kept,
    self_att,
    packed,
    normed_self,
    cross_kept,
    att_low,
    weights,
    row_scales,
    gains,
    means,
    rows,
    value_n,
    queries,
    tops,
    pix_gain,
    features,
    images,
    scale,
):
    bf16, f32 = jnp.bfloat16, jnp.float32
    total_rows, width = cot.shape
    micros, unused, slots = pixels.shape
    latents = means.shape[2]
    half = 3 * width // 4
    full, part = (STRIP // 8, width), (STRIP // 8, half)
    shapes = [full] * 3 + [part] * 4 + [full] * 3 + [(80, 128), (16, width)]
    count = len(shapes)

    def grid(*lead):
        return [(*lead, *shape) for shape in shapes]

    def scratch(shape, dtype=bf16):
        return pltpu.VMEM(shape, dtype)

    def arrays(list_):
        return [jax.ShapeDtypeStruct(shape, bf16) for shape in list_]

    square = (total_rows, width)
    quarter = (FROWS, 128)
    smem = pl.BlockSpec(memory_space=pltpu.SMEM)
    results = pl.pallas_call(
        functools.partial(closing_kernel, scale, images, features),
        out_shape=[
            *arrays(grid(2, 2)),
            *arrays(grid(4, 2, 2)),
            *arrays(grid(4, 2)),
            jax.ShapeDtypeStruct(final.shape, bf16),
            jax.ShapeDtypeStruct(pixels.shape, f32),
            jax.ShapeDtypeStruct((2, 2, *quarter), bf16),
        ],
        in_specs=[smem] + [HBM] * 21 + [VMEM] * 8,
        out_specs=[VMEM] * count + [HBM] * (2 * count + 2) + [VMEM],
        scratch_shapes=[
            *map(scratch, grid(4, 2, 2)),
            *map(scratch, grid(4)),
            *map(scratch, grid(3)),
            *[scratch((4, 2, 2, 2, *shape)) for shape in (full, full, shapes[10])],
            *[
                scratch((4, 2, *lead, *shape))
                for shape in (full, shapes[10])
                for lead in ((2,), ())
            ],
            scratch(square, f32),
            scratch(square, f32),
            *[scratch(square) for _ in range(7)],
            scratch((total_rows, half)),
            scratch((8, width), f32),
            scratch((micros, FROWS, latents)),
            *[scratch((4, 2, FROWS, latents)) for _ in range(micros)],
            scratch((2, FROWS, BLOCK)),
            scratch((2, FROWS, BLOCK // 2), f32),
            scratch((FROWS, latents), f32),
            scratch((384, 128), f32),
            scratch((2, 2, *quarter)),
            scratch((2, *quarter)),
            scratch(quarter),
            scratch(quarter),
            scratch((4, *quarter)),
            pltpu.SemaphoreType.DMA((count, 8)),
            pltpu.SemaphoreType.DMA((count, 8)),
            pltpu.SemaphoreType.DMA((count, 3)),
            pltpu.SemaphoreType.DMA((32,)),
            pltpu.SemaphoreType.DMA((7,)),
            pltpu.SemaphoreType.DMA((7,)),
            pltpu.SemaphoreType.DMA((micros, 7)),
            pltpu.SemaphoreType.DMA((micros, 7)),
            pltpu.SemaphoreType.DMA((2, 2)),
            pltpu.SemaphoreType.DMA((2,)),
            pltpu.SemaphoreType.DMA((8,)),
            pltpu.SemaphoreType.DMA((8,)),
        ],
        compiler_params=remote_params(1, 64 * MIB - 1024),
        name="closing",
    )(
        segs,
        pixels,
        pix_weights,
        cot,
        final,
        *final_kept,
        self_att,
        packed,
        normed_self,
        *cross_kept,
        att_low,
        *weights,
        row_scales,
        gains,
        means,
        rows,
        value_n,
        queries,
        tops,
        pix_gain,
    )
    shards = [
        result.reshape(4 * shape[0], shape[1])
        for result, shape in zip(results[:count], shapes, strict=True)
    ]
    query_sums = results[-1].reshape(4, *quarter).transpose(1, 0, 2).reshape(FROWS, latents)
    return shards, results[-3], results[-2], query_sums


def image_body(
    image_sides,
    pixels,
    latent_array,
    pixel_gain,
    latent_gain,
    query_weight,
    key_weight,
    value_weight,
    cross_out_weight,
    cross_mlp_gain,
    cross_mlp_in,
    cross_mlp_out,
    self_gain,
    self_qkv_weight,
    self_out_weight,
    self_mlp_gain,
    self_mlp_in,
    self_mlp_out,
    cotangent,
):
    position = lax.axis_index("pix")
    micros, images = image_sides.shape[1:]
    capacity, features = pixels.shape[2:]
    row_count, width = latent_array.shape
    latents = row_count * 8
    head_size = width // HEADS
    cross_scale = width ** (-0.5)
    self_scale = head_size ** (-0.5)
    f32, bf16 = jnp.float32, jnp.bfloat16

    def widen(values, columns):
        return jnp.pad(values, ((0, 0), (0, columns - values.shape[1])))

    gains = jnp.stack([latent_gain, cross_mlp_gain, self_gain, self_mlp_gain], 1)
    gains = jnp.pad(gains, ((0, 0), (GAIN_LANE, 384 - GAIN_LANE - 4)))
    shards = (
        latent_array,
        query_weight,
        widen(key_weight.T, 384) + gains,
        widen(value_weight.T, 384),
        cross_out_weight,
        cross_mlp_in,
        cross_mlp_out,
        self_qkv_weight,
        self_out_weight,
        self_mlp_in,
        self_mlp_out,
    )
    splits = (True,) * len(shards)
    lengths = image_sides[0] * image_sides[0]
    ends = jnp.cumsum(lengths, 1)
    firsts = position * capacity + PIECE * jnp.arange(capacity // PIECE, dtype=jnp.int32)
    segs = jnp.sum((firsts[None, :, None] >= ends[:, None, :]).astype(jnp.int32), 2)
    same = jnp.pad((segs[:, 1:] == segs[:, :-1]).astype(jnp.int32), ((0, 0), (1, 0))).reshape(-1)
    here = segs[:, :, None] == jnp.arange(images, dtype=jnp.int32)[None, None, :]
    order = jnp.arange(capacity // PIECE, dtype=jnp.int32)[None, :, None]
    last = jnp.max(jnp.where(here, order, -1), 1).reshape(-1)
    segs = segs.reshape(-1)
    gain_pix = jnp.pad(pixel_gain.astype(f32), (0, FROWS - features))[:, None]
    pixel_rows = jnp.pad(
        pixels[0].transpose(0, 2, 1), ((0, 0), (0, FROWS - features), (0, 0))
    )
    wholes, results = opening(
        same,
        last,
        shards,
        splits,
        pixel_rows,
        cotangent[0],
        gain_pix,
        features,
        cross_scale,
    )
    lat_full, wq, key_t, value_t, wo, w1c, w2c, wqkv, wos, w1s, w2s = wholes
    pix_weights, cot_rows, *kept = results[:13]
    normed_c, active_c, slope_c, normed_self, packed, self_att = kept[:6]
    normed_m, active_s, slope_s, att_low, final = kept[6:]
    normed_lat, queries, query_t, pix_tops, means, rows, row_scales, gain_rows = results[13:]
    final = final.reshape(micros, 8, row_count, width)
    lat_f = lat_full.astype(f32)

    shards, latent_out, pixel_grad, query_sums = closing(
        segs,
        pixel_rows,
        pix_weights,
        cot_rows.reshape(-1, width),
        final,
        (normed_m, active_s, slope_s),
        self_att,
        packed,
        normed_self,
        (normed_c, active_c, slope_c),
        att_low,
        (w2s, w1s, wos, wqkv, w2c, w1c, wo),
        row_scales,
        gain_rows,
        means,
        rows,
        value_t[:, :FROWS].T,
        query_t,
        pix_tops,
        gain_pix,
        features,
        images,
        head_size ** (-0.5),
    )
    f_w2s, f_w1s, f_wos, *f_qkv, f_w2c, f_w1c, f_wo, f_vec, f_lat = shards
    d_gpix = query_sums[GAIN_ROW, :features].astype(f32)

    grad_queries = lax.dot_general(
        query_sums, key_t[:, :FROWS], (((0,), (1,)), ((), ())), preferred_element_type=f32
    )
    grad_queries = (grad_queries * cross_scale).astype(bf16)
    columns = lax.dynamic_slice_in_dim(normed_lat, position * (width // 8), width // 8, 1)
    d_wq = left_matmul(columns, grad_queries)
    query_columns = lax.dynamic_slice_in_dim(queries, position * (width // 8), width // 8, 1)
    d_wk = matmul(query_sums[:features], query_columns) * cross_scale
    grad_norm_lat, d_glat = norm_back(lat_f, gain_rows[0], right_matmul(grad_queries, wq))
    d_glat = lax.dynamic_slice_in_dim(d_glat, position * (width // 8), width // 8, 0)
    grad_norm_rows = lax.dynamic_slice_in_dim(grad_norm_lat, position * row_count, row_count, 0)
    return (
        latent_out[None],
        pixel_grad[:, :features].transpose(0, 2, 1)[None],
        f_lat.astype(f32) + grad_norm_rows,
        d_gpix,
        d_glat,
        d_wq,
        d_wk,
        f_vec[:features].astype(f32),
        f_wo.astype(f32),
        f_vec[FROWS + 2].astype(f32),
        f_w1c.astype(f32),
        f_w2c.astype(f32),
        f_vec[FROWS + 1].astype(f32),
        jnp.concatenate(f_qkv, 1).astype(f32),
        f_wos.astype(f32),
        f_vec[FROWS].astype(f32),
        f_w1s.astype(f32),
        f_w2s.astype(f32),
    )


def solution(mesh):
    fits = dict(mesh.shape) == {"dp": 4, "pix": 8}
    return jax.shard_map(
        image_body if fits else starting_body,
        mesh=mesh,
        in_specs=(
            P("dp", None, None),
            P("dp", None, "pix", None),
            P("pix", None),
            P(),
            P("pix"),
            P("pix", None),
            P(None, "pix"),
            P(None, "pix"),
            P("pix", None),
            P("pix"),
            P("pix", None),
            P("pix", None),
            P("pix"),
            P("pix", None),
            P("pix", None),
            P("pix"),
            P("pix", None),
            P("pix", None),
            P("dp", None, None, "pix", None),
        ),
        out_specs=(
            P("dp", None, None, "pix", None),
            P("dp", None, "pix", None),
            P("pix", None),
            P(),
            P("pix"),
            P("pix", None),
            P(None, "pix"),
            P(None, "pix"),
            P("pix", None),
            P("pix"),
            P("pix", None),
            P("pix", None),
            P("pix"),
            P("pix", None),
            P("pix", None),
            P("pix"),
            P("pix", None),
            P("pix", None),
        ),
        check_vma=False,
    )
```

```python
import functools

import jax
import jax.numpy as jnp
from jax import lax
from jax.experimental import pallas as pl
from jax.experimental.pallas import tpu as pltpu
from jax.sharding import PartitionSpec as P

HEADS = 8
SIDE = 64


highest = lax.Precision.HIGHEST
big_value = 1e30


def layer_norm(values, gain):
    average = jnp.mean(values, -1, keepdims=True)
    centered = values - average
    return centered * lax.rsqrt(jnp.mean(centered * centered, -1, keepdims=True) + 1e-05) * gain


def matmul(left, right):
    return jnp.dot(left, right, preferred_element_type=jnp.float32)


def left_matmul(left, right):
    return lax.dot_general(
        left, right, (((0,), (0,)), ((), ())), preferred_element_type=jnp.float32
    )


def right_matmul(left, right):
    return lax.dot_general(
        left, right, (((1,), (1,)), ((), ())), preferred_element_type=jnp.float32
    )


def norm_back(values, gain, grad):
    unused, pullback = jax.vjp(layer_norm, values, gain)
    return pullback(grad)


def mlp_forward(inputs, gain, w_in, w_out):
    normed = layer_norm(inputs, gain).astype(jnp.bfloat16)
    hidden = matmul(normed, w_in)
    active = jax.nn.gelu(hidden).astype(jnp.bfloat16)
    return (inputs + matmul(active, w_out), (normed, hidden, active))


def mlp_backward(grad, inputs, gain, w_in, w_out, kept):
    normed, hidden, active = kept
    grad_low = grad.astype(jnp.bfloat16)
    grad_out = left_matmul(active, grad_low)
    grad_active = right_matmul(grad_low, w_out)
    unused, pullback = jax.vjp(jax.nn.gelu, hidden)
    grad_hidden = pullback(grad_active)[0].astype(jnp.bfloat16)
    grad_in = left_matmul(normed, grad_hidden)
    grad_normed = right_matmul(grad_hidden, w_in)
    grad_inputs, grad_gain = norm_back(inputs, gain, grad_normed)
    return (grad + grad_inputs, grad_gain, grad_in, grad_out)


def starting_body(
    image_sides,
    pixels,
    latent_array,
    pixel_gain,
    latent_gain,
    query_weight,
    key_weight,
    value_weight,
    cross_out_weight,
    cross_mlp_gain,
    cross_mlp_in,
    cross_mlp_out,
    self_gain,
    self_qkv_weight,
    self_out_weight,
    self_mlp_gain,
    self_mlp_in,
    self_mlp_out,
    cotangent,
):
    pieces = lax.axis_size("pix")
    position = lax.axis_index("pix")
    micros = image_sides.shape[1]
    images = image_sides.shape[2]
    capacity = pixels.shape[2]
    row_count = latent_array.shape[0]
    model_width = latent_array.shape[1]
    head_size = model_width // HEADS
    unit_count = images * HEADS // pieces
    window = min(images, (capacity - 2) // (SIDE * SIDE // 4) + 2)
    cross_scale = model_width ** (-0.5)
    self_scale = head_size ** (-0.5)
    shards = (
        latent_array,
        latent_gain,
        query_weight,
        key_weight,
        value_weight,
        cross_out_weight,
        cross_mlp_gain,
        cross_mlp_in,
        cross_mlp_out,
        self_gain,
        self_qkv_weight,
        self_out_weight,
        self_mlp_gain,
        self_mlp_in,
        self_mlp_out,
    )
    lat_rows = latent_array.astype(jnp.float32)
    gain_pix = pixel_gain.astype(jnp.float32)
    grad_rows = jnp.zeros((row_count, model_width), jnp.float32)
    grad_pix_gain = jnp.zeros(gain_pix.shape, jnp.float32)
    outputs = []
    pixel_grads = []
    totals = None
    for step_index in range(micros):
        gathered = (
            lax.all_gather(shards[0], "pix", axis=0, tiled=True),
            lax.all_gather(shards[1], "pix", axis=0, tiled=True),
            lax.all_gather(shards[2], "pix", axis=0, tiled=True),
            lax.all_gather(shards[3], "pix", axis=1, tiled=True),
            lax.all_gather(shards[4], "pix", axis=1, tiled=True),
            lax.all_gather(shards[5], "pix", axis=0, tiled=True),
            lax.all_gather(shards[6], "pix", axis=0, tiled=True),
            lax.all_gather(shards[7], "pix", axis=0, tiled=True),
            lax.all_gather(shards[8], "pix", axis=0, tiled=True),
            lax.all_gather(shards[9], "pix", axis=0, tiled=True),
            lax.all_gather(shards[10], "pix", axis=0, tiled=True),
            lax.all_gather(shards[11], "pix", axis=0, tiled=True),
            lax.all_gather(shards[12], "pix", axis=0, tiled=True),
            lax.all_gather(shards[13], "pix", axis=0, tiled=True),
            lax.all_gather(shards[14], "pix", axis=0, tiled=True),
        )
        lat_full, g_lat, wq, wk, wv, wo, g_cross, w1c, w2c, g_self, wqkv, wos, g_mlp, w1s, w2s = (
            gathered
        )
        g_lat_f = g_lat.astype(jnp.float32)
        gc_f = g_cross.astype(jnp.float32)
        gs_f = g_self.astype(jnp.float32)
        gm_f = g_mlp.astype(jnp.float32)
        if step_index == 0:
            normed_lat = layer_norm(lat_full.astype(jnp.float32), g_lat_f).astype(jnp.bfloat16)
            queries = matmul(normed_lat, wq).astype(jnp.bfloat16)
        side_list = image_sides[0, step_index]
        lengths = side_list * side_list
        ends = jnp.cumsum(lengths)
        slot_ids = position * capacity + jnp.arange(capacity, dtype=jnp.int32)
        segment = jnp.sum((slot_ids[:, None] >= ends[None, :]).astype(jnp.int32), 1)
        window_ids = segment[0] + jnp.arange(window, dtype=jnp.int32)
        select = (window_ids[:, None] == jnp.arange(images, dtype=jnp.int32)[None, :]).astype(
            jnp.float32
        )
        in_window = segment[None, :] == window_ids[:, None]
        raw_pixels = pixels[0, step_index].astype(jnp.float32)
        normed_pix = layer_norm(raw_pixels, gain_pix).astype(jnp.bfloat16)
        pixel_keys = matmul(normed_pix, wk).astype(jnp.bfloat16)
        pixel_values = matmul(normed_pix, wv).astype(jnp.bfloat16)
        scores = right_matmul(queries, pixel_keys) * cross_scale
        local_top = jnp.max(jnp.where(in_window[:, None, :], scores[None], -big_value), 2)
        image_top = jnp.max(jnp.where(select[:, :, None] > 0, local_top[:, None, :], -big_value), 0)
        image_top = lax.pmax(image_top, "pix")
        window_top = jnp.einsum("wb,br->wr", select, image_top, precision=highest)
        weights = jnp.where(
            in_window[:, None, :], jnp.exp(scores[None] - window_top[:, :, None]), 0.0
        )
        partial_den = jnp.sum(weights, 2)
        partial_num = jnp.einsum(
            "wrc,cd->wrd",
            weights.astype(jnp.bfloat16),
            pixel_values,
            preferred_element_type=jnp.float32,
        )
        full_num = jnp.einsum("wb,wrd->brd", select, partial_num, precision=highest)
        full_den = jnp.einsum("wb,wr->br", select, partial_den, precision=highest)
        num_rows, den_rows = (
            lax.psum_scatter(
                full_num.astype(jnp.bfloat16), "pix", scatter_dimension=1, tiled=True
            ).astype(jnp.float32),
            lax.psum_scatter(
                full_den.astype(jnp.bfloat16), "pix", scatter_dimension=1, tiled=True
            ).astype(jnp.float32),
        )
        attended = num_rows / den_rows[:, :, None]
        attended_low = attended.astype(jnp.bfloat16).reshape(images * row_count, model_width)
        start_rows = jnp.broadcast_to(lat_rows[None], (images, row_count, model_width)).reshape(
            images * row_count, model_width
        )
        after_cross = start_rows + matmul(attended_low, wo)
        after_mlp, cross_kept = mlp_forward(after_cross, gc_f, w1c, w2c)
        normed_self = layer_norm(after_mlp, gs_f).astype(jnp.bfloat16)
        packed = matmul(normed_self, wqkv).astype(jnp.bfloat16)
        packed = packed.reshape(images, row_count, HEADS, 3 * head_size).transpose(0, 2, 1, 3)
        packed = packed.reshape(pieces, unit_count, row_count, 3 * head_size)
        packed = lax.all_to_all(packed, "pix", split_axis=0, concat_axis=2, tiled=True)[0]
        head_query = packed[:, :, :head_size]
        head_key = packed[:, :, head_size : 2 * head_size]
        head_value = packed[:, :, 2 * head_size :]
        self_scores = (
            jnp.einsum("uqd,ukd->uqk", head_query, head_key, preferred_element_type=jnp.float32)
            * self_scale
        )
        self_top = jnp.max(self_scores, 2, keepdims=True)
        self_weights = jnp.exp(self_scores - self_top)
        self_den = jnp.sum(self_weights, 2, keepdims=True)
        self_num = jnp.einsum(
            "uqk,ukd->uqd",
            self_weights.astype(jnp.bfloat16),
            head_value,
            preferred_element_type=jnp.float32,
        )
        self_out = self_num / self_den
        returned = lax.all_to_all(
            self_out.astype(jnp.bfloat16), "pix", split_axis=1, concat_axis=0, tiled=True
        )
        returned = (
            returned.reshape(images, HEADS, row_count, head_size)
            .transpose(0, 2, 1, 3)
            .reshape(images * row_count, model_width)
        )
        after_self = after_mlp + matmul(returned, wos)
        final, final_kept = mlp_forward(after_self, gm_f, w1s, w2s)
        outputs.append(final.astype(jnp.bfloat16).reshape(images, row_count, model_width))
        grad = cotangent[0, step_index].astype(jnp.float32).reshape(images * row_count, model_width)
        grad, d_gm, d_w1s, d_w2s = mlp_backward(grad, after_self, gm_f, w1s, w2s, final_kept)
        grad_low = grad.astype(jnp.bfloat16)
        d_wos = left_matmul(returned, grad_low)
        grad_self = right_matmul(grad_low, wos)
        grad_self = grad_self.reshape(images, row_count, HEADS, head_size).transpose(0, 2, 1, 3)
        grad_self = grad_self.reshape(pieces, unit_count, row_count, head_size)
        grad_self = lax.all_to_all(
            grad_self.astype(jnp.bfloat16), "pix", split_axis=0, concat_axis=2, tiled=True
        ).astype(grad_self.dtype)[0]
        grad_num = (grad_self / self_den).astype(jnp.bfloat16)
        grad_den = -jnp.sum(grad_self * self_out, 2, keepdims=True) / self_den
        again_scores = (
            jnp.einsum("uqd,ukd->uqk", head_query, head_key, preferred_element_type=jnp.float32)
            * self_scale
        )
        again_weights = jnp.exp(again_scores - self_top)
        grad_weights = (
            jnp.einsum("uqd,ukd->uqk", grad_num, head_value, preferred_element_type=jnp.float32)
            + grad_den
        )
        grad_scores = (again_weights * grad_weights).astype(jnp.bfloat16)
        grad_query = (
            jnp.einsum("uqk,ukd->uqd", grad_scores, head_key, preferred_element_type=jnp.float32)
            * self_scale
        )
        grad_key = (
            jnp.einsum("uqk,uqd->ukd", grad_scores, head_query, preferred_element_type=jnp.float32)
            * self_scale
        )
        grad_value = jnp.einsum(
            "uqk,uqd->ukd",
            again_weights.astype(jnp.bfloat16),
            grad_num,
            preferred_element_type=jnp.float32,
        )
        grad_packed = jnp.concatenate([grad_query, grad_key, grad_value], 2).astype(jnp.bfloat16)
        grad_packed = lax.all_to_all(grad_packed, "pix", split_axis=1, concat_axis=0, tiled=True)
        grad_packed = (
            grad_packed.reshape(images, HEADS, row_count, 3 * head_size)
            .transpose(0, 2, 1, 3)
            .reshape(images * row_count, 3 * model_width)
        )
        d_wqkv = left_matmul(normed_self, grad_packed)
        grad_normed = right_matmul(grad_packed, wqkv)
        grad_inputs, d_gs = norm_back(after_mlp, gs_f, grad_normed)
        grad = grad + grad_inputs
        grad, d_gc, d_w1c, d_w2c = mlp_backward(grad, after_cross, gc_f, w1c, w2c, cross_kept)
        grad_rows = grad_rows + jnp.sum(grad.reshape(images, row_count, model_width), 0)
        grad_low = grad.astype(jnp.bfloat16)
        d_wo = left_matmul(attended_low, grad_low)
        grad_cross = right_matmul(grad_low, wo).reshape(images, row_count, model_width)
        cross_gnum = (grad_cross / den_rows[:, :, None]).astype(jnp.bfloat16)
        cross_gden = (-jnp.sum(grad_cross * attended, 2) / den_rows).astype(jnp.bfloat16)
        all_num, all_den = (
            lax.all_gather(cross_gnum, "pix", axis=1, tiled=True),
            lax.all_gather(cross_gden, "pix", axis=1, tiled=True),
        )
        select_low = select.astype(jnp.bfloat16)
        window_num = jnp.einsum(
            "wb,brd->wrd", select_low, all_num, preferred_element_type=jnp.float32
        ).astype(jnp.bfloat16)
        window_den = jnp.einsum(
            "wb,br->wr", select_low, all_den, preferred_element_type=jnp.float32
        )
        scores = right_matmul(queries, pixel_keys) * cross_scale
        weights = jnp.where(
            in_window[:, None, :], jnp.exp(scores[None] - window_top[:, :, None]), 0.0
        )
        cross_gweights = (
            jnp.einsum("wrd,cd->wrc", window_num, pixel_values, preferred_element_type=jnp.float32)
            + window_den[:, :, None]
        )
        cross_gscores = jnp.sum(weights * cross_gweights, 0).astype(jnp.bfloat16)
        query_terms = matmul(cross_gscores, pixel_keys) * cross_scale
        grad_keys = (left_matmul(cross_gscores, queries) * cross_scale).astype(jnp.bfloat16)
        grad_values = jnp.einsum(
            "wrc,wrd->cd",
            weights.astype(jnp.bfloat16),
            window_num,
            preferred_element_type=jnp.float32,
        ).astype(jnp.bfloat16)
        d_wk = left_matmul(normed_pix, grad_keys)
        d_wv = left_matmul(normed_pix, grad_values)
        grad_normed_pix = right_matmul(grad_keys, wk) + right_matmul(grad_values, wv)
        grad_pixels, d_gpix = norm_back(raw_pixels, gain_pix, grad_normed_pix)
        pixel_grads.append(grad_pixels)
        grad_pix_gain = grad_pix_gain + d_gpix
        terms = (
            d_wk,
            d_wv,
            d_wo,
            d_gc,
            d_w1c,
            d_w2c,
            d_gs,
            d_wqkv,
            d_wos,
            d_gm,
            d_w1s,
            d_w2s,
            query_terms,
        )
        reduced = (
            lax.psum_scatter(
                terms[0].astype(jnp.bfloat16), "pix", scatter_dimension=1, tiled=True
            ).astype(jnp.float32),
            lax.psum_scatter(
                terms[1].astype(jnp.bfloat16), "pix", scatter_dimension=1, tiled=True
            ).astype(jnp.float32),
            lax.psum_scatter(
                terms[2].astype(jnp.bfloat16), "pix", scatter_dimension=0, tiled=True
            ).astype(jnp.float32),
            lax.psum_scatter(
                terms[3].astype(jnp.bfloat16), "pix", scatter_dimension=0, tiled=True
            ).astype(jnp.float32),
            lax.psum_scatter(
                terms[4].astype(jnp.bfloat16), "pix", scatter_dimension=0, tiled=True
            ).astype(jnp.float32),
            lax.psum_scatter(
                terms[5].astype(jnp.bfloat16), "pix", scatter_dimension=0, tiled=True
            ).astype(jnp.float32),
            lax.psum_scatter(
                terms[6].astype(jnp.bfloat16), "pix", scatter_dimension=0, tiled=True
            ).astype(jnp.float32),
            lax.psum_scatter(
                terms[7].astype(jnp.bfloat16), "pix", scatter_dimension=0, tiled=True
            ).astype(jnp.float32),
            lax.psum_scatter(
                terms[8].astype(jnp.bfloat16), "pix", scatter_dimension=0, tiled=True
            ).astype(jnp.float32),
            lax.psum_scatter(
                terms[9].astype(jnp.bfloat16), "pix", scatter_dimension=0, tiled=True
            ).astype(jnp.float32),
            lax.psum_scatter(
                terms[10].astype(jnp.bfloat16), "pix", scatter_dimension=0, tiled=True
            ).astype(jnp.float32),
            lax.psum_scatter(
                terms[11].astype(jnp.bfloat16), "pix", scatter_dimension=0, tiled=True
            ).astype(jnp.float32),
            lax.psum_scatter(
                terms[12].astype(jnp.bfloat16), "pix", scatter_dimension=0, tiled=True
            ).astype(jnp.float32),
        )
        totals = reduced if totals is None else jax.tree.map(jnp.add, totals, reduced)
    s_wk, s_wv, s_wo, s_gc, s_w1c, s_w2c, s_gs, s_wqkv, s_wos, s_gm, s_w1s, s_w2s, s_query = totals
    summed = (
        lax.psum(s_wk.astype(jnp.bfloat16), "dp").astype(jnp.float32),
        lax.psum(s_wv.astype(jnp.bfloat16), "dp").astype(jnp.float32),
        lax.psum(s_wo.astype(jnp.bfloat16), "dp").astype(jnp.float32),
        lax.psum(s_gc.astype(jnp.bfloat16), "dp").astype(jnp.float32),
        lax.psum(s_w1c.astype(jnp.bfloat16), "dp").astype(jnp.float32),
        lax.psum(s_w2c.astype(jnp.bfloat16), "dp").astype(jnp.float32),
        lax.psum(s_gs.astype(jnp.bfloat16), "dp").astype(jnp.float32),
        lax.psum(s_wqkv.astype(jnp.bfloat16), "dp").astype(jnp.float32),
        lax.psum(s_wos.astype(jnp.bfloat16), "dp").astype(jnp.float32),
        lax.psum(s_gm.astype(jnp.bfloat16), "dp").astype(jnp.float32),
        lax.psum(s_w1s.astype(jnp.bfloat16), "dp").astype(jnp.float32),
        lax.psum(s_w2s.astype(jnp.bfloat16), "dp").astype(jnp.float32),
        lax.psum(s_query.astype(jnp.bfloat16), "dp").astype(jnp.float32),
        lax.psum(grad_rows.astype(jnp.bfloat16), "dp").astype(jnp.float32),
    )
    (
        f_wk,
        f_wv,
        f_wo,
        f_gc,
        f_w1c,
        f_w2c,
        f_gs,
        f_wqkv,
        f_wos,
        f_gm,
        f_w1s,
        f_w2s,
        query_rows,
        rows_total,
    ) = summed
    query_low = query_rows.astype(jnp.bfloat16)
    normed_rows = lax.dynamic_slice_in_dim(normed_lat, position * row_count, row_count, 0)
    d_wq_part = left_matmul(normed_rows, query_low)
    grad_normed_rows = right_matmul(query_low, wq)
    grad_lat_norm, d_glat_part = norm_back(lat_rows, g_lat_f, grad_normed_rows)
    d_wq, d_glat = (
        lax.psum_scatter(
            d_wq_part.astype(jnp.bfloat16), "pix", scatter_dimension=0, tiled=True
        ).astype(jnp.float32),
        lax.psum_scatter(
            d_glat_part.astype(jnp.bfloat16), "pix", scatter_dimension=0, tiled=True
        ).astype(jnp.float32),
    )
    d_gpix = lax.psum(grad_pix_gain, ("dp", "pix"))
    latent_out = jnp.stack(outputs)[None]
    pixel_out = jnp.stack(pixel_grads)[None]
    return (
        latent_out,
        pixel_out,
        rows_total + grad_lat_norm,
        d_gpix,
        d_glat,
        d_wq,
        f_wk,
        f_wv,
        f_wo,
        f_gc,
        f_w1c,
        f_w2c,
        f_gs,
        f_wqkv,
        f_wos,
        f_gm,
        f_w1s,
        f_w2s,
    )


MESH = pl.DeviceIdType.MESH
HBM = pl.BlockSpec(memory_space=pl.ANY)
VMEM = pl.BlockSpec(memory_space=pltpu.VMEM)
MIB = 1024 * 1024
PIECE = 256
BLOCK = 1024
STRIP = 256
CHUNK = 64
FROWS = 272
DEN_ROW = 261
TOP_ROW = 263
GAIN_LANE = 264
GAIN_ROW = 262


def place():
    dp, pix = lax.axis_index("dp"), lax.axis_index("pix")
    return dp // 2, dp % 2, pix // 2, pix % 2


def device(x, c, z, y):
    return {"dp": x * 2 + c, "pix": z * 2 + y}


def greet(partners):
    barrier = pltpu.get_barrier_semaphore()
    for partner in partners:
        pl.semaphore_signal(barrier, inc=1, device_id=partner, device_id_type=MESH)
    pl.semaphore_wait(barrier, len(partners))


def remote(source, target, sems, index, partner):
    return pltpu.make_async_remote_copy(
        src_ref=source,
        dst_ref=target,
        send_sem=sems[0].at[index],
        recv_sem=sems[1].at[index],
        device_id=partner,
        device_id_type=MESH,
    )


def remote_params(collective_id, vmem=48 * MIB):
    return pltpu.CompilerParams(
        collective_id=collective_id, has_side_effects=True, vmem_limit_bytes=vmem
    )


def normed_block(raw, gain, features):
    values = raw.astype(jnp.float32)
    rows = lax.broadcasted_iota(jnp.int32, values.shape, 0)
    average = jnp.sum(values, 0, keepdims=True) * (1.0 / features)
    centered = jnp.where(rows < features, values - average, 0.0)
    scale = lax.rsqrt(jnp.sum(centered * centered, 0, keepdims=True) * (1.0 / features) + 1e-05)
    unit = centered * scale
    wide = jnp.where(rows == DEN_ROW, 1.0, unit * gain)
    return wide.astype(jnp.bfloat16), unit, scale


def three_parts(row):
    first = row.astype(jnp.bfloat16).astype(jnp.float32)
    rest = row - first
    second = rest.astype(jnp.bfloat16).astype(jnp.float32)
    return first, second, rest - second


def with_rows(tail, den, top):
    rows = lax.broadcasted_iota(jnp.int32, tail.shape, 0) + (FROWS - 16)
    high = den.astype(jnp.bfloat16).astype(jnp.float32)
    first, second, third = three_parts(top)
    tail = jnp.where(rows == DEN_ROW, high, tail)
    tail = jnp.where(rows == DEN_ROW + 1, den - high, tail)
    tail = jnp.where(rows == TOP_ROW, first, tail)
    tail = jnp.where(rows == TOP_ROW + 1, second, tail)
    return jnp.where(rows == TOP_ROW + 2, third, tail)


def read_rows(tail):
    at = DEN_ROW - (FROWS - 16)
    den = tail[at : at + 1] + tail[at + 1 : at + 2]
    at = TOP_ROW - (FROWS - 16)
    top = tail[at : at + 1] + tail[at + 1 : at + 2] + tail[at + 2 : at + 3]
    return den, top


def merge(pieces):
    bodies = [piece[: FROWS - 16].astype(jnp.float32) for piece in pieces]
    tails = [piece[FROWS - 16 :].astype(jnp.float32) for piece in pieces]
    read = [read_rows(tail) for tail in tails]
    top = functools.reduce(jnp.maximum, [row for unused, row in read])
    factors = [jnp.exp(row - top) for unused, row in read]
    body = sum(values * factor for values, factor in zip(bodies, factors, strict=True))
    tail = sum(values * factor for values, factor in zip(tails, factors, strict=True))
    den = sum(row * factor for (row, unused), factor in zip(read, factors, strict=True))
    return body, tail, den, top


def gelu_and_slope(hidden):
    const = (2 / jnp.pi) ** 0.5
    square = hidden * hidden
    bent = jnp.tanh(const * hidden * (1 + 0.044715 * square))
    half = 0.5 * (1 + bent)
    slope = half + 0.5 * hidden * (1 - bent * bent) * const * (1 + 3 * 0.044715 * square)
    return hidden * half, slope


class Gather:
    def __init__(self, shards, wholes, splits, send, recv, local):
        self.shards, self.wholes, self.splits = shards, wholes, splits
        self.sems, self.local = (send, recv), local
        self.place = place()
        x, c, z, y = self.place
        self.core, self.across = device(x, 1 - c, z, y), device(1 - x, c, z, y)
        self.beside = device(x, c, z, 1 - y)
        self.along, self.side, self.over, self.between, self.keep = {}, {}, {}, {}, {}

    def part(self, k, ref):
        x, c, z, y = self.place
        return ref.at[x, c] if self.splits[k] else ref.at[:, c]

    def start(self, k):
        x, c, z, y = self.place
        mine, home = self.part(k, self.shards[k]), self.part(k, self.wholes[k].at[z, y])
        for i in (1, 2, 3):
            target = device(x, c, (z + i) % 4, y)
            self.along[k, i] = remote(mine, home, self.sems, (k, i - 1), target)
            self.along[k, i].start()
        self.side[k, 0] = remote(mine, home, self.sems, (k, 3), self.beside)
        self.side[k, 0].start()
        self.keep[k] = pltpu.make_async_copy(
            self.shards[k], self.wholes[k].at[z, y], self.local.at[k]
        )
        self.keep[k].start()

    def to_side(self, k):
        x, c, z, y = self.place
        for i in (1, 2, 3):
            self.along[k, i].wait_recv()
            block = self.part(k, self.wholes[k].at[(z + 4 - i) % 4, y])
            self.side[k, i] = remote(block, block, self.sems, (k, 3 + i), self.beside)
            self.side[k, i].start()

    def to_over(self, k):
        x, c, z, y = self.place
        for i in range(4):
            self.side[k, i].wait_recv()
            if self.splits[k]:
                if i == 0:
                    block = self.wholes[k].at[z, 1 - y, x, c]
                else:
                    block = self.wholes[k].at[(z + 4 - i) % 4, :, x, c]
                self.over[k, i] = remote(block, block, self.sems, (k, 7 + i), self.across)
                self.over[k, i].start()

    def to_core(self, k):
        x, c, z, y = self.place
        for i in range(4):
            if self.splits[k]:
                self.over[k, i].wait_recv()
            if i == 0:
                block = self.wholes[k].at[z, 1 - y, :, c]
            else:
                block = self.wholes[k].at[(z + 4 - i) % 4, :, :, c]
            self.between[k, i] = remote(block, block, self.sems, (k, 11 + i), self.core)
            self.between[k, i].start()

    def arrive(self, k):
        self.keep[k].wait()
        for i in range(4):
            self.between[k, i].wait_recv()

    def finish(self):
        for group in (self.along, self.side, self.over, self.between):
            for copy in group.values():
                copy.wait_send()


def opening_kernel(splits, scale, features, *refs):
    count = len(splits)
    same, last = refs[:2]
    shards, pixels, cot, pix_gain = refs[2 : count + 2], *refs[count + 2 : count + 5]
    refs = refs[count + 5 :]
    wholes, weights_out, cot_rows = refs[:count], refs[count], refs[count + 1]
    normed_c, active_c, slope_c, normed_s, packed, self_att = refs[count + 2 : count + 8]
    normed_m, active_s, slope_s, att_low, final = refs[count + 8 : count + 13]
    refs = refs[count + 13 :]
    normed_out, queries_out, query_out, tops, means, rows_out, row_scales, gains = refs[:8]
    refs = refs[8:]
    wide, weights, scores_ref, lat, wq, key, total, largest, pieces, sums = refs[:10]
    side_in, own, along_in = refs[10:13]
    value, stream, tile, first, second, third, fourth, left_w, right_w, heads = refs[13:23]
    send, recv, local, own_send, own_recv, load, cot_send, cot_recv, fetch_sem, store_sem = refs[23:]
    x, c, z, y = place()
    micros, unused, slots = pixels.shape
    blocks = slots // BLOCK
    per_block = BLOCK // PIECE
    images = sums.shape[1]
    gather = Gather(shards, wholes, splits, send, recv, local)
    pix, dp = lax.axis_index("pix"), lax.axis_index("dp")
    others = [{"dp": dp, "pix": (pix + i) % 8} for i in range(1, 8)]
    greet([*others, gather.across, gather.core])

    fetch = pltpu.make_async_copy(pixels, wide, load.at[0])
    fetch.start()
    for k in range(3):
        gather.start(k)
    gain = pix_gain[...]

    def norm(start, stop):
        def one(i, carry):
            half = BLOCK // 2
            columns = pl.ds(pl.multiple_of((i % (2 * blocks)) * half, half), half)
            micro = i // (2 * blocks)
            wide[micro, :, columns] = normed_block(wide[micro, :, columns], gain, features)[0]
            return carry

        lax.fori_loop(2 * start, 2 * stop, one, 0)

    fetch.wait()
    norm(0, 2)
    for k in range(3):
        gather.to_side(k)
    for k in range(3, 6):
        gather.start(k)
    norm(2, 4)
    for k in range(3):
        gather.to_over(k)
    for k in range(6, count):
        gather.start(k)
    norm(4, 6)
    for k in range(3):
        gather.to_core(k)
    gather.to_side(3)
    gather.to_side(4)
    norm(6, 2 * blocks)
    gather.to_over(3)
    fetches = []
    for k, target in enumerate((lat, wq, key)):
        gather.arrive(k)
        fetches.append(pltpu.make_async_copy(wholes[k], target, load.at[1 + k]))
        fetches[k].start()
    gather.to_side(5)
    gather.to_over(4)
    for copy in fetches:
        copy.wait()

    lat_values = lat[...].reshape(sums.shape[3], -1).astype(jnp.float32)
    key_values = key[...].reshape(lat_values.shape[1], -1)
    columns = key_values[:, 256:384].astype(jnp.float32).T
    gains[...] = columns[GAIN_LANE - 256 : GAIN_LANE - 248]
    normed = layer_norm(lat_values, gains[0:1])
    normed_out[...] = normed.astype(jnp.bfloat16)
    wq_values = wq[...].reshape(lat_values.shape[1], -1)
    queries_out[...] = matmul(normed_out[...], wq_values).astype(jnp.bfloat16)
    query_t = (
        lax.dot_general(
            key_values, queries_out[...], (((0,), (1,)), ((), ())),
            preferred_element_type=jnp.float32,
        )
        * scale
    )
    query_t = query_t[:FROWS]
    rows = lax.broadcasted_iota(jnp.int32, query_t.shape, 0)
    query_out[...] = jnp.where(rows < features, query_t, 0.0).astype(jnp.bfloat16)

    gather.to_side(6)
    gather.to_over(5)
    gather.to_core(3)
    gather.to_core(4)

    def forward(m):
        total[...] = jnp.zeros_like(total)
        largest[...] = jnp.full(largest.shape, -big_value, jnp.float32)

        def one(b, carry):
            rows = pl.ds(pl.multiple_of(b * BLOCK, BLOCK), BLOCK)
            scores_ref[...] = left_matmul(wide[m, :, rows], query_out[...])
            for k in range(per_block):
                rows = pl.ds(pl.multiple_of(b * BLOCK + k * PIECE, PIECE), PIECE)
                scores = scores_ref[k * PIECE : (k + 1) * PIECE]
                top = jnp.max(scores, 0, keepdims=True)
                low = jnp.exp(scores - top).astype(jnp.bfloat16)
                weights[m, rows, :] = low
                piece = b * per_block + k
                tops[m, piece] = top
                added = matmul(wide[m, :, rows], low)
                before = jnp.where(
                    same[m * blocks * per_block + piece] > 0, largest[...], -big_value
                )
                now = jnp.maximum(before, top)
                largest[...] = now
                older, newer = jnp.exp(before - now), jnp.exp(top - now)
                summed = total[...] * older + added * newer
                total[...] = summed
                pieces[piece, : FROWS - 16] = summed[: FROWS - 16].astype(jnp.bfloat16)
                at = DEN_ROW - (FROWS - 16)
                tail = summed[FROWS - 16 :]
                pieces[piece, FROWS - 16 :] = with_rows(tail, tail[at : at + 1], now).astype(
                    jnp.bfloat16
                )
            return carry

        lax.fori_loop(0, blocks, one, 0)
        for image in range(images):
            index = last[m * images + image]
            present = index >= 0
            piece = pieces[jnp.maximum(index, 0)].astype(jnp.float32)
            sums[m, image, : FROWS - 16] = jnp.where(present, piece[: FROWS - 16], 0.0).astype(
                jnp.bfloat16
            )
            nothing = jnp.zeros((1, piece.shape[1]), jnp.float32)
            absent = with_rows(
                jnp.zeros((16, piece.shape[1]), jnp.float32), nothing, nothing - big_value
            )
            sums[m, image, FROWS - 16 :] = jnp.where(
                present, piece[FROWS - 16 :], absent
            ).astype(jnp.bfloat16)

    own_sems = (own_send, own_recv)
    sides, alongs, keeps = {}, {}, []

    def send_sums(m):
        for i in (1, 2, 3, 0):
            source = sums.at[m, ((z + i) % 4) * 2 + 1 - y]
            sides[m, i] = remote(source, side_in.at[m, i], own_sems, (m, i), gather.beside)
            sides[m, i].start()
        keeps.append(pltpu.make_async_copy(weights.at[m], weights_out.at[m], load.at[4 + m]))
        keeps[-1].start()

    def pass_sums(m):
        for i in (1, 2, 3, 0):
            sides[m, i].wait_recv()
            body, tail, den, top = merge([sums[m, ((z + i) % 4) * 2 + y], side_in[m, i]])
            own[m, i, : FROWS - 16] = body.astype(jnp.bfloat16)
            own[m, i, FROWS - 16 :] = with_rows(tail, den, top).astype(jnp.bfloat16)
            if i:
                target = device(x, c, (z + i) % 4, y)
                alongs[m, i] = remote(
                    own.at[m, i], along_in.at[m, i - 1], own_sems, (m, 3 + i), target
                )
                alongs[m, i].start()

    def finish_sums(m):
        for i in (1, 2, 3):
            alongs[m, i].wait_recv()
        body, tail, den, top = merge([own[m, 0]] + [along_in[m, i] for i in range(3)])
        rows = lax.broadcasted_iota(jnp.int32, tail.shape, 0) + (FROWS - 16)
        means[m, : FROWS - 16] = (body / den).astype(jnp.bfloat16)
        means[m, FROWS - 16 :] = jnp.where(rows < DEN_ROW, tail / den, 0.0).astype(jnp.bfloat16)
        rows_out[m, 0:1] = den
        rows_out[m, 1:2] = top

    forward(0)
    send_sums(0)
    gather.to_side(7)
    gather.to_over(6)
    gather.to_core(5)
    forward(1)
    send_sums(1)
    pass_sums(0)
    gather.to_side(8)
    gather.to_over(7)
    gather.to_core(6)
    pass_sums(1)
    gather.to_side(9)
    gather.to_over(8)
    gather.to_side(10)
    gather.to_core(7)

    loads, stores = {}, {}

    def fetch(number, source, target):
        loads[number] = pltpu.make_async_copy(source, target, fetch_sem.at[number])
        loads[number].start()

    def store(number, source, target):
        stores[number] = pltpu.make_async_copy(source, target, store_sem.at[number])
        stores[number].start()

    def stored(*numbers):
        for number in numbers:
            stores.pop(number).wait()

    def ready(*numbers):
        for number in numbers:
            loads.pop(number).wait()

    gather.arrive(3)
    fetch(0, wholes[3], value)
    gather.arrive(4)
    fetch(1, wholes[4], left_w)
    gather.arrive(5)
    fetch(2, wholes[5], right_w)
    finish_sums(0)
    gather.to_over(9)
    finish_sums(1)
    latents, model = lat_values.shape
    strip_count = stream.shape[0] // STRIP

    def strips(one):
        def step(i, carry):
            one(i, pl.ds(pl.multiple_of(i * STRIP, STRIP), STRIP))
            return carry

        lax.fori_loop(0, strip_count, step, 0)

    def chunks(one):
        def step(j, carry):
            one(pl.ds(pl.multiple_of(j * CHUNK, CHUNK), CHUNK))
            return carry

        lax.fori_loop(0, STRIP // CHUNK, step, 0)

    def square(ref):
        return ref[...].reshape(model, model)

    def add_and_norm(left, weight, number, target, base=None, last_out=None):
        def one(i, strip):
            if base is None:
                stream[strip, :] += matmul(left[strip, :], square(weight))
            else:
                stream[strip, :] = base(i) + matmul(left[strip, :], square(weight))

            def chunk(part):
                at = pl.ds(pl.multiple_of(i * STRIP, STRIP) + part.start, CHUNK)
                values = stream[at, :]
                centered = values - jnp.mean(values, 1, keepdims=True)
                row_scale = lax.rsqrt(jnp.mean(centered * centered, 1, keepdims=True) + 1e-05)
                row_scales[at, 3 - number : 4 - number] = row_scale
                target[at, :] = (centered * row_scale * gains[number : number + 1]).astype(
                    jnp.bfloat16
                )

            chunks(chunk)

        strips(one)

    def through_gelu(left, weight, active, slope):
        def one(i, strip):
            tile[...] = matmul(left[strip, :], square(weight))

            def chunk(part):
                at = pl.ds(pl.multiple_of(i * STRIP, STRIP) + part.start, CHUNK)
                acted, sloped = gelu_and_slope(tile[part, :])
                active[at, :] = acted.astype(jnp.bfloat16)
                slope[at, :] = sloped.astype(jnp.bfloat16)

            chunks(chunk)

        strips(one)

    ready(0)
    for m in range(micros):
        first[m * latents : (m + 1) * latents, :] = lax.dot_general(
            means[m],
            value[...].reshape(model, -1)[:, :FROWS],
            (((0,), (1,)), ((), ())),
            preferred_element_type=jnp.float32,
        ).astype(jnp.bfloat16)
    store(0, first, att_low)
    gather.to_over(10)
    gather.to_core(8)
    ready(1)

    def lat_strip(i):
        return lat[pl.ds((i % 2) * 2, 2)].reshape(STRIP, model).astype(jnp.float32)

    add_and_norm(first, left_w, 1, second, lat_strip)
    store(1, second, normed_c)
    gather.arrive(6)
    fetch(3, wholes[6], left_w)
    ready(2)
    through_gelu(second, right_w, third, fourth)
    store(2, third, active_c)
    store(3, fourth, slope_c)
    gather.to_core(9)
    gather.arrive(7)
    cots = [pltpu.make_async_copy(cot.at[:, pix], cot_rows.at[:, pix], local.at[count])]
    for i, other in enumerate(others):
        source, target = cot.at[:, (pix + i + 1) % 8], cot_rows.at[:, pix]
        cots.append(remote(source, target, (cot_send, cot_recv), i, other))
    for copy in cots:
        copy.start()

    half = heads.shape[2]
    fetch(4, wholes[7].at[:, :, :, :, :, :half], right_w.at[:, :, :, :, :, :half])
    ready(3)
    stored(0)
    add_and_norm(third, left_w, 2, first)
    store(4, first, normed_s)
    fetch(5, wholes[7].at[:, :, :, :, :, half : 2 * half], left_w.at[:, :, :, :, :, :half])
    gather.to_core(10)
    stored(1)
    width = half // 6
    for pair in range(4):
        block = heads.at[pair % 2]
        weight = (right_w, left_w)[pair % 2]
        ready(4 + pair)
        if pair >= 2:
            stored(3 + pair)

        def project(i, strip, block=block, weight=weight):
            product = matmul(first[strip, :], weight[:, :, :, :, :, :half].reshape(model, half))
            block[strip, :] = product.astype(jnp.bfloat16)

        strips(project)
        store(5 + pair, block, packed.at[:, pair * half : (pair + 1) * half])
        if pair < 2:
            columns = pl.ds((pair + 2) * half, half)
            fetch(
                6 + pair,
                wholes[7].at[:, :, :, :, :, columns],
                weight.at[:, :, :, :, :, :half],
            )

        def unit(i, carry, pair=pair, block=block):
            image, head = i // 2, i % 2
            rows = pl.ds(pl.multiple_of(image * latents, latents), latents)

            def columns(part):
                start = pl.multiple_of(head * (3 * width) + part * width, width)
                return pl.ds(start, width)

            query, key_, value_ = (block[rows, columns(part)] for part in range(3))
            scores = right_matmul(query, key_) * width ** (-0.5)
            exps = jnp.exp(scores - jnp.max(scores, 1, keepdims=True))
            den = jnp.sum(exps, 1, keepdims=True)
            out = pl.ds(pl.multiple_of((pair * 2 + head) * width, width), width)
            second[rows, out] = (matmul(exps.astype(jnp.bfloat16), value_) / den).astype(
                jnp.bfloat16
            )
            return carry

        lax.fori_loop(0, 4, unit, 0)
    store(9, second, self_att)
    gather.arrive(8)
    fetch(8, wholes[8], right_w)
    gather.arrive(9)
    fetch(9, wholes[9], left_w)
    ready(8)
    stored(2)
    add_and_norm(second, right_w, 3, third)
    store(10, third, normed_m)
    gather.arrive(10)
    fetch(10, wholes[10], right_w)
    ready(9)
    stored(3, 4)
    through_gelu(third, left_w, fourth, first)
    store(11, fourth, active_s)
    store(12, first, slope_s)
    ready(10)
    stored(9)

    def finish_rows(i, strip):
        second[strip, :] = (
            stream[strip, :] + matmul(fourth[strip, :], square(right_w))
        ).astype(jnp.bfloat16)

    strips(finish_rows)
    store(13, second, final)
    stored(*list(stores))
    for copy in (*keeps, *cots):
        copy.wait()
    gather.finish()
    for copy in (*sides.values(), *alongs.values()):
        copy.wait_send()


def opening(same, last, shards, splits, pixels, cot, gain, features, scale):
    count = len(shards)
    bf16, f32 = jnp.bfloat16, jnp.float32
    micros, unused, slots = pixels.shape
    latents, width = 8 * shards[0].shape[0], shards[0].shape[1]
    views = [shard.reshape(2, 2, shard.shape[0] // 4, shard.shape[1]) for shard in shards]
    outs = [jax.ShapeDtypeStruct((4, 2, *view.shape), view.dtype) for view in views]
    images = cot.shape[1]
    piece = (FROWS, latents)
    total_rows = micros * latents
    square, wide = (total_rows, width), (total_rows, 3 * width)
    kept = [jax.ShapeDtypeStruct(wide if i == 4 else square, bf16) for i in range(11)]
    smem = pl.BlockSpec(memory_space=pltpu.SMEM)
    results = pl.pallas_call(
        functools.partial(opening_kernel, splits, scale, features),
        out_shape=[
            *outs,
            jax.ShapeDtypeStruct((micros, slots, latents), bf16),
            jax.ShapeDtypeStruct(cot.shape, bf16),
            *kept,
            jax.ShapeDtypeStruct((latents, width), bf16),
            jax.ShapeDtypeStruct((latents, width), bf16),
            jax.ShapeDtypeStruct(piece, bf16),
            jax.ShapeDtypeStruct((micros, slots // PIECE, 1, latents), f32),
            jax.ShapeDtypeStruct((micros, *piece), bf16),
            jax.ShapeDtypeStruct((micros, 2, latents), f32),
            jax.ShapeDtypeStruct((total_rows, 128), f32),
            jax.ShapeDtypeStruct((8, width), f32),
        ],
        in_specs=[smem, smem] + [HBM] * (count + 2) + [VMEM],
        out_specs=[HBM] * (count + 13) + [VMEM] * 8,
        scratch_shapes=[
            pltpu.VMEM(pixels.shape, bf16),
            pltpu.VMEM((micros, slots, latents), bf16),
            pltpu.VMEM((BLOCK, latents), f32),
            pltpu.VMEM(outs[0].shape, bf16),
            pltpu.VMEM(outs[1].shape, bf16),
            pltpu.VMEM(outs[2].shape, bf16),
            pltpu.VMEM(piece, f32),
            pltpu.VMEM((1, latents), f32),
            pltpu.VMEM((slots // PIECE, *piece), bf16),
            pltpu.VMEM((micros, images, *piece), bf16),
            pltpu.VMEM((micros, 4, *piece), bf16),
            pltpu.VMEM((micros, 4, *piece), bf16),
            pltpu.VMEM((micros, 3, *piece), bf16),
            pltpu.VMEM(outs[3].shape, bf16),
            pltpu.VMEM(square, f32),
            pltpu.VMEM((STRIP, width), f32),
            *[pltpu.VMEM(square, bf16) for _ in range(4)],
            *[pltpu.VMEM(outs[4].shape, bf16) for _ in range(2)],
            pltpu.VMEM((2, total_rows, 3 * width // 4), bf16),
            pltpu.SemaphoreType.DMA((count, 15)),
            pltpu.SemaphoreType.DMA((count, 15)),
            pltpu.SemaphoreType.DMA((count + 1,)),
            pltpu.SemaphoreType.DMA((micros, 7)),
            pltpu.SemaphoreType.DMA((micros, 7)),
            pltpu.SemaphoreType.DMA((4 + micros,)),
            pltpu.SemaphoreType.DMA((7,)),
            pltpu.SemaphoreType.DMA((7,)),
            pltpu.SemaphoreType.DMA((11,)),
            pltpu.SemaphoreType.DMA((14,)),
        ],
        compiler_params=remote_params(0, 64 * MIB - 1024),
        name="opening",
    )(same, last, *views, pixels, cot, gain)
    wholes = [
        whole.reshape(8 * shard.shape[0], shard.shape[1])
        for whole, shard in zip(results[:count], shards, strict=True)
    ]
    return wholes, results[count:]


class Reduce:
    def __init__(self, staging, own, core_in, over_in, side_in, along_in, finals, temps, sems, local):
        self.staging, self.own = staging, own
        self.core_in, self.over_in, self.side_in = core_in, over_in, side_in
        self.along_in, self.finals, self.temps = along_in, finals, temps
        self.sems, self.local = sems, local
        self.place = place()
        x, c, z, y = self.place
        self.core, self.across = device(x, 1 - c, z, y), device(1 - x, c, z, y)
        self.beside = device(x, c, z, 1 - y)
        self.copies, self.loads, self.keeps, self.slots = {}, {}, {}, {}

    def send(self, k, number, source, target, partner):
        self.copies[k, number] = remote(source, target, self.sems, (k, number), partner)
        self.copies[k, number].start()

    def release(self, slot):
        for k, used in self.slots.items():
            if used == slot:
                self.copies[k, 0].wait_send()
                self.keeps[k].wait()
        self.slots = {k: used for k, used in self.slots.items() if used != slot}

    def push(self, k, slot):
        x, c, z, y = self.place
        staged = self.staging[slot]
        rows, columns = self.own[k].shape[-2:]
        away = staged.at[:, :, :, 1 - c, :rows, :columns]
        self.send(k, 0, away, self.core_in[k], self.core)
        self.keeps[k] = pltpu.make_async_copy(
            staged.at[:, :, :, c, :rows, :columns], self.own[k], self.local.at[k, 0]
        )
        self.keeps[k].start()
        self.slots[k] = slot

    def c1(self, k):
        self.copies[k, 0].wait_recv()
        rows, columns = self.own[k].shape[-2:]
        temp = self.temps[k][0].at[:, :, :, :rows, :columns]
        self.loads[k] = pltpu.make_async_copy(self.core_in[k], temp, self.local.at[k, 1])
        self.loads[k].start()

    def add(self, count, one):
        def step(i, carry):
            one(i)
            return carry

        lax.fori_loop(0, count, step, 0)

    def c2(self, k):
        x, c, z, y = self.place
        own, temp = self.own[k], self.temps[k][0]
        rows, columns = own.shape[-2:]
        if k in self.slots:
            self.keeps[k].wait()
            self.copies[k, 0].wait_send()
            del self.slots[k]
        self.loads[k].wait()

        def one(i):
            own[i // 2, i % 2] = own[i // 2, i % 2] + temp[i // 2, i % 2, :, :rows, :columns]

        self.add(8, one)
        self.send(k, 1, own.at[:, :, 1 - x], self.over_in[k], self.across)

    def x1(self, k):
        self.copies[k, 1].wait_recv()
        rows, columns = self.own[k].shape[-2:]
        temp = self.temps[k][1].at[:, :, :rows, :columns]
        self.loads[k] = pltpu.make_async_copy(self.over_in[k], temp, self.local.at[k, 2])
        self.loads[k].start()

    def x2(self, k):
        x, c, z, y = self.place
        own, temp = self.own[k], self.temps[k][1]
        rows, columns = own.shape[-2:]
        self.loads[k].wait()

        def one(i):
            own[i // 2, i % 2, x] = own[i // 2, i % 2, x] + temp[i // 2, i % 2, :rows, :columns]

        self.add(8, one)
        self.send(k, 2, own.at[:, 1 - y, x], self.side_in[k], self.beside)

    def y(self, k):
        x, c, z, y = self.place
        own, side_in = self.own[k], self.side_in[k]
        self.copies[k, 2].wait_recv()

        def one(i):
            own[i, y, x] = own[i, y, x] + side_in[i]

        self.add(4, one)
        for i in (1, 2, 3):
            target = device(x, c, (z + i) % 4, y)
            self.send(
                k, 2 + i, own.at[(z + i) % 4, y, x], self.along_in[k].at[i - 1], target
            )

    def z(self, k):
        x, c, z, y = self.place
        for i in (1, 2, 3):
            self.copies[k, 2 + i].wait_recv()
        total = self.own[k][z, y, x].astype(jnp.float32)
        for i in range(3):
            total = total + self.along_in[k][i].astype(jnp.float32)
        final = self.finals[k]
        final[x, c] = total.astype(jnp.bfloat16)
        self.send(k, 6, final.at[x, c], final.at[x, c], self.across)

    def b(self, k):
        x, c, z, y = self.place
        final = self.finals[k]
        self.copies[k, 6].wait_recv()
        self.send(k, 7, final.at[:, c], final.at[:, c], self.core)

    def run(self, *stages):
        for name, number in stages:
            getattr(self, name)(number)

    def finish(self):
        for (k, number), copy in self.copies.items():
            if number == 7:
                copy.wait_recv()
            if number or k in self.slots:
                copy.wait_send()
        for k in self.slots:
            self.keeps[k].wait()


def closing_kernel(scale, images, features, *refs):
    segs, pixels, pix_weights, cot, final = refs[:5]
    normed_m, active_s, slope_s, self_att, packed, normed_self, normed_c, active_c, slope_c = refs[5:14]
    att_low, w2s, w1s, wos, wqkv, w2c, w1c, wo = refs[14:22]
    row_scales, gains, means, rows_in, value_n, queries, tops, pix_gain = refs[22:30]
    refs = refs[30:]
    count = 12
    finals, core_in, over_in = refs[:count], refs[count : 2 * count], refs[2 * count : 3 * count]
    out_rows, pixel_out, query_out = refs[3 * count : 3 * count + 3]
    refs = refs[3 * count + 3 :]
    own, side_in, along_in = refs[:count], refs[count : 2 * count], refs[2 * count : 3 * count]
    refs = refs[3 * count :]
    staging, temps = refs[:3], refs[3:7]
    grad, acc, low, back_low, first, second, third, fourth, slope, head_grad = refs[7:17]
    gain_grads, packed_grads = refs[17], refs[18]
    all_grads = refs[19:21]
    raw, out_tile, query_sums, gain_sums = refs[21:25]
    sum_parts, sum_core, sum_over, sum_side, sum_along = refs[25:30]
    send, recv, local, load, row_send, row_recv, grad_send, grad_recv = refs[30:38]
    block_load, block_out, sum_send, sum_recv = refs[38:]
    tile = acc

    x, c, z, y = place()
    pix, dp = lax.axis_index("pix"), lax.axis_index("dp")
    others = [{"dp": dp, "pix": (pix + i) % 8} for i in range(1, 8)]
    temp_of = [temps[0:2]] * 10 + [temps[2:4], temps[0:2]]
    reduce = Reduce(
        staging, own, core_in, over_in, side_in, along_in, finals, temp_of, (send, recv), local
    )
    greet([*others, reduce.core, reduce.across])

    loads = {}

    def fetch(number, source, target):
        loads[number] = pltpu.make_async_copy(source, target, load.at[number])
        loads[number].start()

    def ready(*numbers):
        for number in numbers:
            loads.pop(number).wait()

    fetch(0, cot, low)
    fetch(1, active_s, first)
    fetch(2, w2s, third)
    fetch(3, slope_s, slope)
    fetch(4, normed_m, second)
    fetch(5, w1s, fourth)
    homes = [pltpu.make_async_copy(final.at[:, pix], out_rows.at[:, pix], load.at[31])]
    for i, other in enumerate(others):
        source, target = final.at[:, (pix + i + 1) % 8], out_rows.at[:, pix]
        homes.append(remote(source, target, (row_send, row_recv), i, other))
    for copy in homes:
        copy.start()
    gain_grads[...] = jnp.zeros_like(gain_grads)

    def strips(one, image=None):
        def step(i, carry):
            one(i, pl.ds(pl.multiple_of(i * STRIP, STRIP), STRIP))
            return carry

        count = grad.shape[0] // STRIP
        if image is None:
            lax.fori_loop(0, count, step, 0)
        else:
            per_image = count // means.shape[0]
            lax.fori_loop(image * per_image, (image + 1) * per_image, step, 0)

    def chunks(one):
        def step(j, carry):
            one(pl.ds(pl.multiple_of(j * CHUNK, CHUNK), CHUNK))
            return carry

        lax.fori_loop(0, STRIP // CHUNK, step, 0)

    def weight_grad(k, slot, left, right, columns):
        reduce.release(slot)
        staged = staging[slot]

        def one(i, strip):
            product = left_matmul(left[:, strip], right[:, :columns])
            staged[i, :, :, :, :, :columns] = (
                product.reshape(2, 2, 2, STRIP // 8, columns).astype(jnp.bfloat16)
            )

        strips(one)
        reduce.push(k, slot)

    def through_slope(weight, image=None):
        def one(i, strip):
            tile[:STRIP] = right_matmul(low[strip, :], weight[...])

            def chunk(part):
                at = pl.ds(pl.multiple_of(i * STRIP, STRIP) + part.start, CHUNK)
                back_low[at, :] = (tile[part, :] * slope[at, :].astype(jnp.float32)).astype(
                    jnp.bfloat16
                )

            chunks(chunk)

        strips(one, image)

    def through_norm(number, normed, product, fresh=False, image=None):
        gain = gains[3 - number : 4 - number]
        inverse = 1.0 / gain
        width = gain.shape[1]

        def one(i, strip):
            source = tile
            if product is None:
                source = acc
            else:
                tile[:STRIP] = product(strip)

            def chunk(part):
                at = pl.ds(pl.multiple_of(i * STRIP, STRIP) + part.start, CHUNK)
                upper = source[at if product is None else part, :]
                unit = normed[at, :].astype(jnp.float32) * inverse
                gain_grads[number : number + 1] += jnp.sum(upper * unit, 0, keepdims=True)
                upper = upper * gain
                mean = jnp.sum(upper, 1, keepdims=True) * (1.0 / width)
                tilt = jnp.sum(upper * unit, 1, keepdims=True) * (1.0 / width)
                before = low[at, :].astype(jnp.float32) if fresh else grad[at, :]
                row_scale = row_scales[at, number : number + 1]
                after = before + (upper - mean - unit * tilt) * row_scale
                grad[at, :] = after
                low[at, :] = after.astype(jnp.bfloat16)

            chunks(chunk)

        strips(one, image)

    ready(0, 1)
    weight_grad(0, 0, first, low, 1024)
    fetch(6, self_att, first)
    ready(2, 3)
    through_slope(third)
    fetch(7, wos, third)
    fetch(8, slope_c, slope)
    reduce.run(("c1", 0))
    ready(4)
    weight_grad(1, 1, second, back_low, 1024)
    reduce.run(("c2", 0), ("c1", 1))
    ready(5)
    through_norm(0, second, lambda strip: right_matmul(back_low[strip, :], fourth[...]), True)
    fetch(9, normed_self, second)
    half = 3 * head_grad.shape[1] // 4
    fetch(10, wqkv.at[:, :half], fourth.at[:, :half])
    fetch(11, packed.at[:, :half], back_low.at[:, :half])
    reduce.run(("c2", 1))

    ready(6)
    weight_grad(2, 0, first, low, 1024)
    fetch(12, packed.at[:, half : 2 * half], first.at[:, :half])
    reduce.run(("c1", 2))
    ready(7, 9)
    acc[...] = jnp.zeros_like(acc)
    rows_of_image = means.shape[2]
    width = half // 6
    for pair in range(4):
        ready(11 + pair)
        block = (back_low, first)[pair % 2]

        def unit(i, carry, pair=pair, block=block):
            image, head = i // 2, i % 2
            rows = pl.ds(pl.multiple_of(image * rows_of_image, rows_of_image), rows_of_image)

            def columns(part):
                start = pl.multiple_of(head * (3 * width) + part * width, width)
                return pl.ds(start, width)

            query, key, value = (block[rows, columns(part)] for part in range(3))
            out_rows_ = pl.ds(pl.multiple_of((pair * 2 + head) * width, width), width)
            upper = right_matmul(low[rows, :], third[out_rows_, :])
            upper = upper.astype(jnp.bfloat16)
            scores = right_matmul(key, query) * scale
            weights = jnp.exp(scores - jnp.max(scores, 0, keepdims=True))
            weights = weights * (1.0 / jnp.sum(weights, 0, keepdims=True))
            slopes = right_matmul(value, upper)
            lift = jnp.sum(weights * slopes, 0, keepdims=True)
            grad_scores = (weights * (slopes - lift)).astype(jnp.bfloat16)
            head_grad[rows, columns(0)] = (left_matmul(grad_scores, key) * scale).astype(
                jnp.bfloat16
            )
            head_grad[rows, columns(1)] = (matmul(grad_scores, query) * scale).astype(
                jnp.bfloat16
            )
            head_grad[rows, columns(2)] = matmul(weights.astype(jnp.bfloat16), upper).astype(
                jnp.bfloat16
            )
            return carry

        lax.fori_loop(0, 4, unit, 0)
        if pair < 2:
            start = (pair + 2) * half
            fetch(13 + pair, packed.at[:, start : start + half], block.at[:, :half])
        reduce.run(
            *((("c2", 2), ("x1", 0)), (("c2", 3), ("y", 0), ("x1", 1)), (("c2", 4), ("z", 0), ("y", 1), ("x1", 2)), (("c2", 5), ("b", 0), ("z", 1), ("y", 2), ("x1", 3)))[pair]
        )
        weight_grad(3 + pair, (pair + 1) % 2, second, head_grad, half)
        ready(10 if pair == 0 else 15 + pair)

        def spread(i, strip):
            acc[strip, :] += right_matmul(head_grad[strip, :half], fourth[:, :half])

        strips(spread)
        if pair < 3:
            start = (pair + 1) * half
            fetch(16 + pair, wqkv.at[:, start : start + half], fourth.at[:, :half])
        reduce.run(
            *((("c1", 3), ("x2", 0)), (("c1", 4), ("x2", 1)), (("c1", 5), ("x2", 2)), (("c1", 6), ("x2", 3)))[pair]
        )
    fetch(20, active_c, first)
    fetch(21, w2c, third)
    fetch(22, w1c, fourth)
    through_norm(1, second, None)
    fetch(23, normed_c, second)
    reduce.run(("c2", 6), ("y", 3), ("b", 1), ("z", 2), ("x1", 4))

    ready(20)
    weight_grad(7, 1, first, low, 1024)
    fetch(25, wo, first)
    reduce.run(("x2", 4))
    ready(21, 8, 22, 23, 25)
    micros = means.shape[0]
    grad_sems = (grad_send, grad_recv)
    along = {}

    def upper_rows(i, strip):
        head_grad[strip, :] = right_matmul(low[strip, :], first[...]).astype(jnp.bfloat16)

    for m in range(micros):
        through_slope(third, m)
        through_norm(
            2, second, lambda strip: right_matmul(back_low[strip, :], fourth[...]), False, m
        )
        strips(upper_rows, m)
        rows = pl.ds(m * rows_of_image, rows_of_image)
        sums = right_matmul(value_n[...], head_grad[rows, :]) / rows_in[m, 0:1]
        grad_den = -jnp.sum(sums * means[m].astype(jnp.float32), 0, keepdims=True)
        packed_grads[m, : FROWS - 16] = sums[: FROWS - 16].astype(jnp.bfloat16)
        at = lax.broadcasted_iota(jnp.int32, (16, sums.shape[1]), 0) + (FROWS - 16)
        tail = with_rows(sums[FROWS - 16 :], grad_den, rows_in[m, 1:2])
        packed_grads[m, FROWS - 16 :] = jnp.where(at == DEN_ROW + 1, 0.0, tail).astype(
            jnp.bfloat16
        )
        mine, home = packed_grads.at[m], all_grads[m].at[z, y]
        for i in (1, 2, 3):
            target = device(x, c, (z + i) % 4, y)
            along[m, i] = remote(mine, home, grad_sems, (m, i - 1), target)
            along[m, i].start()
        along[m, 4] = remote(mine, home, grad_sems, (m, 3), reduce.beside)
        along[m, 4].start()
        fetch(26 + m, mine, home)
        reduce.run(
            *(
                (("c1", 7), ("y", 4), ("z", 3), ("b", 2), ("x1", 5)),
                (("c2", 7), ("x2", 5)),
            )[m]
        )
    fetch(24, att_low, third)

    def pass_grads(m):
        for i in (1, 2, 3):
            along[m, i].wait_recv()
            block = all_grads[m].at[(z + 4 - i) % 4, y]
            along[m, 4 + i] = remote(block, block, grad_sems, (m, 3 + i), reduce.beside)
            along[m, 4 + i].start()

    def grads_ready(m):
        ready(26 + m)
        for i in range(4, 8):
            along[m, i].wait_recv()

    weight_grad(8, 0, second, back_low, 1024)
    pass_grads(0)
    reduce.run(("c1", 8), ("y", 5), ("z", 4), ("b", 3), ("x1", 6))
    ready(24)
    weight_grad(9, 1, third, low, 1024)
    reduce.run(("c2", 8), ("x2", 6), ("c1", 9))
    value_grad = sum(
        matmul(means[m], head_grad[m * rows_of_image : (m + 1) * rows_of_image, :])
        for m in range(micros)
    )
    staged = staging[2]
    shards = [
        jnp.concatenate(
            [
                value_grad[:, s * 128 : (s + 1) * 128],
                gain_grads[:, s * 128 : (s + 1) * 128],
                jnp.zeros((320 - FROWS - 8, 128), jnp.float32),
            ],
            0,
        )
        for s in range(8)
    ]
    for s in range(8):
        staged[s // 2, s % 2] = shards[s].reshape(2, 2, 80, 128).astype(jnp.bfloat16)
    reduce.push(10, 2)
    reduce.release(0)
    staged = staging[0]
    for s in range(8):
        at = s * 64
        both = grad[at : at + 64, :] + grad[at + rows_of_image : at + rows_of_image + 64, :]
        staged[s // 2, s % 2, :, :, :16] = both.reshape(2, 2, 16, both.shape[1]).astype(
            jnp.bfloat16
        )
    reduce.push(11, 0)
    reduce.run(("c2", 9), ("c1", 10), ("y", 6), ("c2", 10), ("c1", 11), ("z", 5), ("c2", 11), ("b", 4))

    slots = pixels.shape[2]
    blocks = slots // BLOCK
    pieces = BLOCK // PIECE
    halves = BLOCK // out_tile.shape[2]
    query_sums[...] = jnp.zeros_like(query_sums)
    gain_sums[...] = jnp.zeros_like(gain_sums)
    scores_ref, back_ref, wide = low, acc, slope
    weight_slots = (first, second)

    def block_loads(m, b):
        rows = pl.ds(b * BLOCK, BLOCK)
        slot = b % 2
        return (
            pltpu.make_async_copy(pixels.at[m, :, rows], raw.at[slot], block_load.at[0, slot]),
            pltpu.make_async_copy(
                pix_weights.at[m, rows],
                weight_slots[slot].at[:, :rows_of_image],
                block_load.at[1, slot],
            ),
        )

    def block_store(m, b, part):
        rows = pl.ds(b * BLOCK + part * (BLOCK // halves), BLOCK // halves)
        return pltpu.make_async_copy(
            out_tile.at[part], pixel_out.at[m, :, rows], block_out.at[part]
        )

    def pixels_back(m, after):
        for copy in block_loads(m, 0):
            copy.start()
        for b in range(blocks):
            if b + 1 < blocks:
                for copy in block_loads(m, b + 1):
                    copy.start()
            for copy in block_loads(m, b):
                copy.wait()
            normed, unit_, row_scale = normed_block(raw[b % 2], pix_gain[...], features)
            wide[:FROWS, :] = normed
            weights = weight_slots[b % 2]

            def piece(k, carry, b=b, weights=weights):
                rows = pl.ds(pl.multiple_of(k * PIECE, PIECE), PIECE)
                number = b * pieces + k
                seg = segs[m * blocks * pieces + number]
                image = jnp.minimum(seg, images - 1)
                upper = all_grads[m][image // 2, image % 2]
                unused, top = read_rows(upper[FROWS - 16 :].astype(jnp.float32))
                factor = jnp.where(seg < images, jnp.exp(tops[m, number] - top), 0.0)
                full = weights[rows, :rows_of_image].astype(jnp.float32) * factor
                slopes = left_matmul(wide[:FROWS, rows], upper)
                scores_ref[rows, :rows_of_image] = (full * slopes).astype(jnp.bfloat16)
                back_ref[:FROWS, rows] = right_matmul(upper, full.astype(jnp.bfloat16))
                return carry

            lax.fori_loop(0, pieces, piece, 0)
            scores = scores_ref[:, :rows_of_image]
            query_sums[...] += matmul(wide[:FROWS, :], scores)
            back = back_ref[:FROWS, :] + right_matmul(queries[...], scores)
            at = lax.broadcasted_iota(jnp.int32, back.shape, 0)
            back = jnp.where(at < features, back, 0.0)
            product = back * unit_
            gain_sums[:FROWS] += sum(
                product[:, j * 128 : (j + 1) * 128] for j in range(BLOCK // 128)
            )
            back = back * pix_gain[...]
            mean = jnp.sum(back, 0, keepdims=True) * (1.0 / features)
            tilt = jnp.sum(back * unit_, 0, keepdims=True) * (1.0 / features)
            result = (back - mean - unit_ * tilt) * row_scale
            size = BLOCK // halves
            for part in range(halves):
                if m or b:
                    block_store(m, b, part).wait()
                out_tile[part] = result[:, part * size : (part + 1) * size]
                block_store(m, b, part).start()
            reduce.run(*after[b])

    pass_grads(1)
    grads_ready(0)
    pixels_back(
        0,
        (
            (("x1", 7), ("x2", 7)),
            (("z", 6), ("b", 5), ("y", 7)),
            (("x1", 8), ("x2", 8)),
            (("z", 7), ("b", 6), ("y", 8)),
        ),
    )
    grads_ready(1)
    pixels_back(1, ((("x1", 9), ("x2", 9)), (("z", 8), ("b", 7)), (("x1", 10), ("x2", 10), ("x1", 11), ("x2", 11)), (("y", 9),)))
    for part in range(halves):
        block_store(0, 0, part).wait()

    sums = query_sums[...]
    at = lax.broadcasted_iota(jnp.int32, sums.shape, 0)
    gain_row = jnp.sum(gain_sums[...].T, 0, keepdims=True)
    gain_row = jnp.concatenate([gain_row, jnp.zeros((1, 128), jnp.float32)], 1)
    sums = jnp.where(at == GAIN_ROW, gain_row, sums)
    for j in range(4):
        sum_parts[j // 2, j % 2] = sums[:, j * 128 : (j + 1) * 128].astype(jnp.bfloat16)
    sum_sems = (sum_send, sum_recv)
    copies = [remote(sum_parts.at[1 - c], sum_core, sum_sems, 0, reduce.core)]
    copies[0].start()
    reduce.run(("y", 10), ("y", 11), ("z", 9), ("b", 8))
    copies[0].wait_recv()
    sum_parts[c] = sum_parts[c] + sum_core[...]
    copies.append(remote(sum_parts.at[c, 1 - x], sum_over, sum_sems, 1, reduce.across))
    copies[1].start()
    reduce.run(("z", 10), ("z", 11))
    copies[1].wait_recv()
    sum_parts[c, x] = sum_parts[c, x] + sum_over[...]
    copies.append(remote(sum_parts.at[c, x], sum_side, sum_sems, 2, reduce.beside))
    copies[2].start()
    reduce.run(("b", 9))
    copies[2].wait_recv()
    sum_along[z] = sum_parts[c, x] + sum_side[...]
    for i in (1, 2, 3):
        target = device(x, c, (z + i) % 4, y)
        copies.append(remote(sum_along.at[z], sum_along.at[z], sum_sems, 2 + i, target))
        copies[2 + i].start()
    reduce.run(("b", 10), ("b", 11))
    for i in (1, 2, 3):
        copies[2 + i].wait_recv()
    total = sum(sum_along[i].astype(jnp.float32) for i in range(4))
    query_out[c, x] = total.astype(jnp.bfloat16)
    copies.append(remote(query_out.at[c, x], query_out.at[c, x], sum_sems, 6, reduce.across))
    copies[6].start()
    copies[6].wait_recv()
    copies.append(remote(query_out.at[c], query_out.at[c], sum_sems, 7, reduce.core))
    copies[7].start()
    copies[7].wait_recv()
    for copy in copies:
        copy.wait_send()
    for copy in along.values():
        copy.wait_send()
    for copy in homes:
        copy.wait()
    reduce.finish()


def closing(
    segs,
    pixels,
    pix_weights,
    cot,
    final,
    final_kept,
    self_att,
    packed,
    normed_self,
    cross_kept,
    att_low,
    weights,
    row_scales,
    gains,
    means,
    rows,
    value_n,
    queries,
    tops,
    pix_gain,
    features,
    images,
    scale,
):
    bf16, f32 = jnp.bfloat16, jnp.float32
    total_rows, width = cot.shape
    micros, unused, slots = pixels.shape
    latents = means.shape[2]
    half = 3 * width // 4
    full, part = (STRIP // 8, width), (STRIP // 8, half)
    shapes = [full] * 3 + [part] * 4 + [full] * 3 + [(80, 128), (16, width)]
    count = len(shapes)

    def grid(*lead):
        return [(*lead, *shape) for shape in shapes]

    def scratch(shape, dtype=bf16):
        return pltpu.VMEM(shape, dtype)

    def arrays(list_):
        return [jax.ShapeDtypeStruct(shape, bf16) for shape in list_]

    square = (total_rows, width)
    quarter = (FROWS, 128)
    smem = pl.BlockSpec(memory_space=pltpu.SMEM)
    results = pl.pallas_call(
        functools.partial(closing_kernel, scale, images, features),
        out_shape=[
            *arrays(grid(2, 2)),
            *arrays(grid(4, 2, 2)),
            *arrays(grid(4, 2)),
            jax.ShapeDtypeStruct(final.shape, bf16),
            jax.ShapeDtypeStruct(pixels.shape, f32),
            jax.ShapeDtypeStruct((2, 2, *quarter), bf16),
        ],
        in_specs=[smem] + [HBM] * 21 + [VMEM] * 8,
        out_specs=[VMEM] * count + [HBM] * (2 * count + 2) + [VMEM],
        scratch_shapes=[
            *map(scratch, grid(4, 2, 2)),
            *map(scratch, grid(4)),
            *map(scratch, grid(3)),
            *[scratch((4, 2, 2, 2, *shape)) for shape in (full, full, shapes[10])],
            *[
                scratch((4, 2, *lead, *shape))
                for shape in (full, shapes[10])
                for lead in ((2,), ())
            ],
            scratch(square, f32),
            scratch(square, f32),
            *[scratch(square) for _ in range(7)],
            scratch(square),
            scratch((8, width), f32),
            scratch((micros, FROWS, latents)),
            *[scratch((4, 2, FROWS, latents)) for _ in range(micros)],
            scratch((2, FROWS, BLOCK)),
            scratch((2, FROWS, BLOCK // 2), f32),
            scratch((FROWS, latents), f32),
            scratch((384, 128), f32),
            scratch((2, 2, *quarter)),
            scratch((2, *quarter)),
            scratch(quarter),
            scratch(quarter),
            scratch((4, *quarter)),
            pltpu.SemaphoreType.DMA((count, 8)),
            pltpu.SemaphoreType.DMA((count, 8)),
            pltpu.SemaphoreType.DMA((count, 3)),
            pltpu.SemaphoreType.DMA((32,)),
            pltpu.SemaphoreType.DMA((7,)),
            pltpu.SemaphoreType.DMA((7,)),
            pltpu.SemaphoreType.DMA((micros, 7)),
            pltpu.SemaphoreType.DMA((micros, 7)),
            pltpu.SemaphoreType.DMA((2, 2)),
            pltpu.SemaphoreType.DMA((2,)),
            pltpu.SemaphoreType.DMA((8,)),
            pltpu.SemaphoreType.DMA((8,)),
        ],
        compiler_params=remote_params(1, 64 * MIB - 1024),
        name="closing",
    )(
        segs,
        pixels,
        pix_weights,
        cot,
        final,
        *final_kept,
        self_att,
        packed,
        normed_self,
        *cross_kept,
        att_low,
        *weights,
        row_scales,
        gains,
        means,
        rows,
        value_n,
        queries,
        tops,
        pix_gain,
    )
    shards = [
        result.reshape(4 * shape[0], shape[1])
        for result, shape in zip(results[:count], shapes, strict=True)
    ]
    query_sums = results[-1].reshape(4, *quarter).transpose(1, 0, 2).reshape(FROWS, latents)
    return shards, results[-3], results[-2], query_sums


def image_body(
    image_sides,
    pixels,
    latent_array,
    pixel_gain,
    latent_gain,
    query_weight,
    key_weight,
    value_weight,
    cross_out_weight,
    cross_mlp_gain,
    cross_mlp_in,
    cross_mlp_out,
    self_gain,
    self_qkv_weight,
    self_out_weight,
    self_mlp_gain,
    self_mlp_in,
    self_mlp_out,
    cotangent,
):
    position = lax.axis_index("pix")
    micros, images = image_sides.shape[1:]
    capacity, features = pixels.shape[2:]
    row_count, width = latent_array.shape
    latents = row_count * 8
    head_size = width // HEADS
    cross_scale = width ** (-0.5)
    self_scale = head_size ** (-0.5)
    f32, bf16 = jnp.float32, jnp.bfloat16

    def widen(values, columns):
        return jnp.pad(values, ((0, 0), (0, columns - values.shape[1])))

    gains = jnp.stack([latent_gain, cross_mlp_gain, self_gain, self_mlp_gain], 1)
    gains = jnp.pad(gains, ((0, 0), (GAIN_LANE, 384 - GAIN_LANE - 4)))
    shards = (
        latent_array,
        query_weight,
        widen(key_weight.T, 384) + gains,
        widen(value_weight.T, 384),
        cross_out_weight,
        cross_mlp_in,
        cross_mlp_out,
        self_qkv_weight,
        self_out_weight,
        self_mlp_in,
        self_mlp_out,
    )
    splits = (True,) * len(shards)
    lengths = image_sides[0] * image_sides[0]
    ends = jnp.cumsum(lengths, 1)
    firsts = position * capacity + PIECE * jnp.arange(capacity // PIECE, dtype=jnp.int32)
    segs = jnp.sum((firsts[None, :, None] >= ends[:, None, :]).astype(jnp.int32), 2)
    same = jnp.pad((segs[:, 1:] == segs[:, :-1]).astype(jnp.int32), ((0, 0), (1, 0))).reshape(-1)
    here = segs[:, :, None] == jnp.arange(images, dtype=jnp.int32)[None, None, :]
    order = jnp.arange(capacity // PIECE, dtype=jnp.int32)[None, :, None]
    last = jnp.max(jnp.where(here, order, -1), 1).reshape(-1)
    segs = segs.reshape(-1)
    gain_pix = jnp.pad(pixel_gain.astype(f32), (0, FROWS - features))[:, None]
    pixel_rows = jnp.pad(
        pixels[0].transpose(0, 2, 1), ((0, 0), (0, FROWS - features), (0, 0))
    )
    wholes, results = opening(
        same,
        last,
        shards,
        splits,
        pixel_rows,
        cotangent[0],
        gain_pix,
        features,
        cross_scale,
    )
    lat_full, wq, key_t, value_t, wo, w1c, w2c, wqkv, wos, w1s, w2s = wholes
    pix_weights, cot_rows, *kept = results[:13]
    normed_c, active_c, slope_c, normed_self, packed, self_att = kept[:6]
    normed_m, active_s, slope_s, att_low, final = kept[6:]
    normed_lat, queries, query_t, pix_tops, means, rows, row_scales, gain_rows = results[13:]
    final = final.reshape(micros, 8, row_count, width)
    lat_f = lat_full.astype(f32)

    shards, latent_out, pixel_grad, query_sums = closing(
        segs,
        pixel_rows,
        pix_weights,
        cot_rows.reshape(-1, width),
        final,
        (normed_m, active_s, slope_s),
        self_att,
        packed,
        normed_self,
        (normed_c, active_c, slope_c),
        att_low,
        (w2s, w1s, wos, wqkv, w2c, w1c, wo),
        row_scales,
        gain_rows,
        means,
        rows,
        value_t[:, :FROWS].T,
        query_t,
        pix_tops,
        gain_pix,
        features,
        images,
        head_size ** (-0.5),
    )
    f_w2s, f_w1s, f_wos, *f_qkv, f_w2c, f_w1c, f_wo, f_vec, f_lat = shards
    d_gpix = query_sums[GAIN_ROW, :features].astype(f32)

    grad_queries = lax.dot_general(
        query_sums, key_t[:, :FROWS], (((0,), (1,)), ((), ())), preferred_element_type=f32
    )
    grad_queries = (grad_queries * cross_scale).astype(bf16)
    columns = lax.dynamic_slice_in_dim(normed_lat, position * (width // 8), width // 8, 1)
    d_wq = left_matmul(columns, grad_queries)
    query_columns = lax.dynamic_slice_in_dim(queries, position * (width // 8), width // 8, 1)
    d_wk = matmul(query_sums[:features], query_columns) * cross_scale
    grad_norm_lat, d_glat = norm_back(lat_f, gain_rows[0], right_matmul(grad_queries, wq))
    d_glat = lax.dynamic_slice_in_dim(d_glat, position * (width // 8), width // 8, 0)
    grad_norm_rows = lax.dynamic_slice_in_dim(grad_norm_lat, position * row_count, row_count, 0)
    return (
        latent_out[None],
        pixel_grad[:, :features].transpose(0, 2, 1)[None],
        f_lat.astype(f32) + grad_norm_rows,
        d_gpix,
        d_glat,
        d_wq,
        d_wk,
        f_vec[:features].astype(f32),
        f_wo.astype(f32),
        f_vec[FROWS + 2].astype(f32),
        f_w1c.astype(f32),
        f_w2c.astype(f32),
        f_vec[FROWS + 1].astype(f32),
        jnp.concatenate(f_qkv, 1).astype(f32),
        f_wos.astype(f32),
        f_vec[FROWS].astype(f32),
        f_w1s.astype(f32),
        f_w2s.astype(f32),
    )


def solution(mesh):
    fits = dict(mesh.shape) == {"dp": 4, "pix": 8}
    return jax.shard_map(
        image_body if fits else starting_body,
        mesh=mesh,
        in_specs=(
            P("dp", None, None),
            P("dp", None, "pix", None),
            P("pix", None),
            P(),
            P("pix"),
            P("pix", None),
            P(None, "pix"),
            P(None, "pix"),
            P("pix", None),
            P("pix"),
            P("pix", None),
            P("pix", None),
            P("pix"),
            P("pix", None),
            P("pix", None),
            P("pix"),
            P("pix", None),
            P("pix", None),
            P("dp", None, None, "pix", None),
        ),
        out_specs=(
            P("dp", None, None, "pix", None),
            P("dp", None, "pix", None),
            P("pix", None),
            P(),
            P("pix"),
            P("pix", None),
            P(None, "pix"),
            P(None, "pix"),
            P("pix", None),
            P("pix"),
            P("pix", None),
            P("pix", None),
            P("pix"),
            P("pix", None),
            P("pix", None),
            P("pix"),
            P("pix", None),
            P("pix", None),
        ),
        check_vma=False,
    )
```

```python
import functools

import jax
import jax.numpy as jnp
from jax import lax
from jax.experimental import pallas as pl
from jax.experimental.pallas import tpu as pltpu
from jax.sharding import PartitionSpec as P

HEADS = 8
SIDE = 64


highest = lax.Precision.HIGHEST
big_value = 1e30


def layer_norm(values, gain):
    average = jnp.mean(values, -1, keepdims=True)
    centered = values - average
    return centered * lax.rsqrt(jnp.mean(centered * centered, -1, keepdims=True) + 1e-05) * gain


def matmul(left, right):
    return jnp.dot(left, right, preferred_element_type=jnp.float32)


def left_matmul(left, right):
    return lax.dot_general(
        left, right, (((0,), (0,)), ((), ())), preferred_element_type=jnp.float32
    )


def right_matmul(left, right):
    return lax.dot_general(
        left, right, (((1,), (1,)), ((), ())), preferred_element_type=jnp.float32
    )


def norm_back(values, gain, grad):
    unused, pullback = jax.vjp(layer_norm, values, gain)
    return pullback(grad)


def mlp_forward(inputs, gain, w_in, w_out):
    normed = layer_norm(inputs, gain).astype(jnp.bfloat16)
    hidden = matmul(normed, w_in)
    active = jax.nn.gelu(hidden).astype(jnp.bfloat16)
    return (inputs + matmul(active, w_out), (normed, hidden, active))


def mlp_backward(grad, inputs, gain, w_in, w_out, kept):
    normed, hidden, active = kept
    grad_low = grad.astype(jnp.bfloat16)
    grad_out = left_matmul(active, grad_low)
    grad_active = right_matmul(grad_low, w_out)
    unused, pullback = jax.vjp(jax.nn.gelu, hidden)
    grad_hidden = pullback(grad_active)[0].astype(jnp.bfloat16)
    grad_in = left_matmul(normed, grad_hidden)
    grad_normed = right_matmul(grad_hidden, w_in)
    grad_inputs, grad_gain = norm_back(inputs, gain, grad_normed)
    return (grad + grad_inputs, grad_gain, grad_in, grad_out)


def starting_body(
    image_sides,
    pixels,
    latent_array,
    pixel_gain,
    latent_gain,
    query_weight,
    key_weight,
    value_weight,
    cross_out_weight,
    cross_mlp_gain,
    cross_mlp_in,
    cross_mlp_out,
    self_gain,
    self_qkv_weight,
    self_out_weight,
    self_mlp_gain,
    self_mlp_in,
    self_mlp_out,
    cotangent,
):
    pieces = lax.axis_size("pix")
    position = lax.axis_index("pix")
    micros = image_sides.shape[1]
    images = image_sides.shape[2]
    capacity = pixels.shape[2]
    row_count = latent_array.shape[0]
    model_width = latent_array.shape[1]
    head_size = model_width // HEADS
    unit_count = images * HEADS // pieces
    window = min(images, (capacity - 2) // (SIDE * SIDE // 4) + 2)
    cross_scale = model_width ** (-0.5)
    self_scale = head_size ** (-0.5)
    shards = (
        latent_array,
        latent_gain,
        query_weight,
        key_weight,
        value_weight,
        cross_out_weight,
        cross_mlp_gain,
        cross_mlp_in,
        cross_mlp_out,
        self_gain,
        self_qkv_weight,
        self_out_weight,
        self_mlp_gain,
        self_mlp_in,
        self_mlp_out,
    )
    lat_rows = latent_array.astype(jnp.float32)
    gain_pix = pixel_gain.astype(jnp.float32)
    grad_rows = jnp.zeros((row_count, model_width), jnp.float32)
    grad_pix_gain = jnp.zeros(gain_pix.shape, jnp.float32)
    outputs = []
    pixel_grads = []
    totals = None
    for step_index in range(micros):
        gathered = (
            lax.all_gather(shards[0], "pix", axis=0, tiled=True),
            lax.all_gather(shards[1], "pix", axis=0, tiled=True),
            lax.all_gather(shards[2], "pix", axis=0, tiled=True),
            lax.all_gather(shards[3], "pix", axis=1, tiled=True),
            lax.all_gather(shards[4], "pix", axis=1, tiled=True),
            lax.all_gather(shards[5], "pix", axis=0, tiled=True),
            lax.all_gather(shards[6], "pix", axis=0, tiled=True),
            lax.all_gather(shards[7], "pix", axis=0, tiled=True),
            lax.all_gather(shards[8], "pix", axis=0, tiled=True),
            lax.all_gather(shards[9], "pix", axis=0, tiled=True),
            lax.all_gather(shards[10], "pix", axis=0, tiled=True),
            lax.all_gather(shards[11], "pix", axis=0, tiled=True),
            lax.all_gather(shards[12], "pix", axis=0, tiled=True),
            lax.all_gather(shards[13], "pix", axis=0, tiled=True),
            lax.all_gather(shards[14], "pix", axis=0, tiled=True),
        )
        lat_full, g_lat, wq, wk, wv, wo, g_cross, w1c, w2c, g_self, wqkv, wos, g_mlp, w1s, w2s = (
            gathered
        )
        g_lat_f = g_lat.astype(jnp.float32)
        gc_f = g_cross.astype(jnp.float32)
        gs_f = g_self.astype(jnp.float32)
        gm_f = g_mlp.astype(jnp.float32)
        if step_index == 0:
            normed_lat = layer_norm(lat_full.astype(jnp.float32), g_lat_f).astype(jnp.bfloat16)
            queries = matmul(normed_lat, wq).astype(jnp.bfloat16)
        side_list = image_sides[0, step_index]
        lengths = side_list * side_list
        ends = jnp.cumsum(lengths)
        slot_ids = position * capacity + jnp.arange(capacity, dtype=jnp.int32)
        segment = jnp.sum((slot_ids[:, None] >= ends[None, :]).astype(jnp.int32), 1)
        window_ids = segment[0] + jnp.arange(window, dtype=jnp.int32)
        select = (window_ids[:, None] == jnp.arange(images, dtype=jnp.int32)[None, :]).astype(
            jnp.float32
        )
        in_window = segment[None, :] == window_ids[:, None]
        raw_pixels = pixels[0, step_index].astype(jnp.float32)
        normed_pix = layer_norm(raw_pixels, gain_pix).astype(jnp.bfloat16)
        pixel_keys = matmul(normed_pix, wk).astype(jnp.bfloat16)
        pixel_values = matmul(normed_pix, wv).astype(jnp.bfloat16)
        scores = right_matmul(queries, pixel_keys) * cross_scale
        local_top = jnp.max(jnp.where(in_window[:, None, :], scores[None], -big_value), 2)
        image_top = jnp.max(jnp.where(select[:, :, None] > 0, local_top[:, None, :], -big_value), 0)
        image_top = lax.pmax(image_top, "pix")
        window_top = jnp.einsum("wb,br->wr", select, image_top, precision=highest)
        weights = jnp.where(
            in_window[:, None, :], jnp.exp(scores[None] - window_top[:, :, None]), 0.0
        )
        partial_den = jnp.sum(weights, 2)
        partial_num = jnp.einsum(
            "wrc,cd->wrd",
            weights.astype(jnp.bfloat16),
            pixel_values,
            preferred_element_type=jnp.float32,
        )
        full_num = jnp.einsum("wb,wrd->brd", select, partial_num, precision=highest)
        full_den = jnp.einsum("wb,wr->br", select, partial_den, precision=highest)
        num_rows, den_rows = (
            lax.psum_scatter(
                full_num.astype(jnp.bfloat16), "pix", scatter_dimension=1, tiled=True
            ).astype(jnp.float32),
            lax.psum_scatter(
                full_den.astype(jnp.bfloat16), "pix", scatter_dimension=1, tiled=True
            ).astype(jnp.float32),
        )
        attended = num_rows / den_rows[:, :, None]
        attended_low = attended.astype(jnp.bfloat16).reshape(images * row_count, model_width)
        start_rows = jnp.broadcast_to(lat_rows[None], (images, row_count, model_width)).reshape(
            images * row_count, model_width
        )
        after_cross = start_rows + matmul(attended_low, wo)
        after_mlp, cross_kept = mlp_forward(after_cross, gc_f, w1c, w2c)
        normed_self = layer_norm(after_mlp, gs_f).astype(jnp.bfloat16)
        packed = matmul(normed_self, wqkv).astype(jnp.bfloat16)
        packed = packed.reshape(images, row_count, HEADS, 3 * head_size).transpose(0, 2, 1, 3)
        packed = packed.reshape(pieces, unit_count, row_count, 3 * head_size)
        packed = lax.all_to_all(packed, "pix", split_axis=0, concat_axis=2, tiled=True)[0]
        head_query = packed[:, :, :head_size]
        head_key = packed[:, :, head_size : 2 * head_size]
        head_value = packed[:, :, 2 * head_size :]
        self_scores = (
            jnp.einsum("uqd,ukd->uqk", head_query, head_key, preferred_element_type=jnp.float32)
            * self_scale
        )
        self_top = jnp.max(self_scores, 2, keepdims=True)
        self_weights = jnp.exp(self_scores - self_top)
        self_den = jnp.sum(self_weights, 2, keepdims=True)
        self_num = jnp.einsum(
            "uqk,ukd->uqd",
            self_weights.astype(jnp.bfloat16),
            head_value,
            preferred_element_type=jnp.float32,
        )
        self_out = self_num / self_den
        returned = lax.all_to_all(
            self_out.astype(jnp.bfloat16), "pix", split_axis=1, concat_axis=0, tiled=True
        )
        returned = (
            returned.reshape(images, HEADS, row_count, head_size)
            .transpose(0, 2, 1, 3)
            .reshape(images * row_count, model_width)
        )
        after_self = after_mlp + matmul(returned, wos)
        final, final_kept = mlp_forward(after_self, gm_f, w1s, w2s)
        outputs.append(final.astype(jnp.bfloat16).reshape(images, row_count, model_width))
        grad = cotangent[0, step_index].astype(jnp.float32).reshape(images * row_count, model_width)
        grad, d_gm, d_w1s, d_w2s = mlp_backward(grad, after_self, gm_f, w1s, w2s, final_kept)
        grad_low = grad.astype(jnp.bfloat16)
        d_wos = left_matmul(returned, grad_low)
        grad_self = right_matmul(grad_low, wos)
        grad_self = grad_self.reshape(images, row_count, HEADS, head_size).transpose(0, 2, 1, 3)
        grad_self = grad_self.reshape(pieces, unit_count, row_count, head_size)
        grad_self = lax.all_to_all(
            grad_self.astype(jnp.bfloat16), "pix", split_axis=0, concat_axis=2, tiled=True
        ).astype(grad_self.dtype)[0]
        grad_num = (grad_self / self_den).astype(jnp.bfloat16)
        grad_den = -jnp.sum(grad_self * self_out, 2, keepdims=True) / self_den
        again_scores = (
            jnp.einsum("uqd,ukd->uqk", head_query, head_key, preferred_element_type=jnp.float32)
            * self_scale
        )
        again_weights = jnp.exp(again_scores - self_top)
        grad_weights = (
            jnp.einsum("uqd,ukd->uqk", grad_num, head_value, preferred_element_type=jnp.float32)
            + grad_den
        )
        grad_scores = (again_weights * grad_weights).astype(jnp.bfloat16)
        grad_query = (
            jnp.einsum("uqk,ukd->uqd", grad_scores, head_key, preferred_element_type=jnp.float32)
            * self_scale
        )
        grad_key = (
            jnp.einsum("uqk,uqd->ukd", grad_scores, head_query, preferred_element_type=jnp.float32)
            * self_scale
        )
        grad_value = jnp.einsum(
            "uqk,uqd->ukd",
            again_weights.astype(jnp.bfloat16),
            grad_num,
            preferred_element_type=jnp.float32,
        )
        grad_packed = jnp.concatenate([grad_query, grad_key, grad_value], 2).astype(jnp.bfloat16)
        grad_packed = lax.all_to_all(grad_packed, "pix", split_axis=1, concat_axis=0, tiled=True)
        grad_packed = (
            grad_packed.reshape(images, HEADS, row_count, 3 * head_size)
            .transpose(0, 2, 1, 3)
            .reshape(images * row_count, 3 * model_width)
        )
        d_wqkv = left_matmul(normed_self, grad_packed)
        grad_normed = right_matmul(grad_packed, wqkv)
        grad_inputs, d_gs = norm_back(after_mlp, gs_f, grad_normed)
        grad = grad + grad_inputs
        grad, d_gc, d_w1c, d_w2c = mlp_backward(grad, after_cross, gc_f, w1c, w2c, cross_kept)
        grad_rows = grad_rows + jnp.sum(grad.reshape(images, row_count, model_width), 0)
        grad_low = grad.astype(jnp.bfloat16)
        d_wo = left_matmul(attended_low, grad_low)
        grad_cross = right_matmul(grad_low, wo).reshape(images, row_count, model_width)
        cross_gnum = (grad_cross / den_rows[:, :, None]).astype(jnp.bfloat16)
        cross_gden = (-jnp.sum(grad_cross * attended, 2) / den_rows).astype(jnp.bfloat16)
        all_num, all_den = (
            lax.all_gather(cross_gnum, "pix", axis=1, tiled=True),
            lax.all_gather(cross_gden, "pix", axis=1, tiled=True),
        )
        select_low = select.astype(jnp.bfloat16)
        window_num = jnp.einsum(
            "wb,brd->wrd", select_low, all_num, preferred_element_type=jnp.float32
        ).astype(jnp.bfloat16)
        window_den = jnp.einsum(
            "wb,br->wr", select_low, all_den, preferred_element_type=jnp.float32
        )
        scores = right_matmul(queries, pixel_keys) * cross_scale
        weights = jnp.where(
            in_window[:, None, :], jnp.exp(scores[None] - window_top[:, :, None]), 0.0
        )
        cross_gweights = (
            jnp.einsum("wrd,cd->wrc", window_num, pixel_values, preferred_element_type=jnp.float32)
            + window_den[:, :, None]
        )
        cross_gscores = jnp.sum(weights * cross_gweights, 0).astype(jnp.bfloat16)
        query_terms = matmul(cross_gscores, pixel_keys) * cross_scale
        grad_keys = (left_matmul(cross_gscores, queries) * cross_scale).astype(jnp.bfloat16)
        grad_values = jnp.einsum(
            "wrc,wrd->cd",
            weights.astype(jnp.bfloat16),
            window_num,
            preferred_element_type=jnp.float32,
        ).astype(jnp.bfloat16)
        d_wk = left_matmul(normed_pix, grad_keys)
        d_wv = left_matmul(normed_pix, grad_values)
        grad_normed_pix = right_matmul(grad_keys, wk) + right_matmul(grad_values, wv)
        grad_pixels, d_gpix = norm_back(raw_pixels, gain_pix, grad_normed_pix)
        pixel_grads.append(grad_pixels)
        grad_pix_gain = grad_pix_gain + d_gpix
        terms = (
            d_wk,
            d_wv,
            d_wo,
            d_gc,
            d_w1c,
            d_w2c,
            d_gs,
            d_wqkv,
            d_wos,
            d_gm,
            d_w1s,
            d_w2s,
            query_terms,
        )
        reduced = (
            lax.psum_scatter(
                terms[0].astype(jnp.bfloat16), "pix", scatter_dimension=1, tiled=True
            ).astype(jnp.float32),
            lax.psum_scatter(
                terms[1].astype(jnp.bfloat16), "pix", scatter_dimension=1, tiled=True
            ).astype(jnp.float32),
            lax.psum_scatter(
                terms[2].astype(jnp.bfloat16), "pix", scatter_dimension=0, tiled=True
            ).astype(jnp.float32),
            lax.psum_scatter(
                terms[3].astype(jnp.bfloat16), "pix", scatter_dimension=0, tiled=True
            ).astype(jnp.float32),
            lax.psum_scatter(
                terms[4].astype(jnp.bfloat16), "pix", scatter_dimension=0, tiled=True
            ).astype(jnp.float32),
            lax.psum_scatter(
                terms[5].astype(jnp.bfloat16), "pix", scatter_dimension=0, tiled=True
            ).astype(jnp.float32),
            lax.psum_scatter(
                terms[6].astype(jnp.bfloat16), "pix", scatter_dimension=0, tiled=True
            ).astype(jnp.float32),
            lax.psum_scatter(
                terms[7].astype(jnp.bfloat16), "pix", scatter_dimension=0, tiled=True
            ).astype(jnp.float32),
            lax.psum_scatter(
                terms[8].astype(jnp.bfloat16), "pix", scatter_dimension=0, tiled=True
            ).astype(jnp.float32),
            lax.psum_scatter(
                terms[9].astype(jnp.bfloat16), "pix", scatter_dimension=0, tiled=True
            ).astype(jnp.float32),
            lax.psum_scatter(
                terms[10].astype(jnp.bfloat16), "pix", scatter_dimension=0, tiled=True
            ).astype(jnp.float32),
            lax.psum_scatter(
                terms[11].astype(jnp.bfloat16), "pix", scatter_dimension=0, tiled=True
            ).astype(jnp.float32),
            lax.psum_scatter(
                terms[12].astype(jnp.bfloat16), "pix", scatter_dimension=0, tiled=True
            ).astype(jnp.float32),
        )
        totals = reduced if totals is None else jax.tree.map(jnp.add, totals, reduced)
    s_wk, s_wv, s_wo, s_gc, s_w1c, s_w2c, s_gs, s_wqkv, s_wos, s_gm, s_w1s, s_w2s, s_query = totals
    summed = (
        lax.psum(s_wk.astype(jnp.bfloat16), "dp").astype(jnp.float32),
        lax.psum(s_wv.astype(jnp.bfloat16), "dp").astype(jnp.float32),
        lax.psum(s_wo.astype(jnp.bfloat16), "dp").astype(jnp.float32),
        lax.psum(s_gc.astype(jnp.bfloat16), "dp").astype(jnp.float32),
        lax.psum(s_w1c.astype(jnp.bfloat16), "dp").astype(jnp.float32),
        lax.psum(s_w2c.astype(jnp.bfloat16), "dp").astype(jnp.float32),
        lax.psum(s_gs.astype(jnp.bfloat16), "dp").astype(jnp.float32),
        lax.psum(s_wqkv.astype(jnp.bfloat16), "dp").astype(jnp.float32),
        lax.psum(s_wos.astype(jnp.bfloat16), "dp").astype(jnp.float32),
        lax.psum(s_gm.astype(jnp.bfloat16), "dp").astype(jnp.float32),
        lax.psum(s_w1s.astype(jnp.bfloat16), "dp").astype(jnp.float32),
        lax.psum(s_w2s.astype(jnp.bfloat16), "dp").astype(jnp.float32),
        lax.psum(s_query.astype(jnp.bfloat16), "dp").astype(jnp.float32),
        lax.psum(grad_rows.astype(jnp.bfloat16), "dp").astype(jnp.float32),
    )
    (
        f_wk,
        f_wv,
        f_wo,
        f_gc,
        f_w1c,
        f_w2c,
        f_gs,
        f_wqkv,
        f_wos,
        f_gm,
        f_w1s,
        f_w2s,
        query_rows,
        rows_total,
    ) = summed
    query_low = query_rows.astype(jnp.bfloat16)
    normed_rows = lax.dynamic_slice_in_dim(normed_lat, position * row_count, row_count, 0)
    d_wq_part = left_matmul(normed_rows, query_low)
    grad_normed_rows = right_matmul(query_low, wq)
    grad_lat_norm, d_glat_part = norm_back(lat_rows, g_lat_f, grad_normed_rows)
    d_wq, d_glat = (
        lax.psum_scatter(
            d_wq_part.astype(jnp.bfloat16), "pix", scatter_dimension=0, tiled=True
        ).astype(jnp.float32),
        lax.psum_scatter(
            d_glat_part.astype(jnp.bfloat16), "pix", scatter_dimension=0, tiled=True
        ).astype(jnp.float32),
    )
    d_gpix = lax.psum(grad_pix_gain, ("dp", "pix"))
    latent_out = jnp.stack(outputs)[None]
    pixel_out = jnp.stack(pixel_grads)[None]
    return (
        latent_out,
        pixel_out,
        rows_total + grad_lat_norm,
        d_gpix,
        d_glat,
        d_wq,
        f_wk,
        f_wv,
        f_wo,
        f_gc,
        f_w1c,
        f_w2c,
        f_gs,
        f_wqkv,
        f_wos,
        f_gm,
        f_w1s,
        f_w2s,
    )


MESH = pl.DeviceIdType.MESH
HBM = pl.BlockSpec(memory_space=pl.ANY)
VMEM = pl.BlockSpec(memory_space=pltpu.VMEM)
MIB = 1024 * 1024
PIECE = 256
BLOCK = 1024
STRIP = 256
CHUNK = 64
FROWS = 272
DEN_ROW = 261
TOP_ROW = 263
GAIN_LANE = 264
GAIN_ROW = 262


def place():
    dp, pix = lax.axis_index("dp"), lax.axis_index("pix")
    return dp // 2, dp % 2, pix // 2, pix % 2


def device(x, c, z, y):
    return {"dp": x * 2 + c, "pix": z * 2 + y}


def greet(partners):
    barrier = pltpu.get_barrier_semaphore()
    for partner in partners:
        pl.semaphore_signal(barrier, inc=1, device_id=partner, device_id_type=MESH)
    pl.semaphore_wait(barrier, len(partners))


def remote(source, target, sems, index, partner):
    return pltpu.make_async_remote_copy(
        src_ref=source,
        dst_ref=target,
        send_sem=sems[0].at[index],
        recv_sem=sems[1].at[index],
        device_id=partner,
        device_id_type=MESH,
    )


def remote_params(collective_id, vmem=48 * MIB):
    return pltpu.CompilerParams(
        collective_id=collective_id, has_side_effects=True, vmem_limit_bytes=vmem
    )


def normed_block(raw, gain, features):
    values = raw.astype(jnp.float32)
    rows = lax.broadcasted_iota(jnp.int32, values.shape, 0)
    average = jnp.sum(values, 0, keepdims=True) * (1.0 / features)
    centered = jnp.where(rows < features, values - average, 0.0)
    scale = lax.rsqrt(jnp.sum(centered * centered, 0, keepdims=True) * (1.0 / features) + 1e-05)
    unit = centered * scale
    wide = jnp.where(rows == DEN_ROW, 1.0, unit * gain)
    return wide.astype(jnp.bfloat16), unit, scale


def three_parts(row):
    first = row.astype(jnp.bfloat16).astype(jnp.float32)
    rest = row - first
    second = rest.astype(jnp.bfloat16).astype(jnp.float32)
    return first, second, rest - second


def with_rows(tail, den, top):
    rows = lax.broadcasted_iota(jnp.int32, tail.shape, 0) + (FROWS - 16)
    high = den.astype(jnp.bfloat16).astype(jnp.float32)
    first, second, third = three_parts(top)
    tail = jnp.where(rows == DEN_ROW, high, tail)
    tail = jnp.where(rows == DEN_ROW + 1, den - high, tail)
    tail = jnp.where(rows == TOP_ROW, first, tail)
    tail = jnp.where(rows == TOP_ROW + 1, second, tail)
    return jnp.where(rows == TOP_ROW + 2, third, tail)


def read_rows(tail):
    at = DEN_ROW - (FROWS - 16)
    den = tail[at : at + 1] + tail[at + 1 : at + 2]
    at = TOP_ROW - (FROWS - 16)
    top = tail[at : at + 1] + tail[at + 1 : at + 2] + tail[at + 2 : at + 3]
    return den, top


def merge(pieces):
    bodies = [piece[: FROWS - 16].astype(jnp.float32) for piece in pieces]
    tails = [piece[FROWS - 16 :].astype(jnp.float32) for piece in pieces]
    read = [read_rows(tail) for tail in tails]
    top = functools.reduce(jnp.maximum, [row for unused, row in read])
    factors = [jnp.exp(row - top) for unused, row in read]
    body = sum(values * factor for values, factor in zip(bodies, factors, strict=True))
    tail = sum(values * factor for values, factor in zip(tails, factors, strict=True))
    den = sum(row * factor for (row, unused), factor in zip(read, factors, strict=True))
    return body, tail, den, top


def gelu_and_slope(hidden):
    const = (2 / jnp.pi) ** 0.5
    square = hidden * hidden
    bent = jnp.tanh(const * hidden * (1 + 0.044715 * square))
    half = 0.5 * (1 + bent)
    slope = half + 0.5 * hidden * (1 - bent * bent) * const * (1 + 3 * 0.044715 * square)
    return hidden * half, slope


class Gather:
    def __init__(self, shards, wholes, splits, send, recv, local):
        self.shards, self.wholes, self.splits = shards, wholes, splits
        self.sems, self.local = (send, recv), local
        self.place = place()
        x, c, z, y = self.place
        self.core, self.across = device(x, 1 - c, z, y), device(1 - x, c, z, y)
        self.beside = device(x, c, z, 1 - y)
        self.along, self.side, self.over, self.between, self.keep = {}, {}, {}, {}, {}

    def part(self, k, ref):
        x, c, z, y = self.place
        return ref.at[x, c] if self.splits[k] else ref.at[:, c]

    def start(self, k):
        x, c, z, y = self.place
        mine, home = self.part(k, self.shards[k]), self.part(k, self.wholes[k].at[z, y])
        for i in (1, 2, 3):
            target = device(x, c, (z + i) % 4, y)
            self.along[k, i] = remote(mine, home, self.sems, (k, i - 1), target)
            self.along[k, i].start()
        self.side[k, 0] = remote(mine, home, self.sems, (k, 3), self.beside)
        self.side[k, 0].start()
        self.keep[k] = pltpu.make_async_copy(
            self.shards[k], self.wholes[k].at[z, y], self.local.at[k]
        )
        self.keep[k].start()

    def to_side(self, k):
        x, c, z, y = self.place
        for i in (1, 2, 3):
            self.along[k, i].wait_recv()
            block = self.part(k, self.wholes[k].at[(z + 4 - i) % 4, y])
            self.side[k, i] = remote(block, block, self.sems, (k, 3 + i), self.beside)
            self.side[k, i].start()

    def to_over(self, k):
        x, c, z, y = self.place
        for i in range(4):
            self.side[k, i].wait_recv()
            if self.splits[k]:
                if i == 0:
                    block = self.wholes[k].at[z, 1 - y, x, c]
                else:
                    block = self.wholes[k].at[(z + 4 - i) % 4, :, x, c]
                self.over[k, i] = remote(block, block, self.sems, (k, 7 + i), self.across)
                self.over[k, i].start()

    def to_core(self, k):
        x, c, z, y = self.place
        for i in range(4):
            if self.splits[k]:
                self.over[k, i].wait_recv()
            if i == 0:
                block = self.wholes[k].at[z, 1 - y, :, c]
            else:
                block = self.wholes[k].at[(z + 4 - i) % 4, :, :, c]
            self.between[k, i] = remote(block, block, self.sems, (k, 11 + i), self.core)
            self.between[k, i].start()

    def arrive(self, k):
        self.keep[k].wait()
        for i in range(4):
            self.between[k, i].wait_recv()

    def finish(self):
        for group in (self.along, self.side, self.over, self.between):
            for copy in group.values():
                copy.wait_send()


def opening_kernel(splits, scale, features, *refs):
    count = len(splits)
    same, last = refs[:2]
    shards, pixels, cot, pix_gain = refs[2 : count + 2], *refs[count + 2 : count + 5]
    refs = refs[count + 5 :]
    wholes, weights_out, cot_rows = refs[:count], refs[count], refs[count + 1]
    normed_c, active_c, slope_c, normed_s, packed, self_att = refs[count + 2 : count + 8]
    normed_m, active_s, slope_s, att_low, final = refs[count + 8 : count + 13]
    refs = refs[count + 13 :]
    normed_out, queries_out, query_out, tops, means, rows_out, row_scales, gains = refs[:8]
    refs = refs[8:]
    wide, weights, scores_ref, lat, wq, key, total, largest, pieces, sums = refs[:10]
    side_in, own, along_in = refs[10:13]
    value, stream, tile, first, second, third, fourth, left_w, right_w, heads = refs[13:23]
    send, recv, local, own_send, own_recv, load, cot_send, cot_recv, fetch_sem, store_sem = refs[23:]
    x, c, z, y = place()
    micros, unused, slots = pixels.shape
    blocks = slots // BLOCK
    per_block = BLOCK // PIECE
    images = sums.shape[1]
    gather = Gather(shards, wholes, splits, send, recv, local)
    pix, dp = lax.axis_index("pix"), lax.axis_index("dp")
    others = [{"dp": dp, "pix": (pix + i) % 8} for i in range(1, 8)]
    greet([*others, gather.across, gather.core])

    fetch = pltpu.make_async_copy(pixels, wide, load.at[0])
    fetch.start()
    for k in range(3):
        gather.start(k)
    gain = pix_gain[...]

    def norm(start, stop):
        def one(i, carry):
            half = BLOCK // 2
            columns = pl.ds(pl.multiple_of((i % (2 * blocks)) * half, half), half)
            micro = i // (2 * blocks)
            wide[micro, :, columns] = normed_block(wide[micro, :, columns], gain, features)[0]
            return carry

        lax.fori_loop(2 * start, 2 * stop, one, 0)

    fetch.wait()
    norm(0, 2)
    for k in range(3):
        gather.to_side(k)
    for k in range(3, 6):
        gather.start(k)
    norm(2, 4)
    for k in range(3):
        gather.to_over(k)
    for k in range(6, count):
        gather.start(k)
    norm(4, 6)
    for k in range(3):
        gather.to_core(k)
    gather.to_side(3)
    gather.to_side(4)
    norm(6, 2 * blocks)
    gather.to_over(3)
    fetches = []
    for k, target in enumerate((lat, wq, key)):
        gather.arrive(k)
        fetches.append(pltpu.make_async_copy(wholes[k], target, load.at[1 + k]))
        fetches[k].start()
    gather.to_side(5)
    gather.to_over(4)
    for copy in fetches:
        copy.wait()

    lat_values = lat[...].reshape(sums.shape[3], -1).astype(jnp.float32)
    key_values = key[...].reshape(lat_values.shape[1], -1)
    columns = key_values[:, 256:384].astype(jnp.float32).T
    gains[...] = columns[GAIN_LANE - 256 : GAIN_LANE - 248]
    normed = layer_norm(lat_values, gains[0:1])
    normed_out[...] = normed.astype(jnp.bfloat16)
    wq_values = wq[...].reshape(lat_values.shape[1], -1)
    queries_out[...] = matmul(normed_out[...], wq_values).astype(jnp.bfloat16)
    query_t = (
        lax.dot_general(
            key_values, queries_out[...], (((0,), (1,)), ((), ())),
            preferred_element_type=jnp.float32,
        )
        * scale
    )
    query_t = query_t[:FROWS]
    rows = lax.broadcasted_iota(jnp.int32, query_t.shape, 0)
    query_out[...] = jnp.where(rows < features, query_t, 0.0).astype(jnp.bfloat16)

    gather.to_side(6)
    gather.to_over(5)
    gather.to_core(3)
    gather.to_core(4)

    def forward(m):
        total[...] = jnp.zeros_like(total)
        largest[...] = jnp.full(largest.shape, -big_value, jnp.float32)

        def one(b, carry):
            rows = pl.ds(pl.multiple_of(b * BLOCK, BLOCK), BLOCK)
            scores_ref[...] = left_matmul(wide[m, :, rows], query_out[...])
            for k in range(per_block):
                rows = pl.ds(pl.multiple_of(b * BLOCK + k * PIECE, PIECE), PIECE)
                scores = scores_ref[k * PIECE : (k + 1) * PIECE]
                top = jnp.max(scores, 0, keepdims=True)
                low = jnp.exp(scores - top).astype(jnp.bfloat16)
                weights[m, rows, :] = low
                piece = b * per_block + k
                tops[m, piece] = top
                added = matmul(wide[m, :, rows], low)
                before = jnp.where(
                    same[m, piece] > 0, largest[...], -big_value
                )
                now = jnp.maximum(before, top)
                largest[...] = now
                older, newer = jnp.exp(before - now), jnp.exp(top - now)
                summed = total[...] * older + added * newer
                total[...] = summed
                pieces[piece, : FROWS - 16] = summed[: FROWS - 16].astype(jnp.bfloat16)
                at = DEN_ROW - (FROWS - 16)
                tail = summed[FROWS - 16 :]
                pieces[piece, FROWS - 16 :] = with_rows(tail, tail[at : at + 1], now).astype(
                    jnp.bfloat16
                )
            return carry

        lax.fori_loop(0, blocks, one, 0)
        for image in range(images):
            index = last[m, image]
            present = index >= 0
            piece = pieces[jnp.maximum(index, 0)].astype(jnp.float32)
            sums[m, image, : FROWS - 16] = jnp.where(present, piece[: FROWS - 16], 0.0).astype(
                jnp.bfloat16
            )
            nothing = jnp.zeros((1, piece.shape[1]), jnp.float32)
            absent = with_rows(
                jnp.zeros((16, piece.shape[1]), jnp.float32), nothing, nothing - big_value
            )
            sums[m, image, FROWS - 16 :] = jnp.where(
                present, piece[FROWS - 16 :], absent
            ).astype(jnp.bfloat16)

    own_sems = (own_send, own_recv)
    sides, alongs, keeps = {}, {}, []

    def send_sums(m):
        for i in (1, 2, 3, 0):
            source = sums.at[m, ((z + i) % 4) * 2 + 1 - y]
            sides[m, i] = remote(source, side_in.at[m, i], own_sems, (m, i), gather.beside)
            sides[m, i].start()
        keeps.append(pltpu.make_async_copy(weights.at[m], weights_out.at[m], load.at[4 + m]))
        keeps[-1].start()

    def pass_sums(m):
        for i in (1, 2, 3, 0):
            sides[m, i].wait_recv()
            body, tail, den, top = merge([sums[m, ((z + i) % 4) * 2 + y], side_in[m, i]])
            own[m, i, : FROWS - 16] = body.astype(jnp.bfloat16)
            own[m, i, FROWS - 16 :] = with_rows(tail, den, top).astype(jnp.bfloat16)
            if i:
                target = device(x, c, (z + i) % 4, y)
                alongs[m, i] = remote(
                    own.at[m, i], along_in.at[m, i - 1], own_sems, (m, 3 + i), target
                )
                alongs[m, i].start()

    def finish_sums(m):
        for i in (1, 2, 3):
            alongs[m, i].wait_recv()
        body, tail, den, top = merge([own[m, 0]] + [along_in[m, i] for i in range(3)])
        rows = lax.broadcasted_iota(jnp.int32, tail.shape, 0) + (FROWS - 16)
        means[m, : FROWS - 16] = (body / den).astype(jnp.bfloat16)
        means[m, FROWS - 16 :] = jnp.where(rows < DEN_ROW, tail / den, 0.0).astype(jnp.bfloat16)
        rows_out[m, 0:1] = den
        rows_out[m, 1:2] = top

    forward(0)
    send_sums(0)
    gather.to_side(7)
    gather.to_over(6)
    gather.to_core(5)
    forward(1)
    send_sums(1)
    pass_sums(0)
    gather.to_side(8)
    gather.to_over(7)
    gather.to_core(6)
    pass_sums(1)
    gather.to_side(9)
    gather.to_over(8)
    gather.to_side(10)
    gather.to_core(7)

    loads, stores = {}, {}

    def fetch(number, source, target):
        loads[number] = pltpu.make_async_copy(source, target, fetch_sem.at[number])
        loads[number].start()

    def store(number, source, target):
        stores[number] = pltpu.make_async_copy(source, target, store_sem.at[number])
        stores[number].start()

    def stored(*numbers):
        for number in numbers:
            stores.pop(number).wait()

    def ready(*numbers):
        for number in numbers:
            loads.pop(number).wait()

    gather.arrive(3)
    fetch(0, wholes[3], value)
    gather.arrive(4)
    fetch(1, wholes[4], left_w)
    gather.arrive(5)
    fetch(2, wholes[5], right_w)
    finish_sums(0)
    gather.to_over(9)
    finish_sums(1)
    latents, model = lat_values.shape
    strip_count = stream.shape[0] // STRIP

    def strips(one):
        def step(i, carry):
            one(i, pl.ds(pl.multiple_of(i * STRIP, STRIP), STRIP))
            return carry

        lax.fori_loop(0, strip_count, step, 0)

    def chunks(one):
        def step(j, carry):
            one(pl.ds(pl.multiple_of(j * CHUNK, CHUNK), CHUNK))
            return carry

        lax.fori_loop(0, STRIP // CHUNK, step, 0)

    def square(ref):
        return ref[...].reshape(model, model)

    def add_and_norm(left, weight, number, target, base=None, last_out=None):
        def one(i, strip):
            if base is None:
                stream[strip, :] += matmul(left[strip, :], square(weight))
            else:
                stream[strip, :] = base(i) + matmul(left[strip, :], square(weight))

            def chunk(part):
                at = pl.ds(pl.multiple_of(i * STRIP, STRIP) + part.start, CHUNK)
                values = stream[at, :]
                centered = values - jnp.mean(values, 1, keepdims=True)
                row_scale = lax.rsqrt(jnp.mean(centered * centered, 1, keepdims=True) + 1e-05)
                row_scales[at, 3 - number : 4 - number] = row_scale
                target[at, :] = (centered * row_scale * gains[number : number + 1]).astype(
                    jnp.bfloat16
                )

            chunks(chunk)

        strips(one)

    def through_gelu(left, weight, active, slope):
        def one(i, strip):
            tile[...] = matmul(left[strip, :], square(weight))

            def chunk(part):
                at = pl.ds(pl.multiple_of(i * STRIP, STRIP) + part.start, CHUNK)
                acted, sloped = gelu_and_slope(tile[part, :])
                active[at, :] = acted.astype(jnp.bfloat16)
                slope[at, :] = sloped.astype(jnp.bfloat16)

            chunks(chunk)

        strips(one)

    ready(0)
    for m in range(micros):
        first[m * latents : (m + 1) * latents, :] = lax.dot_general(
            means[m],
            value[...].reshape(model, -1)[:, :FROWS],
            (((0,), (1,)), ((), ())),
            preferred_element_type=jnp.float32,
        ).astype(jnp.bfloat16)
    store(0, first, att_low)
    gather.to_over(10)
    gather.to_core(8)
    ready(1)

    def lat_strip(i):
        return lat[pl.ds((i % 2) * 2, 2)].reshape(STRIP, model).astype(jnp.float32)

    add_and_norm(first, left_w, 1, second, lat_strip)
    store(1, second, normed_c)
    gather.arrive(6)
    fetch(3, wholes[6], left_w)
    ready(2)
    through_gelu(second, right_w, third, fourth)
    store(2, third, active_c)
    store(3, fourth, slope_c)
    gather.to_core(9)
    gather.arrive(7)
    cots = [pltpu.make_async_copy(cot.at[:, pix], cot_rows.at[:, pix], local.at[count])]
    for i, other in enumerate(others):
        source, target = cot.at[:, (pix + i + 1) % 8], cot_rows.at[:, pix]
        cots.append(remote(source, target, (cot_send, cot_recv), i, other))
    for copy in cots:
        copy.start()

    half = heads.shape[2]
    fetch(4, wholes[7].at[:, :, :, :, :, :half], right_w.at[:, :, :, :, :, :half])
    ready(3)
    stored(0)
    add_and_norm(third, left_w, 2, first)
    store(4, first, normed_s)
    fetch(5, wholes[7].at[:, :, :, :, :, half : 2 * half], left_w.at[:, :, :, :, :, :half])
    gather.to_core(10)
    stored(1)
    width = half // 6
    for pair in range(4):
        block = heads.at[pair % 2]
        weight = (right_w, left_w)[pair % 2]
        ready(4 + pair)
        if pair >= 2:
            stored(3 + pair)

        def project(i, strip, block=block, weight=weight):
            product = matmul(first[strip, :], weight[:, :, :, :, :, :half].reshape(model, half))
            block[strip, :] = product.astype(jnp.bfloat16)

        strips(project)
        store(5 + pair, block, packed.at[:, pair * half : (pair + 1) * half])
        if pair < 2:
            columns = pl.ds((pair + 2) * half, half)
            fetch(
                6 + pair,
                wholes[7].at[:, :, :, :, :, columns],
                weight.at[:, :, :, :, :, :half],
            )

        def unit(i, carry, pair=pair, block=block):
            image, head = i // 2, i % 2
            rows = pl.ds(pl.multiple_of(image * latents, latents), latents)

            def columns(part):
                start = pl.multiple_of(head * (3 * width) + part * width, width)
                return pl.ds(start, width)

            query, key_, value_ = (block[rows, columns(part)] for part in range(3))
            scores = right_matmul(query, key_) * width ** (-0.5)
            exps = jnp.exp(scores - jnp.max(scores, 1, keepdims=True))
            den = jnp.sum(exps, 1, keepdims=True)
            out = pl.ds(pl.multiple_of((pair * 2 + head) * width, width), width)
            second[rows, out] = (matmul(exps.astype(jnp.bfloat16), value_) / den).astype(
                jnp.bfloat16
            )
            return carry

        lax.fori_loop(0, 4, unit, 0)
    store(9, second, self_att)
    gather.arrive(8)
    fetch(8, wholes[8], right_w)
    gather.arrive(9)
    fetch(9, wholes[9], left_w)
    ready(8)
    stored(2)
    add_and_norm(second, right_w, 3, third)
    store(10, third, normed_m)
    gather.arrive(10)
    fetch(10, wholes[10], right_w)
    ready(9)
    stored(3, 4)
    through_gelu(third, left_w, fourth, first)
    store(11, fourth, active_s)
    store(12, first, slope_s)
    ready(10)
    stored(9)

    def finish_rows(i, strip):
        second[strip, :] = (
            stream[strip, :] + matmul(fourth[strip, :], square(right_w))
        ).astype(jnp.bfloat16)

    strips(finish_rows)
    store(13, second, final)
    stored(*list(stores))
    for copy in (*keeps, *cots):
        copy.wait()
    gather.finish()
    for copy in (*sides.values(), *alongs.values()):
        copy.wait_send()


def opening(same, last, shards, splits, pixels, cot, gain, features, scale):
    count = len(shards)
    bf16, f32 = jnp.bfloat16, jnp.float32
    micros, unused, slots = pixels.shape
    latents, width = 8 * shards[0].shape[0], shards[0].shape[1]
    views = [shard.reshape(2, 2, shard.shape[0] // 4, shard.shape[1]) for shard in shards]
    outs = [jax.ShapeDtypeStruct((4, 2, *view.shape), view.dtype) for view in views]
    images = cot.shape[1]
    piece = (FROWS, latents)
    total_rows = micros * latents
    square, wide = (total_rows, width), (total_rows, 3 * width)
    kept = [jax.ShapeDtypeStruct(wide if i == 4 else square, bf16) for i in range(11)]
    smem = pl.BlockSpec(memory_space=pltpu.SMEM)
    results = pl.pallas_call(
        functools.partial(opening_kernel, splits, scale, features),
        out_shape=[
            *outs,
            jax.ShapeDtypeStruct((micros, slots, latents), bf16),
            jax.ShapeDtypeStruct(cot.shape, bf16),
            *kept,
            jax.ShapeDtypeStruct((latents, width), bf16),
            jax.ShapeDtypeStruct((latents, width), bf16),
            jax.ShapeDtypeStruct(piece, bf16),
            jax.ShapeDtypeStruct((micros, slots // PIECE, 1, latents), f32),
            jax.ShapeDtypeStruct((micros, *piece), bf16),
            jax.ShapeDtypeStruct((micros, 2, latents), f32),
            jax.ShapeDtypeStruct((total_rows, 128), f32),
            jax.ShapeDtypeStruct((8, width), f32),
        ],
        in_specs=[smem, smem] + [HBM] * (count + 2) + [VMEM],
        out_specs=[HBM] * (count + 13) + [VMEM] * 8,
        scratch_shapes=[
            pltpu.VMEM(pixels.shape, bf16),
            pltpu.VMEM((micros, slots, latents), bf16),
            pltpu.VMEM((BLOCK, latents), f32),
            pltpu.VMEM(outs[0].shape, bf16),
            pltpu.VMEM(outs[1].shape, bf16),
            pltpu.VMEM(outs[2].shape, bf16),
            pltpu.VMEM(piece, f32),
            pltpu.VMEM((1, latents), f32),
            pltpu.VMEM((slots // PIECE, *piece), bf16),
            pltpu.VMEM((micros, images, *piece), bf16),
            pltpu.VMEM((micros, 4, *piece), bf16),
            pltpu.VMEM((micros, 4, *piece), bf16),
            pltpu.VMEM((micros, 3, *piece), bf16),
            pltpu.VMEM(outs[3].shape, bf16),
            pltpu.VMEM(square, f32),
            pltpu.VMEM((STRIP, width), f32),
            *[pltpu.VMEM(square, bf16) for _ in range(4)],
            *[pltpu.VMEM(outs[4].shape, bf16) for _ in range(2)],
            pltpu.VMEM((2, total_rows, 3 * width // 4), bf16),
            pltpu.SemaphoreType.DMA((count, 15)),
            pltpu.SemaphoreType.DMA((count, 15)),
            pltpu.SemaphoreType.DMA((count + 1,)),
            pltpu.SemaphoreType.DMA((micros, 7)),
            pltpu.SemaphoreType.DMA((micros, 7)),
            pltpu.SemaphoreType.DMA((4 + micros,)),
            pltpu.SemaphoreType.DMA((7,)),
            pltpu.SemaphoreType.DMA((7,)),
            pltpu.SemaphoreType.DMA((11,)),
            pltpu.SemaphoreType.DMA((14,)),
        ],
        compiler_params=remote_params(0, 64 * MIB - 1024),
        name="opening",
    )(same, last, *views, pixels, cot, gain)
    wholes = [
        whole.reshape(8 * shard.shape[0], shard.shape[1])
        for whole, shard in zip(results[:count], shards, strict=True)
    ]
    return wholes, results[count:]


class Reduce:
    def __init__(self, staging, own, core_in, over_in, side_in, along_in, finals, temps, sems, local):
        self.staging, self.own = staging, own
        self.core_in, self.over_in, self.side_in = core_in, over_in, side_in
        self.along_in, self.finals, self.temps = along_in, finals, temps
        self.sems, self.local = sems, local
        self.place = place()
        x, c, z, y = self.place
        self.core, self.across = device(x, 1 - c, z, y), device(1 - x, c, z, y)
        self.beside = device(x, c, z, 1 - y)
        self.copies, self.loads, self.keeps, self.slots = {}, {}, {}, {}

    def send(self, k, number, source, target, partner):
        self.copies[k, number] = remote(source, target, self.sems, (k, number), partner)
        self.copies[k, number].start()

    def release(self, slot):
        for k, used in self.slots.items():
            if used == slot:
                self.copies[k, 0].wait_send()
                self.keeps[k].wait()
        self.slots = {k: used for k, used in self.slots.items() if used != slot}

    def push(self, k, slot):
        x, c, z, y = self.place
        staged = self.staging[slot]
        rows, columns = self.own[k].shape[-2:]
        away = staged.at[:, :, :, 1 - c, :rows, :columns]
        self.send(k, 0, away, self.core_in[k], self.core)
        self.keeps[k] = pltpu.make_async_copy(
            staged.at[:, :, :, c, :rows, :columns], self.own[k], self.local.at[k, 0]
        )
        self.keeps[k].start()
        self.slots[k] = slot

    def c1(self, k):
        self.copies[k, 0].wait_recv()
        rows, columns = self.own[k].shape[-2:]
        temp = self.temps[k][0].at[:, :, :, :rows, :columns]
        self.loads[k] = pltpu.make_async_copy(self.core_in[k], temp, self.local.at[k, 1])
        self.loads[k].start()

    def add(self, count, one):
        def step(i, carry):
            one(i)
            return carry

        lax.fori_loop(0, count, step, 0)

    def c2(self, k):
        x, c, z, y = self.place
        own, temp = self.own[k], self.temps[k][0]
        rows, columns = own.shape[-2:]
        if k in self.slots:
            self.keeps[k].wait()
            self.copies[k, 0].wait_send()
            del self.slots[k]
        self.loads[k].wait()

        def one(i):
            own[i // 2, i % 2] = own[i // 2, i % 2] + temp[i // 2, i % 2, :, :rows, :columns]

        self.add(8, one)
        self.send(k, 1, own.at[:, :, 1 - x], self.over_in[k], self.across)

    def x1(self, k):
        self.copies[k, 1].wait_recv()
        rows, columns = self.own[k].shape[-2:]
        temp = self.temps[k][1].at[:, :, :rows, :columns]
        self.loads[k] = pltpu.make_async_copy(self.over_in[k], temp, self.local.at[k, 2])
        self.loads[k].start()

    def x2(self, k):
        x, c, z, y = self.place
        own, temp = self.own[k], self.temps[k][1]
        rows, columns = own.shape[-2:]
        self.loads[k].wait()

        def one(i):
            own[i // 2, i % 2, x] = own[i // 2, i % 2, x] + temp[i // 2, i % 2, :rows, :columns]

        self.add(8, one)
        self.send(k, 2, own.at[:, 1 - y, x], self.side_in[k], self.beside)

    def y(self, k):
        x, c, z, y = self.place
        own, side_in = self.own[k], self.side_in[k]
        self.copies[k, 2].wait_recv()

        def one(i):
            own[i, y, x] = own[i, y, x] + side_in[i]

        self.add(4, one)
        for i in (1, 2, 3):
            target = device(x, c, (z + i) % 4, y)
            self.send(
                k, 2 + i, own.at[(z + i) % 4, y, x], self.along_in[k].at[i - 1], target
            )

    def z(self, k):
        x, c, z, y = self.place
        for i in (1, 2, 3):
            self.copies[k, 2 + i].wait_recv()
        total = self.own[k][z, y, x].astype(jnp.float32)
        for i in range(3):
            total = total + self.along_in[k][i].astype(jnp.float32)
        final = self.finals[k]
        final[x, c] = total.astype(jnp.bfloat16)
        self.send(k, 6, final.at[x, c], final.at[x, c], self.across)

    def b(self, k):
        x, c, z, y = self.place
        final = self.finals[k]
        self.copies[k, 6].wait_recv()
        self.send(k, 7, final.at[:, c], final.at[:, c], self.core)

    def run(self, *stages):
        for name, number in stages:
            getattr(self, name)(number)

    def finish(self):
        for (k, number), copy in self.copies.items():
            if number == 7:
                copy.wait_recv()
            if number or k in self.slots:
                copy.wait_send()
        for k in self.slots:
            self.keeps[k].wait()


def closing_kernel(scale, images, features, *refs):
    segs, pixels, pix_weights, cot, final = refs[:5]
    normed_m, active_s, slope_s, self_att, packed, normed_self, normed_c, active_c, slope_c = refs[5:14]
    att_low, w2s, w1s, wos, wqkv, w2c, w1c, wo = refs[14:22]
    row_scales, gains, means, rows_in, value_n, queries, tops, pix_gain = refs[22:30]
    refs = refs[30:]
    count = 12
    finals, core_in, over_in = refs[:count], refs[count : 2 * count], refs[2 * count : 3 * count]
    out_rows, pixel_out, query_out = refs[3 * count : 3 * count + 3]
    refs = refs[3 * count + 3 :]
    own, side_in, along_in = refs[:count], refs[count : 2 * count], refs[2 * count : 3 * count]
    refs = refs[3 * count :]
    staging, temps = refs[:3], refs[3:7]
    grad, acc, low, back_low, first, second, third, fourth, slope, head_grad = refs[7:17]
    gain_grads, packed_grads = refs[17], refs[18]
    all_grads = refs[19:21]
    raw, out_tile, query_sums, gain_sums = refs[21:25]
    sum_parts, sum_core, sum_over, sum_side, sum_along = refs[25:30]
    send, recv, local, load, row_send, row_recv, grad_send, grad_recv = refs[30:38]
    block_load, block_out, sum_send, sum_recv = refs[38:]
    tile = acc

    x, c, z, y = place()
    pix, dp = lax.axis_index("pix"), lax.axis_index("dp")
    others = [{"dp": dp, "pix": (pix + i) % 8} for i in range(1, 8)]
    temp_of = [temps[0:2]] * 10 + [temps[2:4], temps[0:2]]
    reduce = Reduce(
        staging, own, core_in, over_in, side_in, along_in, finals, temp_of, (send, recv), local
    )
    greet([*others, reduce.core, reduce.across])

    loads = {}

    def fetch(number, source, target):
        loads[number] = pltpu.make_async_copy(source, target, load.at[number])
        loads[number].start()

    def ready(*numbers):
        for number in numbers:
            loads.pop(number).wait()

    fetch(0, cot, low)
    fetch(1, active_s, first)
    fetch(2, w2s, third)
    fetch(3, slope_s, slope)
    fetch(4, normed_m, second)
    fetch(5, w1s, fourth)
    homes = [pltpu.make_async_copy(final.at[:, pix], out_rows.at[:, pix], load.at[31])]
    for i, other in enumerate(others):
        source, target = final.at[:, (pix + i + 1) % 8], out_rows.at[:, pix]
        homes.append(remote(source, target, (row_send, row_recv), i, other))
    for copy in homes:
        copy.start()
    gain_grads[...] = jnp.zeros_like(gain_grads)

    def strips(one, image=None):
        def step(i, carry):
            one(i, pl.ds(pl.multiple_of(i * STRIP, STRIP), STRIP))
            return carry

        count = grad.shape[0] // STRIP
        if image is None:
            lax.fori_loop(0, count, step, 0)
        else:
            per_image = count // means.shape[0]
            lax.fori_loop(image * per_image, (image + 1) * per_image, step, 0)

    def chunks(one):
        def step(j, carry):
            one(pl.ds(pl.multiple_of(j * CHUNK, CHUNK), CHUNK))
            return carry

        lax.fori_loop(0, STRIP // CHUNK, step, 0)

    def weight_grad(k, slot, left, right, columns):
        reduce.release(slot)
        staged = staging[slot]

        def one(i, strip):
            product = left_matmul(left[:, strip], right[:, :columns])
            staged[i, :, :, :, :, :columns] = (
                product.reshape(2, 2, 2, STRIP // 8, columns).astype(jnp.bfloat16)
            )

        strips(one)
        reduce.push(k, slot)

    def through_slope(weight, image=None):
        def one(i, strip):
            tile[:STRIP] = right_matmul(low[strip, :], weight[...])

            def chunk(part):
                at = pl.ds(pl.multiple_of(i * STRIP, STRIP) + part.start, CHUNK)
                back_low[at, :] = (tile[part, :] * slope[at, :].astype(jnp.float32)).astype(
                    jnp.bfloat16
                )

            chunks(chunk)

        strips(one, image)

    def through_norm(number, normed, product, fresh=False, image=None):
        gain = gains[3 - number : 4 - number]
        inverse = 1.0 / gain
        width = gain.shape[1]

        def one(i, strip):
            source = tile
            if product is None:
                source = acc
            else:
                tile[:STRIP] = product(strip)

            def chunk(part):
                at = pl.ds(pl.multiple_of(i * STRIP, STRIP) + part.start, CHUNK)
                upper = source[at if product is None else part, :]
                unit = normed[at, :].astype(jnp.float32) * inverse
                gain_grads[number : number + 1] += jnp.sum(upper * unit, 0, keepdims=True)
                upper = upper * gain
                mean = jnp.sum(upper, 1, keepdims=True) * (1.0 / width)
                tilt = jnp.sum(upper * unit, 1, keepdims=True) * (1.0 / width)
                before = low[at, :].astype(jnp.float32) if fresh else grad[at, :]
                row_scale = row_scales[at, number : number + 1]
                after = before + (upper - mean - unit * tilt) * row_scale
                grad[at, :] = after
                low[at, :] = after.astype(jnp.bfloat16)

            chunks(chunk)

        strips(one, image)

    ready(0, 1)
    weight_grad(0, 0, first, low, 1024)
    fetch(6, self_att, first)
    ready(2, 3)
    through_slope(third)
    fetch(7, wos, third)
    fetch(8, slope_c, slope)
    reduce.run(("c1", 0))
    ready(4)
    weight_grad(1, 1, second, back_low, 1024)
    reduce.run(("c2", 0), ("c1", 1))
    ready(5)
    through_norm(0, second, lambda strip: right_matmul(back_low[strip, :], fourth[...]), True)
    fetch(9, normed_self, second)
    half = 3 * head_grad.shape[1] // 4
    fetch(10, wqkv.at[:, :half], fourth.at[:, :half])
    fetch(11, packed.at[:, :half], back_low.at[:, :half])
    reduce.run(("c2", 1))

    ready(6)
    weight_grad(2, 0, first, low, 1024)
    fetch(12, packed.at[:, half : 2 * half], first.at[:, :half])
    reduce.run(("c1", 2))
    ready(7, 9)
    acc[...] = jnp.zeros_like(acc)
    rows_of_image = means.shape[2]
    width = half // 6
    for pair in range(4):
        ready(11 + pair)
        block = (back_low, first)[pair % 2]

        def unit(i, carry, pair=pair, block=block):
            image, head = i // 2, i % 2
            rows = pl.ds(pl.multiple_of(image * rows_of_image, rows_of_image), rows_of_image)

            def columns(part):
                start = pl.multiple_of(head * (3 * width) + part * width, width)
                return pl.ds(start, width)

            query, key, value = (block[rows, columns(part)] for part in range(3))
            out_rows_ = pl.ds(pl.multiple_of((pair * 2 + head) * width, width), width)
            upper = right_matmul(low[rows, :], third[out_rows_, :])
            upper = upper.astype(jnp.bfloat16)
            scores = right_matmul(key, query) * scale
            weights = jnp.exp(scores - jnp.max(scores, 0, keepdims=True))
            weights = weights * (1.0 / jnp.sum(weights, 0, keepdims=True))
            slopes = right_matmul(value, upper)
            lift = jnp.sum(weights * slopes, 0, keepdims=True)
            grad_scores = (weights * (slopes - lift)).astype(jnp.bfloat16)
            head_grad[rows, columns(0)] = (left_matmul(grad_scores, key) * scale).astype(
                jnp.bfloat16
            )
            head_grad[rows, columns(1)] = (matmul(grad_scores, query) * scale).astype(
                jnp.bfloat16
            )
            head_grad[rows, columns(2)] = matmul(weights.astype(jnp.bfloat16), upper).astype(
                jnp.bfloat16
            )
            return carry

        lax.fori_loop(0, 4, unit, 0)
        if pair < 2:
            start = (pair + 2) * half
            fetch(13 + pair, packed.at[:, start : start + half], block.at[:, :half])
        reduce.run(
            *((("c2", 2), ("x1", 0)), (("c2", 3), ("y", 0), ("x1", 1)), (("c2", 4), ("z", 0), ("y", 1), ("x1", 2)), (("c2", 5), ("b", 0), ("z", 1), ("y", 2), ("x1", 3)))[pair]
        )
        weight_grad(3 + pair, (pair + 1) % 2, second, head_grad, half)
        ready(10 if pair == 0 else 15 + pair)

        def spread(i, strip):
            acc[strip, :] += right_matmul(head_grad[strip, :half], fourth[:, :half])

        strips(spread)
        if pair < 3:
            start = (pair + 1) * half
            fetch(16 + pair, wqkv.at[:, start : start + half], fourth.at[:, :half])
        reduce.run(
            *((("c1", 3), ("x2", 0)), (("c1", 4), ("x2", 1)), (("c1", 5), ("x2", 2)), (("c1", 6), ("x2", 3)))[pair]
        )
    fetch(20, active_c, first)
    fetch(21, w2c, third)
    fetch(22, w1c, fourth)
    through_norm(1, second, None)
    fetch(23, normed_c, second)
    reduce.run(("c2", 6), ("y", 3), ("b", 1), ("z", 2), ("x1", 4))

    ready(20)
    weight_grad(7, 1, first, low, 1024)
    fetch(25, wo, first)
    reduce.run(("x2", 4))
    ready(21, 8, 22, 23, 25)
    micros = means.shape[0]
    grad_sems = (grad_send, grad_recv)
    along = {}

    def upper_rows(i, strip):
        head_grad[strip, :] = right_matmul(low[strip, :], first[...]).astype(jnp.bfloat16)

    for m in range(micros):
        through_slope(third, m)
        through_norm(
            2, second, lambda strip: right_matmul(back_low[strip, :], fourth[...]), False, m
        )
        strips(upper_rows, m)
        rows = pl.ds(m * rows_of_image, rows_of_image)
        sums = right_matmul(value_n[...], head_grad[rows, :]) / rows_in[m, 0:1]
        grad_den = -jnp.sum(sums * means[m].astype(jnp.float32), 0, keepdims=True)
        packed_grads[m, : FROWS - 16] = sums[: FROWS - 16].astype(jnp.bfloat16)
        at = lax.broadcasted_iota(jnp.int32, (16, sums.shape[1]), 0) + (FROWS - 16)
        tail = with_rows(sums[FROWS - 16 :], grad_den, rows_in[m, 1:2])
        packed_grads[m, FROWS - 16 :] = jnp.where(at == DEN_ROW + 1, 0.0, tail).astype(
            jnp.bfloat16
        )
        mine, home = packed_grads.at[m], all_grads[m].at[z, y]
        for i in (1, 2, 3):
            target = device(x, c, (z + i) % 4, y)
            along[m, i] = remote(mine, home, grad_sems, (m, i - 1), target)
            along[m, i].start()
        along[m, 4] = remote(mine, home, grad_sems, (m, 3), reduce.beside)
        along[m, 4].start()
        fetch(26 + m, mine, home)
        reduce.run(
            *(
                (("c1", 7), ("y", 4), ("z", 3), ("b", 2), ("x1", 5)),
                (("c2", 7), ("x2", 5)),
            )[m]
        )
    fetch(24, att_low, third)

    def pass_grads(m):
        for i in (1, 2, 3):
            along[m, i].wait_recv()
            block = all_grads[m].at[(z + 4 - i) % 4, y]
            along[m, 4 + i] = remote(block, block, grad_sems, (m, 3 + i), reduce.beside)
            along[m, 4 + i].start()

    def grads_ready(m):
        ready(26 + m)
        for i in range(4, 8):
            along[m, i].wait_recv()

    weight_grad(8, 0, second, back_low, 1024)
    pass_grads(0)
    reduce.run(("c1", 8), ("y", 5), ("z", 4), ("b", 3), ("x1", 6))
    ready(24)
    weight_grad(9, 1, third, low, 1024)
    reduce.run(("c2", 8), ("x2", 6), ("c1", 9))
    value_grad = sum(
        matmul(means[m], head_grad[m * rows_of_image : (m + 1) * rows_of_image, :])
        for m in range(micros)
    )
    staged = staging[2]
    shards = [
        jnp.concatenate(
            [
                value_grad[:, s * 128 : (s + 1) * 128],
                gain_grads[:, s * 128 : (s + 1) * 128],
                jnp.zeros((320 - FROWS - 8, 128), jnp.float32),
            ],
            0,
        )
        for s in range(8)
    ]
    for s in range(8):
        staged[s // 2, s % 2] = shards[s].reshape(2, 2, 80, 128).astype(jnp.bfloat16)
    reduce.push(10, 2)
    reduce.release(0)
    staged = staging[0]
    for s in range(8):
        at = s * 64
        both = grad[at : at + 64, :] + grad[at + rows_of_image : at + rows_of_image + 64, :]
        staged[s // 2, s % 2, :, :, :16] = both.reshape(2, 2, 16, both.shape[1]).astype(
            jnp.bfloat16
        )
    reduce.push(11, 0)
    reduce.run(("c2", 9), ("c1", 10), ("y", 6), ("c2", 10), ("c1", 11), ("z", 5), ("c2", 11), ("b", 4))

    slots = pixels.shape[2]
    blocks = slots // BLOCK
    pieces = BLOCK // PIECE
    halves = BLOCK // out_tile.shape[2]
    query_sums[...] = jnp.zeros_like(query_sums)
    gain_sums[...] = jnp.zeros_like(gain_sums)
    scores_ref, back_ref, wide = low, acc, slope
    weight_slots = (first, second)

    def block_loads(m, b):
        rows = pl.ds(b * BLOCK, BLOCK)
        slot = b % 2
        return (
            pltpu.make_async_copy(pixels.at[m, :, rows], raw.at[slot], block_load.at[0, slot]),
            pltpu.make_async_copy(
                pix_weights.at[m, rows],
                weight_slots[slot].at[:, :rows_of_image],
                block_load.at[1, slot],
            ),
        )

    def block_store(m, b, part):
        rows = pl.ds(b * BLOCK + part * (BLOCK // halves), BLOCK // halves)
        return pltpu.make_async_copy(
            out_tile.at[part], pixel_out.at[m, :, rows], block_out.at[part]
        )

    def pixels_back(m, after):
        for copy in block_loads(m, 0):
            copy.start()
        for b in range(blocks):
            if b + 1 < blocks:
                for copy in block_loads(m, b + 1):
                    copy.start()
            for copy in block_loads(m, b):
                copy.wait()
            normed, unit_, row_scale = normed_block(raw[b % 2], pix_gain[...], features)
            wide[:FROWS, :] = normed
            weights = weight_slots[b % 2]

            def piece(k, carry, b=b, weights=weights):
                rows = pl.ds(pl.multiple_of(k * PIECE, PIECE), PIECE)
                number = b * pieces + k
                seg = segs[m, number]
                image = jnp.minimum(seg, images - 1)
                upper = all_grads[m][image // 2, image % 2]
                unused, top = read_rows(upper[FROWS - 16 :].astype(jnp.float32))
                factor = jnp.where(seg < images, jnp.exp(tops[m, number] - top), 0.0)
                full = weights[rows, :rows_of_image].astype(jnp.float32) * factor
                slopes = left_matmul(wide[:FROWS, rows], upper)
                scores_ref[rows, :rows_of_image] = (full * slopes).astype(jnp.bfloat16)
                back_ref[:FROWS, rows] = right_matmul(upper, full.astype(jnp.bfloat16))
                return carry

            lax.fori_loop(0, pieces, piece, 0)
            scores = scores_ref[:, :rows_of_image]
            query_sums[...] += matmul(wide[:FROWS, :], scores)
            back = back_ref[:FROWS, :] + right_matmul(queries[...], scores)
            at = lax.broadcasted_iota(jnp.int32, back.shape, 0)
            back = jnp.where(at < features, back, 0.0)
            product = back * unit_
            gain_sums[:FROWS] += sum(
                product[:, j * 128 : (j + 1) * 128] for j in range(BLOCK // 128)
            )
            back = back * pix_gain[...]
            mean = jnp.sum(back, 0, keepdims=True) * (1.0 / features)
            tilt = jnp.sum(back * unit_, 0, keepdims=True) * (1.0 / features)
            result = (back - mean - unit_ * tilt) * row_scale
            size = BLOCK // halves
            for part in range(halves):
                if m or b:
                    block_store(m, b, part).wait()
                out_tile[part] = result[:, part * size : (part + 1) * size]
                block_store(m, b, part).start()
            reduce.run(*after[b])

    pass_grads(1)
    grads_ready(0)
    pixels_back(
        0,
        (
            (("x1", 7), ("x2", 7)),
            (("z", 6), ("b", 5), ("y", 7)),
            (("x1", 8), ("x2", 8)),
            (("z", 7), ("b", 6), ("y", 8)),
        ),
    )
    grads_ready(1)
    pixels_back(1, ((("x1", 9), ("x2", 9)), (("z", 8), ("b", 7)), (("x1", 10), ("x2", 10), ("x1", 11), ("x2", 11)), (("y", 9),)))
    for part in range(halves):
        block_store(0, 0, part).wait()

    sums = query_sums[...]
    at = lax.broadcasted_iota(jnp.int32, sums.shape, 0)
    gain_row = jnp.sum(gain_sums[...].T, 0, keepdims=True)
    gain_row = jnp.concatenate([gain_row, jnp.zeros((1, 128), jnp.float32)], 1)
    sums = jnp.where(at == GAIN_ROW, gain_row, sums)
    for j in range(4):
        sum_parts[j // 2, j % 2] = sums[:, j * 128 : (j + 1) * 128].astype(jnp.bfloat16)
    sum_sems = (sum_send, sum_recv)
    copies = [remote(sum_parts.at[1 - c], sum_core, sum_sems, 0, reduce.core)]
    copies[0].start()
    reduce.run(("y", 10), ("y", 11), ("z", 9), ("b", 8))
    copies[0].wait_recv()
    sum_parts[c] = sum_parts[c] + sum_core[...]
    copies.append(remote(sum_parts.at[c, 1 - x], sum_over, sum_sems, 1, reduce.across))
    copies[1].start()
    reduce.run(("z", 10), ("z", 11))
    copies[1].wait_recv()
    sum_parts[c, x] = sum_parts[c, x] + sum_over[...]
    copies.append(remote(sum_parts.at[c, x], sum_side, sum_sems, 2, reduce.beside))
    copies[2].start()
    reduce.run(("b", 9))
    copies[2].wait_recv()
    sum_along[z] = sum_parts[c, x] + sum_side[...]
    for i in (1, 2, 3):
        target = device(x, c, (z + i) % 4, y)
        copies.append(remote(sum_along.at[z], sum_along.at[z], sum_sems, 2 + i, target))
        copies[2 + i].start()
    reduce.run(("b", 10), ("b", 11))
    for i in (1, 2, 3):
        copies[2 + i].wait_recv()
    total = sum(sum_along[i].astype(jnp.float32) for i in range(4))
    query_out[c, x] = total.astype(jnp.bfloat16)
    copies.append(remote(query_out.at[c, x], query_out.at[c, x], sum_sems, 6, reduce.across))
    copies[6].start()
    copies[6].wait_recv()
    copies.append(remote(query_out.at[c], query_out.at[c], sum_sems, 7, reduce.core))
    copies[7].start()
    copies[7].wait_recv()
    for copy in copies:
        copy.wait_send()
    for copy in along.values():
        copy.wait_send()
    for copy in homes:
        copy.wait()
    reduce.finish()


def closing(
    segs,
    pixels,
    pix_weights,
    cot,
    final,
    final_kept,
    self_att,
    packed,
    normed_self,
    cross_kept,
    att_low,
    weights,
    row_scales,
    gains,
    means,
    rows,
    value_n,
    queries,
    tops,
    pix_gain,
    features,
    images,
    scale,
):
    bf16, f32 = jnp.bfloat16, jnp.float32
    total_rows, width = cot.shape
    micros, unused, slots = pixels.shape
    latents = means.shape[2]
    half = 3 * width // 4
    full, part = (STRIP // 8, width), (STRIP // 8, half)
    shapes = [full] * 3 + [part] * 4 + [full] * 3 + [(80, 128), (16, width)]
    count = len(shapes)

    def grid(*lead):
        return [(*lead, *shape) for shape in shapes]

    def scratch(shape, dtype=bf16):
        return pltpu.VMEM(shape, dtype)

    def arrays(list_):
        return [jax.ShapeDtypeStruct(shape, bf16) for shape in list_]

    square = (total_rows, width)
    quarter = (FROWS, 128)
    smem = pl.BlockSpec(memory_space=pltpu.SMEM)
    results = pl.pallas_call(
        functools.partial(closing_kernel, scale, images, features),
        out_shape=[
            *arrays(grid(2, 2)),
            *arrays(grid(4, 2, 2)),
            *arrays(grid(4, 2)),
            jax.ShapeDtypeStruct(final.shape, bf16),
            jax.ShapeDtypeStruct(pixels.shape, f32),
            jax.ShapeDtypeStruct((2, 2, *quarter), bf16),
        ],
        in_specs=[smem] + [HBM] * 21 + [VMEM] * 8,
        out_specs=[VMEM] * count + [HBM] * (2 * count + 2) + [VMEM],
        scratch_shapes=[
            *map(scratch, grid(4, 2, 2)),
            *map(scratch, grid(4)),
            *map(scratch, grid(3)),
            *[scratch((4, 2, 2, 2, *shape)) for shape in (full, full, shapes[10])],
            *[
                scratch((4, 2, *lead, *shape))
                for shape in (full, shapes[10])
                for lead in ((2,), ())
            ],
            scratch(square, f32),
            scratch(square, f32),
            *[scratch(square) for _ in range(7)],
            scratch(square),
            scratch((8, width), f32),
            scratch((micros, FROWS, latents)),
            *[scratch((4, 2, FROWS, latents)) for _ in range(micros)],
            scratch((2, FROWS, BLOCK)),
            scratch((2, FROWS, BLOCK // 2), f32),
            scratch((FROWS, latents), f32),
            scratch((384, 128), f32),
            scratch((2, 2, *quarter)),
            scratch((2, *quarter)),
            scratch(quarter),
            scratch(quarter),
            scratch((4, *quarter)),
            pltpu.SemaphoreType.DMA((count, 8)),
            pltpu.SemaphoreType.DMA((count, 8)),
            pltpu.SemaphoreType.DMA((count, 3)),
            pltpu.SemaphoreType.DMA((32,)),
            pltpu.SemaphoreType.DMA((7,)),
            pltpu.SemaphoreType.DMA((7,)),
            pltpu.SemaphoreType.DMA((micros, 7)),
            pltpu.SemaphoreType.DMA((micros, 7)),
            pltpu.SemaphoreType.DMA((2, 2)),
            pltpu.SemaphoreType.DMA((2,)),
            pltpu.SemaphoreType.DMA((8,)),
            pltpu.SemaphoreType.DMA((8,)),
        ],
        compiler_params=remote_params(1, 64 * MIB - 1024),
        name="closing",
    )(
        segs,
        pixels,
        pix_weights,
        cot,
        final,
        *final_kept,
        self_att,
        packed,
        normed_self,
        *cross_kept,
        att_low,
        *weights,
        row_scales,
        gains,
        means,
        rows,
        value_n,
        queries,
        tops,
        pix_gain,
    )
    shards = [
        result.reshape(4 * shape[0], shape[1])
        for result, shape in zip(results[:count], shapes, strict=True)
    ]
    query_sums = results[-1].reshape(4, *quarter).transpose(1, 0, 2).reshape(FROWS, latents)
    return shards, results[-3], results[-2], query_sums


def image_body(
    image_sides,
    pixels,
    latent_array,
    pixel_gain,
    latent_gain,
    query_weight,
    key_weight,
    value_weight,
    cross_out_weight,
    cross_mlp_gain,
    cross_mlp_in,
    cross_mlp_out,
    self_gain,
    self_qkv_weight,
    self_out_weight,
    self_mlp_gain,
    self_mlp_in,
    self_mlp_out,
    cotangent,
):
    position = lax.axis_index("pix")
    micros, images = image_sides.shape[1:]
    capacity, features = pixels.shape[2:]
    row_count, width = latent_array.shape
    latents = row_count * 8
    head_size = width // HEADS
    cross_scale = width ** (-0.5)
    self_scale = head_size ** (-0.5)
    f32, bf16 = jnp.float32, jnp.bfloat16

    def widen(values, columns):
        return jnp.pad(values, ((0, 0), (0, columns - values.shape[1])))

    gains = jnp.stack([latent_gain, cross_mlp_gain, self_gain, self_mlp_gain], 1)
    gains = jnp.pad(gains, ((0, 0), (GAIN_LANE, 384 - GAIN_LANE - 4)))
    shards = (
        latent_array,
        query_weight,
        widen(key_weight.T, 384) + gains,
        widen(value_weight.T, 384),
        cross_out_weight,
        cross_mlp_in,
        cross_mlp_out,
        self_qkv_weight,
        self_out_weight,
        self_mlp_in,
        self_mlp_out,
    )
    splits = (True,) * len(shards)
    lengths = image_sides[0] * image_sides[0]
    ends = jnp.cumsum(lengths, 1)
    firsts = position * capacity + PIECE * jnp.arange(capacity // PIECE, dtype=jnp.int32)
    segs = jnp.sum((firsts[None, :, None] >= ends[:, None, :]).astype(jnp.int32), 2)
    same = jnp.pad((segs[:, 1:] == segs[:, :-1]).astype(jnp.int32), ((0, 0), (1, 0)))
    here = segs[:, :, None] == jnp.arange(images, dtype=jnp.int32)[None, None, :]
    order = jnp.arange(capacity // PIECE, dtype=jnp.int32)[None, :, None]
    last = jnp.max(jnp.where(here, order, -1), 1)
    gain_pix = jnp.pad(pixel_gain.astype(f32), (0, FROWS - features))[:, None]
    pixel_rows = jnp.pad(
        pixels[0].transpose(0, 2, 1), ((0, 0), (0, FROWS - features), (0, 0))
    )
    wholes, results = opening(
        same,
        last,
        shards,
        splits,
        pixel_rows,
        cotangent[0],
        gain_pix,
        features,
        cross_scale,
    )
    lat_full, wq, key_t, value_t, wo, w1c, w2c, wqkv, wos, w1s, w2s = wholes
    pix_weights, cot_rows, *kept = results[:13]
    normed_c, active_c, slope_c, normed_self, packed, self_att = kept[:6]
    normed_m, active_s, slope_s, att_low, final = kept[6:]
    normed_lat, queries, query_t, pix_tops, means, rows, row_scales, gain_rows = results[13:]
    final = final.reshape(micros, 8, row_count, width)
    lat_f = lat_full.astype(f32)

    shards, latent_out, pixel_grad, query_sums = closing(
        segs,
        pixel_rows,
        pix_weights,
        cot_rows.reshape(-1, width),
        final,
        (normed_m, active_s, slope_s),
        self_att,
        packed,
        normed_self,
        (normed_c, active_c, slope_c),
        att_low,
        (w2s, w1s, wos, wqkv, w2c, w1c, wo),
        row_scales,
        gain_rows,
        means,
        rows,
        value_t[:, :FROWS].T,
        query_t,
        pix_tops,
        gain_pix,
        features,
        images,
        head_size ** (-0.5),
    )
    f_w2s, f_w1s, f_wos, *f_qkv, f_w2c, f_w1c, f_wo, f_vec, f_lat = shards
    d_gpix = query_sums[GAIN_ROW, :features].astype(f32)

    grad_queries = lax.dot_general(
        query_sums, key_t[:, :FROWS], (((0,), (1,)), ((), ())), preferred_element_type=f32
    )
    grad_queries = (grad_queries * cross_scale).astype(bf16)
    columns = lax.dynamic_slice_in_dim(normed_lat, position * (width // 8), width // 8, 1)
    d_wq = left_matmul(columns, grad_queries)
    query_columns = lax.dynamic_slice_in_dim(queries, position * (width // 8), width // 8, 1)
    d_wk = matmul(query_sums[:features], query_columns) * cross_scale
    grad_norm_lat, d_glat = norm_back(lat_f, gain_rows[0], right_matmul(grad_queries, wq))
    d_glat = lax.dynamic_slice_in_dim(d_glat, position * (width // 8), width // 8, 0)
    grad_norm_rows = lax.dynamic_slice_in_dim(grad_norm_lat, position * row_count, row_count, 0)
    return (
        latent_out[None],
        pixel_grad[:, :features].transpose(0, 2, 1)[None],
        f_lat.astype(f32) + grad_norm_rows,
        d_gpix,
        d_glat,
        d_wq,
        d_wk,
        f_vec[:features].astype(f32),
        f_wo.astype(f32),
        f_vec[FROWS + 2].astype(f32),
        f_w1c.astype(f32),
        f_w2c.astype(f32),
        f_vec[FROWS + 1].astype(f32),
        jnp.concatenate(f_qkv, 1).astype(f32),
        f_wos.astype(f32),
        f_vec[FROWS].astype(f32),
        f_w1s.astype(f32),
        f_w2s.astype(f32),
    )


def solution(mesh):
    fits = dict(mesh.shape) == {"dp": 4, "pix": 8}
    return jax.shard_map(
        image_body if fits else starting_body,
        mesh=mesh,
        in_specs=(
            P("dp", None, None),
            P("dp", None, "pix", None),
            P("pix", None),
            P(),
            P("pix"),
            P("pix", None),
            P(None, "pix"),
            P(None, "pix"),
            P("pix", None),
            P("pix"),
            P("pix", None),
            P("pix", None),
            P("pix"),
            P("pix", None),
            P("pix", None),
            P("pix"),
            P("pix", None),
            P("pix", None),
            P("dp", None, None, "pix", None),
        ),
        out_specs=(
            P("dp", None, None, "pix", None),
            P("dp", None, "pix", None),
            P("pix", None),
            P(),
            P("pix"),
            P("pix", None),
            P(None, "pix"),
            P(None, "pix"),
            P("pix", None),
            P("pix"),
            P("pix", None),
            P("pix", None),
            P("pix"),
            P("pix", None),
            P("pix", None),
            P("pix"),
            P("pix", None),
            P("pix", None),
        ),
        check_vma=False,
    )
```
